32 devices in a mesh: ctx: 8 (over y, x, core), tp: 4 (over z).
Axes of the slice: x: 2, y: 2, z: 4, core: 2. Of those that a mesh axis runs over, the one named last changes fastest.
Arguments:
- tokens: bfloat16 [12288, 2048], P(('ctx', 'tp')), may hold values from -6 to 6
- teacher: bfloat16 [12288, 2048], P(('ctx', 'tp')), may hold values from -6 to 6
- seq_lens: int32 [3], replicated, may hold values from 1024 to 4096, as said below
- block_order: int32 [3, 16], replicated, may hold values from 0 to 15, each once within a row
- in_gain: float32 [2048], replicated, may hold values from 0.5 to 1.5
- w_query: bfloat16 [2048, 2048], P('ctx', 'tp'), may hold values from -0.125 to 0.125
- key_weight_matrix: bfloat16 [2048, 1024], P('ctx', 'tp'), may hold values from -0.125 to 0.125
- value_weight_matrix: bfloat16 [2048, 1024], P('ctx', 'tp'), may hold values from -0.125 to 0.125
- q_gain: float32 [128], replicated, may hold values from 0.5 to 1.5
- k_gain: float32 [128], replicated, may hold values from 0.5 to 1.5
- w_out: bfloat16 [2048, 2048], P('tp', 'ctx'), may hold values from -1 to 1
- post_gain: float32 [2048], replicated, may hold values from 0.5 to 1.5
- w_gate: bfloat16 [2048, 6144], P('ctx', 'tp'), may hold values from -0.125 to 0.125
- w_up: bfloat16 [2048, 6144], P('ctx', 'tp'), may hold values from -0.125 to 0.125
- w_down: bfloat16 [6144, 2048], P('tp', 'ctx'), may hold values from -0.078125 to 0.078125
Outputs:
- output: bfloat16 [12288, 2048], P(('ctx', 'tp'))
- loss: float32 [], replicated
- d_tokens: bfloat16 [12288, 2048], P(('ctx', 'tp'))
- grad_in_gain: float32 [2048], replicated
- grad_w_query: float32 [2048, 2048], P('ctx', 'tp')
- grad_w_key: float32 [2048, 1024], P('ctx', 'tp')
- grad_w_value: float32 [2048, 1024], P('ctx', 'tp')
- grad_q_gain: float32 [128], replicated
- grad_k_gain: float32 [128], replicated
- grad_w_out: float32 [2048, 2048], P('tp', 'ctx')
- grad_post_gain: float32 [2048], replicated
- grad_w_gate: float32 [2048, 6144], P('ctx', 'tp')
- grad_w_up: float32 [2048, 6144], P('ctx', 'tp')
- grad_w_down: float32 [6144, 2048], P('tp', 'ctx')
The draws below stay inside these ranges and needn't reach their ends.
Inputs may be any that keep to these rules, and one draw needn't show every extreme that they name: `seq_lens`: one sequence, drawn from the seed, has all 4096 slots valid. `block_order`: each row names every block of its sequence once.
All inputs are finite; a program needn't handle non-finite values.
Results may differ from the reference program's by a relative error of at most 0.024.
Values may be sent and summed in bfloat16 or wider, within the bound.
A program may use at most 256 MiB of HBM per device.

```python
import math
import jax
import jax.numpy as jnp
from jax import lax

MODEL_WIDTH = 2048
QUERY_HEADS = 16
KEY_VALUE_HEADS = 8
HEAD_SIZE = 128
FF = 6144
SEQS = 3
BLK = 256
SEQLEN = 4096
TOKENS = 12288
N_CTX = 8


def draw_seq_lens(key, part):
    key = jax.random.fold_in(key, 7)
    first_key, second_key = jax.random.split(key)
    lengths = jax.random.randint(first_key, (SEQS,), SEQLEN // 4, SEQLEN + 1)
    chosen = jax.random.randint(second_key, (), 0, SEQS)
    return jnp.where(jnp.arange(SEQS) == chosen, SEQLEN, lengths).astype(jnp.int32)


def level_of(key, shape, cuts, low, largest):
    def one(position, shards_of):
        steps = jax.random.uniform(jax.random.fold_in(jax.random.fold_in(key, 6), position), (shards_of,), jnp.float32, low / len(cuts), largest / len(cuts))
        return jnp.repeat(jnp.exp(steps), shape[position] // shards_of).reshape((-1,) + (1,) * (len(shape) - position - 1))

    level = one(*cuts[0])
    for cut in cuts[1:]:
        level = level * one(*cut)
    return level


def scatter_about(own_key, dims, deviation, reach, shards=(), held_as=jnp.bfloat16):
    array = deviation * jax.random.normal(own_key, dims, jnp.float32)
    if shards:
        array = array * level_of(own_key, dims, shards, -0.22, 0.18)
    return jnp.clip(array, -reach, reach).astype(held_as)


def setup_inputs(seed: int = 0) -> dict:
    arg_keys = jax.random.split(jax.random.key(seed), 16)
    tokens = scatter_about(arg_keys[0], (TOKENS, MODEL_WIDTH), 1.0, 6.0, ((0, 32),))
    teacher = scatter_about(arg_keys[1], (TOKENS, MODEL_WIDTH), 1.0, 6.0, ((0, 32),))
    seq_lens = draw_seq_lens(jax.random.fold_in(arg_keys[15], 71), 0)
    block_order = jax.vmap(lambda own: jax.random.permutation(own, 2 * N_CTX))(jax.random.split(arg_keys[3], SEQS)).reshape((SEQS, 2 * N_CTX)).astype(jnp.int32)
    in_gain = jnp.clip(1.0 + 0.1 * jax.random.normal(arg_keys[4], (MODEL_WIDTH,), jnp.float32), 0.5, 1.5)
    w_query = scatter_about(arg_keys[5], (MODEL_WIDTH, QUERY_HEADS * HEAD_SIZE), MODEL_WIDTH ** -0.5, 0.125, ((0, 8), (1, 4)))
    key_weight_matrix = scatter_about(arg_keys[6], (MODEL_WIDTH, KEY_VALUE_HEADS * HEAD_SIZE), MODEL_WIDTH ** -0.5, 0.125, ((0, 8), (1, 4)))
    value_weight_matrix = scatter_about(arg_keys[7], (MODEL_WIDTH, KEY_VALUE_HEADS * HEAD_SIZE), MODEL_WIDTH ** -0.5, 0.125, ((0, 8), (1, 4)))
    q_gain = jnp.clip(1.0 + 0.1 * jax.random.normal(arg_keys[8], (HEAD_SIZE,), jnp.float32), 0.5, 1.5)
    k_gain = jnp.clip(1.0 + 0.1 * jax.random.normal(arg_keys[9], (HEAD_SIZE,), jnp.float32), 0.5, 1.5)
    w_out = scatter_about(arg_keys[10], (QUERY_HEADS * HEAD_SIZE, MODEL_WIDTH), (QUERY_HEADS * HEAD_SIZE // 64) ** -0.5, 1.0, ((0, 4), (1, 8)))
    post_gain = jnp.clip(1.0 + 0.1 * jax.random.normal(arg_keys[11], (MODEL_WIDTH,), jnp.float32), 0.5, 1.5)
    w_gate = scatter_about(arg_keys[12], (MODEL_WIDTH, FF), MODEL_WIDTH ** -0.5, 0.125, ((0, 8), (1, 4)))
    w_up = scatter_about(arg_keys[13], (MODEL_WIDTH, FF), MODEL_WIDTH ** -0.5, 0.125, ((0, 8), (1, 4)))
    w_down = scatter_about(arg_keys[14], (FF, MODEL_WIDTH), FF ** -0.5, 0.078125, ((0, 4), (1, 8)))
    return {"tokens": tokens, "teacher": teacher, "seq_lens": seq_lens, "block_order": block_order, "in_gain": in_gain, "w_query": w_query, "key_weight_matrix": key_weight_matrix, "value_weight_matrix": value_weight_matrix, "q_gain": q_gain, "k_gain": k_gain, "w_out": w_out, "post_gain": post_gain, "w_gate": w_gate, "w_up": w_up, "w_down": w_down}


EPS = 1e-06
THETA = 1000000.0
FLOOR = -1e+30

@jax.custom_vjp
def reduced_precision(v):
    return lax.optimization_barrier(v.astype(jnp.bfloat16)).astype(jnp.float32)

@jax.custom_vjp
def reduced_backward(v):
    return v

def low_keep(v):
    return (reduced_precision(v), None)

def low_pass(kept, grad):
    return (grad,)

def back_keep(v):
    return (v, None)

def back_low(kept, grad):
    return (reduced_precision(grad),)
reduced_precision.defvjp(low_keep, low_pass)
reduced_backward.defvjp(back_keep, back_low)

def matrix_product(left, right):
    return jnp.dot(left, right, precision=lax.Precision.HIGHEST, preferred_element_type=jnp.float32)

def rms_norm(value, gain):
    return value * lax.rsqrt(lax.optimization_barrier(jnp.mean(value * value, axis=-1, keepdims=True)) + EPS) * gain

def rotate(value, cosine, sine):
    half = value.shape[-1] // 2
    first = value[..., :half]
    second = value[..., half:]
    return jnp.concatenate([first * cosine - second * sine, second * cosine + first * sine], axis=-1)

def per_sequence_rows(value):
    trailing = value.shape[1:]
    value = value.reshape((N_CTX, SEQS, 2 * BLK) + trailing)
    return jnp.swapaxes(value, 0, 1).reshape((SEQS, N_CTX * 2 * BLK) + trailing)

def by_device(value):
    trailing = value.shape[2:]
    value = value.reshape((SEQS, N_CTX, 2 * BLK) + trailing)
    return jnp.swapaxes(value, 0, 1).reshape((N_CTX * SEQS * 2 * BLK,) + trailing)

def attend_block(query_rows_all, query_pos, keys, value_rows, key_pos, length):
    scores = jnp.einsum('qkgd,lkd->kgql', query_rows_all, keys, precision=lax.Precision.HIGHEST) * HEAD_SIZE ** (-0.5)
    allowed = (key_pos[None, :] <= query_pos[:, None]) & (key_pos[None, :] < length)
    scores = reduced_backward(jnp.where(allowed[None, None], scores, FLOOR))
    probs = reduced_precision(jax.nn.softmax(scores, axis=-1))
    return jnp.einsum('kgql,lkd->qkgd', probs, value_rows, precision=lax.Precision.HIGHEST)

def attention(query_rows_all, keys, value_rows, positions, lengths):
    group_width = QUERY_HEADS // KEY_VALUE_HEADS
    block_rows = math.gcd(512, N_CTX * 2 * BLK)
    sequence_query_rows = per_sequence_rows(query_rows_all.reshape(-1, KEY_VALUE_HEADS, group_width, HEAD_SIZE))
    seq_keys = per_sequence_rows(keys)
    seq_values = per_sequence_rows(value_rows)
    seq_pos = per_sequence_rows(positions)

    def one_sequence(inputs):
        these_queries, these_keys, these_values, these_pos, length = inputs

        def one_block(pieces):
            return attend_block(pieces[0], pieces[1], these_keys, these_values, these_pos, length)
        blocks = (these_queries.reshape((-1, block_rows) + these_queries.shape[1:]), these_pos.reshape(-1, block_rows))
        return lax.map(jax.checkpoint(one_block), blocks).reshape(these_queries.shape)
    result = lax.map(one_sequence, (sequence_query_rows, seq_keys, seq_values, seq_pos, lengths))
    return by_device(result).reshape(-1, QUERY_HEADS * HEAD_SIZE)

def forward(stream, in_gain, w_query, key_weight_matrix, value_weight_matrix, q_gain, k_gain, w_out, post_gain, w_gate, w_up, w_down, cosine, sine, positions, lengths):
    normalized_input = reduced_precision(rms_norm(stream, in_gain))
    query_lin = reduced_backward(matrix_product(normalized_input, w_query)).reshape(-1, QUERY_HEADS, HEAD_SIZE)
    key_linear = reduced_backward(matrix_product(normalized_input, key_weight_matrix)).reshape(-1, KEY_VALUE_HEADS, HEAD_SIZE)
    value_rows = reduced_backward(reduced_precision(matrix_product(normalized_input, value_weight_matrix))).reshape(-1, KEY_VALUE_HEADS, HEAD_SIZE)
    query_rows_all = reduced_precision(rotate(rms_norm(query_lin, q_gain), cosine, sine))
    keys = reduced_precision(rotate(rms_norm(key_linear, k_gain), cosine, sine))
    mixed = reduced_backward(reduced_precision(attention(query_rows_all, keys, value_rows, positions, lengths)))
    middle = stream + reduced_backward(matrix_product(mixed, w_out))
    post = reduced_precision(rms_norm(middle, post_gain))
    gate = reduced_backward(matrix_product(post, w_gate))
    up_val = reduced_backward(matrix_product(post, w_up))
    hidden = reduced_precision(jax.nn.silu(gate) * up_val)
    return middle + reduced_backward(matrix_product(hidden, w_down))

def reference(tokens, teacher, seq_lens, block_order, in_gain, w_query, key_weight_matrix, value_weight_matrix, q_gain, k_gain, w_out, post_gain, w_gate, w_up, w_down):
    order = jnp.transpose(block_order.reshape(SEQS, N_CTX, 2), (1, 0, 2))
    grid_pos = order[..., None] * BLK + jnp.arange(BLK, dtype=jnp.int32)
    positions = grid_pos.reshape(-1).astype(jnp.int32)
    valid = (grid_pos < seq_lens[None, :, None, None]).reshape(-1).astype(jnp.float32)
    inverse = THETA ** (-jnp.arange(0, HEAD_SIZE, 2, dtype=jnp.float32) / HEAD_SIZE)
    angle = positions.astype(jnp.float32)[:, None] * inverse[None, :]
    cosine = jnp.cos(angle)[:, None, :]
    sine = jnp.sin(angle)[:, None, :]

    def layer(stream, gain_one, query_w, key_w, value_w, gain_q, gain_k, out_w, gain_two, gate_w, up_w, down_w):
        return forward(stream, gain_one, query_w, key_w, value_w, gain_q, gain_k, out_w, gain_two, gate_w, up_w, down_w, cosine, sine, positions, seq_lens)
    result, pull = jax.vjp(layer, tokens.astype(jnp.float32), in_gain, w_query.astype(jnp.float32), key_weight_matrix.astype(jnp.float32), value_weight_matrix.astype(jnp.float32), q_gain, k_gain, w_out.astype(jnp.float32), post_gain, w_gate.astype(jnp.float32), w_up.astype(jnp.float32), w_down.astype(jnp.float32))
    diff = (result - teacher.astype(jnp.float32)) * valid[:, None]
    count = jnp.sum(seq_lens).astype(jnp.float32)
    loss = 0.5 * jnp.sum(diff * diff) / (count * MODEL_WIDTH)
    grads = pull(diff)
    return (result.astype(jnp.bfloat16), loss, grads[0].astype(jnp.bfloat16), grads[1], grads[2], grads[3], grads[4], grads[5], grads[6], grads[7], grads[8], grads[9], grads[10], grads[11])
```

```python
import functools

import jax
import jax.numpy as jnp
from jax import lax
from jax.experimental import pallas as pl
from jax.experimental.pallas import tpu as pltpu
from jax.sharding import PartitionSpec as P

MODEL_WIDTH = 2048
HEAD_SIZE = 128
SEQS = 3
BLK = 256


EPS = 1e-06
THETA = 1000000.0
FLOOR = -1e30


def from_behind(x, axis, by):
    count = lax.axis_size(axis)
    return lax.ppermute(x, axis, [(i, (i + by) % count) for i in range(count)])


def rms_scale(value):
    return lax.rsqrt(jnp.mean(value * value, axis=-1, keepdims=True) + EPS)


def rms_back(value, scale, grad_normed):
    return scale * grad_normed - value * scale**3 * jnp.mean(
        grad_normed * value, axis=-1, keepdims=True
    )


def rotate(value, cosine, sine):
    half = value.shape[-1] // 2
    first = value[..., :half]
    second = value[..., half:]
    return jnp.concatenate(
        [first * cosine - second * sine, second * cosine + first * sine], axis=-1
    )


def rotate_back(grad, cosine, sine):
    half = grad.shape[-1] // 2
    first = grad[..., :half]
    second = grad[..., half:]
    return jnp.concatenate(
        [first * cosine + second * sine, second * cosine - first * sine], axis=-1
    )


def matmul(left, right):
    return jnp.dot(left, right, preferred_element_type=jnp.float32)


def matmul_tn(left, right):
    return lax.dot_general(
        left, right, (((0,), (0,)), ((), ())), preferred_element_type=jnp.float32
    )


def matmul_nt(left, right):
    return lax.dot_general(
        left, right, (((1,), (1,)), ((), ())), preferred_element_type=jnp.float32
    )


def row_slice(value, start, count):
    return lax.dynamic_slice_in_dim(value, start, count, 0)


def local(
    tokens,
    teacher,
    seq_lens,
    block_order,
    in_gain,
    w_query,
    key_weight_matrix,
    value_weight_matrix,
    q_gain,
    k_gain,
    w_out,
    post_gain,
    w_gate,
    w_up,
    w_down,
):
    ctx_count = lax.axis_size("ctx")
    ctx_index = lax.axis_index("ctx")
    tp_index = lax.axis_index("tp")
    tok_rows = tokens.shape[0]
    ctx_rows = tok_rows * lax.axis_size("tp")
    block_span = 2 * BLK
    q_heads = w_query.shape[1] // HEAD_SIZE
    kv_heads = key_weight_matrix.shape[1] // HEAD_SIZE
    group_width = q_heads // kv_heads
    scale_qk = HEAD_SIZE ** (-0.5)
    weights = (
        lax.all_gather(w_query, "ctx", axis=0, tiled=True),
        lax.all_gather(key_weight_matrix, "ctx", axis=0, tiled=True),
        lax.all_gather(value_weight_matrix, "ctx", axis=0, tiled=True),
        lax.all_gather(w_out, "ctx", axis=1, tiled=True),
        lax.all_gather(w_gate, "ctx", axis=0, tiled=True),
        lax.all_gather(w_up, "ctx", axis=0, tiled=True),
        lax.all_gather(w_down, "ctx", axis=1, tiled=True),
    )
    wq_full, wk_full, wv_full, wo_full, wg_full, wu_full, wd_full = weights
    offsets = jnp.arange(BLK, dtype=jnp.int32)

    def block_positions(owner):
        columns = lax.dynamic_slice_in_dim(block_order, 2 * owner, 2, 1)
        return (columns[:, :, None] * BLK + offsets).reshape(SEQS, block_span)

    query_pos = block_positions(ctx_index)
    flat_pos = query_pos.reshape(-1)
    inverse = THETA ** (-jnp.arange(0, HEAD_SIZE, 2, dtype=jnp.float32) / HEAD_SIZE)
    angle = flat_pos.astype(jnp.float32)[:, None] * inverse[None, :]
    cosine = jnp.cos(angle)[:, None, :]
    sine = jnp.sin(angle)[:, None, :]
    stream = tokens.astype(jnp.float32)
    scale_in = rms_scale(stream)
    unit_in = stream * scale_in
    normed_rows = (unit_in * in_gain).astype(jnp.bfloat16)
    normed_all = lax.all_gather(normed_rows, "tp", axis=0, tiled=True)
    query_lin = matmul(normed_all, wq_full).reshape(ctx_rows, q_heads, HEAD_SIZE)
    key_linear = matmul(normed_all, wk_full).reshape(ctx_rows, kv_heads, HEAD_SIZE)
    value_low = (
        matmul(normed_all, wv_full)
        .astype(jnp.bfloat16)
        .reshape(SEQS, block_span, kv_heads, HEAD_SIZE)
    )
    query_scale = rms_scale(query_lin)
    query_unit = query_lin * query_scale
    query_low = (
        rotate(query_unit * q_gain, cosine, sine)
        .astype(jnp.bfloat16)
        .reshape(SEQS, block_span, kv_heads, group_width, HEAD_SIZE)
    )
    key_scale = rms_scale(key_linear)
    key_unit = key_linear * key_scale
    key_low = (
        rotate(key_unit * k_gain, cosine, sine)
        .astype(jnp.bfloat16)
        .reshape(SEQS, block_span, kv_heads, HEAD_SIZE)
    )

    def scores_of(keys, key_pos):
        raw = (
            jnp.einsum("sqkgd,slkd->skgql", query_low, keys, preferred_element_type=jnp.float32)
            * scale_qk
        )
        allowed = (key_pos[:, None, :] <= query_pos[:, :, None]) & (
            key_pos[:, None, :] < seq_lens[:, None, None]
        )
        allowed = allowed[:, None, None, :, :]
        return (jnp.where(allowed, raw, FLOOR), allowed)

    def absorb(state, keys, value_rows, owner):
        running_top, running_total, running_acc = state
        scores, allowed = scores_of(keys, block_positions(owner))
        new_top = jnp.maximum(running_top, jnp.max(scores, axis=-1))
        weights_now = jnp.where(allowed, jnp.exp(scores - new_top[..., None]), 0.0)
        shrink = jnp.exp(running_top - new_top)
        running_total = running_total * shrink + jnp.sum(weights_now, axis=-1)
        running_acc = running_acc * shrink[..., None] + jnp.einsum(
            "skgql,slkd->skgqd",
            weights_now.astype(jnp.bfloat16),
            value_rows,
            preferred_element_type=jnp.float32,
        )
        return (new_top, running_total, running_acc)

    stat_shape = (SEQS, kv_heads, group_width, block_span)
    initial = (
        jnp.full(stat_shape, FLOOR, jnp.float32),
        jnp.zeros(stat_shape, jnp.float32),
        jnp.zeros(stat_shape + (HEAD_SIZE,), jnp.float32),
    )
    first_state = absorb(initial, key_low, value_low, ctx_index)

    def cycle_turn(carry, turn):
        keys, value_rows, state = carry
        keys, value_rows = from_behind((keys, value_rows), "ctx", 1)
        owner = (ctx_index - turn) % ctx_count
        state = absorb(state, keys, value_rows, owner)
        return ((keys, value_rows, state), (keys, value_rows))

    (unused_keys, unused_values, final_state), (kept_keys, kept_values) = lax.scan(
        cycle_turn, (key_low, value_low, first_state), jnp.arange(1, ctx_count, dtype=jnp.int32)
    )
    all_keys = jnp.concatenate([key_low[None], kept_keys], axis=0)
    all_values = jnp.concatenate([value_low[None], kept_values], axis=0)
    top_final, total_final, acc_final = final_state
    log_total = top_final + jnp.log(total_final)
    attn_exact = acc_final / total_final[..., None]
    mixed_low = (
        jnp.transpose(attn_exact, (0, 3, 1, 2, 4))
        .reshape(ctx_rows, q_heads * HEAD_SIZE)
        .astype(jnp.bfloat16)
    )
    middle = stream + lax.psum_scatter(
        matmul(row_slice(mixed_low, jnp.int32(0), lax.axis_size("tp") * tok_rows), wo_full).astype(
            jnp.bfloat16
        ),
        "tp",
        scatter_dimension=0,
        tiled=True,
    ).astype(jnp.float32)
    scale_post = rms_scale(middle)
    unit_post = middle * scale_post
    post_rows = (unit_post * post_gain).astype(jnp.bfloat16)
    post_all = lax.all_gather(post_rows, "tp", axis=0, tiled=True)
    gate = matmul(post_all, wg_full)
    up_val = matmul(post_all, wu_full)
    sigma = jax.nn.sigmoid(gate)
    active = gate * sigma
    hidden_low = (active * up_val).astype(jnp.bfloat16)
    result = middle + lax.psum_scatter(
        matmul(row_slice(hidden_low, jnp.int32(0), lax.axis_size("tp") * tok_rows), wd_full).astype(
            jnp.bfloat16
        ),
        "tp",
        scatter_dimension=0,
        tiled=True,
    ).astype(jnp.float32)
    output = result.astype(jnp.bfloat16)
    valid_all = (query_pos < seq_lens[:, None]).reshape(-1).astype(jnp.float32)
    valid_rows = row_slice(valid_all, tp_index * tok_rows, tok_rows)
    diff = (result - teacher.astype(jnp.float32)) * valid_rows[:, None]
    error_local = jnp.sum(diff * diff)
    diff_low = diff.astype(jnp.bfloat16)
    diff_all = lax.all_gather(diff_low, "tp", axis=0, tiled=True)
    weights_two = (
        lax.all_gather(w_query, "ctx", axis=0, tiled=True),
        lax.all_gather(key_weight_matrix, "ctx", axis=0, tiled=True),
        lax.all_gather(value_weight_matrix, "ctx", axis=0, tiled=True),
        lax.all_gather(w_out, "ctx", axis=1, tiled=True),
        lax.all_gather(w_gate, "ctx", axis=0, tiled=True),
        lax.all_gather(w_up, "ctx", axis=0, tiled=True),
        lax.all_gather(w_down, "ctx", axis=1, tiled=True),
    )
    bq_full, bk_full, bv_full, bo_full, bg_full, bu_full, bd_full = weights_two
    grad_wd = matmul_tn(hidden_low, diff_all)
    d_hidden = matmul_nt(diff_all, bd_full)
    d_gate = (d_hidden * up_val * sigma * (1.0 + gate * (1.0 - sigma))).astype(jnp.bfloat16)
    d_up = (d_hidden * active).astype(jnp.bfloat16)
    grad_wg = matmul_tn(post_all, d_gate)
    grad_wu = matmul_tn(post_all, d_up)
    start = jnp.int32(0)
    d_post = lax.psum_scatter(
        (
            matmul_nt(row_slice(d_gate, start, lax.axis_size("tp") * tok_rows), bg_full)
            + matmul_nt(row_slice(d_up, start, lax.axis_size("tp") * tok_rows), bu_full)
        ).astype(jnp.bfloat16),
        "tp",
        scatter_dimension=0,
        tiled=True,
    ).astype(jnp.float32)
    grad_post_local = jnp.sum(d_post * unit_post, axis=0)
    d_middle = diff + rms_back(middle, scale_post, d_post * post_gain)
    d_mid_low = d_middle.astype(jnp.bfloat16)
    d_mid_all = lax.all_gather(d_mid_low, "tp", axis=0, tiled=True)
    grad_wo = matmul_tn(mixed_low, d_mid_all)
    d_mixed = matmul_nt(d_mid_all, bo_full).astype(jnp.bfloat16)
    d_mixed_grid = jnp.transpose(
        d_mixed.reshape(SEQS, block_span, kv_heads, group_width, HEAD_SIZE), (0, 2, 3, 1, 4)
    )
    delta = jnp.sum(d_mixed_grid.astype(jnp.float32) * attn_exact, axis=-1)

    def revisit(carry, turn):
        grad_queries, grad_keys, grad_values = carry
        owner = (ctx_index - turn) % ctx_count
        keys = all_keys[turn]
        value_rows = all_values[turn]
        scores, allowed = scores_of(keys, block_positions(owner))
        probs = jnp.where(allowed, jnp.exp(scores - log_total[..., None]), 0.0)
        probs_low = probs.astype(jnp.bfloat16)
        d_probs = jnp.einsum(
            "skgqd,slkd->skgql", d_mixed_grid, value_rows, preferred_element_type=jnp.float32
        )
        d_scores = (probs * (d_probs - delta[..., None])).astype(jnp.bfloat16)
        grad_queries = grad_queries + jnp.einsum(
            "skgql,slkd->skgqd", d_scores, keys, preferred_element_type=jnp.float32
        )
        grad_keys = grad_keys + jnp.einsum(
            "skgql,sqkgd->slkd", d_scores, query_low, preferred_element_type=jnp.float32
        )
        grad_values = grad_values + jnp.einsum(
            "skgql,skgqd->slkd", probs_low, d_mixed_grid, preferred_element_type=jnp.float32
        )
        grad_keys, grad_values = (
            from_behind(grad_keys.astype(jnp.bfloat16), "ctx", 1).astype(grad_keys.dtype),
            from_behind(grad_values.astype(jnp.bfloat16), "ctx", 1).astype(grad_values.dtype),
        )
        return ((grad_queries, grad_keys, grad_values), None)

    kv_shape = (SEQS, block_span, kv_heads, HEAD_SIZE)
    start_carry = (
        jnp.zeros(stat_shape + (HEAD_SIZE,), jnp.float32),
        jnp.zeros(kv_shape, jnp.float32),
        jnp.zeros(kv_shape, jnp.float32),
    )
    (grad_queries, grad_keys, grad_values), unused_out = lax.scan(
        revisit, start_carry, jnp.arange(ctx_count, dtype=jnp.int32)
    )
    grad_queries = (
        jnp.transpose(grad_queries, (0, 3, 1, 2, 4)).reshape(ctx_rows, q_heads, HEAD_SIZE)
        * scale_qk
    )
    grad_keys = grad_keys.reshape(ctx_rows, kv_heads, HEAD_SIZE) * scale_qk
    d_values = grad_values.reshape(ctx_rows, kv_heads * HEAD_SIZE).astype(jnp.bfloat16)
    query_back = rotate_back(grad_queries, cosine, sine)
    grad_q_local = jnp.sum(query_back * query_unit, axis=(0, 1))
    d_query_lin = (
        rms_back(query_lin, query_scale, query_back * q_gain)
        .reshape(ctx_rows, q_heads * HEAD_SIZE)
        .astype(jnp.bfloat16)
    )
    key_back = rotate_back(grad_keys, cosine, sine)
    grad_k_local = jnp.sum(key_back * key_unit, axis=(0, 1))
    d_key_lin = (
        rms_back(key_linear, key_scale, key_back * k_gain)
        .reshape(ctx_rows, kv_heads * HEAD_SIZE)
        .astype(jnp.bfloat16)
    )
    grad_wq = matmul_tn(normed_all, d_query_lin)
    grad_wk = matmul_tn(normed_all, d_key_lin)
    grad_wv = matmul_tn(normed_all, d_values)
    start = jnp.int32(0)
    part_query = matmul_nt(row_slice(d_query_lin, start, lax.axis_size("tp") * tok_rows), bq_full)
    part_key = matmul_nt(row_slice(d_key_lin, start, lax.axis_size("tp") * tok_rows), bk_full)
    part_value = matmul_nt(row_slice(d_values, start, lax.axis_size("tp") * tok_rows), bv_full)
    d_normed = lax.psum_scatter(
        (part_query + part_key + part_value).astype(jnp.bfloat16),
        "tp",
        scatter_dimension=0,
        tiled=True,
    ).astype(jnp.float32)
    grad_in_local = jnp.sum(d_normed * unit_in, axis=0)
    d_tokens = (d_middle + rms_back(stream, scale_in, d_normed * in_gain)).astype(jnp.bfloat16)
    summed = (
        lax.psum_scatter(
            grad_wq.astype(jnp.bfloat16), "ctx", scatter_dimension=0, tiled=True
        ).astype(jnp.float32),
        lax.psum_scatter(
            grad_wk.astype(jnp.bfloat16), "ctx", scatter_dimension=0, tiled=True
        ).astype(jnp.float32),
        lax.psum_scatter(
            grad_wv.astype(jnp.bfloat16), "ctx", scatter_dimension=0, tiled=True
        ).astype(jnp.float32),
        lax.psum_scatter(
            grad_wo.astype(jnp.bfloat16), "ctx", scatter_dimension=1, tiled=True
        ).astype(jnp.float32),
        lax.psum_scatter(
            grad_wg.astype(jnp.bfloat16), "ctx", scatter_dimension=0, tiled=True
        ).astype(jnp.float32),
        lax.psum_scatter(
            grad_wu.astype(jnp.bfloat16), "ctx", scatter_dimension=0, tiled=True
        ).astype(jnp.float32),
        lax.psum_scatter(
            grad_wd.astype(jnp.bfloat16), "ctx", scatter_dimension=1, tiled=True
        ).astype(jnp.float32),
    )
    totals = lax.psum(
        (grad_in_local, grad_q_local, grad_k_local, grad_post_local, error_local), ("ctx", "tp")
    )
    count_valid = jnp.sum(seq_lens).astype(jnp.float32)
    loss = 0.5 * totals[4] / (count_valid * MODEL_WIDTH)
    return (
        output,
        loss,
        d_tokens,
        totals[0],
        summed[0],
        summed[1],
        summed[2],
        totals[1],
        totals[2],
        summed[3],
        totals[3],
        summed[4],
        summed[5],
        summed[6],
    )


F32 = jnp.float32
BF16 = jnp.bfloat16
MESH = pl.DeviceIdType.MESH
VMEM_LIMIT = 62 << 20
LOG2E = 1.4426950408889634
UNIT = 128
KEYS = 512
CORE_GROUPS = [[0, 2, 4, 6], [1, 3, 5, 7]]
SIBLING = [(i, i ^ 1) for i in range(8)]


def spec_vmem():
    return pl.BlockSpec(memory_space=pltpu.VMEM)


def spec_any():
    return pl.BlockSpec(memory_space=pl.ANY)


def spec_smem():
    return pl.BlockSpec(memory_space=pltpu.SMEM)


def plane_neighbours():
    me = lax.axis_index("ctx")
    core = lax.rem(me, 2)
    x = lax.rem(me // 2, 2)
    y = me // 4
    sib = me + 1 - 2 * core
    nx = me + 2 - 4 * x
    ny = me + 4 - 8 * y
    dg = nx + 4 - 8 * y
    return me, sib, nx, ny, dg


def greet(devices):
    barrier = pltpu.get_barrier_semaphore()
    for device in devices:
        pl.semaphore_signal(barrier, inc=1, device_id={"ctx": device}, device_id_type=MESH)
    pl.semaphore_wait(barrier, len(devices))


def pick(step, options):
    value = options[0]
    for i in range(1, len(options)):
        value = jnp.where(step == i, options[i], value)
    return value


SUBS = 4


class Gather:
    def __init__(self, x_ref, xs, local_sem, send_sems, recv_sems):
        self.x_ref, self.xs = x_ref, xs
        self.local_sem, self.send_sems, self.recv_sems = local_sem, send_sems, recv_sems
        self.me, self.sib, self.nx, self.ny, self.dg = plane_neighbours()
        self.shift = self.sib - self.me
        self.piece = x_ref.shape[0] // SUBS

    def part(self, block, s):
        return self.xs.at[block, pl.ds(s * self.piece, self.piece)]

    def remote(self, src, kind, block, s, device):
        return pltpu.make_async_remote_copy(
            src_ref=src,
            dst_ref=self.part(block, s),
            send_sem=self.send_sems.at[kind, s],
            recv_sem=self.recv_sems.at[block, s],
            device_id={"ctx": device},
            device_id_type=MESH,
        )

    def own(self, s):
        return self.x_ref.at[pl.ds(s * self.piece, self.piece)]

    def start(self):
        greet((self.sib, self.nx, self.ny))
        for s in range(SUBS):
            t = (s + SUBS // 2) % SUBS
            self.remote(self.own(s), 0, self.me, s, self.nx).start()
            self.remote(self.own(t), 1, self.me, t, self.ny).start()
        for s in range(SUBS):
            self.remote(self.own(s), 2, self.me, s, self.sib).start()
        keep = pltpu.make_async_copy(self.x_ref, self.xs.at[self.me], self.local_sem)
        keep.start()
        keep.wait()

    def arrived(self, block, s):
        self.remote(self.part(block, s), 0, block, s, self.sib).wait_recv()

    def relay(self, kind, block, s, device):
        self.remote(self.part(block, s), kind, block, s, device).start()

    def before(self, step):
        half = SUBS // 2

        @pl.when(step == 1)
        def _():
            for s in range(SUBS):
                self.arrived(self.sib, s)

        @pl.when(step == 2)
        def _():
            for s in range(SUBS):
                self.arrived(self.nx, s)
                if s < half:
                    self.relay(3, self.nx, s, self.ny)
                self.relay(4, self.nx, s, self.sib)
                t = (s + half) % SUBS
                self.arrived(self.ny, t)
                if t >= half:
                    self.relay(3, self.ny, t, self.nx)
                self.relay(5, self.ny, t, self.sib)

        @pl.when(step == 3)
        def _():
            for s in range(SUBS):
                self.arrived(self.nx + self.shift, s)

        @pl.when(step == 4)
        def _():
            for s in (0, half):
                self.arrived(self.dg, s)
                self.relay(6, self.dg, s, self.sib)

        @pl.when(step == 5)
        def _():
            for s in range(SUBS):
                self.arrived(self.ny + self.shift, s)

        @pl.when(step == 6)
        def _():
            for s in range(SUBS):
                if s % half:
                    self.arrived(self.dg, s)
                    self.relay(6, self.dg, s, self.sib)

        @pl.when(step == 7)
        def _():
            for s in range(SUBS):
                self.arrived(self.dg + self.shift, s)

    def block(self, step):
        near = (self.me, self.nx, self.ny, self.dg)
        return pick(step, [b + o for b in near for o in (0, self.shift)])

    def finish(self):
        for s in range(SUBS):
            for kind in range(7):
                self.remote(self.part(self.me, s), kind, self.me, s, self.sib).wait_send()


def gather_scratch(rows, width):
    return [
        pltpu.VMEM((8, rows, width), BF16),
        pltpu.SemaphoreType.DMA,
        pltpu.SemaphoreType.DMA((7, SUBS)),
        pltpu.SemaphoreType.DMA((8, SUBS)),
    ]


def nn(left, right):
    return lax.dot_general(left, right, (((1,), (0,)), ((), ())), preferred_element_type=F32)


def nt(left, right):
    return lax.dot_general(left, right, (((1,), (1,)), ((), ())), preferred_element_type=F32)


def tn(left, right):
    return lax.dot_general(left, right, (((0,), (0,)), ((), ())), preferred_element_type=F32)


def qkv_kernel(x_ref, w_ref, all_ref, qkv_ref, xs, local_sem, send_sems, recv_sems, keep_sems):
    ring = Gather(x_ref, xs, local_sem, send_sems, recv_sems)
    rows = x_ref.shape[0]
    ring.start()

    def keep(block):
        return pltpu.make_async_copy(xs.at[block], all_ref.at[block], keep_sems.at[block])

    def turn(step, carry):
        ring.before(step)
        block = ring.block(step)
        keep(block).start()
        qkv_ref[pl.ds(block * rows, rows), :] = nn(xs[block], w_ref[...])
        return carry

    lax.fori_loop(0, 8, turn, 0)
    ring.finish()
    for block in range(8):
        keep(block).wait()


def gather_qkv(normed, w_qkv):
    rows, width = normed.shape
    return pl.pallas_call(
        qkv_kernel,
        out_shape=(
            jax.ShapeDtypeStruct((8, rows, width), BF16),
            jax.ShapeDtypeStruct((8 * rows, w_qkv.shape[1]), F32),
        ),
        in_specs=[spec_vmem(), spec_vmem()],
        out_specs=(spec_any(), spec_vmem()),
        scratch_shapes=gather_scratch(rows, width) + [pltpu.SemaphoreType.DMA((8,))],
        compiler_params=pltpu.CompilerParams(
            collective_id=1, has_side_effects=True, vmem_limit_bytes=VMEM_LIMIT
        ),
        name="gather_qkv",
    )(normed, w_qkv)


def up_kernel(
    x_ref, w_ref, all_ref, a_ref, b_ref, h_ref, xs, local_sem, send_sems, recv_sems, keep_sems, stage, stage_sems
):
    ring = Gather(x_ref, xs, local_sem, send_sems, recv_sems)
    rows = x_ref.shape[0]
    halves, _, wide = w_ref.shape
    cols = wide // 2
    outs = (a_ref, b_ref, h_ref)
    ring.start()

    def keep(block):
        return pltpu.make_async_copy(xs.at[block], all_ref.at[block], keep_sems.at[block])

    def put(slot, n, block):
        return pltpu.make_async_copy(
            stage.at[slot, n], outs[n].at[pl.ds(block * rows, rows)], stage_sems.at[slot, n]
        )

    def turn(step, carry):
        ring.before(step)
        block = ring.block(step)
        keep(block).start()
        slot = lax.rem(step, 2)

        @pl.when(step >= 2)
        def _():
            for n in range(3):
                put(slot, n, block).wait()

        for z in range(halves):
            both = nn(xs[block], w_ref[z])
            gate, up = both[:, :cols], both[:, cols:]
            sigma = jax.nn.sigmoid(gate)
            active = gate * sigma
            here = slice(z * cols, (z + 1) * cols)
            stage[slot, 0, :, here] = (up * sigma * (1.0 + gate * (1.0 - sigma))).astype(BF16)
            stage[slot, 1, :, here] = active.astype(BF16)
            stage[slot, 2, :, here] = (active * up).astype(BF16)
        for n in range(3):
            put(slot, n, block).start()
        return carry

    lax.fori_loop(0, 8, turn, 0)
    ring.finish()
    for block in range(8):
        keep(block).wait()
    for slot in range(2):
        for n in range(3):
            put(slot, n, 0).wait()


def gather_up(post, w_gu):
    rows, width = post.shape
    halves, _, wide = w_gu.shape
    ff = halves * wide // 2
    flat = jax.ShapeDtypeStruct((8 * rows, ff), BF16)
    return pl.pallas_call(
        up_kernel,
        out_shape=(jax.ShapeDtypeStruct((8, rows, width), BF16), flat, flat, flat),
        in_specs=[spec_vmem(), spec_vmem()],
        out_specs=(spec_any(),) * 4,
        scratch_shapes=gather_scratch(rows, width)
        + [
            pltpu.SemaphoreType.DMA((8,)),
            pltpu.VMEM((2, 3, rows, ff), BF16),
            pltpu.SemaphoreType.DMA((2, 3)),
        ],
        compiler_params=pltpu.CompilerParams(
            collective_id=2, has_side_effects=True, vmem_limit_bytes=VMEM_LIMIT
        ),
        name="gather_up",
    )(post, w_gu)


def down_back_kernel(
    x_ref, w_ref, a_ref, b_ref, h_ref, d_ref, gw_ref, xs, local_sem, send_sems, recv_sems, stage, stage_sems
):
    ring = Gather(x_ref, xs, local_sem, send_sems, recv_sems)
    rows = x_ref.shape[0]
    ff = w_ref.shape[0]
    cols = ff // 2
    width = x_ref.shape[1]
    ring.start()
    gw_ref[...] = jnp.zeros_like(gw_ref)

    def put(slot, block):
        return pltpu.make_async_copy(
            stage.at[slot], d_ref.at[pl.ds(block * rows, rows)], stage_sems.at[slot]
        )

    def turn(step, carry):
        ring.before(step)
        block = ring.block(step)
        slot = lax.rem(step, 2)

        @pl.when(step >= 2)
        def _():
            put(slot, block).wait()

        here = pl.ds(block * rows, rows)
        for z in range(2):
            part = slice(z * cols, (z + 1) * cols)
            grad = nt(xs[block], w_ref[part, :])
            stage[slot, :, 2 * z * cols : (2 * z + 1) * cols] = (
                grad * a_ref[here, part].astype(F32)
            ).astype(BF16)
            stage[slot, :, (2 * z + 1) * cols : (2 * z + 2) * cols] = (
                grad * b_ref[here, part].astype(F32)
            ).astype(BF16)
        put(slot, block).start()

        @pl.when(slot == 1)
        def _():
            pair = block // 2
            hidden = h_ref[pl.ds(pair * 2 * rows, 2 * rows), :]
            for n in range(0, width, 512):
                seen = xs[pl.ds(pair * 2, 2), :, n : n + 512].reshape(2 * rows, 512)
                gw_ref[:, n : n + 512] += tn(hidden, seen)

        return carry

    lax.fori_loop(0, 8, turn, 0)
    ring.finish()
    for slot in range(2):
        put(slot, 0).wait()


def gather_down_back(diff, w_down, a, b, hidden):
    rows, width = diff.shape
    ff = w_down.shape[0]
    return pl.pallas_call(
        down_back_kernel,
        out_shape=(
            jax.ShapeDtypeStruct((8 * rows, 2 * ff), BF16),
            jax.ShapeDtypeStruct((ff, width), F32),
        ),
        in_specs=[spec_vmem()] * 5,
        out_specs=(spec_any(), spec_vmem()),
        scratch_shapes=gather_scratch(rows, width)
        + [pltpu.VMEM((2, rows, 2 * ff), BF16), pltpu.SemaphoreType.DMA((2,))],
        compiler_params=pltpu.CompilerParams(
            collective_id=3, has_side_effects=True, vmem_limit_bytes=VMEM_LIMIT
        ),
        name="gather_down_back",
    )(diff, w_down, a, b, hidden)


def out_back_kernel(x_ref, w_ref, m_ref, d_ref, gw_ref, xs, local_sem, send_sems, recv_sems):
    ring = Gather(x_ref, xs, local_sem, send_sems, recv_sems)
    rows, width = x_ref.shape
    ring.start()
    gw_ref[...] = jnp.zeros_like(gw_ref)

    def turn(step, carry):
        ring.before(step)
        block = ring.block(step)
        d_ref[pl.ds(block * rows, rows), :] = nt(xs[block], w_ref[...]).astype(BF16)

        @pl.when(lax.rem(step, 2) == 1)
        def _():
            pair = block // 2
            mixed = m_ref[pl.ds(pair * 2 * rows, 2 * rows), :]
            for n in range(0, width, 512):
                seen = xs[pl.ds(pair * 2, 2), :, n : n + 512].reshape(2 * rows, 512)
                gw_ref[:, n : n + 512] += tn(mixed, seen)

        return carry

    lax.fori_loop(0, 8, turn, 0)
    ring.finish()


def gather_out_back(d_mid, w_out, mixed):
    rows, width = d_mid.shape
    heads = w_out.shape[0]
    return pl.pallas_call(
        out_back_kernel,
        out_shape=(
            jax.ShapeDtypeStruct((8 * rows, heads), BF16),
            jax.ShapeDtypeStruct((heads, width), F32),
        ),
        in_specs=[spec_vmem()] * 3,
        out_specs=(spec_vmem(), spec_vmem()),
        scratch_shapes=gather_scratch(rows, width),
        compiler_params=pltpu.CompilerParams(
            collective_id=4, has_side_effects=True, vmem_limit_bytes=VMEM_LIMIT
        ),
        name="gather_out_back",
    )(d_mid, w_out, mixed)


def scatter_kernel(
    product, a_ref, w_ref, o_ref, to_sib, from_sib, own, diag_out, diag_in, x_out, y_out, x_in, y_in, sends, recvs
):
    me, sib, nx, ny, dg = plane_neighbours()
    shift = sib - me
    rows, width = o_ref.shape
    half = rows // 2
    first, second = pl.ds(0, half), pl.ds(half, half)
    greet((sib, nx, ny))

    def remote(src, dst, n, device):
        return pltpu.make_async_remote_copy(
            src_ref=src,
            dst_ref=dst,
            send_sem=sends.at[n],
            recv_sem=recvs.at[n],
            device_id={"ctx": device},
            device_id_type=MESH,
        )

    def sibling(n):
        return remote(to_sib.at[n], from_sib.at[n], n, sib)

    diag_x = remote(diag_out.at[first], diag_in.at[first], 4, nx)
    diag_y = remote(diag_out.at[second], diag_in.at[second], 5, ny)
    x_first = remote(x_out.at[first], x_in.at[first], 6, nx)
    x_second = remote(x_out.at[second], x_in.at[second], 7, nx)
    y_first = remote(y_out.at[first], y_in.at[first], 8, ny)
    y_second = remote(y_out.at[second], y_in.at[second], 9, ny)
    order = [b + o for b in (dg, nx, ny, me) for o in (shift, 0)]

    def chip_sum(n, at):
        return own[n, at].astype(F32) + from_sib[n, at].astype(F32)

    def turn(step, carry):
        block = pick(step, order)
        n = step // 2

        @pl.when(lax.rem(step, 2) == 0)
        def _():
            product(a_ref, w_ref, block, rows, to_sib, n)
            sibling(n).start()

        @pl.when(lax.rem(step, 2) == 1)
        def _():
            product(a_ref, w_ref, block, rows, own, n)
            sibling(n).wait_recv()

        @pl.when(step == 1)
        def _():
            diag_out[first] = chip_sum(0, first).astype(BF16)
            diag_x.start()
            diag_out[second] = chip_sum(0, second).astype(BF16)
            diag_y.start()

        @pl.when(step == 3)
        def _():
            x_out[first] = chip_sum(1, first).astype(BF16)
            x_first.start()

        @pl.when(step == 5)
        def _():
            y_out[second] = chip_sum(2, second).astype(BF16)
            y_second.start()
            diag_x.wait_recv()
            y_out[first] = (chip_sum(2, first) + diag_in[first].astype(F32)).astype(BF16)
            y_first.start()
            diag_y.wait_recv()
            x_out[second] = (chip_sum(1, second) + diag_in[second].astype(F32)).astype(BF16)
            x_second.start()

        return carry

    lax.fori_loop(0, 8, turn, 0)
    x_first.wait_recv()
    y_second.wait_recv()
    x_second.wait_recv()
    y_first.wait_recv()
    for at in (first, second):
        o_ref[at] = chip_sum(3, at) + x_in[at].astype(F32) + y_in[at].astype(F32)
    for n in range(4):
        sibling(n).wait_send()
    for copy in (diag_x, diag_y, x_first, x_second, y_first, y_second):
        copy.wait_send()


def product_nn(a_ref, w_ref, block, rows, out, n):
    left = a_ref[pl.ds(block * rows, rows), :]
    for c in range(0, w_ref.shape[1], 512):
        out[n, :, c : c + 512] = nn(left, w_ref[:, c : c + 512]).astype(BF16)


def product_nt(a_ref, w_ref, block, rows, out, n):
    left = a_ref[pl.ds(block * rows, rows), :]
    for c in range(0, w_ref.shape[0], 512):
        out[n, :, c : c + 512] = nt(left, w_ref[c : c + 512, :]).astype(BF16)


def product_nt_halves(a_ref, w_ref, block, rows, out, n):
    wide = w_ref.shape[2]
    here = pl.ds(block * rows, rows)
    for c in range(0, w_ref.shape[1], 512):
        total = nt(a_ref[here, :wide], w_ref[0, c : c + 512, :])
        total += nt(a_ref[here, wide:], w_ref[1, c : c + 512, :])
        out[n, :, c : c + 512] = total.astype(BF16)


def scatter_sum(product, a, w, width, collective_id, name):
    rows = a.shape[0] // 8
    four = pltpu.VMEM((4, rows, width), BF16)
    one = pltpu.VMEM((rows, width), BF16)
    return pl.pallas_call(
        functools.partial(scatter_kernel, product),
        out_shape=jax.ShapeDtypeStruct((rows, width), F32),
        in_specs=[spec_vmem(), spec_vmem()],
        out_specs=spec_vmem(),
        scratch_shapes=[four, four, four]
        + [one] * 6
        + [pltpu.SemaphoreType.DMA((10,)), pltpu.SemaphoreType.DMA((10,))],
        compiler_params=pltpu.CompilerParams(
            collective_id=collective_id, has_side_effects=True, vmem_limit_bytes=VMEM_LIMIT
        ),
        name=name,
    )(a, w)


class Places:
    def __init__(self, order_ref, lens_ref):
        self.order, self.lens = order_ref, lens_ref
        self.plane = lax.axis_index("tp")
        self.seq0 = (3 * self.plane) // 4
        self.seq1 = (3 * self.plane + 2) // 4

    def position(self, seq, quarter, c):
        return 2 * self.order[seq, 2 * c + quarter // 2] + lax.rem(quarter, 2)

    def unit(self, u):
        c = u // 3
        g = 3 * self.plane + lax.rem(u, 3)
        seq = g // 4
        return seq, seq - self.seq0, self.position(seq, lax.rem(g, 4), c)

    def each(self, visit):
        for slot, seq in ((0, self.seq0), (1, self.seq1)):

            @pl.when((slot == 0) | (self.seq1 != self.seq0))
            def _():
                def one(i, carry):
                    quarter, c = i // 8, lax.rem(i, 8)
                    g = 4 * seq + quarter
                    away = g // 3 - self.plane
                    row = pl.multiple_of((c * 3 + lax.rem(g, 3)) * UNIT, UNIT)
                    visit(slot, self.position(seq, quarter, c), away, row)
                    return carry

                lax.fori_loop(0, 32, one, 0)

    def fetch(self, sources, keys, values, key_sem, value_sem):
        def visit(slot, position, away, row):
            at = pl.ds(pl.multiple_of(position * UNIT, UNIT), UNIT)
            for n, source in enumerate(sources):

                @pl.when(away == n - 1)
                def _():
                    pltpu.make_async_copy(
                        source.at[pl.ds(row, UNIT), pl.ds(0, HEAD_SIZE)], keys.at[slot, at], key_sem.at[slot]
                    ).start()
                    pltpu.make_async_copy(
                        source.at[pl.ds(row, UNIT), pl.ds(HEAD_SIZE, HEAD_SIZE)],
                        values.at[slot, at, pl.ds(0, HEAD_SIZE)],
                        value_sem.at[slot],
                    ).start()

        self.each(visit)
        for slot in range(2):

            @pl.when((slot == 0) | (self.seq1 != self.seq0))
            def _():
                pltpu.make_async_copy(keys.at[slot], keys.at[slot], key_sem.at[slot]).wait()
                pltpu.make_async_copy(keys.at[slot], keys.at[slot], value_sem.at[slot]).wait()


def attend_kernel(
    order_ref, lens_ref, q_ref, lo_ref, own_ref, hi_ref, o_ref, lse_ref, keys, values, acc, key_sem, value_sem
):
    places = Places(order_ref, lens_ref)
    values[:, :, HEAD_SIZE:] = jnp.ones((2, values.shape[1], HEAD_SIZE), BF16)
    places.fetch((lo_ref, own_ref, hi_ref), keys, values, key_sem, value_sem)

    def one_unit(u, carry):
        seq, slot, position = places.unit(u)
        length = lens_ref[seq]
        rows = pl.ds(pl.multiple_of(u * UNIT, UNIT), UNIT)
        both = q_ref[rows, :]
        queries = jnp.concatenate([both[:, :HEAD_SIZE], both[:, HEAD_SIZE:]], axis=0)
        clear = jnp.minimum(position * UNIT, length) // KEYS
        acc[...] = jnp.zeros_like(acc)

        def part(block, masked):
            at = pl.ds(pl.multiple_of(block * KEYS, KEYS), KEYS)
            weights = jnp.exp2(nt(queries, keys[slot, at, :]))
            if masked:
                key_pos = block * KEYS + lax.broadcasted_iota(jnp.int32, weights.shape, 1)
                query_pos = position * UNIT + lax.rem(
                    lax.broadcasted_iota(jnp.int32, weights.shape, 0), UNIT
                )
                weights = jnp.where((key_pos <= query_pos) & (key_pos < length), weights, 0.0)
            acc[...] += nn(weights.astype(BF16), values[slot, at, :])

        def full(block, carry):
            part(block, False)
            return carry

        lax.fori_loop(0, clear, full, 0)
        part(clear, True)
        total = acc[:, HEAD_SIZE:]
        mixed = (acc[:, :HEAD_SIZE] / total).astype(BF16)
        o_ref[rows, :] = jnp.concatenate([mixed[:UNIT], mixed[UNIT:]], axis=1)
        lse_ref[u] = jnp.transpose(jnp.log2(total))[:8, :]
        return carry

    lax.fori_loop(0, q_ref.shape[0] // UNIT, one_unit, 0)


def attend(order, lens, q, lo, own, hi, seq_len):
    rows = q.shape[0]
    return pl.pallas_call(
        attend_kernel,
        out_shape=(
            jax.ShapeDtypeStruct(q.shape, BF16),
            jax.ShapeDtypeStruct((rows // UNIT, 8, 2 * UNIT), F32),
        ),
        in_specs=[spec_smem(), spec_smem(), spec_vmem(), spec_any(), spec_any(), spec_any()],
        out_specs=(spec_vmem(), spec_vmem()),
        scratch_shapes=[
            pltpu.VMEM((2, seq_len, HEAD_SIZE), BF16),
            pltpu.VMEM((2, seq_len, 2 * HEAD_SIZE), BF16),
            pltpu.VMEM((2 * UNIT, 2 * HEAD_SIZE), F32),
            pltpu.SemaphoreType.DMA((2,)),
            pltpu.SemaphoreType.DMA((2,)),
        ],
        compiler_params=pltpu.CompilerParams(vmem_limit_bytes=VMEM_LIMIT),
        name="attend",
    )(order, lens, q, lo, own, hi)


def attend_back_kernel(
    order_ref,
    lens_ref,
    q_ref,
    do_ref,
    o_ref,
    lse_ref,
    lo_ref,
    own_ref,
    hi_ref,
    dq_ref,
    dlo_ref,
    down_ref,
    dhi_ref,
    keys,
    values,
    dkeys,
    dvalues,
    dq_acc,
    key_sem,
    value_sem,
):
    places = Places(order_ref, lens_ref)
    dkeys[...] = jnp.zeros_like(dkeys)
    dvalues[...] = jnp.zeros_like(dvalues)
    places.fetch((lo_ref, own_ref, hi_ref), keys, values, key_sem, value_sem)

    def stacked(ref, rows):
        both = ref[rows, :]
        return jnp.concatenate([both[:, :HEAD_SIZE], both[:, HEAD_SIZE:]], axis=0)

    def one_unit(u, carry):
        seq, slot, position = places.unit(u)
        length = lens_ref[seq]
        rows = pl.ds(pl.multiple_of(u * UNIT, UNIT), UNIT)
        queries = stacked(q_ref, rows)
        grads = stacked(do_ref, rows)
        product = grads.astype(F32) * stacked(o_ref, rows).astype(F32)
        delta = jnp.sum(jnp.transpose(product), axis=0, keepdims=True)
        lse = lse_ref[u][:1, :]
        clear = jnp.minimum(position * UNIT, length) // KEYS
        dq_acc[...] = jnp.zeros_like(dq_acc)

        def part(block, masked):
            at = pl.ds(pl.multiple_of(block * KEYS, KEYS), KEYS)
            key = keys[slot, at, :]
            probs = jnp.exp2(nt(key, queries) - lse)
            if masked:
                key_pos = block * KEYS + lax.broadcasted_iota(jnp.int32, probs.shape, 0)
                query_pos = position * UNIT + lax.rem(
                    lax.broadcasted_iota(jnp.int32, probs.shape, 1), UNIT
                )
                probs = jnp.where((key_pos <= query_pos) & (key_pos < length), probs, 0.0)
            d_scores = (probs * (nt(values[slot, at, :], grads) - delta)).astype(BF16)
            dvalues[slot, at, :] += nn(probs.astype(BF16), grads)
            dkeys[slot, at, :] += nn(d_scores, queries)
            dq_acc[...] += tn(d_scores, key)

        def full(block, carry):
            part(block, False)
            return carry

        lax.fori_loop(0, clear, full, 0)
        part(clear, True)
        dq_ref[rows, :] = jnp.concatenate([dq_acc[:UNIT, :], dq_acc[UNIT:, :]], axis=1)
        return carry

    lax.fori_loop(0, q_ref.shape[0] // UNIT, one_unit, 0)
    dlo_ref[...] = jnp.zeros_like(dlo_ref)
    dhi_ref[...] = jnp.zeros_like(dhi_ref)

    def spread(slot, position, away, row):
        at = pl.ds(pl.multiple_of(position * UNIT, UNIT), UNIT)
        for n, out in enumerate((dlo_ref, down_ref, dhi_ref)):

            @pl.when(away == n - 1)
            def _():
                out[pl.ds(row, UNIT), :HEAD_SIZE] = (dkeys[slot, at, :] * (1.0 / LOG2E)).astype(out.dtype)
                out[pl.ds(row, UNIT), HEAD_SIZE:] = dvalues[slot, at, :].astype(out.dtype)

    places.each(spread)


def attend_back(order, lens, q, d_mixed, mixed, lse, lo, own, hi, seq_len):
    flat = jax.ShapeDtypeStruct(q.shape, BF16)
    wide = jax.ShapeDtypeStruct(q.shape, F32)
    held = pltpu.VMEM((2, seq_len, HEAD_SIZE), BF16)
    summed = pltpu.VMEM((2, seq_len, HEAD_SIZE), F32)
    return pl.pallas_call(
        attend_back_kernel,
        out_shape=(wide, flat, wide, flat),
        in_specs=[spec_smem(), spec_smem()] + [spec_vmem()] * 4 + [spec_any()] * 3,
        out_specs=(spec_vmem(),) * 4,
        scratch_shapes=[
            held,
            held,
            summed,
            summed,
            pltpu.VMEM((2 * UNIT, HEAD_SIZE), F32),
            pltpu.SemaphoreType.DMA((2,)),
            pltpu.SemaphoreType.DMA((2,)),
        ],
        compiler_params=pltpu.CompilerParams(vmem_limit_bytes=VMEM_LIMIT),
        name="attend_back",
    )(order, lens, q, d_mixed, mixed, lse, lo, own, hi)


def angles(block_order, ctx_rows, tok_rows):
    inverse = THETA ** (-jnp.arange(0, HEAD_SIZE, 2, dtype=F32) / HEAD_SIZE)
    starts = jnp.arange(2 * block_order.shape[1], dtype=jnp.int32) * UNIT
    coarse = starts.astype(F32)[:, None] * inverse[None, :]
    fine = jnp.arange(UNIT, dtype=F32)[:, None] * inverse[None, :]
    units = tok_rows // UNIT
    g = lax.axis_index("tp") * units + jnp.arange(units, dtype=jnp.int32)
    seq, quarter = g // 4, g % 4
    c = jnp.arange(lax.axis_size("ctx"), dtype=jnp.int32)
    where = 2 * block_order[seq[None, :], 2 * c[:, None] + (quarter // 2)[None, :]] + (quarter % 2)[None, :]
    where = where.reshape(-1)
    cos_a, sin_a = jnp.cos(coarse)[where][:, None, :], jnp.sin(coarse)[where][:, None, :]
    cos_b, sin_b = jnp.cos(fine)[None], jnp.sin(fine)[None]
    half = HEAD_SIZE // 2
    cosine = (cos_a * cos_b - sin_a * sin_b).reshape(-1, 1, half)
    sine = (sin_a * cos_b + cos_a * sin_b).reshape(-1, 1, half)
    return cosine, sine


def from_sibling(parts, core):
    mine = lax.dynamic_slice_in_dim(parts, 2 * core, 2, 0)
    other = lax.dynamic_slice_in_dim(parts, 2 - 2 * core, 2, 0)
    got = lax.ppermute(other, "ctx", SIBLING)
    low = jnp.where(core == 0, mine, got)
    high = jnp.where(core == 0, got, mine)
    return low, high


def local_plane(
    tokens,
    teacher,
    seq_lens,
    block_order,
    in_gain,
    w_query,
    key_weight_matrix,
    value_weight_matrix,
    q_gain,
    k_gain,
    w_out,
    post_gain,
    w_gate,
    w_up,
    w_down,
):
    me = lax.axis_index("ctx")
    core = me % 2
    plane = lax.axis_index("tp")
    tok_rows, width = tokens.shape
    plane_rows = 8 * tok_rows
    seq_len = 2 * 8 * BLK
    scale_qk = HEAD_SIZE ** (-0.5)
    deep = width // 8
    stream = tokens.astype(F32)
    scale_in = rms_scale(stream)
    unit_in = stream * scale_in
    normed_rows = (unit_in * in_gain).astype(BF16)

    def to_heads(home):
        gathered = lax.all_gather(home, "tp", axis=0, tiled=True)
        return lax.all_to_all(gathered, "ctx", 0, 0, tiled=True)

    qkv_home = jnp.concatenate(
        [
            w_query.reshape(deep, 2, 2 * HEAD_SIZE),
            key_weight_matrix.reshape(deep, 2, HEAD_SIZE),
            value_weight_matrix.reshape(deep, 2, HEAD_SIZE),
        ],
        axis=2,
    )
    w_qkv = to_heads(jnp.transpose(qkv_home, (1, 0, 2))).reshape(width, 4 * HEAD_SIZE)
    w_o = jnp.transpose(to_heads(w_out.reshape(2, 2 * HEAD_SIZE, deep)), (1, 0, 2)).reshape(
        2 * HEAD_SIZE, width
    )

    cols = w_gate.shape[1] // 4
    gu_home = jnp.transpose(
        jnp.concatenate([w_gate.reshape(deep, 4, cols), w_up.reshape(deep, 4, cols)], axis=2), (1, 0, 2)
    )
    gu_part = lax.all_to_all(gu_home, "ctx", 0, 0, axis_index_groups=CORE_GROUPS, tiled=True)
    gu_low, gu_high = from_sibling(lax.all_gather(gu_part, "tp", axis=0), core)
    w_gu = jnp.stack([gu_low, gu_high], axis=2).reshape(2, width, 2 * cols)
    down_part = lax.all_to_all(
        w_down.reshape(4, cols, deep), "ctx", 0, 0, axis_index_groups=CORE_GROUPS, tiled=True
    )
    down_low, down_high = from_sibling(lax.all_gather(down_part, "tp", axis=0), core)
    w_d = jnp.transpose(jnp.stack([down_low, down_high], axis=2), (0, 3, 1, 2, 4)).reshape(2 * cols, width)

    normed_all, qkv = gather_qkv(normed_rows, w_qkv)
    cosine, sine = angles(block_order, plane_rows, tok_rows)
    query_lin = qkv[:, : 2 * HEAD_SIZE].reshape(plane_rows, 2, HEAD_SIZE)
    key_lin = qkv[:, 2 * HEAD_SIZE : 3 * HEAD_SIZE].reshape(plane_rows, 1, HEAD_SIZE)
    query_scale = rms_scale(query_lin)
    query_unit = query_lin * query_scale
    key_scale = rms_scale(key_lin)
    key_unit = key_lin * key_scale
    queries = (
        (rotate(query_unit * q_gain, cosine, sine) * (scale_qk * LOG2E))
        .astype(BF16)
        .reshape(plane_rows, 2 * HEAD_SIZE)
    )
    keys = rotate(key_unit * k_gain, cosine, sine).astype(BF16).reshape(plane_rows, HEAD_SIZE)
    kv = jnp.concatenate([keys, qkv[:, 3 * HEAD_SIZE :].astype(BF16)], axis=1)
    upward = [(0, 1), (1, 2), (2, 3)]
    downward = [(1, 0), (2, 1), (3, 2)]
    kv_lo = lax.ppermute(kv, "tp", upward)
    kv_hi = lax.ppermute(kv, "tp", downward)
    mixed, lse = attend(block_order, seq_lens, queries, kv_lo, kv, kv_hi, seq_len)
    middle = stream + scatter_sum(product_nn, mixed, w_o, width, 5, "scatter_out")
    scale_post = rms_scale(middle)
    unit_post = middle * scale_post
    post_rows = (unit_post * post_gain).astype(BF16)
    post_all, slope, active, hidden = gather_up(post_rows, w_gu)
    result = middle + scatter_sum(product_nn, hidden, w_d, width, 6, "scatter_down")
    output = result.astype(BF16)

    row = plane * tok_rows + jnp.arange(tok_rows, dtype=jnp.int32)
    seq, rest = row // (2 * BLK), row % (2 * BLK)
    position = block_order[seq, 2 * me + rest // BLK] * BLK + rest % BLK
    valid = (position < seq_lens[seq]).astype(F32)
    diff = (result - teacher.astype(F32)) * valid[:, None]
    error_local = jnp.sum(diff * diff)
    diff_low = diff.astype(BF16)
    d_gu, grad_wd = gather_down_back(diff_low, w_d, slope, active, hidden)
    d_post = scatter_sum(product_nt_halves, d_gu, w_gu, width, 7, "scatter_post")

    def home_sum(parts):
        mine = lax.dynamic_index_in_dim(parts, core, 2, keepdims=False)
        other = lax.dynamic_index_in_dim(parts, 1 - core, 2, keepdims=False)
        got = lax.ppermute(other, "ctx", SIBLING)
        low = jnp.where(core == 0, mine, got)
        high = jnp.where(core == 0, got, mine)
        total = lax.psum_scatter(
            jnp.concatenate([low, high], axis=0), "tp", scatter_dimension=0, tiled=True
        )
        return lax.all_to_all(total[0], "ctx", 0, 0, axis_index_groups=CORE_GROUPS, tiled=True)

    grad_down = home_sum(
        jnp.transpose(grad_wd.astype(BF16).reshape(2, cols, 4, 2, deep), (0, 2, 3, 1, 4))
    ).reshape(4 * cols, deep)
    post_flat = post_all.reshape(plane_rows, width)
    grad_gu = jnp.stack(
        [matmul_tn(post_flat, d_gu[:, z * 2 * cols : (z + 1) * 2 * cols]).astype(BF16) for z in range(2)]
    )
    gu_sum = home_sum(grad_gu.reshape(2, 4, 2, deep, 2 * cols))
    gu_sum = jnp.transpose(gu_sum, (1, 0, 2))
    grad_gate = gu_sum[:, :, :cols].reshape(deep, 4 * cols)
    grad_up = gu_sum[:, :, cols:].reshape(deep, 4 * cols)

    grad_post_local = jnp.sum(d_post * unit_post, axis=0)
    d_middle = diff + rms_back(middle, scale_post, d_post * post_gain)
    d_mixed, grad_wo = gather_out_back(d_middle.astype(BF16), w_o, mixed)

    def home_heads(parts):
        swapped = lax.all_to_all(parts.astype(BF16), "ctx", 0, 0, tiled=True)
        return lax.psum_scatter(swapped, "tp", scatter_dimension=0, tiled=True)

    grad_out = home_heads(jnp.transpose(grad_wo.reshape(2 * HEAD_SIZE, 8, deep), (1, 0, 2))).reshape(
        4 * HEAD_SIZE, deep
    )
    d_queries, to_lo, d_kv, to_hi = attend_back(
        block_order, seq_lens, queries, d_mixed, mixed, lse, kv_lo, kv, kv_hi, seq_len
    )
    d_kv = (
        d_kv
        + lax.ppermute(to_lo, "tp", downward).astype(F32)
        + lax.ppermute(to_hi, "tp", upward).astype(F32)
    )
    query_back = rotate_back(
        d_queries.reshape(plane_rows, 2, HEAD_SIZE) * scale_qk, cosine, sine
    )
    grad_q_local = jnp.sum(query_back * query_unit, axis=(0, 1))
    d_query_lin = rms_back(query_lin, query_scale, query_back * q_gain).reshape(plane_rows, 2 * HEAD_SIZE)
    key_back = rotate_back(d_kv[:, :HEAD_SIZE].reshape(plane_rows, 1, HEAD_SIZE), cosine, sine)
    grad_k_local = jnp.sum(key_back * key_unit, axis=(0, 1))
    d_key_lin = rms_back(key_lin, key_scale, key_back * k_gain).reshape(plane_rows, HEAD_SIZE)
    d_qkv = jnp.concatenate([d_query_lin, d_key_lin, d_kv[:, HEAD_SIZE:]], axis=1).astype(BF16)
    d_normed = scatter_sum(product_nt, d_qkv, w_qkv, width, 8, "scatter_normed")
    grad_qkv = home_heads(
        matmul_tn(normed_all.reshape(plane_rows, width), d_qkv).reshape(8, deep, 4 * HEAD_SIZE)
    )
    grad_qkv = jnp.transpose(grad_qkv, (1, 0, 2))
    grad_query = grad_qkv[:, :, : 2 * HEAD_SIZE].reshape(deep, 4 * HEAD_SIZE)
    grad_key = grad_qkv[:, :, 2 * HEAD_SIZE : 3 * HEAD_SIZE].reshape(deep, 2 * HEAD_SIZE)
    grad_value = grad_qkv[:, :, 3 * HEAD_SIZE :].reshape(deep, 2 * HEAD_SIZE)
    grad_in_local = jnp.sum(d_normed * unit_in, axis=0)
    d_tokens = (d_middle + rms_back(stream, scale_in, d_normed * in_gain)).astype(BF16)
    totals = lax.psum(
        (grad_in_local, grad_q_local, grad_k_local, grad_post_local, error_local), ("ctx", "tp")
    )
    count_valid = jnp.sum(seq_lens).astype(F32)
    loss = 0.5 * totals[4] / (count_valid * MODEL_WIDTH)
    return (
        output,
        loss,
        d_tokens,
        totals[0],
        grad_query.astype(F32),
        grad_key.astype(F32),
        grad_value.astype(F32),
        totals[1],
        totals[2],
        grad_out.astype(F32),
        totals[3],
        grad_gate.astype(F32),
        grad_up.astype(F32),
        grad_down.astype(F32),
    )


def solution(mesh):
    in_specs = (
        P(("ctx", "tp"), None),
        P(("ctx", "tp"), None),
        P(),
        P(),
        P(),
        P("ctx", "tp"),
        P("ctx", "tp"),
        P("ctx", "tp"),
        P(),
        P(),
        P("tp", "ctx"),
        P(),
        P("ctx", "tp"),
        P("ctx", "tp"),
        P("tp", "ctx"),
    )
    out_specs = (
        P(("ctx", "tp"), None),
        P(),
        P(("ctx", "tp"), None),
        P(),
        P("ctx", "tp"),
        P("ctx", "tp"),
        P("ctx", "tp"),
        P(),
        P(),
        P("tp", "ctx"),
        P(),
        P("ctx", "tp"),
        P("ctx", "tp"),
        P("tp", "ctx"),
    )
    body = local_plane if (mesh.shape["ctx"], mesh.shape["tp"]) == (8, 4) else local
    return jax.shard_map(body, mesh=mesh, in_specs=in_specs, out_specs=out_specs, check_vma=False)
```

```python
import functools

import jax
import jax.numpy as jnp
from jax import lax
from jax.experimental import pallas as pl
from jax.experimental.pallas import tpu as pltpu
from jax.sharding import PartitionSpec as P

MODEL_WIDTH = 2048
HEAD_SIZE = 128
SEQS = 3
BLK = 256


EPS = 1e-06
THETA = 1000000.0
FLOOR = -1e30


def from_behind(x, axis, by):
    count = lax.axis_size(axis)
    return lax.ppermute(x, axis, [(i, (i + by) % count) for i in range(count)])


def rms_scale(value):
    return lax.rsqrt(jnp.mean(value * value, axis=-1, keepdims=True) + EPS)


def rms_back(value, scale, grad_normed):
    return scale * grad_normed - value * scale**3 * jnp.mean(
        grad_normed * value, axis=-1, keepdims=True
    )


def rotate(value, cosine, sine):
    half = value.shape[-1] // 2
    first = value[..., :half]
    second = value[..., half:]
    return jnp.concatenate(
        [first * cosine - second * sine, second * cosine + first * sine], axis=-1
    )


def rotate_back(grad, cosine, sine):
    half = grad.shape[-1] // 2
    first = grad[..., :half]
    second = grad[..., half:]
    return jnp.concatenate(
        [first * cosine + second * sine, second * cosine - first * sine], axis=-1
    )


def matmul(left, right):
    return jnp.dot(left, right, preferred_element_type=jnp.float32)


def matmul_tn(left, right):
    return lax.dot_general(
        left, right, (((0,), (0,)), ((), ())), preferred_element_type=jnp.float32
    )


def matmul_nt(left, right):
    return lax.dot_general(
        left, right, (((1,), (1,)), ((), ())), preferred_element_type=jnp.float32
    )


def row_slice(value, start, count):
    return lax.dynamic_slice_in_dim(value, start, count, 0)


def local(
    tokens,
    teacher,
    seq_lens,
    block_order,
    in_gain,
    w_query,
    key_weight_matrix,
    value_weight_matrix,
    q_gain,
    k_gain,
    w_out,
    post_gain,
    w_gate,
    w_up,
    w_down,
):
    ctx_count = lax.axis_size("ctx")
    ctx_index = lax.axis_index("ctx")
    tp_index = lax.axis_index("tp")
    tok_rows = tokens.shape[0]
    ctx_rows = tok_rows * lax.axis_size("tp")
    block_span = 2 * BLK
    q_heads = w_query.shape[1] // HEAD_SIZE
    kv_heads = key_weight_matrix.shape[1] // HEAD_SIZE
    group_width = q_heads // kv_heads
    scale_qk = HEAD_SIZE ** (-0.5)
    weights = (
        lax.all_gather(w_query, "ctx", axis=0, tiled=True),
        lax.all_gather(key_weight_matrix, "ctx", axis=0, tiled=True),
        lax.all_gather(value_weight_matrix, "ctx", axis=0, tiled=True),
        lax.all_gather(w_out, "ctx", axis=1, tiled=True),
        lax.all_gather(w_gate, "ctx", axis=0, tiled=True),
        lax.all_gather(w_up, "ctx", axis=0, tiled=True),
        lax.all_gather(w_down, "ctx", axis=1, tiled=True),
    )
    wq_full, wk_full, wv_full, wo_full, wg_full, wu_full, wd_full = weights
    offsets = jnp.arange(BLK, dtype=jnp.int32)

    def block_positions(owner):
        columns = lax.dynamic_slice_in_dim(block_order, 2 * owner, 2, 1)
        return (columns[:, :, None] * BLK + offsets).reshape(SEQS, block_span)

    query_pos = block_positions(ctx_index)
    flat_pos = query_pos.reshape(-1)
    inverse = THETA ** (-jnp.arange(0, HEAD_SIZE, 2, dtype=jnp.float32) / HEAD_SIZE)
    angle = flat_pos.astype(jnp.float32)[:, None] * inverse[None, :]
    cosine = jnp.cos(angle)[:, None, :]
    sine = jnp.sin(angle)[:, None, :]
    stream = tokens.astype(jnp.float32)
    scale_in = rms_scale(stream)
    unit_in = stream * scale_in
    normed_rows = (unit_in * in_gain).astype(jnp.bfloat16)
    normed_all = lax.all_gather(normed_rows, "tp", axis=0, tiled=True)
    query_lin = matmul(normed_all, wq_full).reshape(ctx_rows, q_heads, HEAD_SIZE)
    key_linear = matmul(normed_all, wk_full).reshape(ctx_rows, kv_heads, HEAD_SIZE)
    value_low = (
        matmul(normed_all, wv_full)
        .astype(jnp.bfloat16)
        .reshape(SEQS, block_span, kv_heads, HEAD_SIZE)
    )
    query_scale = rms_scale(query_lin)
    query_unit = query_lin * query_scale
    query_low = (
        rotate(query_unit * q_gain, cosine, sine)
        .astype(jnp.bfloat16)
        .reshape(SEQS, block_span, kv_heads, group_width, HEAD_SIZE)
    )
    key_scale = rms_scale(key_linear)
    key_unit = key_linear * key_scale
    key_low = (
        rotate(key_unit * k_gain, cosine, sine)
        .astype(jnp.bfloat16)
        .reshape(SEQS, block_span, kv_heads, HEAD_SIZE)
    )

    def scores_of(keys, key_pos):
        raw = (
            jnp.einsum("sqkgd,slkd->skgql", query_low, keys, preferred_element_type=jnp.float32)
            * scale_qk
        )
        allowed = (key_pos[:, None, :] <= query_pos[:, :, None]) & (
            key_pos[:, None, :] < seq_lens[:, None, None]
        )
        allowed = allowed[:, None, None, :, :]
        return (jnp.where(allowed, raw, FLOOR), allowed)

    def absorb(state, keys, value_rows, owner):
        running_top, running_total, running_acc = state
        scores, allowed = scores_of(keys, block_positions(owner))
        new_top = jnp.maximum(running_top, jnp.max(scores, axis=-1))
        weights_now = jnp.where(allowed, jnp.exp(scores - new_top[..., None]), 0.0)
        shrink = jnp.exp(running_top - new_top)
        running_total = running_total * shrink + jnp.sum(weights_now, axis=-1)
        running_acc = running_acc * shrink[..., None] + jnp.einsum(
            "skgql,slkd->skgqd",
            weights_now.astype(jnp.bfloat16),
            value_rows,
            preferred_element_type=jnp.float32,
        )
        return (new_top, running_total, running_acc)

    stat_shape = (SEQS, kv_heads, group_width, block_span)
    initial = (
        jnp.full(stat_shape, FLOOR, jnp.float32),
        jnp.zeros(stat_shape, jnp.float32),
        jnp.zeros(stat_shape + (HEAD_SIZE,), jnp.float32),
    )
    first_state = absorb(initial, key_low, value_low, ctx_index)

    def cycle_turn(carry, turn):
        keys, value_rows, state = carry
        keys, value_rows = from_behind((keys, value_rows), "ctx", 1)
        owner = (ctx_index - turn) % ctx_count
        state = absorb(state, keys, value_rows, owner)
        return ((keys, value_rows, state), (keys, value_rows))

    (unused_keys, unused_values, final_state), (kept_keys, kept_values) = lax.scan(
        cycle_turn, (key_low, value_low, first_state), jnp.arange(1, ctx_count, dtype=jnp.int32)
    )
    all_keys = jnp.concatenate([key_low[None], kept_keys], axis=0)
    all_values = jnp.concatenate([value_low[None], kept_values], axis=0)
    top_final, total_final, acc_final = final_state
    log_total = top_final + jnp.log(total_final)
    attn_exact = acc_final / total_final[..., None]
    mixed_low = (
        jnp.transpose(attn_exact, (0, 3, 1, 2, 4))
        .reshape(ctx_rows, q_heads * HEAD_SIZE)
        .astype(jnp.bfloat16)
    )
    middle = stream + lax.psum_scatter(
        matmul(row_slice(mixed_low, jnp.int32(0), lax.axis_size("tp") * tok_rows), wo_full).astype(
            jnp.bfloat16
        ),
        "tp",
        scatter_dimension=0,
        tiled=True,
    ).astype(jnp.float32)
    scale_post = rms_scale(middle)
    unit_post = middle * scale_post
    post_rows = (unit_post * post_gain).astype(jnp.bfloat16)
    post_all = lax.all_gather(post_rows, "tp", axis=0, tiled=True)
    gate = matmul(post_all, wg_full)
    up_val = matmul(post_all, wu_full)
    sigma = jax.nn.sigmoid(gate)
    active = gate * sigma
    hidden_low = (active * up_val).astype(jnp.bfloat16)
    result = middle + lax.psum_scatter(
        matmul(row_slice(hidden_low, jnp.int32(0), lax.axis_size("tp") * tok_rows), wd_full).astype(
            jnp.bfloat16
        ),
        "tp",
        scatter_dimension=0,
        tiled=True,
    ).astype(jnp.float32)
    output = result.astype(jnp.bfloat16)
    valid_all = (query_pos < seq_lens[:, None]).reshape(-1).astype(jnp.float32)
    valid_rows = row_slice(valid_all, tp_index * tok_rows, tok_rows)
    diff = (result - teacher.astype(jnp.float32)) * valid_rows[:, None]
    error_local = jnp.sum(diff * diff)
    diff_low = diff.astype(jnp.bfloat16)
    diff_all = lax.all_gather(diff_low, "tp", axis=0, tiled=True)
    weights_two = (
        lax.all_gather(w_query, "ctx", axis=0, tiled=True),
        lax.all_gather(key_weight_matrix, "ctx", axis=0, tiled=True),
        lax.all_gather(value_weight_matrix, "ctx", axis=0, tiled=True),
        lax.all_gather(w_out, "ctx", axis=1, tiled=True),
        lax.all_gather(w_gate, "ctx", axis=0, tiled=True),
        lax.all_gather(w_up, "ctx", axis=0, tiled=True),
        lax.all_gather(w_down, "ctx", axis=1, tiled=True),
    )
    bq_full, bk_full, bv_full, bo_full, bg_full, bu_full, bd_full = weights_two
    grad_wd = matmul_tn(hidden_low, diff_all)
    d_hidden = matmul_nt(diff_all, bd_full)
    d_gate = (d_hidden * up_val * sigma * (1.0 + gate * (1.0 - sigma))).astype(jnp.bfloat16)
    d_up = (d_hidden * active).astype(jnp.bfloat16)
    grad_wg = matmul_tn(post_all, d_gate)
    grad_wu = matmul_tn(post_all, d_up)
    start = jnp.int32(0)
    d_post = lax.psum_scatter(
        (
            matmul_nt(row_slice(d_gate, start, lax.axis_size("tp") * tok_rows), bg_full)
            + matmul_nt(row_slice(d_up, start, lax.axis_size("tp") * tok_rows), bu_full)
        ).astype(jnp.bfloat16),
        "tp",
        scatter_dimension=0,
        tiled=True,
    ).astype(jnp.float32)
    grad_post_local = jnp.sum(d_post * unit_post, axis=0)
    d_middle = diff + rms_back(middle, scale_post, d_post * post_gain)
    d_mid_low = d_middle.astype(jnp.bfloat16)
    d_mid_all = lax.all_gather(d_mid_low, "tp", axis=0, tiled=True)
    grad_wo = matmul_tn(mixed_low, d_mid_all)
    d_mixed = matmul_nt(d_mid_all, bo_full).astype(jnp.bfloat16)
    d_mixed_grid = jnp.transpose(
        d_mixed.reshape(SEQS, block_span, kv_heads, group_width, HEAD_SIZE), (0, 2, 3, 1, 4)
    )
    delta = jnp.sum(d_mixed_grid.astype(jnp.float32) * attn_exact, axis=-1)

    def revisit(carry, turn):
        grad_queries, grad_keys, grad_values = carry
        owner = (ctx_index - turn) % ctx_count
        keys = all_keys[turn]
        value_rows = all_values[turn]
        scores, allowed = scores_of(keys, block_positions(owner))
        probs = jnp.where(allowed, jnp.exp(scores - log_total[..., None]), 0.0)
        probs_low = probs.astype(jnp.bfloat16)
        d_probs = jnp.einsum(
            "skgqd,slkd->skgql", d_mixed_grid, value_rows, preferred_element_type=jnp.float32
        )
        d_scores = (probs * (d_probs - delta[..., None])).astype(jnp.bfloat16)
        grad_queries = grad_queries + jnp.einsum(
            "skgql,slkd->skgqd", d_scores, keys, preferred_element_type=jnp.float32
        )
        grad_keys = grad_keys + jnp.einsum(
            "skgql,sqkgd->slkd", d_scores, query_low, preferred_element_type=jnp.float32
        )
        grad_values = grad_values + jnp.einsum(
            "skgql,skgqd->slkd", probs_low, d_mixed_grid, preferred_element_type=jnp.float32
        )
        grad_keys, grad_values = (
            from_behind(grad_keys.astype(jnp.bfloat16), "ctx", 1).astype(grad_keys.dtype),
            from_behind(grad_values.astype(jnp.bfloat16), "ctx", 1).astype(grad_values.dtype),
        )
        return ((grad_queries, grad_keys, grad_values), None)

    kv_shape = (SEQS, block_span, kv_heads, HEAD_SIZE)
    start_carry = (
        jnp.zeros(stat_shape + (HEAD_SIZE,), jnp.float32),
        jnp.zeros(kv_shape, jnp.float32),
        jnp.zeros(kv_shape, jnp.float32),
    )
    (grad_queries, grad_keys, grad_values), unused_out = lax.scan(
        revisit, start_carry, jnp.arange(ctx_count, dtype=jnp.int32)
    )
    grad_queries = (
        jnp.transpose(grad_queries, (0, 3, 1, 2, 4)).reshape(ctx_rows, q_heads, HEAD_SIZE)
        * scale_qk
    )
    grad_keys = grad_keys.reshape(ctx_rows, kv_heads, HEAD_SIZE) * scale_qk
    d_values = grad_values.reshape(ctx_rows, kv_heads * HEAD_SIZE).astype(jnp.bfloat16)
    query_back = rotate_back(grad_queries, cosine, sine)
    grad_q_local = jnp.sum(query_back * query_unit, axis=(0, 1))
    d_query_lin = (
        rms_back(query_lin, query_scale, query_back * q_gain)
        .reshape(ctx_rows, q_heads * HEAD_SIZE)
        .astype(jnp.bfloat16)
    )
    key_back = rotate_back(grad_keys, cosine, sine)
    grad_k_local = jnp.sum(key_back * key_unit, axis=(0, 1))
    d_key_lin = (
        rms_back(key_linear, key_scale, key_back * k_gain)
        .reshape(ctx_rows, kv_heads * HEAD_SIZE)
        .astype(jnp.bfloat16)
    )
    grad_wq = matmul_tn(normed_all, d_query_lin)
    grad_wk = matmul_tn(normed_all, d_key_lin)
    grad_wv = matmul_tn(normed_all, d_values)
    start = jnp.int32(0)
    part_query = matmul_nt(row_slice(d_query_lin, start, lax.axis_size("tp") * tok_rows), bq_full)
    part_key = matmul_nt(row_slice(d_key_lin, start, lax.axis_size("tp") * tok_rows), bk_full)
    part_value = matmul_nt(row_slice(d_values, start, lax.axis_size("tp") * tok_rows), bv_full)
    d_normed = lax.psum_scatter(
        (part_query + part_key + part_value).astype(jnp.bfloat16),
        "tp",
        scatter_dimension=0,
        tiled=True,
    ).astype(jnp.float32)
    grad_in_local = jnp.sum(d_normed * unit_in, axis=0)
    d_tokens = (d_middle + rms_back(stream, scale_in, d_normed * in_gain)).astype(jnp.bfloat16)
    summed = (
        lax.psum_scatter(
            grad_wq.astype(jnp.bfloat16), "ctx", scatter_dimension=0, tiled=True
        ).astype(jnp.float32),
        lax.psum_scatter(
            grad_wk.astype(jnp.bfloat16), "ctx", scatter_dimension=0, tiled=True
        ).astype(jnp.float32),
        lax.psum_scatter(
            grad_wv.astype(jnp.bfloat16), "ctx", scatter_dimension=0, tiled=True
        ).astype(jnp.float32),
        lax.psum_scatter(
            grad_wo.astype(jnp.bfloat16), "ctx", scatter_dimension=1, tiled=True
        ).astype(jnp.float32),
        lax.psum_scatter(
            grad_wg.astype(jnp.bfloat16), "ctx", scatter_dimension=0, tiled=True
        ).astype(jnp.float32),
        lax.psum_scatter(
            grad_wu.astype(jnp.bfloat16), "ctx", scatter_dimension=0, tiled=True
        ).astype(jnp.float32),
        lax.psum_scatter(
            grad_wd.astype(jnp.bfloat16), "ctx", scatter_dimension=1, tiled=True
        ).astype(jnp.float32),
    )
    totals = lax.psum(
        (grad_in_local, grad_q_local, grad_k_local, grad_post_local, error_local), ("ctx", "tp")
    )
    count_valid = jnp.sum(seq_lens).astype(jnp.float32)
    loss = 0.5 * totals[4] / (count_valid * MODEL_WIDTH)
    return (
        output,
        loss,
        d_tokens,
        totals[0],
        summed[0],
        summed[1],
        summed[2],
        totals[1],
        totals[2],
        summed[3],
        totals[3],
        summed[4],
        summed[5],
        summed[6],
    )


F32 = jnp.float32
BF16 = jnp.bfloat16
MESH = pl.DeviceIdType.MESH
VMEM_LIMIT = 62 << 20


def busy(us):
    return pl.CostEstimate(flops=0, bytes_accessed=us * 3_000_000, transcendentals=0)

LOG2E = 1.4426950408889634
UNIT = 128
KEYS = 512
CORE_GROUPS = [[0, 2, 4, 6], [1, 3, 5, 7]]
SIBLING = [(i, i ^ 1) for i in range(8)]


def spec_vmem():
    return pl.BlockSpec(memory_space=pltpu.VMEM)


def spec_any():
    return pl.BlockSpec(memory_space=pl.ANY)


def spec_smem():
    return pl.BlockSpec(memory_space=pltpu.SMEM)


def plane_neighbours():
    me = lax.axis_index("ctx")
    core = lax.rem(me, 2)
    x = lax.rem(me // 2, 2)
    y = me // 4
    sib = me + 1 - 2 * core
    nx = me + 2 - 4 * x
    ny = me + 4 - 8 * y
    dg = nx + 4 - 8 * y
    return me, sib, nx, ny, dg


def greet(devices):
    barrier = pltpu.get_barrier_semaphore()
    for device in devices:
        pl.semaphore_signal(barrier, inc=1, device_id={"ctx": device}, device_id_type=MESH)
    pl.semaphore_wait(barrier, len(devices))


def pick(step, options):
    value = options[0]
    for i in range(1, len(options)):
        value = jnp.where(step == i, options[i], value)
    return value


SUBS = 4


def on_ctx(device):
    return {"ctx": device}


def on_plane(plane):
    return {"tp": plane}


def send(src, dst, send_sem, recv_sem, where):
    return pltpu.make_async_remote_copy(
        src_ref=src,
        dst_ref=dst,
        send_sem=send_sem,
        recv_sem=recv_sem,
        device_id=where,
        device_id_type=MESH,
    )


class Gather:
    def __init__(self, x_ref, xs, local_sem, send_sems, recv_sems):
        self.x_ref, self.xs = x_ref, xs
        self.local_sem, self.send_sems, self.recv_sems = local_sem, send_sems, recv_sems
        self.me, self.sib, self.nx, self.ny, self.dg = plane_neighbours()
        self.shift = self.sib - self.me
        self.piece = x_ref.shape[0] // SUBS

    def part(self, block, s):
        return self.xs.at[block, pl.ds(s * self.piece, self.piece)]

    def remote(self, src, kind, block, s, device):
        return send(
            src, self.part(block, s), self.send_sems.at[kind, s], self.recv_sems.at[block, s], on_ctx(device)
        )

    def own(self, s):
        return self.x_ref.at[pl.ds(s * self.piece, self.piece)]

    def start(self):
        for s in range(SUBS):
            t = (s + SUBS // 2) % SUBS
            self.remote(self.own(s), 0, self.me, s, self.nx).start()
            self.remote(self.own(t), 1, self.me, t, self.ny).start()
        for s in range(SUBS):
            self.remote(self.own(s), 2, self.me, s, self.sib).start()
        keep = pltpu.make_async_copy(self.x_ref, self.xs.at[self.me], self.local_sem)
        keep.start()
        keep.wait()

    def arrived(self, block, s):
        self.remote(self.part(block, s), 0, block, s, self.sib).wait_recv()

    def relay(self, kind, block, s, device):
        self.remote(self.part(block, s), kind, block, s, device).start()

    def before(self, step):
        half = SUBS // 2

        @pl.when(step == 1)
        def _():
            for s in range(SUBS):
                self.arrived(self.sib, s)

        @pl.when(step == 2)
        def _():
            for s in range(SUBS):
                self.arrived(self.nx, s)
                if s < half:
                    self.relay(3, self.nx, s, self.ny)
                self.relay(4, self.nx, s, self.sib)
                t = (s + half) % SUBS
                self.arrived(self.ny, t)
                if t >= half:
                    self.relay(3, self.ny, t, self.nx)
                self.relay(5, self.ny, t, self.sib)

        @pl.when(step == 3)
        def _():
            for s in range(SUBS):
                self.arrived(self.nx + self.shift, s)

        @pl.when(step == 4)
        def _():
            for s in (0, half):
                self.arrived(self.dg, s)
                self.relay(6, self.dg, s, self.sib)

        @pl.when(step == 5)
        def _():
            for s in range(SUBS):
                self.arrived(self.ny + self.shift, s)

        @pl.when(step == 6)
        def _():
            for s in range(SUBS):
                if s % half:
                    self.arrived(self.dg, s)
                    self.relay(6, self.dg, s, self.sib)

        @pl.when(step == 7)
        def _():
            for s in range(SUBS):
                self.arrived(self.dg + self.shift, s)

    def block(self, step):
        near = (self.me, self.nx, self.ny, self.dg)
        return pick(step, [b + o for b in near for o in (0, self.shift)])

    def finish(self):
        for s in range(SUBS):
            for kind in range(7):
                self.remote(self.part(self.me, s), kind, self.me, s, self.sib).wait_send()


def gather_scratch(rows, width):
    return [
        pltpu.VMEM((8, rows, width), BF16),
        pltpu.SemaphoreType.DMA,
        pltpu.SemaphoreType.DMA((7, SUBS)),
        pltpu.SemaphoreType.DMA((8, SUBS)),
    ]


class Scatter:
    def __init__(self, to_sib, from_sib, own, diag_out, diag_in, x_out, y_out, x_in, y_in, sends, recvs):
        self.to_sib, self.from_sib, self.own = to_sib, from_sib, own
        self.diag_out, self.diag_in = diag_out, diag_in
        self.x_out, self.y_out, self.x_in, self.y_in = x_out, y_out, x_in, y_in
        self.sends, self.recvs = sends, recvs
        self.me, self.sib, self.nx, self.ny, self.dg = plane_neighbours()
        half = diag_out.shape[0] // 2
        self.first, self.second = first, second = pl.ds(0, half), pl.ds(half, half)
        nx, ny = self.nx, self.ny
        self.diag_x = self.remote(diag_out.at[first], diag_in.at[first], 4, nx)
        self.diag_y = self.remote(diag_out.at[second], diag_in.at[second], 5, ny)
        self.x_first = self.remote(x_out.at[first], x_in.at[first], 6, nx)
        self.x_second = self.remote(x_out.at[second], x_in.at[second], 7, nx)
        self.y_first = self.remote(y_out.at[first], y_in.at[first], 8, ny)
        self.y_second = self.remote(y_out.at[second], y_in.at[second], 9, ny)

    def remote(self, src, dst, n, device):
        return send(src, dst, self.sends.at[n], self.recvs.at[n], on_ctx(device))

    def sibling(self, n):
        return self.remote(self.to_sib.at[n], self.from_sib.at[n], n, self.sib)

    def block(self, step):
        shift = self.sib - self.me
        return pick(step, [b + o for b in (self.dg, self.nx, self.ny, self.me) for o in (shift, 0)])

    def chip_sum(self, n, at):
        return self.own[n, at].astype(F32) + self.from_sib[n, at].astype(F32)

    def step(self, step, product):
        block = self.block(step)
        n = step // 2
        first, second = self.first, self.second

        @pl.when(lax.rem(step, 2) == 0)
        def _():
            product(block, self.to_sib, n)
            self.sibling(n).start()

        @pl.when(lax.rem(step, 2) == 1)
        def _():
            product(block, self.own, n)
            self.sibling(n).wait_recv()

        @pl.when(step == 1)
        def _():
            self.diag_out[first] = self.chip_sum(0, first).astype(BF16)
            self.diag_x.start()
            self.diag_out[second] = self.chip_sum(0, second).astype(BF16)
            self.diag_y.start()

        @pl.when(step == 3)
        def _():
            self.x_out[first] = self.chip_sum(1, first).astype(BF16)
            self.x_first.start()

        @pl.when(step == 5)
        def _():
            self.y_out[second] = self.chip_sum(2, second).astype(BF16)
            self.y_second.start()
            self.diag_x.wait_recv()
            self.y_out[first] = (self.chip_sum(2, first) + self.diag_in[first].astype(F32)).astype(BF16)
            self.y_first.start()
            self.diag_y.wait_recv()
            self.x_out[second] = (self.chip_sum(1, second) + self.diag_in[second].astype(F32)).astype(BF16)
            self.x_second.start()

    def finish(self, o_ref):
        self.x_first.wait_recv()
        self.y_first.wait_recv()
        first, second = self.first, self.second
        o_ref[first] = (
            self.chip_sum(3, first) + self.x_in[first].astype(F32) + self.y_in[first].astype(F32)
        ).astype(o_ref.dtype)
        self.x_second.wait_recv()
        self.y_second.wait_recv()
        o_ref[second] = (
            self.chip_sum(3, second) + self.x_in[second].astype(F32) + self.y_in[second].astype(F32)
        ).astype(o_ref.dtype)
        for n in range(4):
            self.sibling(n).wait_send()
        for copy in (self.diag_x, self.diag_y, self.x_first, self.x_second, self.y_first, self.y_second):
            copy.wait_send()


def scatter_scratch(rows, width):
    four = pltpu.VMEM((4, rows, width), BF16)
    one = pltpu.VMEM((rows, width), BF16)
    return [four] * 3 + [one] * 6 + [pltpu.SemaphoreType.DMA((10,)), pltpu.SemaphoreType.DMA((10,))]


N_SCATTER = 11


def nn(left, right):
    return lax.dot_general(left, right, (((1,), (0,)), ((), ())), preferred_element_type=F32)


def nt(left, right):
    return lax.dot_general(left, right, (((1,), (1,)), ((), ())), preferred_element_type=F32)


def tn(left, right):
    return lax.dot_general(left, right, (((0,), (0,)), ((), ())), preferred_element_type=F32)


def comm_params(collective_id):
    return pltpu.CompilerParams(
        collective_id=collective_id, has_side_effects=True, vmem_limit_bytes=VMEM_LIMIT
    )


def greet_column(devices):
    barrier = pltpu.get_barrier_semaphore()
    plane, planes = lax.axis_index("tp"), lax.axis_size("tp")
    for device in devices:
        pl.semaphore_signal(barrier, inc=1, device_id=on_ctx(device), device_id_type=MESH)
    for step in (1, planes - 1):
        where = on_plane(lax.rem(plane + step, planes))
        pl.semaphore_signal(barrier, inc=1, device_id=where, device_id_type=MESH)
    pl.semaphore_wait(barrier, len(devices) + 2)


class Line:
    def __init__(self, up_src, down_src, from_lo, from_hi, sends, recvs, rows, back):
        self.up_src, self.down_src, self.from_lo, self.from_hi = up_src, down_src, from_lo, from_hi
        self.sends, self.recvs = sends, recvs
        self.units = rows // UNIT
        self.back = back
        self.plane, self.planes = lax.axis_index("tp"), lax.axis_size("tp")

    def at(self, block, i):
        return pl.ds(pl.multiple_of((block * self.units + i) * UNIT, UNIT), UNIT)

    def up(self, block, i):
        at, n = self.at(block, i), block * self.units + i
        return send(self.up_src.at[at], self.from_lo.at[at], self.sends.at[0, n], self.recvs.at[0, n], on_plane(self.plane + 1))

    def down(self, block, i):
        at, n = self.at(block, i), block * self.units + i
        return send(self.down_src.at[at], self.from_hi.at[at], self.sends.at[1, n], self.recvs.at[1, n], on_plane(self.plane - 1))

    def each(self, block, ups, downs):
        for i in range(self.units):
            up = i < self.plane + 1 if self.back else i >= self.plane
            down = i >= self.plane - 1 if self.back else i < self.plane

            @pl.when(up & (self.plane < self.planes - 1))
            def _():
                ups(self.up(block, i))

            @pl.when(down & (self.plane > 0))
            def _():
                downs(self.down(block, i))

    def start(self, block):
        self.each(block, lambda copy: copy.start(), lambda copy: copy.start())

    def sent(self, block):
        self.each(block, lambda copy: copy.wait_send(), lambda copy: copy.wait_send())

    def arrived(self, block):
        for i in range(self.units):
            below = i < self.plane if self.back else i >= self.plane - 1
            above = i >= self.plane if self.back else i < self.plane + 1

            @pl.when(below & (self.plane > 0))
            def _():
                self.up(block, i).wait_recv()

            @pl.when(above & (self.plane < self.planes - 1))
            def _():
                self.down(block, i).wait_recv()


class Turn:
    def __init__(self, ca_ref, sa_ref, cb_ref, sb_ref, unit):
        ca, sa = ca_ref[pl.ds(unit, 1), :], sa_ref[pl.ds(unit, 1), :]
        cb, sb = cb_ref[...], sb_ref[...]
        self.cosine = ca * cb - sa * sb
        sine = sa * cb + ca * sb
        lane = lax.broadcasted_iota(jnp.int32, sine.shape, 1)
        self.sine = jnp.where(lane < HEAD_SIZE // 2, -sine, sine)

    def forth(self, v):
        return v * self.cosine + pltpu.roll(v, HEAD_SIZE // 2, 1) * self.sine

    def back(self, v):
        return v * self.cosine - pltpu.roll(v, HEAD_SIZE // 2, 1) * self.sine


def others(me):
    _, sib, nx, ny, dg = plane_neighbours()
    shift = sib - me
    return (dg, dg + shift, nx, nx + shift, ny, ny + shift, sib)


def qkv_kernel(
    x_ref,
    slab_ref,
    qg_ref,
    kg_ref,
    ca_ref,
    sa_ref,
    cb_ref,
    sb_ref,
    all_ref,
    w_out_ref,
    q_ref,
    kv_ref,
    lo_ref,
    hi_ref,
    lin_ref,
    xs,
    local_sem,
    send_sems,
    recv_sems,
    keep_sems,
    w,
    w_local,
    w_sends,
    w_recvs,
    kv_sends,
    kv_recvs,
):
    ring = Gather(x_ref, xs, local_sem, send_sems, recv_sems)
    me = ring.me
    rows = x_ref.shape[0]
    deep = slab_ref.shape[1]
    away = others(me)
    greet_column(away)

    def weight(device, n):
        return send(slab_ref.at[device], w.at[pl.ds(me * deep, deep)], w_sends.at[n], w_recvs.at[me], on_ctx(device))

    def weight_from(device):
        return send(slab_ref.at[device], w.at[pl.ds(device * deep, deep)], w_sends.at[0], w_recvs.at[device], on_ctx(device))

    for n, device in enumerate(away):
        weight(device, n).start()
    own_weight = pltpu.make_async_copy(slab_ref.at[me], w.at[pl.ds(me * deep, deep)], w_local)
    own_weight.start()
    ring.start()
    own_weight.wait()
    for device in away:
        weight_from(device).wait_recv()
    keep_w = pltpu.make_async_copy(w, w_out_ref, w_local)
    keep_w.start()

    def keep(block):
        return pltpu.make_async_copy(xs.at[block], all_ref.at[block], keep_sems.at[block])

    line = Line(kv_ref, kv_ref, lo_ref, hi_ref, kv_sends, kv_recvs, rows, False)

    def head(v, gain_ref, turn):
        scale = lax.rsqrt(jnp.mean(v * v, axis=-1, keepdims=True) + EPS)
        return turn.forth(v * scale * gain_ref[...])

    def turn(step, carry):
        ring.before(step)
        block = ring.block(step)
        keep(block).start()
        lin = nn(xs[block], w[...])
        lin_ref[pl.ds(pl.multiple_of(block * rows, rows), rows), :] = lin[:, : 3 * HEAD_SIZE]
        for i in range(rows // UNIT):
            unit = block * (rows // UNIT) + i
            rotation = Turn(ca_ref, sa_ref, cb_ref, sb_ref, unit)
            here = pl.ds(pl.multiple_of(unit * UNIT, UNIT), UNIT)
            part = lin[i * UNIT : (i + 1) * UNIT]
            for h in range(2):
                lanes = slice(h * HEAD_SIZE, (h + 1) * HEAD_SIZE)
                query = head(part[:, lanes], qg_ref, rotation)
                q_ref[here, lanes] = (query * (HEAD_SIZE**-0.5 * LOG2E)).astype(BF16)
            key = head(part[:, 2 * HEAD_SIZE : 3 * HEAD_SIZE], kg_ref, rotation)
            kv_ref[here, :HEAD_SIZE] = key.astype(BF16)
            kv_ref[here, HEAD_SIZE:] = part[:, 3 * HEAD_SIZE :].astype(BF16)
        line.start(block)
        return carry

    lax.fori_loop(0, 8, turn, 0)
    ring.finish()
    keep_w.wait()
    for n, device in enumerate(away):
        weight(device, n).wait_send()
    for block in range(8):
        keep(block).wait()

    def settle(block, carry):
        line.sent(block)
        line.arrived(block)
        return carry

    lax.fori_loop(0, 8, settle, 0)


def gather_qkv(normed, slab, q_gain, k_gain, tables):
    rows, width = normed.shape
    _, deep, cols = slab.shape
    flat = jax.ShapeDtypeStruct((8 * rows, 2 * HEAD_SIZE), BF16)
    return pl.pallas_call(
        qkv_kernel,
        out_shape=(
            jax.ShapeDtypeStruct((8, rows, width), BF16),
            jax.ShapeDtypeStruct((8 * deep, cols), BF16),
            flat,
            flat,
            flat,
            flat,
            jax.ShapeDtypeStruct((8 * rows, 3 * HEAD_SIZE), F32),
        ),
        in_specs=[spec_vmem(), spec_any()] + [spec_vmem()] * 6,
        out_specs=(spec_any(), spec_any(), spec_vmem(), spec_vmem(), spec_any(), spec_any(), spec_vmem()),
        scratch_shapes=gather_scratch(rows, width)
        + [
            pltpu.SemaphoreType.DMA((8,)),
            pltpu.VMEM((8 * deep, cols), BF16),
            pltpu.SemaphoreType.DMA,
            pltpu.SemaphoreType.DMA((7,)),
            pltpu.SemaphoreType.DMA((8,)),
            pltpu.SemaphoreType.DMA((2, 8 * rows // UNIT)),
            pltpu.SemaphoreType.DMA((2, 8 * rows // UNIT)),
        ],
        compiler_params=comm_params(1),
        cost_estimate=busy(80),
        name="gather_qkv",
    )(normed, slab, q_gain.reshape(1, -1), k_gain.reshape(1, -1), *tables)


class Halves:
    def __init__(self, parts, at, local_sems, send_sems, recv_sems):
        self.parts, self.at = parts, at
        self.local_sems, self.send_sems, self.recv_sems = local_sems, send_sems, recv_sems
        self.me, self.sib = plane_neighbours()[:2]
        self.core = lax.rem(self.me, 2)

    def own(self, z, p):
        n = 4 * z + p
        return pltpu.make_async_copy(
            self.parts.at[2 * self.core + z, p], self.at(z, 2 * p + self.core), self.local_sems.at[n]
        )

    def swap(self, z, p):
        n = 4 * z + p
        return send(
            self.parts.at[2 - 2 * self.core + z, p],
            self.at(z, 2 * p + self.core),
            self.send_sems.at[n],
            self.recv_sems.at[n],
            on_ctx(self.sib),
        )

    def each(self):
        return [(z, p) for z in range(2) for p in range(4)]

    def start(self):
        for z, p in self.each():
            self.swap(z, p).start()
            self.own(z, p).start()

    def ready(self):
        for z, p in self.each():
            self.own(z, p).wait()
            n = 4 * z + p
            send(
                self.parts.at[2 * self.core + z, p],
                self.at(z, 2 * p + 1 - self.core),
                self.send_sems.at[n],
                self.recv_sems.at[n],
                on_ctx(self.sib),
            ).wait_recv()

    def finish(self):
        for z, p in self.each():
            self.swap(z, p).wait_send()


class Shares:
    def __init__(self, out, local_sems, send_sems, recv_sems):
        self.out = out
        self.local_sems, self.send_sems, self.recv_sems = local_sems, send_sems, recv_sems
        self.me, self.sib = plane_neighbours()[:2]
        self.core = lax.rem(self.me, 2)

    def own(self, tile, z, p):
        return pltpu.make_async_copy(tile, self.out.at[2 * self.core + z, p], self.local_sems.at[z, p])

    def other(self, tile, z, p):
        return send(
            tile,
            self.out.at[2 * self.core + z, p],
            self.send_sems.at[z, p],
            self.recv_sems.at[z, p],
            on_ctx(self.sib),
        )

    def arrive(self):
        for z in range(2):
            for p in range(4):
                there = self.out.at[2 - 2 * self.core + z, p]
                send(
                    there, there, self.send_sems.at[z, p], self.recv_sems.at[z, p], on_ctx(self.sib)
                ).wait_recv()


SHARES_SCRATCH = [pltpu.SemaphoreType.DMA((2, 4))] * 3
HALVES_SCRATCH = [pltpu.SemaphoreType.DMA((8,))] * 3


def up_kernel(
    x_ref,
    gate_ref,
    up_ref,
    all_ref,
    w_out_ref,
    a_ref,
    b_ref,
    h_ref,
    xs,
    local_sem,
    send_sems,
    recv_sems,
    keep_sems,
    stage,
    stage_sems,
    w,
    w_sem,
    *w_sems,
):
    ring = Gather(x_ref, xs, local_sem, send_sems, recv_sems)
    rows = x_ref.shape[0]
    halves, width, wide = w.shape
    deep = width // 8
    cols = wide // 2
    outs = (a_ref, b_ref, h_ref)
    greet((ring.sib, ring.nx, ring.ny))
    ring.start()
    gates = Halves(gate_ref, lambda z, c: w.at[z, pl.ds(c * deep, deep), pl.ds(0, cols)], *w_sems[:3])
    ups = Halves(up_ref, lambda z, c: w.at[z, pl.ds(c * deep, deep), pl.ds(cols, cols)], *w_sems[3:])
    gates.start()
    ups.start()
    gates.ready()
    ups.ready()
    keep_w = pltpu.make_async_copy(w, w_out_ref, w_sem)
    keep_w.start()

    def keep(block):
        return pltpu.make_async_copy(xs.at[block], all_ref.at[block], keep_sems.at[block])

    def put(slot, n, block):
        return pltpu.make_async_copy(
            stage.at[slot, n], outs[n].at[pl.ds(block * rows, rows)], stage_sems.at[slot, n]
        )

    def turn(step, carry):
        ring.before(step)
        block = ring.block(step)
        keep(block).start()
        slot = lax.rem(step, 2)

        @pl.when(step >= 2)
        def _():
            for n in range(3):
                put(slot, n, block).wait()

        for z in range(halves):
            both = nn(xs[block], w[z])
            gate, up = both[:, :cols], both[:, cols:]
            sigma = jax.nn.sigmoid(gate)
            active = gate * sigma
            here = slice(z * cols, (z + 1) * cols)
            stage[slot, 0, :, here] = (up * sigma * (1.0 + gate * (1.0 - sigma))).astype(BF16)
            stage[slot, 1, :, here] = active.astype(BF16)
            stage[slot, 2, :, here] = (active * up).astype(BF16)
        for n in range(3):
            put(slot, n, block).start()
        return carry

    lax.fori_loop(0, 8, turn, 0)
    ring.finish()
    gates.finish()
    ups.finish()
    keep_w.wait()
    for block in range(8):
        keep(block).wait()
    for slot in range(2):
        for n in range(3):
            put(slot, n, 0).wait()


def gather_up(post, gate_parts, up_parts):
    rows, width = post.shape
    wide = 2 * gate_parts.shape[-1]
    flat = jax.ShapeDtypeStruct((8 * rows, wide), BF16)
    return pl.pallas_call(
        up_kernel,
        out_shape=(
            jax.ShapeDtypeStruct((8, rows, width), BF16),
            jax.ShapeDtypeStruct((2, width, wide), BF16),
            flat,
            flat,
            flat,
        ),
        in_specs=[spec_vmem(), spec_any(), spec_any()],
        out_specs=(spec_any(),) * 5,
        scratch_shapes=gather_scratch(rows, width)
        + [
            pltpu.SemaphoreType.DMA((8,)),
            pltpu.VMEM((2, 3, rows, wide), BF16),
            pltpu.SemaphoreType.DMA((2, 3)),
            pltpu.VMEM((2, width, wide), BF16),
            pltpu.SemaphoreType.DMA,
        ]
        + HALVES_SCRATCH * 2,
        compiler_params=comm_params(2),
        cost_estimate=busy(62),
        name="gather_up",
    )(post, gate_parts, up_parts)


def down_kernel(h_ref, parts_ref, o_ref, w_out_ref, *scratch):
    rs = Scatter(*scratch[:N_SCATTER])
    w, w_sem, w_local, w_sends, w_recvs = scratch[N_SCATTER:]
    rows = o_ref.shape[0]
    _, _, cols, deep = parts_ref.shape
    greet((rs.sib, rs.nx, rs.ny))
    weight = Halves(
        parts_ref,
        lambda z, c: w.at[pl.ds(z * cols, cols), pl.ds(pl.multiple_of(c * deep, deep), deep)],
        w_local,
        w_sends,
        w_recvs,
    )
    weight.start()
    weight.ready()
    keep_w = pltpu.make_async_copy(w, w_out_ref, w_sem)
    keep_w.start()

    def product(block, out, n):
        left = h_ref[pl.ds(pl.multiple_of(block * rows, rows), rows), :]
        for c in range(0, w.shape[1], 512):
            out[n, :, c : c + 512] = nn(left, w[:, c : c + 512]).astype(BF16)

    def turn(step, carry):
        rs.step(step, product)
        return carry

    lax.fori_loop(0, 8, turn, 0)
    rs.finish(o_ref)
    weight.finish()
    keep_w.wait()


def scatter_down(hidden, parts):
    rows = hidden.shape[0] // 8
    ff = hidden.shape[1]
    width = 8 * parts.shape[-1]
    return pl.pallas_call(
        down_kernel,
        out_shape=(jax.ShapeDtypeStruct((rows, width), F32), jax.ShapeDtypeStruct((ff, width), BF16)),
        in_specs=[spec_vmem(), spec_any()],
        out_specs=(spec_vmem(), spec_any()),
        scratch_shapes=scatter_scratch(rows, width)
        + [pltpu.VMEM((ff, width), BF16), pltpu.SemaphoreType.DMA]
        + HALVES_SCRATCH,
        compiler_params=comm_params(6),
        cost_estimate=busy(62),
        name="scatter_down",
    )(hidden, parts)


def down_back_kernel(
    x_ref,
    w_ref,
    a_ref,
    b_ref,
    h_ref,
    d_ref,
    gw_ref,
    xs,
    local_sem,
    send_sems,
    recv_sems,
    stage,
    stage_sems,
    total,
    low,
    s_local,
    s_sends,
    s_recvs,
):
    ring = Gather(x_ref, xs, local_sem, send_sems, recv_sems)
    rows = x_ref.shape[0]
    ff = w_ref.shape[0]
    cols = ff // 2
    width = x_ref.shape[1]
    greet((ring.sib, ring.nx, ring.ny))
    ring.start()
    total[...] = jnp.zeros_like(total)
    shares = Shares(gw_ref, s_local, s_sends, s_recvs)
    deep = width // 8

    def tile(z, c):
        return low.at[pl.ds(z * cols, cols), pl.ds(pl.multiple_of(c * deep, deep), deep)]

    def put(slot, block):
        return pltpu.make_async_copy(
            stage.at[slot], d_ref.at[pl.ds(block * rows, rows)], stage_sems.at[slot]
        )

    def turn(step, carry):
        ring.before(step)
        block = ring.block(step)
        slot = lax.rem(step, 2)

        @pl.when(step >= 2)
        def _():
            put(slot, block).wait()

        here = pl.ds(block * rows, rows)
        for z in range(2):
            part = slice(z * cols, (z + 1) * cols)
            grad = nt(xs[block], w_ref[part, :])
            stage[slot, :, 2 * z * cols : (2 * z + 1) * cols] = (
                grad * a_ref[here, part].astype(F32)
            ).astype(BF16)
            stage[slot, :, (2 * z + 1) * cols : (2 * z + 2) * cols] = (
                grad * b_ref[here, part].astype(F32)
            ).astype(BF16)
        put(slot, block).start()

        @pl.when(slot == 1)
        def _():
            pair = block // 2
            hidden = h_ref[pl.ds(pair * 2 * rows, 2 * rows), :]
            for n in range(0, width, 512):
                seen = xs[pl.ds(pair * 2, 2), :, n : n + 512].reshape(2 * rows, 512)
                total[:, n : n + 512] += tn(hidden, seen)

        return carry

    lax.fori_loop(0, 8, turn, 0)
    ring.finish()
    low[...] = total[...].astype(BF16)
    core = shares.core
    for z in range(2):
        for p in range(4):
            shares.other(tile(z, 2 * p + 1 - core), z, p).start()
            shares.own(tile(z, 2 * p + core), z, p).start()
    for slot in range(2):
        put(slot, 0).wait()
    shares.arrive()
    for z in range(2):
        for p in range(4):
            shares.other(tile(z, 2 * p + 1 - core), z, p).wait_send()
            shares.own(tile(z, 2 * p + core), z, p).wait()


def gather_down_back(diff, w_down, a, b, hidden):
    rows, width = diff.shape
    ff = w_down.shape[0]
    return pl.pallas_call(
        down_back_kernel,
        out_shape=(
            jax.ShapeDtypeStruct((8 * rows, 2 * ff), BF16),
            jax.ShapeDtypeStruct((4, 4, ff // 2, width // 8), BF16),
        ),
        in_specs=[spec_vmem()] * 5,
        out_specs=(spec_any(), spec_any()),
        scratch_shapes=gather_scratch(rows, width)
        + [
            pltpu.VMEM((2, rows, 2 * ff), BF16),
            pltpu.SemaphoreType.DMA((2,)),
            pltpu.VMEM((ff, width), F32),
            pltpu.VMEM((ff, width), BF16),
        ]
        + SHARES_SCRATCH,
        compiler_params=comm_params(3),
        cost_estimate=busy(66),
        name="gather_down_back",
    )(diff, w_down, a, b, hidden)


def mix_kernel(
    mixed_ref,
    tokens_ref,
    gain_ref,
    w0_ref,
    w1_ref,
    w2_ref,
    w3_ref,
    middle_ref,
    post_ref,
    rows_ref,
    w_ref,
    held,
    w,
    m_sems,
    m_sends,
    m_recvs,
    w_local,
    w_sends,
    w_recvs,
    keep_sems,
):
    me, sib, nx, ny, dg = plane_neighbours()
    shift = sib - me
    away = others(me)
    rows, width = held.shape
    deep = width // 8
    greet(away)

    def block(c):
        return pl.ds(pl.multiple_of(c * rows, rows), rows)

    def lanes(c):
        return pl.ds(pl.multiple_of(c * deep, deep), deep)

    def give(n, c):
        return send(mixed_ref.at[block(c)], held.at[:, lanes(me)], m_sends.at[n], m_recvs.at[me], on_ctx(c))

    def take(c):
        return send(mixed_ref.at[block(c)], held.at[:, lanes(c)], m_sends.at[0], m_recvs.at[c], on_ctx(c))

    for n, c in enumerate(away):
        give(n, c).start()
    own = pltpu.make_async_copy(mixed_ref.at[block(me)], held.at[:, lanes(me)], m_sems)
    own.start()
    parts = ((w0_ref, me), (w1_ref, nx), (w2_ref, ny), (w3_ref, dg))

    def swap(n):
        part, c = parts[n]
        return send(part, w.at[:, lanes(c)], w_sends.at[n], w_recvs.at[n], on_ctx(sib))

    def place(n):
        part, c = parts[n]
        return pltpu.make_async_copy(part, w.at[:, lanes(c)], w_local.at[n])

    for n in range(4):
        swap(n).start()
        place(n).start()
    for n in range(4):
        place(n).wait()
        there = w.at[:, lanes(parts[n][1] + shift)]
        send(there, there, w_sends.at[n], w_recvs.at[n], on_ctx(sib)).wait_recv()
    own.wait()
    for c in away:
        take(c).wait_recv()
    keep_rows = pltpu.make_async_copy(held, rows_ref, keep_sems.at[0])
    keep_rows.start()
    keep_w = pltpu.make_async_copy(w, w_ref, keep_sems.at[1])
    keep_w.start()
    total = jnp.zeros((rows, 1), F32)
    for n in range(0, width, 512):
        at = slice(n, n + 512)
        middle = tokens_ref[:, at].astype(F32) + nn(held[...], w[:, at])
        middle_ref[:, at] = middle
        total += jnp.sum(middle * middle, axis=-1, keepdims=True)
    scale = lax.rsqrt(total / width + EPS)
    for n in range(0, width, 512):
        at = slice(n, n + 512)
        post_ref[:, at] = (middle_ref[:, at] * scale * gain_ref[:, at]).astype(BF16)
    for n, c in enumerate(away):
        give(n, c).wait_send()
    for n in range(4):
        swap(n).wait_send()
    keep_rows.wait()
    keep_w.wait()


def mix(mixed, tokens, post_gain, parts):
    rows, width = tokens.shape
    dma = pltpu.SemaphoreType.DMA
    return pl.pallas_call(
        mix_kernel,
        out_shape=(
            jax.ShapeDtypeStruct((rows, width), F32),
            jax.ShapeDtypeStruct((rows, width), BF16),
            jax.ShapeDtypeStruct((rows, width), BF16),
            jax.ShapeDtypeStruct((width, width), BF16),
        ),
        in_specs=[spec_any(), spec_vmem(), spec_vmem()] + [spec_any()] * 4,
        out_specs=(spec_vmem(), spec_vmem(), spec_any(), spec_any()),
        scratch_shapes=[
            pltpu.VMEM((rows, width), BF16),
            pltpu.VMEM((width, width), BF16),
            dma,
            dma((7,)),
            dma((8,)),
            dma((4,)),
            dma((4,)),
            dma((4,)),
            dma((2,)),
        ],
        compiler_params=comm_params(5),
        cost_estimate=busy(28),
        name="mix",
    )(mixed, tokens, post_gain.reshape(1, -1), *parts)


def mix_back_kernel(
    d_ref,
    w_ref,
    rows_ref,
    dm_ref,
    g0_ref,
    g1_ref,
    g2_ref,
    g3_ref,
    stage,
    to_sib,
    from_sib,
    own,
    out_sem,
    out_sends,
    out_recvs,
    s_sends,
    s_recvs,
    g_sems,
):
    me, sib, nx, ny, dg = plane_neighbours()
    shift = sib - me
    away = others(me)
    rows, width = d_ref.shape
    deep = width // 8
    greet(away)
    outs = (g0_ref, g1_ref, g2_ref, g3_ref)
    chips = (me, nx, ny, dg)

    def block(c):
        return pl.ds(pl.multiple_of(c * rows, rows), rows)

    def give(n, c):
        return send(stage.at[c], dm_ref.at[block(me)], out_sends.at[n], out_recvs.at[me], on_ctx(c))

    def take(c):
        return send(stage.at[c], dm_ref.at[block(c)], out_sends.at[0], out_recvs.at[c], on_ctx(c))

    def heads(n, carry):
        c = pick(n, away + (me,))
        at = pl.ds(pl.multiple_of(c * deep, deep), deep)
        stage[c] = nt(d_ref[...], w_ref[at, :]).astype(BF16)

        @pl.when(n < 7)
        def _():
            give(n, c).start()

        return carry

    lax.fori_loop(0, 8, heads, 0)
    keep = pltpu.make_async_copy(stage.at[me], dm_ref.at[block(me)], out_sem)
    keep.start()

    def swap(n):
        return send(to_sib.at[n], from_sib.at[n], s_sends.at[n], s_recvs.at[n], on_ctx(sib))

    def grad(n, out, c):
        at = pl.ds(pl.multiple_of(c * deep, deep), deep)
        out[n] = tn(rows_ref[...], d_ref[:, at]).astype(BF16)

    def theirs(n, carry):
        grad(n, to_sib, pick(n, chips) + shift)
        swap(n).start()
        return carry

    def ours(n, carry):
        grad(n, own, pick(n, chips))
        return carry

    lax.fori_loop(0, 4, theirs, 0)
    lax.fori_loop(0, 4, ours, 0)
    for n in range(4):
        swap(n).wait_recv()
        own[n] = (own[n].astype(F32) + from_sib[n].astype(F32)).astype(BF16)
        pltpu.make_async_copy(own.at[n], outs[n], g_sems.at[n]).start()
    for c in away:
        take(c).wait_recv()
    keep.wait()
    for n, c in enumerate(away):
        give(n, c).wait_send()
    for n in range(4):
        swap(n).wait_send()
        pltpu.make_async_copy(own.at[n], outs[n], g_sems.at[n]).wait()


def mix_back(d_mid, w, mixed_rows):
    rows, width = d_mid.shape
    deep = width // 8
    dma = pltpu.SemaphoreType.DMA
    four = pltpu.VMEM((4, width, deep), BF16)
    return pl.pallas_call(
        mix_back_kernel,
        out_shape=(jax.ShapeDtypeStruct((8 * rows, deep), BF16),)
        + (jax.ShapeDtypeStruct((width, deep), BF16),) * 4,
        in_specs=[spec_vmem()] * 3,
        out_specs=(spec_any(),) * 5,
        scratch_shapes=[
            pltpu.VMEM((8, rows, deep), BF16),
            four,
            four,
            four,
            dma,
            dma((7,)),
            dma((8,)),
            dma((4,)),
            dma((4,)),
            dma((4,)),
        ],
        compiler_params=comm_params(4),
        cost_estimate=busy(26),
        name="mix_back",
    )(d_mid, w, mixed_rows)


def columns(all_ref, slices, sems, c, slot):
    deep = slices.shape[-1]
    return pltpu.make_async_copy(
        all_ref.at[:, :, pl.ds(pl.multiple_of(c * deep, deep), deep)], slices.at[slot], sems.at[slot]
    )


def post_back_kernel(d_ref, w_ref, all_ref, o_ref, gw_ref, *scratch):
    rs = Scatter(*scratch[:N_SCATTER])
    slices, slice_sems, tile, s_local, s_sends, s_recvs = scratch[N_SCATTER:]
    shares = Shares(gw_ref, s_local, s_sends, s_recvs)
    rows = o_ref.shape[0]
    _, width, wide = w_ref.shape
    plane_rows = d_ref.shape[0]
    deep = width // 8
    greet((rs.sib, rs.nx, rs.ny))
    columns(all_ref, slices, slice_sems, 0, 0).start()

    def product(block, out, n):
        here = pl.ds(pl.multiple_of(block * rows, rows), rows)
        for c in range(0, width, 512):
            total = nt(d_ref[here, :wide], w_ref[0, c : c + 512, :])
            total += nt(d_ref[here, wide:], w_ref[1, c : c + 512, :])
            out[n, :, c : c + 512] = total.astype(BF16)

    def put(slot, p, act):
        @pl.when(slot == shares.core)
        def _():
            for z in range(2):
                copy = shares.own(tile.at[slot, z], z, p)
                copy.start() if act == "start" else copy.wait()

        @pl.when(slot != shares.core)
        def _():
            for z in range(2):
                copy = shares.other(tile.at[slot, z], z, p)
                copy.start() if act == "start" else copy.wait_send()

    def grad(c):
        slot = lax.rem(c, 2)
        columns(all_ref, slices, slice_sems, c, slot).wait()

        @pl.when(c < 7)
        def _():
            columns(all_ref, slices, slice_sems, c + 1, 1 - slot).start()

        @pl.when(c >= 2)
        def _():
            put(slot, c // 2 - 1, "wait")

        seen = slices[slot].reshape(plane_rows, deep)
        for z in range(2):
            tile[slot, z] = tn(seen, d_ref[:, z * wide : (z + 1) * wide]).astype(BF16)
        put(slot, c // 2, "start")

    def turn(t, carry):
        is_grad = ((t >= 5) & (t < 8)) | (t >= 11)

        @pl.when(is_grad)
        def _():
            grad(jnp.where(t < 8, t - 5, t - 8))

        @pl.when(jnp.logical_not(is_grad))
        def _():
            rs.step(jnp.where(t < 5, t, t - 3), product)

        return carry

    lax.fori_loop(0, 16, turn, 0)
    rs.finish(o_ref)
    for slot in range(2):
        put(slot, 3, "wait")
    shares.arrive()


def scatter_post(d_gu, w_gu, post_all):
    _, rows, width = post_all.shape
    wide = w_gu.shape[-1]
    deep = width // 8
    return pl.pallas_call(
        post_back_kernel,
        out_shape=(
            jax.ShapeDtypeStruct((rows, width), F32),
            jax.ShapeDtypeStruct((4, 4, deep, wide), BF16),
        ),
        in_specs=[spec_vmem(), spec_vmem(), spec_any()],
        out_specs=(spec_vmem(), spec_any()),
        scratch_shapes=scatter_scratch(rows, width)
        + [
            pltpu.VMEM((2, 8, rows, deep), BF16),
            pltpu.SemaphoreType.DMA((2,)),
            pltpu.VMEM((2, 2, deep, wide), BF16),
        ]
        + SHARES_SCRATCH,
        compiler_params=comm_params(7),
        cost_estimate=busy(66),
        name="scatter_post",
    )(d_gu, w_gu, post_all)


def normed_back_kernel(
    dq_ref,
    dkv_ref,
    to_lo_ref,
    to_hi_ref,
    lin_ref,
    w_ref,
    all_ref,
    swap_a_ref,
    swap_b_ref,
    qg_ref,
    kg_ref,
    ca_ref,
    sa_ref,
    cb_ref,
    sb_ref,
    o_ref,
    gw_ref,
    gains_ref,
    swapped_a_ref,
    swapped_b_ref,
    *scratch,
):
    rs = Scatter(*scratch[:N_SCATTER])
    (
        from_lo,
        from_hi,
        d_lin,
        slices,
        slice_sems,
        tiles,
        tiles_in,
        planes_in,
        z_sends,
        z_recvs,
        t_sends,
        t_recvs,
        p_sends,
        p_recvs,
        c_local,
        c_sends,
        c_recvs,
    ) = scratch[N_SCATTER:]
    me = rs.me
    plane, planes = lax.axis_index("tp"), lax.axis_size("tp")
    rows, width = o_ref.shape
    deep = width // 8
    plane_rows = dq_ref.shape[0]
    units = rows // UNIT
    wide = 2 * HEAD_SIZE
    away = others(me)
    order = [b + o for b in (rs.dg, rs.nx, rs.ny, me) for o in (rs.sib - me, 0)]
    far = [lax.rem(plane + step, planes) for step in range(1, planes)]

    from_lo[...] = jnp.zeros_like(from_lo)
    from_hi[...] = jnp.zeros_like(from_hi)
    line = Line(to_hi_ref, to_lo_ref, from_lo, from_hi, z_sends, z_recvs, rows, True)
    barrier = pltpu.get_barrier_semaphore()
    for where in [on_ctx(c) for c in away] + [on_plane(p) for p in far]:
        pl.semaphore_signal(barrier, inc=1, device_id=where, device_id_type=MESH)
    pl.semaphore_wait(barrier, len(away) + len(far))

    def at_block(block):
        return pl.ds(pl.multiple_of(block * rows, rows), rows)

    for block in order:
        line.start(block)
    columns(all_ref, slices, slice_sems, order[0], 0).start()
    gains_ref[...] = jnp.zeros_like(gains_ref)

    def head_back(grad, lin, gain_ref, rotation):
        back = rotation.back(grad)
        scale = lax.rsqrt(jnp.mean(lin * lin, axis=-1, keepdims=True) + EPS)
        normal = lin * scale
        gained = back * gain_ref[...]
        d = scale * (gained - normal * jnp.mean(gained * normal, axis=-1, keepdims=True))
        return d.astype(BF16), jnp.sum(back * normal, axis=0, keepdims=True)

    def rotation_of(unit):
        return Turn(ca_ref, sa_ref, cb_ref, sb_ref, unit)

    def prepare_queries(unit, carry):
        rotation = rotation_of(unit)
        here = pl.ds(pl.multiple_of(unit * UNIT, UNIT), UNIT)
        for h in range(2):
            lanes = slice(h * HEAD_SIZE, (h + 1) * HEAD_SIZE)
            d, gain = head_back(dq_ref[here, lanes] * HEAD_SIZE**-0.5, lin_ref[here, lanes], qg_ref, rotation)
            d_lin[here, lanes] = d
            gains_ref[0:1, :] += gain
        return carry

    def prepare_keys(block):
        line.arrived(block)
        for i in range(units):
            unit = block * units + i
            here = pl.ds(pl.multiple_of(unit * UNIT, UNIT), UNIT)
            d_kv = dkv_ref[here, :] + from_lo[here, :].astype(F32) + from_hi[here, :].astype(F32)
            lanes = slice(2 * HEAD_SIZE, 3 * HEAD_SIZE)
            d, gain = head_back(d_kv[:, :HEAD_SIZE], lin_ref[here, lanes], kg_ref, rotation_of(unit))
            d_lin[here, lanes] = d
            gains_ref[1:2, :] += gain
            d_lin[here, 3 * HEAD_SIZE :] = d_kv[:, HEAD_SIZE:].astype(BF16)

    def tile_to(part, n, device):
        return send(
            tiles.at[part, device],
            tiles_in.at[part, me],
            t_sends.at[part, n],
            t_recvs.at[part, me],
            on_ctx(device),
        )

    def tile_from(part, device):
        return send(
            tiles.at[part, device],
            tiles_in.at[part, device],
            t_sends.at[part, 0],
            t_recvs.at[part, device],
            on_ctx(device),
        )

    def grads(part):
        def grad(n, carry):
            c = pick(n, order)
            slot = lax.rem(n, 2)
            columns(all_ref, slices, slice_sems, c, slot).wait()

            @pl.when((n < 7) | (part == 0))
            def _():
                columns(all_ref, slices, slice_sems, pick(lax.rem(n + 1, 8), order), 1 - slot).start()

            lanes = slice(part * wide, (part + 1) * wide)
            value = tn(slices[slot].reshape(plane_rows, deep), d_lin[:, lanes]).astype(BF16)

            @pl.when(n < 7)
            def _():
                tiles[part, c] = value
                tile_to(part, n, c).start()

            @pl.when(n == 7)
            def _():
                tiles_in[part, me] = value

            return carry

        lax.fori_loop(0, 8, grad, 0)

    def pair(part, p):
        return tiles_in.at[part, pl.ds(2 * p, 2)]

    def to_plane(part, n):
        return send(
            pair(part, far[n]),
            planes_in.at[part, plane],
            p_sends.at[part, n],
            p_recvs.at[part, plane],
            on_plane(far[n]),
        )

    def from_plane(part, p):
        return send(pair(part, p), planes_in.at[part, p], p_sends.at[part, 0], p_recvs.at[part, p], on_plane(p))

    def spread(part):
        for device in away:
            tile_from(part, device).wait_recv()
        for n in range(len(far)):
            to_plane(part, n).start()

    def collect(part):
        total = tiles_in[part, pl.ds(2 * plane, 2)].astype(F32)
        for p in far:
            from_plane(part, p).wait_recv()
            total += planes_in[part, p].astype(F32)
        gw_ref[part] = total

    def product(block, out, n):
        left = d_lin[at_block(block), :]
        for c in range(0, width, 512):
            out[n, :, c : c + 512] = nt(left, w_ref[c : c + 512, :]).astype(BF16)

    def turn(step, carry):
        prepare_keys(rs.block(step))
        rs.step(step, product)
        return carry

    lax.fori_loop(0, plane_rows // UNIT, prepare_queries, 0)
    grads(0)
    lax.fori_loop(0, 8, turn, 0)
    grads(1)
    chip = me // 2
    chips = (rs.dg, rs.nx, rs.ny)
    swaps = ((swap_a_ref, swapped_a_ref), (swap_b_ref, swapped_b_ref))

    def swap_own(i):
        return pltpu.make_async_copy(swaps[i][0].at[chip], swaps[i][1].at[chip], c_local.at[i])

    def swap_to(i, n):
        there = chips[n]
        return send(
            swaps[i][0].at[there // 2], swaps[i][1].at[chip], c_sends.at[i, n], c_recvs.at[i, chip], on_ctx(there)
        )

    def swap_from(i, n):
        there = chips[n] // 2
        return send(
            swaps[i][0].at[there], swaps[i][1].at[there], c_sends.at[i, n], c_recvs.at[i, there], on_ctx(chips[n])
        )

    for i in range(2):
        swap_own(i).start()
        for n in range(3):
            swap_to(i, n).start()
    spread(0)
    rs.finish(o_ref)
    spread(1)
    collect(0)
    collect(1)
    for i in range(2):
        swap_own(i).wait()
        for n in range(3):
            swap_from(i, n).wait_recv()
            swap_to(i, n).wait_send()
    for part in range(2):
        for n, device in enumerate(order[:7]):
            tile_to(part, n, device).wait_send()
        for n in range(len(far)):
            to_plane(part, n).wait_send()

    def settle(block, carry):
        line.sent(block)
        return carry

    lax.fori_loop(0, 8, settle, 0)


def scatter_normed(d_queries, d_kv, to_lo, to_hi, lin, w_qkv, normed_all, swaps, q_gain, k_gain, tables):
    _, rows, width = normed_all.shape
    deep = width // 8
    cols = w_qkv.shape[1]
    half = pltpu.VMEM(to_lo.shape, BF16)
    tiles = pltpu.VMEM((2, 8, deep, cols // 2), BF16)
    dma = pltpu.SemaphoreType.DMA
    return pl.pallas_call(
        normed_back_kernel,
        out_shape=(
            jax.ShapeDtypeStruct((rows, width), F32),
            jax.ShapeDtypeStruct((2, 2, deep, cols // 2), F32),
            jax.ShapeDtypeStruct((8, HEAD_SIZE), F32),
            jax.ShapeDtypeStruct(swaps[0].shape, BF16),
            jax.ShapeDtypeStruct(swaps[1].shape, BF16),
        ),
        in_specs=[spec_vmem()] * 2
        + [spec_any()] * 2
        + [spec_vmem()] * 2
        + [spec_any()] * 3
        + [spec_vmem()] * 6,
        out_specs=(spec_vmem(),) * 3 + (spec_any(),) * 2,
        scratch_shapes=scatter_scratch(rows, width)
        + [
            half,
            half,
            pltpu.VMEM((8 * rows, cols), BF16),
            pltpu.VMEM((2, 8, rows, deep), BF16),
            dma((2,)),
            tiles,
            tiles,
            pltpu.VMEM((2, 4, 2, deep, cols // 2), BF16),
            dma((2, 8 * rows // UNIT)),
            dma((2, 8 * rows // UNIT)),
            dma((2, 7)),
            dma((2, 8)),
            dma((2, 3)),
            dma((2, 4)),
            dma((2,)),
            dma((2, 3)),
            dma((2, 4)),
        ],
        compiler_params=comm_params(8),
        cost_estimate=busy(110),
        name="scatter_normed",
    )(
        d_queries,
        d_kv,
        to_lo,
        to_hi,
        lin,
        w_qkv,
        normed_all,
        *swaps,
        q_gain.reshape(1, -1),
        k_gain.reshape(1, -1),
        *tables,
    )


def total_kernel(v_ref, o_ref, held, held_planes, sends, recvs):
    me = lax.axis_index("ctx")
    plane, planes = lax.axis_index("tp"), lax.axis_size("tp")
    away = others(me)
    far = [lax.rem(plane + step, planes) for step in range(1, planes)]
    barrier = pltpu.get_barrier_semaphore()
    for where in [on_ctx(c) for c in away] + [on_plane(p) for p in far]:
        pl.semaphore_signal(barrier, inc=1, device_id=where, device_id_type=MESH)
    pl.semaphore_wait(barrier, len(away) + len(far))
    held[me] = v_ref[...]
    for n, c in enumerate(away):
        send(held.at[me], held.at[me], sends.at[n], recvs.at[me], on_ctx(c)).start()
    for c in away:
        send(held.at[c], held.at[c], sends.at[0], recvs.at[c], on_ctx(c)).wait_recv()
    value = held[0]
    for c in range(1, 8):
        value += held[c]
    held_planes[plane] = value
    for n, p in enumerate(far):
        send(
            held_planes.at[plane], held_planes.at[plane], sends.at[7 + n], recvs.at[8 + plane], on_plane(p)
        ).start()
    for p in far:
        send(held_planes.at[p], held_planes.at[p], sends.at[0], recvs.at[8 + p], on_plane(p)).wait_recv()
    value = held_planes[0]
    for p in range(1, 4):
        value += held_planes[p]
    o_ref[...] = value
    for n, c in enumerate(away):
        send(held.at[me], held.at[me], sends.at[n], recvs.at[me], on_ctx(c)).wait_send()
    for n, p in enumerate(far):
        send(
            held_planes.at[plane], held_planes.at[plane], sends.at[7 + n], recvs.at[8 + plane], on_plane(p)
        ).wait_send()


def total_of(values):
    return pl.pallas_call(
        total_kernel,
        out_shape=jax.ShapeDtypeStruct(values.shape, F32),
        in_specs=[spec_vmem()],
        out_specs=spec_vmem(),
        scratch_shapes=[
            pltpu.VMEM((8,) + values.shape, F32),
            pltpu.VMEM((4,) + values.shape, F32),
            pltpu.SemaphoreType.DMA((10,)),
            pltpu.SemaphoreType.DMA((12,)),
        ],
        compiler_params=pltpu.CompilerParams(collective_id=9, has_side_effects=True),
        cost_estimate=busy(12),
        name="total_of",
    )(values)


class Places:
    def __init__(self, order_ref, lens_ref):
        self.order, self.lens = order_ref, lens_ref
        self.plane = lax.axis_index("tp")
        self.seq0 = (3 * self.plane) // 4
        self.seq1 = (3 * self.plane + 2) // 4

    def position(self, seq, quarter, c):
        return 2 * self.order[seq, 2 * c + quarter // 2] + lax.rem(quarter, 2)

    def unit(self, u):
        c = u // 3
        g = 3 * self.plane + lax.rem(u, 3)
        seq = g // 4
        return seq, seq - self.seq0, self.position(seq, lax.rem(g, 4), c)

    def each(self, visit):
        for slot, seq in ((0, self.seq0), (1, self.seq1)):

            @pl.when((slot == 0) | (self.seq1 != self.seq0))
            def _():
                def one(i, carry):
                    quarter, c = i // 8, lax.rem(i, 8)
                    g = 4 * seq + quarter
                    away = g // 3 - self.plane
                    row = pl.multiple_of((c * 3 + lax.rem(g, 3)) * UNIT, UNIT)
                    visit(slot, self.position(seq, quarter, c), away, row)
                    return carry

                lax.fori_loop(0, 32, one, 0)

    def fetch(self, sources, keys, values, key_sem, value_sem):
        def visit(slot, position, away, row):
            at = pl.ds(pl.multiple_of(position * UNIT, UNIT), UNIT)
            for n, source in enumerate(sources):

                @pl.when(away == n - 1)
                def _():
                    pltpu.make_async_copy(
                        source.at[pl.ds(row, UNIT), pl.ds(0, HEAD_SIZE)], keys.at[slot, at], key_sem.at[slot]
                    ).start()
                    pltpu.make_async_copy(
                        source.at[pl.ds(row, UNIT), pl.ds(HEAD_SIZE, HEAD_SIZE)],
                        values.at[slot, at, pl.ds(0, HEAD_SIZE)],
                        value_sem.at[slot],
                    ).start()

        self.each(visit)
        for slot in range(2):

            @pl.when((slot == 0) | (self.seq1 != self.seq0))
            def _():
                pltpu.make_async_copy(keys.at[slot], keys.at[slot], key_sem.at[slot]).wait()
                pltpu.make_async_copy(keys.at[slot], keys.at[slot], value_sem.at[slot]).wait()


def attend_kernel(
    order_ref, lens_ref, q_ref, lo_ref, own_ref, hi_ref, o_ref, lse_ref, keys, values, acc, key_sem, value_sem
):
    places = Places(order_ref, lens_ref)
    values[:, :, HEAD_SIZE:] = jnp.ones((2, values.shape[1], HEAD_SIZE), BF16)
    places.fetch((lo_ref, own_ref, hi_ref), keys, values, key_sem, value_sem)

    def one_unit(u, carry):
        seq, slot, position = places.unit(u)
        length = lens_ref[seq]
        rows = pl.ds(pl.multiple_of(u * UNIT, UNIT), UNIT)
        both = q_ref[rows, :]
        queries = jnp.concatenate([both[:, :HEAD_SIZE], both[:, HEAD_SIZE:]], axis=0)
        clear = jnp.minimum(position * UNIT, length) // KEYS
        acc[...] = jnp.zeros_like(acc)

        def part(block, masked):
            at = pl.ds(pl.multiple_of(block * KEYS, KEYS), KEYS)
            weights = jnp.exp2(nt(queries, keys[slot, at, :]))
            if masked:
                key_pos = block * KEYS + lax.broadcasted_iota(jnp.int32, weights.shape, 1)
                query_pos = position * UNIT + lax.rem(
                    lax.broadcasted_iota(jnp.int32, weights.shape, 0), UNIT
                )
                weights = jnp.where((key_pos <= query_pos) & (key_pos < length), weights, 0.0)
            acc[...] += nn(weights.astype(BF16), values[slot, at, :])

        def full(block, carry):
            part(block, False)
            return carry

        lax.fori_loop(0, clear, full, 0)
        part(clear, True)
        total = acc[:, HEAD_SIZE:]
        mixed = (acc[:, :HEAD_SIZE] / total).astype(BF16)
        o_ref[rows, :] = jnp.concatenate([mixed[:UNIT], mixed[UNIT:]], axis=1)
        lse_ref[u] = jnp.transpose(jnp.log2(total))[:8, :]
        return carry

    lax.fori_loop(0, q_ref.shape[0] // UNIT, one_unit, 0)


def attend(order, lens, q, lo, own, hi, seq_len):
    rows = q.shape[0]
    return pl.pallas_call(
        attend_kernel,
        out_shape=(
            jax.ShapeDtypeStruct(q.shape, BF16),
            jax.ShapeDtypeStruct((rows // UNIT, 8, 2 * UNIT), F32),
        ),
        in_specs=[spec_smem(), spec_smem(), spec_vmem(), spec_any(), spec_any(), spec_any()],
        out_specs=(spec_vmem(), spec_vmem()),
        scratch_shapes=[
            pltpu.VMEM((2, seq_len, HEAD_SIZE), BF16),
            pltpu.VMEM((2, seq_len, 2 * HEAD_SIZE), BF16),
            pltpu.VMEM((2 * UNIT, 2 * HEAD_SIZE), F32),
            pltpu.SemaphoreType.DMA((2,)),
            pltpu.SemaphoreType.DMA((2,)),
        ],
        compiler_params=pltpu.CompilerParams(vmem_limit_bytes=VMEM_LIMIT),
        cost_estimate=busy(50),
        name="attend",
    )(order, lens, q, lo, own, hi)


def attend_back_kernel(
    order_ref,
    lens_ref,
    q_ref,
    do_ref,
    o_ref,
    lse_ref,
    lo_ref,
    own_ref,
    hi_ref,
    dq_ref,
    dlo_ref,
    down_ref,
    dhi_ref,
    keys,
    values,
    dkeys,
    dvalues,
    dq_acc,
    key_sem,
    value_sem,
):
    places = Places(order_ref, lens_ref)
    dkeys[...] = jnp.zeros_like(dkeys)
    dvalues[...] = jnp.zeros_like(dvalues)
    places.fetch((lo_ref, own_ref, hi_ref), keys, values, key_sem, value_sem)

    def stacked(ref, rows):
        both = ref[rows, :]
        return jnp.concatenate([both[:, :HEAD_SIZE], both[:, HEAD_SIZE:]], axis=0)

    def one_unit(u, carry):
        seq, slot, position = places.unit(u)
        length = lens_ref[seq]
        rows = pl.ds(pl.multiple_of(u * UNIT, UNIT), UNIT)
        queries = stacked(q_ref, rows)
        grads = stacked(do_ref, rows)
        product = grads.astype(F32) * stacked(o_ref, rows).astype(F32)
        delta = jnp.sum(jnp.transpose(product), axis=0, keepdims=True)
        lse = lse_ref[u][:1, :]
        clear = jnp.minimum(position * UNIT, length) // KEYS
        dq_acc[...] = jnp.zeros_like(dq_acc)

        def part(block, masked):
            at = pl.ds(pl.multiple_of(block * KEYS, KEYS), KEYS)
            key = keys[slot, at, :]
            probs = jnp.exp2(nt(key, queries) - lse)
            if masked:
                key_pos = block * KEYS + lax.broadcasted_iota(jnp.int32, probs.shape, 0)
                query_pos = position * UNIT + lax.rem(
                    lax.broadcasted_iota(jnp.int32, probs.shape, 1), UNIT
                )
                probs = jnp.where((key_pos <= query_pos) & (key_pos < length), probs, 0.0)
            d_scores = (probs * (nt(values[slot, at, :], grads) - delta)).astype(BF16)
            dvalues[slot, at, :] += nn(probs.astype(BF16), grads)
            dkeys[slot, at, :] += nn(d_scores, queries)
            dq_acc[...] += tn(d_scores, key)

        def full(block, carry):
            part(block, False)
            return carry

        lax.fori_loop(0, clear, full, 0)
        part(clear, True)
        dq_ref[rows, :] = jnp.concatenate([dq_acc[:UNIT, :], dq_acc[UNIT:, :]], axis=1)
        return carry

    lax.fori_loop(0, q_ref.shape[0] // UNIT, one_unit, 0)
    dlo_ref[...] = jnp.zeros_like(dlo_ref)
    dhi_ref[...] = jnp.zeros_like(dhi_ref)

    def spread(slot, position, away, row):
        at = pl.ds(pl.multiple_of(position * UNIT, UNIT), UNIT)
        for n, out in enumerate((dlo_ref, down_ref, dhi_ref)):

            @pl.when(away == n - 1)
            def _():
                out[pl.ds(row, UNIT), :HEAD_SIZE] = (dkeys[slot, at, :] * (1.0 / LOG2E)).astype(out.dtype)
                out[pl.ds(row, UNIT), HEAD_SIZE:] = dvalues[slot, at, :].astype(out.dtype)

    places.each(spread)


def attend_back(order, lens, q, d_mixed, mixed, lse, lo, own, hi, seq_len):
    flat = jax.ShapeDtypeStruct(q.shape, BF16)
    wide = jax.ShapeDtypeStruct(q.shape, F32)
    held = pltpu.VMEM((2, seq_len, HEAD_SIZE), BF16)
    summed = pltpu.VMEM((2, seq_len, HEAD_SIZE), F32)
    return pl.pallas_call(
        attend_back_kernel,
        out_shape=(wide, flat, wide, flat),
        in_specs=[spec_smem(), spec_smem()] + [spec_vmem()] * 4 + [spec_any()] * 3,
        out_specs=(spec_vmem(),) * 4,
        scratch_shapes=[
            held,
            held,
            summed,
            summed,
            pltpu.VMEM((2 * UNIT, HEAD_SIZE), F32),
            pltpu.SemaphoreType.DMA((2,)),
            pltpu.SemaphoreType.DMA((2,)),
        ],
        compiler_params=pltpu.CompilerParams(vmem_limit_bytes=VMEM_LIMIT),
        cost_estimate=busy(75),
        name="attend_back",
    )(order, lens, q, d_mixed, mixed, lse, lo, own, hi)


def angles(block_order, tok_rows):
    inverse = THETA ** (-jnp.arange(0, HEAD_SIZE, 2, dtype=F32) / HEAD_SIZE)
    inverse = jnp.concatenate([inverse, inverse])
    units = tok_rows // UNIT
    g = lax.axis_index("tp") * units + jnp.arange(units, dtype=jnp.int32)
    seq, quarter = g // 4, g % 4
    c = jnp.arange(lax.axis_size("ctx"), dtype=jnp.int32)
    where = 2 * block_order[seq[None, :], 2 * c[:, None] + (quarter // 2)[None, :]] + (quarter % 2)[None, :]
    starts = (where.reshape(-1) * UNIT).astype(F32)
    coarse = starts[:, None] * inverse[None, :]
    fine = jnp.arange(UNIT, dtype=F32)[:, None] * inverse[None, :]
    return jnp.cos(coarse), jnp.sin(coarse), jnp.cos(fine), jnp.sin(fine)


def after(value, *earlier):
    return lax.optimization_barrier((value,) + earlier)[0]


def local_plane(
    tokens,
    teacher,
    seq_lens,
    block_order,
    in_gain,
    w_query,
    key_weight_matrix,
    value_weight_matrix,
    q_gain,
    k_gain,
    w_out,
    post_gain,
    w_gate,
    w_up,
    w_down,
):
    me = lax.axis_index("ctx")
    core = me % 2
    plane = lax.axis_index("tp")
    tok_rows, width = tokens.shape
    plane_rows = 8 * tok_rows
    seq_len = 2 * 8 * BLK
    deep = width // 8
    cols = w_gate.shape[1] // 4
    stream = tokens.astype(F32)
    scale_in = rms_scale(stream)
    unit_in = stream * scale_in
    normed_rows = (unit_in * in_gain).astype(BF16)

    qkv_home = jnp.concatenate(
        [
            w_query.reshape(deep, 2, 2 * HEAD_SIZE),
            key_weight_matrix.reshape(deep, 2, HEAD_SIZE),
            value_weight_matrix.reshape(deep, 2, HEAD_SIZE),
        ],
        axis=2,
    )
    qkv_slab = lax.all_gather(jnp.transpose(qkv_home, (1, 0, 2)), "tp", axis=0, tiled=True)

    def to_chips(home):
        return lax.all_to_all(home, "ctx", 0, 0, axis_index_groups=CORE_GROUPS, tiled=True)

    gate_part = to_chips(jnp.transpose(w_gate.reshape(deep, 4, cols), (1, 0, 2)))
    up_part = to_chips(jnp.transpose(w_up.reshape(deep, 4, cols), (1, 0, 2)))
    down_part = to_chips(w_down.reshape(4, cols, deep))
    gate_parts = lax.all_gather(after(gate_part, up_part, down_part), "tp", axis=0)
    tables = angles(block_order, tok_rows)
    normed_all, w_qkv, queries, kv, kv_lo, kv_hi, lin = gather_qkv(
        normed_rows, after(qkv_slab, gate_part, up_part, down_part), q_gain, k_gain, tables
    )
    out_part = lax.all_gather(after(w_out, gate_part, up_part, down_part), "tp", axis=0, tiled=True)
    out_parts = [out_part] + [lax.ppermute(out_part, "ctx", [(i, i ^ n) for i in range(8)]) for n in (2, 4, 6)]
    up_parts = lax.all_gather(after(up_part, kv), "tp", axis=0)
    mixed, lse = attend(block_order, seq_lens, after(queries, gate_parts, out_part), kv_lo, kv, kv_hi, seq_len)
    down_parts = lax.all_gather(after(down_part, kv), "tp", axis=0)
    middle, post_rows, mixed_rows, w_o = mix(mixed, tokens, post_gain, out_parts)
    post_all, w_gu, slope, active, hidden = gather_up(post_rows, gate_parts, up_parts)
    summed, w_d = scatter_down(hidden, down_parts)
    result = middle + summed
    output = result.astype(BF16)

    row = plane * tok_rows + jnp.arange(tok_rows, dtype=jnp.int32)
    seq, rest = row // (2 * BLK), row % (2 * BLK)
    position = block_order[seq, 2 * me + rest // BLK] * BLK + rest % BLK
    valid = (position < seq_lens[seq]).astype(F32)
    diff = (result - teacher.astype(F32)) * valid[:, None]
    error_local = jnp.sum(diff * diff)
    diff_low = diff.astype(BF16)
    d_gu, grad_wd = gather_down_back(diff_low, w_d, slope, active, hidden)
    d_post, grad_gu = scatter_post(d_gu, w_gu, post_all)

    def home_sum(parts):
        return lax.psum_scatter(parts, "tp", scatter_dimension=0, tiled=True)[0]

    grad_down = home_sum(grad_wd)
    grad_gu = home_sum(grad_gu)
    scale_post = rms_scale(middle)
    unit_post = middle * scale_post
    grad_post_local = jnp.sum(d_post * unit_post, axis=0)
    d_middle = diff + rms_back(middle, scale_post, d_post * post_gain)
    d_mixed, *grad_wo = mix_back(d_middle.astype(BF16), w_o, mixed_rows)
    grad_wo = [grad_wo[0]] + [
        lax.ppermute(grad_wo[m], "ctx", [(i, i ^ n) for i in range(8)]) for m, n in ((1, 2), (2, 4), (3, 6))
    ]

    d_queries, to_lo, d_kv, to_hi = attend_back(
        block_order,
        seq_lens,
        queries,
        d_mixed,
        mixed,
        lse,
        kv_lo,
        kv,
        kv_hi,
        seq_len,
    )
    grad_out = lax.psum_scatter(
        sum(after(g, d_queries).astype(F32) for g in grad_wo).astype(BF16), "tp", scatter_dimension=0, tiled=True
    )
    d_normed, grad_qkv, grad_gains, gu_sum, grad_down = scatter_normed(
        d_queries,
        d_kv,
        to_lo,
        to_hi,
        lin,
        w_qkv,
        normed_all,
        (grad_gu, grad_down),
        q_gain,
        k_gain,
        tables,
    )
    grad_down = grad_down.reshape(4 * cols, deep)
    gu_sum = jnp.transpose(gu_sum, (1, 0, 2))
    grad_gate = gu_sum[:, :, :cols].reshape(deep, 4 * cols)
    grad_up = gu_sum[:, :, cols:].reshape(deep, 4 * cols)
    grad_qkv = jnp.transpose(grad_qkv, (0, 2, 1, 3))
    grad_query = grad_qkv[0].reshape(deep, 4 * HEAD_SIZE)
    grad_key = grad_qkv[1, :, :, :HEAD_SIZE].reshape(deep, 2 * HEAD_SIZE)
    grad_value = grad_qkv[1, :, :, HEAD_SIZE:].reshape(deep, 2 * HEAD_SIZE)
    grad_in_local = jnp.sum(d_normed * unit_in, axis=0)
    d_tokens = (d_middle + rms_back(stream, scale_in, d_normed * in_gain)).astype(BF16)
    lanes = width // HEAD_SIZE
    totals = total_of(
        jnp.concatenate(
            [
                grad_in_local.reshape(lanes, HEAD_SIZE),
                grad_post_local.reshape(lanes, HEAD_SIZE),
                grad_gains[:2],
                jnp.full((6, HEAD_SIZE), error_local),
            ],
            axis=0,
        )
    )
    count_valid = jnp.sum(seq_lens).astype(F32)
    loss = 0.5 * totals[2 * lanes + 2, 0] / (count_valid * MODEL_WIDTH)
    return (
        output,
        loss,
        d_tokens,
        totals[:lanes].reshape(width),
        grad_query,
        grad_key,
        grad_value,
        totals[2 * lanes],
        totals[2 * lanes + 1],
        after(grad_out, d_normed).astype(F32),
        totals[lanes : 2 * lanes].reshape(width),
        grad_gate.astype(F32),
        grad_up.astype(F32),
        grad_down.astype(F32),
    )


def solution(mesh):
    in_specs = (
        P(("ctx", "tp"), None),
        P(("ctx", "tp"), None),
        P(),
        P(),
        P(),
        P("ctx", "tp"),
        P("ctx", "tp"),
        P("ctx", "tp"),
        P(),
        P(),
        P("tp", "ctx"),
        P(),
        P("ctx", "tp"),
        P("ctx", "tp"),
        P("tp", "ctx"),
    )
    out_specs = (
        P(("ctx", "tp"), None),
        P(),
        P(("ctx", "tp"), None),
        P(),
        P("ctx", "tp"),
        P("ctx", "tp"),
        P("ctx", "tp"),
        P(),
        P(),
        P("tp", "ctx"),
        P(),
        P("ctx", "tp"),
        P("ctx", "tp"),
        P("tp", "ctx"),
    )
    body = local_plane if (mesh.shape["ctx"], mesh.shape["tp"]) == (8, 4) else local
    return jax.shard_map(body, mesh=mesh, in_specs=in_specs, out_specs=out_specs, check_vma=False)
```

```python
import functools

import jax
import jax.numpy as jnp
from jax import lax
from jax.experimental import pallas as pl
from jax.experimental.pallas import tpu as pltpu
from jax.sharding import PartitionSpec as P

MODEL_WIDTH = 2048
HEAD_SIZE = 128
SEQS = 3
BLK = 256


EPS = 1e-06
THETA = 1000000.0
FLOOR = -1e30


def from_behind(x, axis, by):
    count = lax.axis_size(axis)
    return lax.ppermute(x, axis, [(i, (i + by) % count) for i in range(count)])


def rms_scale(value):
    return lax.rsqrt(jnp.mean(value * value, axis=-1, keepdims=True) + EPS)


def rms_back(value, scale, grad_normed):
    return scale * grad_normed - value * scale**3 * jnp.mean(
        grad_normed * value, axis=-1, keepdims=True
    )


def rotate(value, cosine, sine):
    half = value.shape[-1] // 2
    first = value[..., :half]
    second = value[..., half:]
    return jnp.concatenate(
        [first * cosine - second * sine, second * cosine + first * sine], axis=-1
    )


def rotate_back(grad, cosine, sine):
    half = grad.shape[-1] // 2
    first = grad[..., :half]
    second = grad[..., half:]
    return jnp.concatenate(
        [first * cosine + second * sine, second * cosine - first * sine], axis=-1
    )


def matmul(left, right):
    return jnp.dot(left, right, preferred_element_type=jnp.float32)


def matmul_tn(left, right):
    return lax.dot_general(
        left, right, (((0,), (0,)), ((), ())), preferred_element_type=jnp.float32
    )


def matmul_nt(left, right):
    return lax.dot_general(
        left, right, (((1,), (1,)), ((), ())), preferred_element_type=jnp.float32
    )


def row_slice(value, start, count):
    return lax.dynamic_slice_in_dim(value, start, count, 0)


def local(
    tokens,
    teacher,
    seq_lens,
    block_order,
    in_gain,
    w_query,
    key_weight_matrix,
    value_weight_matrix,
    q_gain,
    k_gain,
    w_out,
    post_gain,
    w_gate,
    w_up,
    w_down,
):
    ctx_count = lax.axis_size("ctx")
    ctx_index = lax.axis_index("ctx")
    tp_index = lax.axis_index("tp")
    tok_rows = tokens.shape[0]
    ctx_rows = tok_rows * lax.axis_size("tp")
    block_span = 2 * BLK
    q_heads = w_query.shape[1] // HEAD_SIZE
    kv_heads = key_weight_matrix.shape[1] // HEAD_SIZE
    group_width = q_heads // kv_heads
    scale_qk = HEAD_SIZE ** (-0.5)
    weights = (
        lax.all_gather(w_query, "ctx", axis=0, tiled=True),
        lax.all_gather(key_weight_matrix, "ctx", axis=0, tiled=True),
        lax.all_gather(value_weight_matrix, "ctx", axis=0, tiled=True),
        lax.all_gather(w_out, "ctx", axis=1, tiled=True),
        lax.all_gather(w_gate, "ctx", axis=0, tiled=True),
        lax.all_gather(w_up, "ctx", axis=0, tiled=True),
        lax.all_gather(w_down, "ctx", axis=1, tiled=True),
    )
    wq_full, wk_full, wv_full, wo_full, wg_full, wu_full, wd_full = weights
    offsets = jnp.arange(BLK, dtype=jnp.int32)

    def block_positions(owner):
        columns = lax.dynamic_slice_in_dim(block_order, 2 * owner, 2, 1)
        return (columns[:, :, None] * BLK + offsets).reshape(SEQS, block_span)

    query_pos = block_positions(ctx_index)
    flat_pos = query_pos.reshape(-1)
    inverse = THETA ** (-jnp.arange(0, HEAD_SIZE, 2, dtype=jnp.float32) / HEAD_SIZE)
    angle = flat_pos.astype(jnp.float32)[:, None] * inverse[None, :]
    cosine = jnp.cos(angle)[:, None, :]
    sine = jnp.sin(angle)[:, None, :]
    stream = tokens.astype(jnp.float32)
    scale_in = rms_scale(stream)
    unit_in = stream * scale_in
    normed_rows = (unit_in * in_gain).astype(jnp.bfloat16)
    normed_all = lax.all_gather(normed_rows, "tp", axis=0, tiled=True)
    query_lin = matmul(normed_all, wq_full).reshape(ctx_rows, q_heads, HEAD_SIZE)
    key_linear = matmul(normed_all, wk_full).reshape(ctx_rows, kv_heads, HEAD_SIZE)
    value_low = (
        matmul(normed_all, wv_full)
        .astype(jnp.bfloat16)
        .reshape(SEQS, block_span, kv_heads, HEAD_SIZE)
    )
    query_scale = rms_scale(query_lin)
    query_unit = query_lin * query_scale
    query_low = (
        rotate(query_unit * q_gain, cosine, sine)
        .astype(jnp.bfloat16)
        .reshape(SEQS, block_span, kv_heads, group_width, HEAD_SIZE)
    )
    key_scale = rms_scale(key_linear)
    key_unit = key_linear * key_scale
    key_low = (
        rotate(key_unit * k_gain, cosine, sine)
        .astype(jnp.bfloat16)
        .reshape(SEQS, block_span, kv_heads, HEAD_SIZE)
    )

    def scores_of(keys, key_pos):
        raw = (
            jnp.einsum("sqkgd,slkd->skgql", query_low, keys, preferred_element_type=jnp.float32)
            * scale_qk
        )
        allowed = (key_pos[:, None, :] <= query_pos[:, :, None]) & (
            key_pos[:, None, :] < seq_lens[:, None, None]
        )
        allowed = allowed[:, None, None, :, :]
        return (jnp.where(allowed, raw, FLOOR), allowed)

    def absorb(state, keys, value_rows, owner):
        running_top, running_total, running_acc = state
        scores, allowed = scores_of(keys, block_positions(owner))
        new_top = jnp.maximum(running_top, jnp.max(scores, axis=-1))
        weights_now = jnp.where(allowed, jnp.exp(scores - new_top[..., None]), 0.0)
        shrink = jnp.exp(running_top - new_top)
        running_total = running_total * shrink + jnp.sum(weights_now, axis=-1)
        running_acc = running_acc * shrink[..., None] + jnp.einsum(
            "skgql,slkd->skgqd",
            weights_now.astype(jnp.bfloat16),
            value_rows,
            preferred_element_type=jnp.float32,
        )
        return (new_top, running_total, running_acc)

    stat_shape = (SEQS, kv_heads, group_width, block_span)
    initial = (
        jnp.full(stat_shape, FLOOR, jnp.float32),
        jnp.zeros(stat_shape, jnp.float32),
        jnp.zeros(stat_shape + (HEAD_SIZE,), jnp.float32),
    )
    first_state = absorb(initial, key_low, value_low, ctx_index)

    def cycle_turn(carry, turn):
        keys, value_rows, state = carry
        keys, value_rows = from_behind((keys, value_rows), "ctx", 1)
        owner = (ctx_index - turn) % ctx_count
        state = absorb(state, keys, value_rows, owner)
        return ((keys, value_rows, state), (keys, value_rows))

    (unused_keys, unused_values, final_state), (kept_keys, kept_values) = lax.scan(
        cycle_turn, (key_low, value_low, first_state), jnp.arange(1, ctx_count, dtype=jnp.int32)
    )
    all_keys = jnp.concatenate([key_low[None], kept_keys], axis=0)
    all_values = jnp.concatenate([value_low[None], kept_values], axis=0)
    top_final, total_final, acc_final = final_state
    log_total = top_final + jnp.log(total_final)
    attn_exact = acc_final / total_final[..., None]
    mixed_low = (
        jnp.transpose(attn_exact, (0, 3, 1, 2, 4))
        .reshape(ctx_rows, q_heads * HEAD_SIZE)
        .astype(jnp.bfloat16)
    )
    middle = stream + lax.psum_scatter(
        matmul(row_slice(mixed_low, jnp.int32(0), lax.axis_size("tp") * tok_rows), wo_full).astype(
            jnp.bfloat16
        ),
        "tp",
        scatter_dimension=0,
        tiled=True,
    ).astype(jnp.float32)
    scale_post = rms_scale(middle)
    unit_post = middle * scale_post
    post_rows = (unit_post * post_gain).astype(jnp.bfloat16)
    post_all = lax.all_gather(post_rows, "tp", axis=0, tiled=True)
    gate = matmul(post_all, wg_full)
    up_val = matmul(post_all, wu_full)
    sigma = jax.nn.sigmoid(gate)
    active = gate * sigma
    hidden_low = (active * up_val).astype(jnp.bfloat16)
    result = middle + lax.psum_scatter(
        matmul(row_slice(hidden_low, jnp.int32(0), lax.axis_size("tp") * tok_rows), wd_full).astype(
            jnp.bfloat16
        ),
        "tp",
        scatter_dimension=0,
        tiled=True,
    ).astype(jnp.float32)
    output = result.astype(jnp.bfloat16)
    valid_all = (query_pos < seq_lens[:, None]).reshape(-1).astype(jnp.float32)
    valid_rows = row_slice(valid_all, tp_index * tok_rows, tok_rows)
    diff = (result - teacher.astype(jnp.float32)) * valid_rows[:, None]
    error_local = jnp.sum(diff * diff)
    diff_low = diff.astype(jnp.bfloat16)
    diff_all = lax.all_gather(diff_low, "tp", axis=0, tiled=True)
    weights_two = (
        lax.all_gather(w_query, "ctx", axis=0, tiled=True),
        lax.all_gather(key_weight_matrix, "ctx", axis=0, tiled=True),
        lax.all_gather(value_weight_matrix, "ctx", axis=0, tiled=True),
        lax.all_gather(w_out, "ctx", axis=1, tiled=True),
        lax.all_gather(w_gate, "ctx", axis=0, tiled=True),
        lax.all_gather(w_up, "ctx", axis=0, tiled=True),
        lax.all_gather(w_down, "ctx", axis=1, tiled=True),
    )
    bq_full, bk_full, bv_full, bo_full, bg_full, bu_full, bd_full = weights_two
    grad_wd = matmul_tn(hidden_low, diff_all)
    d_hidden = matmul_nt(diff_all, bd_full)
    d_gate = (d_hidden * up_val * sigma * (1.0 + gate * (1.0 - sigma))).astype(jnp.bfloat16)
    d_up = (d_hidden * active).astype(jnp.bfloat16)
    grad_wg = matmul_tn(post_all, d_gate)
    grad_wu = matmul_tn(post_all, d_up)
    start = jnp.int32(0)
    d_post = lax.psum_scatter(
        (
            matmul_nt(row_slice(d_gate, start, lax.axis_size("tp") * tok_rows), bg_full)
            + matmul_nt(row_slice(d_up, start, lax.axis_size("tp") * tok_rows), bu_full)
        ).astype(jnp.bfloat16),
        "tp",
        scatter_dimension=0,
        tiled=True,
    ).astype(jnp.float32)
    grad_post_local = jnp.sum(d_post * unit_post, axis=0)
    d_middle = diff + rms_back(middle, scale_post, d_post * post_gain)
    d_mid_low = d_middle.astype(jnp.bfloat16)
    d_mid_all = lax.all_gather(d_mid_low, "tp", axis=0, tiled=True)
    grad_wo = matmul_tn(mixed_low, d_mid_all)
    d_mixed = matmul_nt(d_mid_all, bo_full).astype(jnp.bfloat16)
    d_mixed_grid = jnp.transpose(
        d_mixed.reshape(SEQS, block_span, kv_heads, group_width, HEAD_SIZE), (0, 2, 3, 1, 4)
    )
    delta = jnp.sum(d_mixed_grid.astype(jnp.float32) * attn_exact, axis=-1)

    def revisit(carry, turn):
        grad_queries, grad_keys, grad_values = carry
        owner = (ctx_index - turn) % ctx_count
        keys = all_keys[turn]
        value_rows = all_values[turn]
        scores, allowed = scores_of(keys, block_positions(owner))
        probs = jnp.where(allowed, jnp.exp(scores - log_total[..., None]), 0.0)
        probs_low = probs.astype(jnp.bfloat16)
        d_probs = jnp.einsum(
            "skgqd,slkd->skgql", d_mixed_grid, value_rows, preferred_element_type=jnp.float32
        )
        d_scores = (probs * (d_probs - delta[..., None])).astype(jnp.bfloat16)
        grad_queries = grad_queries + jnp.einsum(
            "skgql,slkd->skgqd", d_scores, keys, preferred_element_type=jnp.float32
        )
        grad_keys = grad_keys + jnp.einsum(
            "skgql,sqkgd->slkd", d_scores, query_low, preferred_element_type=jnp.float32
        )
        grad_values = grad_values + jnp.einsum(
            "skgql,skgqd->slkd", probs_low, d_mixed_grid, preferred_element_type=jnp.float32
        )
        grad_keys, grad_values = (
            from_behind(grad_keys.astype(jnp.bfloat16), "ctx", 1).astype(grad_keys.dtype),
            from_behind(grad_values.astype(jnp.bfloat16), "ctx", 1).astype(grad_values.dtype),
        )
        return ((grad_queries, grad_keys, grad_values), None)

    kv_shape = (SEQS, block_span, kv_heads, HEAD_SIZE)
    start_carry = (
        jnp.zeros(stat_shape + (HEAD_SIZE,), jnp.float32),
        jnp.zeros(kv_shape, jnp.float32),
        jnp.zeros(kv_shape, jnp.float32),
    )
    (grad_queries, grad_keys, grad_values), unused_out = lax.scan(
        revisit, start_carry, jnp.arange(ctx_count, dtype=jnp.int32)
    )
    grad_queries = (
        jnp.transpose(grad_queries, (0, 3, 1, 2, 4)).reshape(ctx_rows, q_heads, HEAD_SIZE)
        * scale_qk
    )
    grad_keys = grad_keys.reshape(ctx_rows, kv_heads, HEAD_SIZE) * scale_qk
    d_values = grad_values.reshape(ctx_rows, kv_heads * HEAD_SIZE).astype(jnp.bfloat16)
    query_back = rotate_back(grad_queries, cosine, sine)
    grad_q_local = jnp.sum(query_back * query_unit, axis=(0, 1))
    d_query_lin = (
        rms_back(query_lin, query_scale, query_back * q_gain)
        .reshape(ctx_rows, q_heads * HEAD_SIZE)
        .astype(jnp.bfloat16)
    )
    key_back = rotate_back(grad_keys, cosine, sine)
    grad_k_local = jnp.sum(key_back * key_unit, axis=(0, 1))
    d_key_lin = (
        rms_back(key_linear, key_scale, key_back * k_gain)
        .reshape(ctx_rows, kv_heads * HEAD_SIZE)
        .astype(jnp.bfloat16)
    )
    grad_wq = matmul_tn(normed_all, d_query_lin)
    grad_wk = matmul_tn(normed_all, d_key_lin)
    grad_wv = matmul_tn(normed_all, d_values)
    start = jnp.int32(0)
    part_query = matmul_nt(row_slice(d_query_lin, start, lax.axis_size("tp") * tok_rows), bq_full)
    part_key = matmul_nt(row_slice(d_key_lin, start, lax.axis_size("tp") * tok_rows), bk_full)
    part_value = matmul_nt(row_slice(d_values, start, lax.axis_size("tp") * tok_rows), bv_full)
    d_normed = lax.psum_scatter(
        (part_query + part_key + part_value).astype(jnp.bfloat16),
        "tp",
        scatter_dimension=0,
        tiled=True,
    ).astype(jnp.float32)
    grad_in_local = jnp.sum(d_normed * unit_in, axis=0)
    d_tokens = (d_middle + rms_back(stream, scale_in, d_normed * in_gain)).astype(jnp.bfloat16)
    summed = (
        lax.psum_scatter(
            grad_wq.astype(jnp.bfloat16), "ctx", scatter_dimension=0, tiled=True
        ).astype(jnp.float32),
        lax.psum_scatter(
            grad_wk.astype(jnp.bfloat16), "ctx", scatter_dimension=0, tiled=True
        ).astype(jnp.float32),
        lax.psum_scatter(
            grad_wv.astype(jnp.bfloat16), "ctx", scatter_dimension=0, tiled=True
        ).astype(jnp.float32),
        lax.psum_scatter(
            grad_wo.astype(jnp.bfloat16), "ctx", scatter_dimension=1, tiled=True
        ).astype(jnp.float32),
        lax.psum_scatter(
            grad_wg.astype(jnp.bfloat16), "ctx", scatter_dimension=0, tiled=True
        ).astype(jnp.float32),
        lax.psum_scatter(
            grad_wu.astype(jnp.bfloat16), "ctx", scatter_dimension=0, tiled=True
        ).astype(jnp.float32),
        lax.psum_scatter(
            grad_wd.astype(jnp.bfloat16), "ctx", scatter_dimension=1, tiled=True
        ).astype(jnp.float32),
    )
    totals = lax.psum(
        (grad_in_local, grad_q_local, grad_k_local, grad_post_local, error_local), ("ctx", "tp")
    )
    count_valid = jnp.sum(seq_lens).astype(jnp.float32)
    loss = 0.5 * totals[4] / (count_valid * MODEL_WIDTH)
    return (
        output,
        loss,
        d_tokens,
        totals[0],
        summed[0],
        summed[1],
        summed[2],
        totals[1],
        totals[2],
        summed[3],
        totals[3],
        summed[4],
        summed[5],
        summed[6],
    )


F32 = jnp.float32
BF16 = jnp.bfloat16
MESH = pl.DeviceIdType.MESH
VMEM_LIMIT = 62 << 20


def busy(us):
    return pl.CostEstimate(flops=0, bytes_accessed=us * 3_000_000, transcendentals=0)

LOG2E = 1.4426950408889634
UNIT = 128
KEYS = 512
CORE_GROUPS = [[0, 2, 4, 6], [1, 3, 5, 7]]
SIBLING = [(i, i ^ 1) for i in range(8)]


def spec_vmem():
    return pl.BlockSpec(memory_space=pltpu.VMEM)


def spec_any():
    return pl.BlockSpec(memory_space=pl.ANY)


def spec_smem():
    return pl.BlockSpec(memory_space=pltpu.SMEM)


def plane_neighbours():
    me = lax.axis_index("ctx")
    core = lax.rem(me, 2)
    x = lax.rem(me // 2, 2)
    y = me // 4
    sib = me + 1 - 2 * core
    nx = me + 2 - 4 * x
    ny = me + 4 - 8 * y
    dg = nx + 4 - 8 * y
    return me, sib, nx, ny, dg


def greet(devices):
    barrier = pltpu.get_barrier_semaphore()
    for device in devices:
        pl.semaphore_signal(barrier, inc=1, device_id={"ctx": device}, device_id_type=MESH)
    pl.semaphore_wait(barrier, len(devices))


def pick(step, options):
    value = options[0]
    for i in range(1, len(options)):
        value = jnp.where(step == i, options[i], value)
    return value


SUBS = 4


def on_ctx(device):
    return {"ctx": device}


def on_plane(plane):
    return {"tp": plane}


def send(src, dst, send_sem, recv_sem, where):
    return pltpu.make_async_remote_copy(
        src_ref=src,
        dst_ref=dst,
        send_sem=send_sem,
        recv_sem=recv_sem,
        device_id=where,
        device_id_type=MESH,
    )


class Gather:
    def __init__(self, x_ref, xs, local_sem, send_sems, recv_sems):
        self.x_ref, self.xs = x_ref, xs
        self.local_sem, self.send_sems, self.recv_sems = local_sem, send_sems, recv_sems
        self.me, self.sib, self.nx, self.ny, self.dg = plane_neighbours()
        self.shift = self.sib - self.me
        self.piece = x_ref.shape[0] // SUBS

    def part(self, block, s):
        return self.xs.at[block, pl.ds(s * self.piece, self.piece)]

    def remote(self, src, kind, block, s, device):
        return send(
            src, self.part(block, s), self.send_sems.at[kind, s], self.recv_sems.at[block, s], on_ctx(device)
        )

    def own(self, s):
        return self.x_ref.at[pl.ds(s * self.piece, self.piece)]

    def start(self):
        for s in range(SUBS):
            t = (s + SUBS // 2) % SUBS
            self.remote(self.own(s), 0, self.me, s, self.nx).start()
            self.remote(self.own(t), 1, self.me, t, self.ny).start()
        for s in range(SUBS):
            self.remote(self.own(s), 2, self.me, s, self.sib).start()
        keep = pltpu.make_async_copy(self.x_ref, self.xs.at[self.me], self.local_sem)
        keep.start()
        keep.wait()

    def arrived(self, block, s):
        self.remote(self.part(block, s), 0, block, s, self.sib).wait_recv()

    def relay(self, kind, block, s, device):
        self.remote(self.part(block, s), kind, block, s, device).start()

    def before(self, step):
        half = SUBS // 2

        @pl.when(step == 1)
        def _():
            for s in range(SUBS):
                self.arrived(self.sib, s)

        @pl.when(step == 2)
        def _():
            for s in range(SUBS):
                self.arrived(self.nx, s)
                if s < half:
                    self.relay(3, self.nx, s, self.ny)
                self.relay(4, self.nx, s, self.sib)
                t = (s + half) % SUBS
                self.arrived(self.ny, t)
                if t >= half:
                    self.relay(3, self.ny, t, self.nx)
                self.relay(5, self.ny, t, self.sib)

        @pl.when(step == 3)
        def _():
            for s in range(SUBS):
                self.arrived(self.nx + self.shift, s)

        @pl.when(step == 4)
        def _():
            for s in (0, half):
                self.arrived(self.dg, s)
                self.relay(6, self.dg, s, self.sib)

        @pl.when(step == 5)
        def _():
            for s in range(SUBS):
                self.arrived(self.ny + self.shift, s)

        @pl.when(step == 6)
        def _():
            for s in range(SUBS):
                if s % half:
                    self.arrived(self.dg, s)
                    self.relay(6, self.dg, s, self.sib)

        @pl.when(step == 7)
        def _():
            for s in range(SUBS):
                self.arrived(self.dg + self.shift, s)

    def block(self, step):
        near = (self.me, self.nx, self.ny, self.dg)
        return pick(step, [b + o for b in near for o in (0, self.shift)])

    def finish(self):
        for s in range(SUBS):
            for kind in range(7):
                self.remote(self.part(self.me, s), kind, self.me, s, self.sib).wait_send()


def gather_scratch(rows, width):
    return [
        pltpu.VMEM((8, rows, width), BF16),
        pltpu.SemaphoreType.DMA,
        pltpu.SemaphoreType.DMA((7, SUBS)),
        pltpu.SemaphoreType.DMA((8, SUBS)),
    ]


class Scatter:
    def __init__(self, to_sib, from_sib, own, diag_out, diag_in, x_out, y_out, x_in, y_in, sends, recvs):
        self.to_sib, self.from_sib, self.own = to_sib, from_sib, own
        self.diag_out, self.diag_in = diag_out, diag_in
        self.x_out, self.y_out, self.x_in, self.y_in = x_out, y_out, x_in, y_in
        self.sends, self.recvs = sends, recvs
        self.me, self.sib, self.nx, self.ny, self.dg = plane_neighbours()
        half = diag_out.shape[0] // 2
        self.first, self.second = first, second = pl.ds(0, half), pl.ds(half, half)
        nx, ny = self.nx, self.ny
        self.diag_x = self.remote(diag_out.at[first], diag_in.at[first], 4, nx)
        self.diag_y = self.remote(diag_out.at[second], diag_in.at[second], 5, ny)
        self.x_first = self.remote(x_out.at[first], x_in.at[first], 6, nx)
        self.x_second = self.remote(x_out.at[second], x_in.at[second], 7, nx)
        self.y_first = self.remote(y_out.at[first], y_in.at[first], 8, ny)
        self.y_second = self.remote(y_out.at[second], y_in.at[second], 9, ny)

    def remote(self, src, dst, n, device):
        return send(src, dst, self.sends.at[n], self.recvs.at[n], on_ctx(device))

    def sibling(self, n):
        return self.remote(self.to_sib.at[n], self.from_sib.at[n], n, self.sib)

    def block(self, step):
        shift = self.sib - self.me
        return pick(step, [b + o for b in (self.dg, self.nx, self.ny, self.me) for o in (shift, 0)])

    def chip_sum(self, n, at):
        return self.own[n, at].astype(F32) + self.from_sib[n, at].astype(F32)

    def step(self, step, product, late=False):
        block = self.block(step)
        n = step // 2
        first, second = self.first, self.second

        @pl.when(lax.rem(step, 2) == 0)
        def _():
            product(block, self.to_sib, n)
            self.sibling(n).start()

        @pl.when(lax.rem(step, 2) == 1)
        def _():
            product(block, self.own, n)
            self.sibling(n).wait_recv()

        @pl.when(step == 1)
        def _():
            self.diag_out[first] = self.chip_sum(0, first).astype(BF16)
            self.diag_x.start()
            self.diag_out[second] = self.chip_sum(0, second).astype(BF16)
            self.diag_y.start()

        @pl.when(step == 3)
        def _():
            self.x_out[first] = self.chip_sum(1, first).astype(BF16)
            self.x_first.start()

        @pl.when(step == 5)
        def _():
            self.y_out[second] = self.chip_sum(2, second).astype(BF16)
            self.y_second.start()
            if not late:
                self.second_wave()

    def second_wave(self):
        first, second = self.first, self.second
        self.diag_x.wait_recv()
        self.y_out[first] = (self.chip_sum(2, first) + self.diag_in[first].astype(F32)).astype(BF16)
        self.y_first.start()
        self.diag_y.wait_recv()
        self.x_out[second] = (self.chip_sum(1, second) + self.diag_in[second].astype(F32)).astype(BF16)
        self.x_second.start()

    def finish(self, o_ref):
        self.x_first.wait_recv()
        self.y_first.wait_recv()
        first, second = self.first, self.second
        o_ref[first] = (
            self.chip_sum(3, first) + self.x_in[first].astype(F32) + self.y_in[first].astype(F32)
        ).astype(o_ref.dtype)
        self.x_second.wait_recv()
        self.y_second.wait_recv()
        o_ref[second] = (
            self.chip_sum(3, second) + self.x_in[second].astype(F32) + self.y_in[second].astype(F32)
        ).astype(o_ref.dtype)
        for n in range(4):
            self.sibling(n).wait_send()
        for copy in (self.diag_x, self.diag_y, self.x_first, self.x_second, self.y_first, self.y_second):
            copy.wait_send()


def scatter_scratch(rows, width):
    four = pltpu.VMEM((4, rows, width), BF16)
    one = pltpu.VMEM((rows, width), BF16)
    return [four] * 3 + [one] * 6 + [pltpu.SemaphoreType.DMA((10,)), pltpu.SemaphoreType.DMA((10,))]


N_SCATTER = 11


def nn(left, right):
    return lax.dot_general(left, right, (((1,), (0,)), ((), ())), preferred_element_type=F32)


def nt(left, right):
    return lax.dot_general(left, right, (((1,), (1,)), ((), ())), preferred_element_type=F32)


def tn(left, right):
    return lax.dot_general(left, right, (((0,), (0,)), ((), ())), preferred_element_type=F32)


def comm_params(collective_id):
    return pltpu.CompilerParams(
        collective_id=collective_id, has_side_effects=True, vmem_limit_bytes=VMEM_LIMIT
    )


def greet_column(devices):
    barrier = pltpu.get_barrier_semaphore()
    plane, planes = lax.axis_index("tp"), lax.axis_size("tp")
    for device in devices:
        pl.semaphore_signal(barrier, inc=1, device_id=on_ctx(device), device_id_type=MESH)
    for step in (1, planes - 1):
        where = on_plane(lax.rem(plane + step, planes))
        pl.semaphore_signal(barrier, inc=1, device_id=where, device_id_type=MESH)
    pl.semaphore_wait(barrier, len(devices) + 2)


class Line:
    def __init__(self, up_src, down_src, from_lo, from_hi, sends, recvs, rows, back):
        self.up_src, self.down_src, self.from_lo, self.from_hi = up_src, down_src, from_lo, from_hi
        self.sends, self.recvs = sends, recvs
        self.units = rows // UNIT
        self.back = back
        self.plane, self.planes = lax.axis_index("tp"), lax.axis_size("tp")

    def at(self, block, i):
        return pl.ds(pl.multiple_of((block * self.units + i) * UNIT, UNIT), UNIT)

    def up(self, block, i):
        at, n = self.at(block, i), block * self.units + i
        return send(self.up_src.at[at], self.from_lo.at[at], self.sends.at[0, n], self.recvs.at[0, n], on_plane(self.plane + 1))

    def down(self, block, i):
        at, n = self.at(block, i), block * self.units + i
        return send(self.down_src.at[at], self.from_hi.at[at], self.sends.at[1, n], self.recvs.at[1, n], on_plane(self.plane - 1))

    def each(self, block, ups, downs):
        for i in range(self.units):
            up = i < self.plane + 1 if self.back else i >= self.plane
            down = i >= self.plane - 1 if self.back else i < self.plane

            @pl.when(up & (self.plane < self.planes - 1))
            def _():
                ups(self.up(block, i))

            @pl.when(down & (self.plane > 0))
            def _():
                downs(self.down(block, i))

    def start(self, block):
        self.each(block, lambda copy: copy.start(), lambda copy: copy.start())

    def sent(self, block):
        self.each(block, lambda copy: copy.wait_send(), lambda copy: copy.wait_send())

    def arrived(self, block):
        for i in range(self.units):
            below = i < self.plane if self.back else i >= self.plane - 1
            above = i >= self.plane if self.back else i < self.plane + 1

            @pl.when(below & (self.plane > 0))
            def _():
                self.up(block, i).wait_recv()

            @pl.when(above & (self.plane < self.planes - 1))
            def _():
                self.down(block, i).wait_recv()


class LineGather:
    def __init__(self, src, dst, local_sem, send_sems, recv_sems):
        self.src, self.dst = src, dst
        self.local_sem, self.send_sems, self.recv_sems = local_sem, send_sems, recv_sems
        self.plane, self.planes = lax.axis_index("tp"), lax.axis_size("tp")
        self.pieces = src.shape[0]

    def own(self):
        return pltpu.make_async_copy(self.src, self.dst.at[self.plane], self.local_sem)

    def copy(self, way, hop, n, origin):
        src = self.src.at[n] if hop == 0 else self.dst.at[origin, n]
        return send(
            src,
            self.dst.at[origin, n],
            self.send_sems.at[way, hop, n],
            self.recv_sems.at[origin, n],
            on_plane(self.plane + 1 - 2 * way),
        )

    def each(self, hop, visit):
        for way in range(2):
            origin = self.plane - hop if way == 0 else self.plane + hop
            inside = origin >= 0 if way == 0 else origin < self.planes
            going = self.plane < self.planes - 1 if way == 0 else self.plane > 0

            @pl.when(inside & going)
            def _():
                for n in range(self.pieces):
                    visit(self.copy(way, hop, n, origin))

    def hop(self, hop):
        if hop == 0:
            self.own().start()

        def go(copy):
            if hop > 0:
                copy.wait_recv()
            copy.start()

        self.each(hop, go)

    def finish(self):
        self.own().wait()
        for way in range(2):
            last = self.plane == self.planes - 1 if way == 0 else self.plane == 0

            @pl.when(last)
            def _():
                for hop in range(1, 4):
                    origin = self.plane - hop if way == 0 else self.plane + hop
                    for n in range(self.pieces):
                        self.copy(way, 0, n, origin).wait_recv()

        for hop in range(3):
            self.each(hop, lambda copy: copy.wait_send())


def line_scratch(pieces):
    dma = pltpu.SemaphoreType.DMA
    return [dma, dma((2, 3, pieces)), dma((4, pieces))]


class Turn:
    def __init__(self, ca_ref, sa_ref, cb_ref, sb_ref, unit):
        ca, sa = ca_ref[pl.ds(unit, 1), :], sa_ref[pl.ds(unit, 1), :]
        cb, sb = cb_ref[...], sb_ref[...]
        self.cosine = ca * cb - sa * sb
        sine = sa * cb + ca * sb
        lane = lax.broadcasted_iota(jnp.int32, sine.shape, 1)
        self.sine = jnp.where(lane < HEAD_SIZE // 2, -sine, sine)

    def forth(self, v):
        return v * self.cosine + pltpu.roll(v, HEAD_SIZE // 2, 1) * self.sine

    def back(self, v):
        return v * self.cosine - pltpu.roll(v, HEAD_SIZE // 2, 1) * self.sine


def others(me):
    _, sib, nx, ny, dg = plane_neighbours()
    shift = sib - me
    return (dg, dg + shift, nx, nx + shift, ny, ny + shift, sib)


def qkv_kernel(
    x_ref,
    slab_ref,
    qg_ref,
    kg_ref,
    ca_ref,
    sa_ref,
    cb_ref,
    sb_ref,
    gate_ref,
    out_ref,
    all_ref,
    w_out_ref,
    q_ref,
    kv_ref,
    lo_ref,
    hi_ref,
    lin_ref,
    gates_ref,
    outs_ref,
    xs,
    local_sem,
    send_sems,
    recv_sems,
    keep_sems,
    w,
    w_local,
    w_sends,
    w_recvs,
    kv_sends,
    kv_recvs,
    *line_sems,
):
    ring = Gather(x_ref, xs, local_sem, send_sems, recv_sems)
    me = ring.me
    rows = x_ref.shape[0]
    deep = slab_ref.shape[1]
    away = others(me)
    greet_column(away)

    def weight(device, n):
        return send(slab_ref.at[device], w.at[pl.ds(me * deep, deep)], w_sends.at[n], w_recvs.at[me], on_ctx(device))

    def weight_from(device):
        return send(slab_ref.at[device], w.at[pl.ds(device * deep, deep)], w_sends.at[0], w_recvs.at[device], on_ctx(device))

    gathers = (
        LineGather(out_ref, outs_ref, *line_sems[:3]),
        LineGather(gate_ref, gates_ref, *line_sems[3:]),
    )
    for n, device in enumerate(away):
        weight(device, n).start()
    for gather in gathers:
        gather.hop(0)
    own_weight = pltpu.make_async_copy(slab_ref.at[me], w.at[pl.ds(me * deep, deep)], w_local)
    own_weight.start()
    ring.start()
    own_weight.wait()
    for device in away:
        weight_from(device).wait_recv()
    keep_w = pltpu.make_async_copy(w, w_out_ref, w_local)
    keep_w.start()

    def keep(block):
        return pltpu.make_async_copy(xs.at[block], all_ref.at[block], keep_sems.at[block])

    line = Line(kv_ref, kv_ref, lo_ref, hi_ref, kv_sends, kv_recvs, rows, False)

    def head(v, gain_ref, turn):
        scale = lax.rsqrt(jnp.mean(v * v, axis=-1, keepdims=True) + EPS)
        return turn.forth(v * scale * gain_ref[...])

    def turn(step, carry):
        for hop in (1, 2):

            @pl.when(step == 2 * hop)
            def _():
                for gather in gathers:
                    gather.hop(hop)

        ring.before(step)
        block = ring.block(step)
        keep(block).start()
        lin = nn(xs[block], w[...])
        lin_ref[pl.ds(pl.multiple_of(block * rows, rows), rows), :] = lin[:, : 3 * HEAD_SIZE]
        for i in range(rows // UNIT):
            unit = block * (rows // UNIT) + i
            rotation = Turn(ca_ref, sa_ref, cb_ref, sb_ref, unit)
            here = pl.ds(pl.multiple_of(unit * UNIT, UNIT), UNIT)
            part = lin[i * UNIT : (i + 1) * UNIT]
            for h in range(2):
                lanes = slice(h * HEAD_SIZE, (h + 1) * HEAD_SIZE)
                query = head(part[:, lanes], qg_ref, rotation)
                q_ref[here, lanes] = (query * (HEAD_SIZE**-0.5 * LOG2E)).astype(BF16)
            key = head(part[:, 2 * HEAD_SIZE : 3 * HEAD_SIZE], kg_ref, rotation)
            kv_ref[here, :HEAD_SIZE] = key.astype(BF16)
            kv_ref[here, HEAD_SIZE:] = part[:, 3 * HEAD_SIZE :].astype(BF16)
        line.start(block)
        return carry

    lax.fori_loop(0, 8, turn, 0)
    ring.finish()
    keep_w.wait()
    for n, device in enumerate(away):
        weight(device, n).wait_send()
    for block in range(8):
        keep(block).wait()

    def settle(block, carry):
        line.sent(block)
        line.arrived(block)
        return carry

    lax.fori_loop(0, 8, settle, 0)
    for gather in gathers:
        gather.finish()


def gather_qkv(normed, slab, q_gain, k_gain, tables, gate, out):
    rows, width = normed.shape
    _, deep, cols = slab.shape
    flat = jax.ShapeDtypeStruct((8 * rows, 2 * HEAD_SIZE), BF16)
    return pl.pallas_call(
        qkv_kernel,
        out_shape=(
            jax.ShapeDtypeStruct((8, rows, width), BF16),
            jax.ShapeDtypeStruct((8 * deep, cols), BF16),
            flat,
            flat,
            flat,
            flat,
            jax.ShapeDtypeStruct((8 * rows, 3 * HEAD_SIZE), F32),
            jax.ShapeDtypeStruct((4,) + gate.shape, BF16),
            jax.ShapeDtypeStruct((4,) + out.shape, BF16),
        ),
        in_specs=[spec_vmem(), spec_any()] + [spec_vmem()] * 6 + [spec_any()] * 2,
        out_specs=(spec_any(), spec_any(), spec_vmem(), spec_vmem(), spec_any(), spec_any(), spec_vmem())
        + (spec_any(),) * 2,
        scratch_shapes=gather_scratch(rows, width)
        + [
            pltpu.SemaphoreType.DMA((8,)),
            pltpu.VMEM((8 * deep, cols), BF16),
            pltpu.SemaphoreType.DMA,
            pltpu.SemaphoreType.DMA((7,)),
            pltpu.SemaphoreType.DMA((8,)),
            pltpu.SemaphoreType.DMA((2, 8 * rows // UNIT)),
            pltpu.SemaphoreType.DMA((2, 8 * rows // UNIT)),
        ]
        + line_scratch(out.shape[0])
        + line_scratch(gate.shape[0]),
        compiler_params=comm_params(1),
        cost_estimate=busy(80),
        name="gather_qkv",
    )(normed, slab, q_gain.reshape(1, -1), k_gain.reshape(1, -1), *tables, gate, out)


class Halves:
    def __init__(self, parts, at, local_sems, send_sems, recv_sems):
        self.parts, self.at = parts, at
        self.local_sems, self.send_sems, self.recv_sems = local_sems, send_sems, recv_sems
        self.me, self.sib = plane_neighbours()[:2]
        self.core = lax.rem(self.me, 2)

    def own(self, z, p):
        n = 4 * z + p
        return pltpu.make_async_copy(
            self.parts.at[2 * self.core + z, p], self.at(z, 2 * p + self.core), self.local_sems.at[n]
        )

    def swap(self, z, p):
        n = 4 * z + p
        return send(
            self.parts.at[2 - 2 * self.core + z, p],
            self.at(z, 2 * p + self.core),
            self.send_sems.at[n],
            self.recv_sems.at[n],
            on_ctx(self.sib),
        )

    def each(self):
        return [(z, p) for z in range(2) for p in range(4)]

    def start(self):
        for z, p in self.each():
            self.swap(z, p).start()
            self.own(z, p).start()

    def ready(self):
        for z, p in self.each():
            self.own(z, p).wait()
            n = 4 * z + p
            send(
                self.parts.at[2 * self.core + z, p],
                self.at(z, 2 * p + 1 - self.core),
                self.send_sems.at[n],
                self.recv_sems.at[n],
                on_ctx(self.sib),
            ).wait_recv()

    def finish(self):
        for z, p in self.each():
            self.swap(z, p).wait_send()


class Shares:
    def __init__(self, out, local_sems, send_sems, recv_sems):
        self.out = out
        self.local_sems, self.send_sems, self.recv_sems = local_sems, send_sems, recv_sems
        self.me, self.sib = plane_neighbours()[:2]
        self.core = lax.rem(self.me, 2)

    def own(self, tile, z, p):
        return pltpu.make_async_copy(tile, self.out.at[2 * self.core + z, p], self.local_sems.at[z, p])

    def other(self, tile, z, p):
        return send(
            tile,
            self.out.at[2 * self.core + z, p],
            self.send_sems.at[z, p],
            self.recv_sems.at[z, p],
            on_ctx(self.sib),
        )

    def arrive(self):
        for z in range(2):
            for p in range(4):
                there = self.out.at[2 - 2 * self.core + z, p]
                send(
                    there, there, self.send_sems.at[z, p], self.recv_sems.at[z, p], on_ctx(self.sib)
                ).wait_recv()


SHARES_SCRATCH = [pltpu.SemaphoreType.DMA((2, 4))] * 3
HALVES_SCRATCH = [pltpu.SemaphoreType.DMA((8,))] * 3


def up_kernel(
    x_ref,
    gate_ref,
    up_ref,
    all_ref,
    w_out_ref,
    a_ref,
    b_ref,
    h_ref,
    xs,
    local_sem,
    send_sems,
    recv_sems,
    keep_sems,
    stage,
    stage_sems,
    w,
    w_sem,
    *w_sems,
):
    ring = Gather(x_ref, xs, local_sem, send_sems, recv_sems)
    rows = x_ref.shape[0]
    halves, width, wide = w.shape
    deep = width // 8
    cols = wide // 2
    outs = (a_ref, b_ref, h_ref)
    greet((ring.sib, ring.nx, ring.ny))
    ring.start()
    gates = Halves(gate_ref, lambda z, c: w.at[z, pl.ds(c * deep, deep), pl.ds(0, cols)], *w_sems[:3])
    ups = Halves(up_ref, lambda z, c: w.at[z, pl.ds(c * deep, deep), pl.ds(cols, cols)], *w_sems[3:])
    gates.start()
    ups.start()
    gates.ready()
    ups.ready()
    keep_w = pltpu.make_async_copy(w, w_out_ref, w_sem)
    keep_w.start()

    def keep(block):
        return pltpu.make_async_copy(xs.at[block], all_ref.at[block], keep_sems.at[block])

    def put(slot, n, block):
        return pltpu.make_async_copy(
            stage.at[slot, n], outs[n].at[pl.ds(block * rows, rows)], stage_sems.at[slot, n]
        )

    def turn(step, carry):
        ring.before(step)
        block = ring.block(step)
        keep(block).start()
        slot = lax.rem(step, 2)

        @pl.when(step >= 2)
        def _():
            for n in range(3):
                put(slot, n, block).wait()

        for z in range(halves):
            both = nn(xs[block], w[z])
            gate, up = both[:, :cols], both[:, cols:]
            sigma = jax.nn.sigmoid(gate)
            active = gate * sigma
            here = slice(z * cols, (z + 1) * cols)
            stage[slot, 0, :, here] = (up * sigma * (1.0 + gate * (1.0 - sigma))).astype(BF16)
            stage[slot, 1, :, here] = active.astype(BF16)
            stage[slot, 2, :, here] = (active * up).astype(BF16)
        for n in range(3):
            put(slot, n, block).start()
        return carry

    lax.fori_loop(0, 8, turn, 0)
    ring.finish()
    gates.finish()
    ups.finish()
    keep_w.wait()
    for block in range(8):
        keep(block).wait()
    for slot in range(2):
        for n in range(3):
            put(slot, n, 0).wait()


def gather_up(post, gate_parts, up_parts):
    rows, width = post.shape
    wide = 2 * gate_parts.shape[-1]
    flat = jax.ShapeDtypeStruct((8 * rows, wide), BF16)
    return pl.pallas_call(
        up_kernel,
        out_shape=(
            jax.ShapeDtypeStruct((8, rows, width), BF16),
            jax.ShapeDtypeStruct((2, width, wide), BF16),
            flat,
            flat,
            flat,
        ),
        in_specs=[spec_vmem(), spec_any(), spec_any()],
        out_specs=(spec_any(),) * 5,
        scratch_shapes=gather_scratch(rows, width)
        + [
            pltpu.SemaphoreType.DMA((8,)),
            pltpu.VMEM((2, 3, rows, wide), BF16),
            pltpu.SemaphoreType.DMA((2, 3)),
            pltpu.VMEM((2, width, wide), BF16),
            pltpu.SemaphoreType.DMA,
        ]
        + HALVES_SCRATCH * 2,
        compiler_params=comm_params(2),
        cost_estimate=busy(62),
        name="gather_up",
    )(post, gate_parts, up_parts)


def down_kernel(h_ref, parts_ref, middle_ref, teacher_ref, valid_ref, o_ref, low_ref, diff_ref, error_ref, w_out_ref, *scratch):
    rs = Scatter(*scratch[:N_SCATTER])
    w, w_sem, w_local, w_sends, w_recvs = scratch[N_SCATTER:]
    rows = o_ref.shape[0]
    _, _, cols, deep = parts_ref.shape
    greet((rs.sib, rs.nx, rs.ny))
    weight = Halves(
        parts_ref,
        lambda z, c: w.at[pl.ds(z * cols, cols), pl.ds(pl.multiple_of(c * deep, deep), deep)],
        w_local,
        w_sends,
        w_recvs,
    )
    weight.start()
    weight.ready()
    keep_w = pltpu.make_async_copy(w, w_out_ref, w_sem)
    keep_w.start()

    def product(block, out, n):
        left = h_ref[pl.ds(pl.multiple_of(block * rows, rows), rows), :]
        for c in range(0, w.shape[1], 512):
            out[n, :, c : c + 512] = nn(left, w[:, c : c + 512]).astype(BF16)

    def turn(step, carry):
        rs.step(step, product)
        return carry

    lax.fori_loop(0, 8, turn, 0)
    rs.finish(diff_ref)
    error = jnp.zeros((rows, HEAD_SIZE), F32)
    for n in range(0, diff_ref.shape[1], HEAD_SIZE):
        at = slice(n, n + HEAD_SIZE)
        result = middle_ref[:, at] + diff_ref[:, at]
        o_ref[:, at] = result.astype(BF16)
        diff = (result - teacher_ref[:, at].astype(F32)) * valid_ref[...]
        diff_ref[:, at] = diff
        low_ref[:, at] = diff.astype(BF16)
        error += diff * diff
    error_ref[...] = jnp.sum(error, axis=0, keepdims=True)
    weight.finish()
    keep_w.wait()


def scatter_down(hidden, parts, middle, teacher, valid):
    rows, width = middle.shape
    ff = hidden.shape[1]
    low = jax.ShapeDtypeStruct((rows, width), BF16)
    return pl.pallas_call(
        down_kernel,
        out_shape=(
            low,
            low,
            jax.ShapeDtypeStruct((rows, width), F32),
            jax.ShapeDtypeStruct((1, HEAD_SIZE), F32),
            jax.ShapeDtypeStruct((ff, width), BF16),
        ),
        in_specs=[spec_vmem(), spec_any()] + [spec_vmem()] * 3,
        out_specs=(spec_vmem(),) * 4 + (spec_any(),),
        scratch_shapes=scatter_scratch(rows, width)
        + [pltpu.VMEM((ff, width), BF16), pltpu.SemaphoreType.DMA]
        + HALVES_SCRATCH,
        compiler_params=comm_params(6),
        cost_estimate=busy(62),
        name="scatter_down",
    )(hidden, parts, middle, teacher, valid)


def down_back_kernel(
    x_ref,
    w_ref,
    a_ref,
    b_ref,
    h_ref,
    d_ref,
    gw_ref,
    xs,
    local_sem,
    send_sems,
    recv_sems,
    stage,
    stage_sems,
    total,
    low,
    s_local,
    s_sends,
    s_recvs,
):
    ring = Gather(x_ref, xs, local_sem, send_sems, recv_sems)
    rows = x_ref.shape[0]
    ff = w_ref.shape[0]
    cols = ff // 2
    width = x_ref.shape[1]
    greet((ring.sib, ring.nx, ring.ny))
    ring.start()
    total[...] = jnp.zeros_like(total)
    shares = Shares(gw_ref, s_local, s_sends, s_recvs)
    deep = width // 8

    def tile(z, c):
        return low.at[pl.ds(z * cols, cols), pl.ds(pl.multiple_of(c * deep, deep), deep)]

    def put(slot, block):
        return pltpu.make_async_copy(
            stage.at[slot], d_ref.at[pl.ds(block * rows, rows)], stage_sems.at[slot]
        )

    def turn(step, carry):
        ring.before(step)
        block = ring.block(step)
        slot = lax.rem(step, 2)

        @pl.when(step >= 2)
        def _():
            put(slot, block).wait()

        here = pl.ds(block * rows, rows)
        for z in range(2):
            part = slice(z * cols, (z + 1) * cols)
            grad = nt(xs[block], w_ref[part, :])
            stage[slot, :, 2 * z * cols : (2 * z + 1) * cols] = (
                grad * a_ref[here, part].astype(F32)
            ).astype(BF16)
            stage[slot, :, (2 * z + 1) * cols : (2 * z + 2) * cols] = (
                grad * b_ref[here, part].astype(F32)
            ).astype(BF16)
        put(slot, block).start()

        @pl.when(slot == 1)
        def _():
            pair = block // 2
            hidden = h_ref[pl.ds(pair * 2 * rows, 2 * rows), :]
            for n in range(0, width, 512):
                seen = xs[pl.ds(pair * 2, 2), :, n : n + 512].reshape(2 * rows, 512)
                total[:, n : n + 512] += tn(hidden, seen)

        return carry

    lax.fori_loop(0, 8, turn, 0)
    ring.finish()
    low[...] = total[...].astype(BF16)
    core = shares.core
    for z in range(2):
        for p in range(4):
            shares.other(tile(z, 2 * p + 1 - core), z, p).start()
            shares.own(tile(z, 2 * p + core), z, p).start()
    for slot in range(2):
        put(slot, 0).wait()
    shares.arrive()
    for z in range(2):
        for p in range(4):
            shares.other(tile(z, 2 * p + 1 - core), z, p).wait_send()
            shares.own(tile(z, 2 * p + core), z, p).wait()


def gather_down_back(diff, w_down, a, b, hidden):
    rows, width = diff.shape
    ff = w_down.shape[0]
    return pl.pallas_call(
        down_back_kernel,
        out_shape=(
            jax.ShapeDtypeStruct((8 * rows, 2 * ff), BF16),
            jax.ShapeDtypeStruct((4, 4, ff // 2, width // 8), BF16),
        ),
        in_specs=[spec_vmem()] * 5,
        out_specs=(spec_any(), spec_any()),
        scratch_shapes=gather_scratch(rows, width)
        + [
            pltpu.VMEM((2, rows, 2 * ff), BF16),
            pltpu.SemaphoreType.DMA((2,)),
            pltpu.VMEM((ff, width), F32),
            pltpu.VMEM((ff, width), BF16),
        ]
        + SHARES_SCRATCH,
        compiler_params=comm_params(3),
        cost_estimate=busy(66),
        name="gather_down_back",
    )(diff, w_down, a, b, hidden)


def mix_kernel(
    mixed_ref,
    tokens_ref,
    gain_ref,
    w0_ref,
    w1_ref,
    w2_ref,
    w3_ref,
    middle_ref,
    post_ref,
    rows_ref,
    w_ref,
    held,
    w,
    m_sems,
    m_sends,
    m_recvs,
    w_local,
    w_sends,
    w_recvs,
    keep_sems,
):
    me, sib, nx, ny, dg = plane_neighbours()
    shift = sib - me
    away = others(me)
    rows, width = held.shape
    deep = width // 8
    greet(away)

    def block(c):
        return pl.ds(pl.multiple_of(c * rows, rows), rows)

    def lanes(c):
        return pl.ds(pl.multiple_of(c * deep, deep), deep)

    def give(n, c):
        return send(mixed_ref.at[block(c)], held.at[:, lanes(me)], m_sends.at[n], m_recvs.at[me], on_ctx(c))

    def take(c):
        return send(mixed_ref.at[block(c)], held.at[:, lanes(c)], m_sends.at[0], m_recvs.at[c], on_ctx(c))

    for n, c in enumerate(away):
        give(n, c).start()
    own = pltpu.make_async_copy(mixed_ref.at[block(me)], held.at[:, lanes(me)], m_sems)
    own.start()
    parts = ((w0_ref, me), (w1_ref, nx), (w2_ref, ny), (w3_ref, dg))

    def swap(n):
        part, c = parts[n]
        return send(part, w.at[:, lanes(c)], w_sends.at[n], w_recvs.at[n], on_ctx(sib))

    def place(n):
        part, c = parts[n]
        return pltpu.make_async_copy(part, w.at[:, lanes(c)], w_local.at[n])

    for n in range(4):
        swap(n).start()
        place(n).start()
    for n in range(4):
        place(n).wait()
        there = w.at[:, lanes(parts[n][1] + shift)]
        send(there, there, w_sends.at[n], w_recvs.at[n], on_ctx(sib)).wait_recv()
    own.wait()
    for c in away:
        take(c).wait_recv()
    keep_rows = pltpu.make_async_copy(held, rows_ref, keep_sems.at[0])
    keep_rows.start()
    keep_w = pltpu.make_async_copy(w, w_ref, keep_sems.at[1])
    keep_w.start()
    total = jnp.zeros((rows, 1), F32)
    for n in range(0, width, 512):
        at = slice(n, n + 512)
        middle = tokens_ref[:, at].astype(F32) + nn(held[...], w[:, at])
        middle_ref[:, at] = middle
        total += jnp.sum(middle * middle, axis=-1, keepdims=True)
    scale = lax.rsqrt(total / width + EPS)
    for n in range(0, width, 512):
        at = slice(n, n + 512)
        post_ref[:, at] = (middle_ref[:, at] * scale * gain_ref[:, at]).astype(BF16)
    for n, c in enumerate(away):
        give(n, c).wait_send()
    for n in range(4):
        swap(n).wait_send()
    keep_rows.wait()
    keep_w.wait()


def mix(mixed, tokens, post_gain, parts):
    rows, width = tokens.shape
    dma = pltpu.SemaphoreType.DMA
    return pl.pallas_call(
        mix_kernel,
        out_shape=(
            jax.ShapeDtypeStruct((rows, width), F32),
            jax.ShapeDtypeStruct((rows, width), BF16),
            jax.ShapeDtypeStruct((rows, width), BF16),
            jax.ShapeDtypeStruct((width, width), BF16),
        ),
        in_specs=[spec_any(), spec_vmem(), spec_vmem()] + [spec_any()] * 4,
        out_specs=(spec_vmem(), spec_vmem(), spec_any(), spec_any()),
        scratch_shapes=[
            pltpu.VMEM((rows, width), BF16),
            pltpu.VMEM((width, width), BF16),
            dma,
            dma((7,)),
            dma((8,)),
            dma((4,)),
            dma((4,)),
            dma((4,)),
            dma((2,)),
        ],
        compiler_params=comm_params(5),
        cost_estimate=busy(28),
        name="mix",
    )(mixed, tokens, post_gain.reshape(1, -1), *parts)


def mix_back_kernel(
    post_ref,
    middle_ref,
    diff_ref,
    gain_ref,
    w_ref,
    rows_ref,
    swap_ref,
    dm_ref,
    d_middle_ref,
    gp_ref,
    g0_ref,
    g1_ref,
    g2_ref,
    g3_ref,
    swapped_ref,
    d_ref,
    stage,
    to_sib,
    from_sib,
    own,
    out_sem,
    out_sends,
    out_recvs,
    s_sends,
    s_recvs,
    g_sems,
    *c_sems,
):
    me, sib, nx, ny, dg = plane_neighbours()
    shift = sib - me
    away = others(me)
    rows, width = d_ref.shape
    deep = width // 8
    greet(away)
    weight_swap = ChipSwap(swap_ref, swapped_ref, *c_sems)
    weight_swap.start()
    squares = jnp.zeros((rows, HEAD_SIZE), F32)
    dots = jnp.zeros((rows, HEAD_SIZE), F32)
    cuts = [slice(n, n + HEAD_SIZE) for n in range(0, width, HEAD_SIZE)]
    for at in cuts:
        middle = middle_ref[:, at]
        squares += middle * middle
        dots += post_ref[:, at] * gain_ref[:, at] * middle
    scale = lax.rsqrt(jnp.sum(squares, axis=-1, keepdims=True) / width + EPS)
    pull = scale * scale * scale * (jnp.sum(dots, axis=-1, keepdims=True) / width)
    for at in cuts:
        middle, post = middle_ref[:, at], post_ref[:, at]
        gp_ref[:, at] = jnp.sum(post * (middle * scale), axis=0, keepdims=True)
        d_middle = diff_ref[:, at] + scale * (post * gain_ref[:, at]) - middle * pull
        d_middle_ref[:, at] = d_middle
        d_ref[:, at] = d_middle.astype(BF16)
    outs = (g0_ref, g1_ref, g2_ref, g3_ref)
    chips = (me, nx, ny, dg)

    def block(c):
        return pl.ds(pl.multiple_of(c * rows, rows), rows)

    def give(n, c):
        return send(stage.at[c], dm_ref.at[block(me)], out_sends.at[n], out_recvs.at[me], on_ctx(c))

    def take(c):
        return send(stage.at[c], dm_ref.at[block(c)], out_sends.at[0], out_recvs.at[c], on_ctx(c))

    def heads(n, carry):
        c = pick(n, away + (me,))
        at = pl.ds(pl.multiple_of(c * deep, deep), deep)
        stage[c] = nt(d_ref[...], w_ref[at, :]).astype(BF16)

        @pl.when(n < 7)
        def _():
            give(n, c).start()

        return carry

    lax.fori_loop(0, 8, heads, 0)
    keep = pltpu.make_async_copy(stage.at[me], dm_ref.at[block(me)], out_sem)
    keep.start()

    def swap(n):
        return send(to_sib.at[n], from_sib.at[n], s_sends.at[n], s_recvs.at[n], on_ctx(sib))

    def grad(n, out, c):
        at = pl.ds(pl.multiple_of(c * deep, deep), deep)
        out[n] = tn(rows_ref[...], d_ref[:, at]).astype(BF16)

    def theirs(n, carry):
        grad(n, to_sib, pick(n, chips) + shift)
        swap(n).start()
        return carry

    def ours(n, carry):
        grad(n, own, pick(n, chips))
        return carry

    lax.fori_loop(0, 4, theirs, 0)
    lax.fori_loop(0, 4, ours, 0)
    for n in range(4):
        swap(n).wait_recv()
        own[n] = (own[n].astype(F32) + from_sib[n].astype(F32)).astype(BF16)
        pltpu.make_async_copy(own.at[n], outs[n], g_sems.at[n]).start()
    for c in away:
        take(c).wait_recv()
    keep.wait()
    for n, c in enumerate(away):
        give(n, c).wait_send()
    for n in range(4):
        swap(n).wait_send()
        pltpu.make_async_copy(own.at[n], outs[n], g_sems.at[n]).wait()
    weight_swap.finish()


def mix_back(d_post, middle, diff, post_gain, w, mixed_rows, swap):
    rows, width = middle.shape
    deep = width // 8
    dma = pltpu.SemaphoreType.DMA
    four = pltpu.VMEM((4, width, deep), BF16)
    return pl.pallas_call(
        mix_back_kernel,
        out_shape=(
            jax.ShapeDtypeStruct((8 * rows, deep), BF16),
            jax.ShapeDtypeStruct((rows, width), F32),
            jax.ShapeDtypeStruct((1, width), F32),
        )
        + (jax.ShapeDtypeStruct((width, deep), BF16),) * 4
        + (jax.ShapeDtypeStruct(swap.shape, BF16),),
        in_specs=[spec_vmem()] * 6 + [spec_any()],
        out_specs=(spec_any(), spec_vmem(), spec_vmem()) + (spec_any(),) * 5,
        scratch_shapes=[
            pltpu.VMEM((rows, width), BF16),
            pltpu.VMEM((8, rows, deep), BF16),
            four,
            four,
            four,
            dma,
            dma((7,)),
            dma((8,)),
            dma((4,)),
            dma((4,)),
            dma((4,)),
        ]
        + SWAP_SCRATCH,
        compiler_params=comm_params(4),
        cost_estimate=busy(26),
        name="mix_back",
    )(d_post, middle, diff, post_gain.reshape(1, -1), w, mixed_rows, swap)


class ChipSwap:
    def __init__(self, src, dst, local_sem, send_sems, recv_sems):
        self.src, self.dst = src, dst
        self.local_sem, self.send_sems, self.recv_sems = local_sem, send_sems, recv_sems
        me, _, nx, ny, dg = plane_neighbours()
        self.chip, self.away = me // 2, (dg, nx, ny)

    def own(self):
        return pltpu.make_async_copy(self.src.at[self.chip], self.dst.at[self.chip], self.local_sem)

    def to(self, n):
        there = self.away[n]
        return send(
            self.src.at[there // 2], self.dst.at[self.chip], self.send_sems.at[n], self.recv_sems.at[self.chip], on_ctx(there)
        )

    def start(self):
        self.own().start()
        for n in range(3):
            self.to(n).start()

    def finish(self):
        self.own().wait()
        for n in range(3):
            there = self.away[n] // 2
            send(
                self.src.at[there], self.dst.at[there], self.send_sems.at[n], self.recv_sems.at[there], on_ctx(self.away[n])
            ).wait_recv()
            self.to(n).wait_send()


SWAP_SCRATCH = [pltpu.SemaphoreType.DMA, pltpu.SemaphoreType.DMA((3,)), pltpu.SemaphoreType.DMA((4,))]


def columns(all_ref, slices, sems, c, slot):
    deep = slices.shape[-1]
    return pltpu.make_async_copy(
        all_ref.at[:, :, pl.ds(pl.multiple_of(c * deep, deep), deep)], slices.at[slot], sems.at[slot]
    )


def post_back_kernel(d_ref, w_ref, all_ref, o_ref, gw_ref, *scratch):
    rs = Scatter(*scratch[:N_SCATTER])
    slices, slice_sems, tile, s_local, s_sends, s_recvs = scratch[N_SCATTER:]
    shares = Shares(gw_ref, s_local, s_sends, s_recvs)
    rows = o_ref.shape[0]
    _, width, wide = w_ref.shape
    plane_rows = d_ref.shape[0]
    deep = width // 8
    greet((rs.sib, rs.nx, rs.ny))
    columns(all_ref, slices, slice_sems, 0, 0).start()

    def product(block, out, n):
        here = pl.ds(pl.multiple_of(block * rows, rows), rows)
        for c in range(0, width, 512):
            total = nt(d_ref[here, :wide], w_ref[0, c : c + 512, :])
            total += nt(d_ref[here, wide:], w_ref[1, c : c + 512, :])
            out[n, :, c : c + 512] = total.astype(BF16)

    def put(slot, p, act):
        @pl.when(slot == shares.core)
        def _():
            for z in range(2):
                copy = shares.own(tile.at[slot, z], z, p)
                copy.start() if act == "start" else copy.wait()

        @pl.when(slot != shares.core)
        def _():
            for z in range(2):
                copy = shares.other(tile.at[slot, z], z, p)
                copy.start() if act == "start" else copy.wait_send()

    def grad(c):
        slot = lax.rem(c, 2)
        columns(all_ref, slices, slice_sems, c, slot).wait()

        @pl.when(c < 7)
        def _():
            columns(all_ref, slices, slice_sems, c + 1, 1 - slot).start()

        @pl.when(c >= 2)
        def _():
            put(slot, c // 2 - 1, "wait")

        seen = slices[slot].reshape(plane_rows, deep)
        for z in range(2):
            tile[slot, z] = tn(seen, d_ref[:, z * wide : (z + 1) * wide]).astype(BF16)
        put(slot, c // 2, "start")

    def turn(t, carry):
        is_grad = ((t >= 5) & (t < 8)) | (t >= 11)

        @pl.when(is_grad)
        def _():
            grad(jnp.where(t < 8, t - 5, t - 8))

        @pl.when(jnp.logical_not(is_grad))
        def _():
            rs.step(jnp.where(t < 5, t, t - 3), product)

        return carry

    lax.fori_loop(0, 16, turn, 0)
    rs.finish(o_ref)
    for slot in range(2):
        put(slot, 3, "wait")
    shares.arrive()


def scatter_post(d_gu, w_gu, post_all):
    _, rows, width = post_all.shape
    wide = w_gu.shape[-1]
    deep = width // 8
    return pl.pallas_call(
        post_back_kernel,
        out_shape=(
            jax.ShapeDtypeStruct((rows, width), F32),
            jax.ShapeDtypeStruct((4, 4, deep, wide), BF16),
        ),
        in_specs=[spec_vmem(), spec_vmem(), spec_any()],
        out_specs=(spec_vmem(), spec_any()),
        scratch_shapes=scatter_scratch(rows, width)
        + [
            pltpu.VMEM((2, 8, rows, deep), BF16),
            pltpu.SemaphoreType.DMA((2,)),
            pltpu.VMEM((2, 2, deep, wide), BF16),
        ]
        + SHARES_SCRATCH,
        compiler_params=comm_params(7),
        cost_estimate=busy(66),
        name="scatter_post",
    )(d_gu, w_gu, post_all)


def normed_back_kernel(
    dq_ref,
    dkv_ref,
    to_lo_ref,
    to_hi_ref,
    lin_ref,
    w_ref,
    all_ref,
    swap_ref,
    wo_ref,
    qg_ref,
    kg_ref,
    ca_ref,
    sa_ref,
    cb_ref,
    sb_ref,
    o_ref,
    gw_ref,
    gains_ref,
    swapped_ref,
    wo_planes_ref,
    *scratch,
):
    rs = Scatter(*scratch[:N_SCATTER])
    (
        from_lo,
        from_hi,
        d_lin,
        slices,
        slice_sems,
        tiles,
        tiles_in,
        planes_in,
        z_sends,
        z_recvs,
        t_sends,
        t_recvs,
        p_sends,
        p_recvs,
        o_local,
        o_sends,
        o_recvs,
        *c_sems,
    ) = scratch[N_SCATTER:]
    me = rs.me
    plane, planes = lax.axis_index("tp"), lax.axis_size("tp")
    rows, width = o_ref.shape
    deep = width // 8
    plane_rows = dq_ref.shape[0]
    units = rows // UNIT
    wide = 2 * HEAD_SIZE
    away = others(me)
    order = [b + o for b in (rs.dg, rs.nx, rs.ny, me) for o in (rs.sib - me, 0)]
    far = [lax.rem(plane + step, planes) for step in range(1, planes)]

    from_lo[...] = jnp.zeros_like(from_lo)
    from_hi[...] = jnp.zeros_like(from_hi)
    line = Line(to_hi_ref, to_lo_ref, from_lo, from_hi, z_sends, z_recvs, rows, True)
    barrier = pltpu.get_barrier_semaphore()
    for where in [on_ctx(c) for c in away] + [on_plane(p) for p in far]:
        pl.semaphore_signal(barrier, inc=1, device_id=where, device_id_type=MESH)
    pl.semaphore_wait(barrier, len(away) + len(far))

    def at_block(block):
        return pl.ds(pl.multiple_of(block * rows, rows), rows)

    for block in order:
        line.start(block)
    columns(all_ref, slices, slice_sems, order[0], 0).start()
    gains_ref[...] = jnp.zeros_like(gains_ref)

    def head_back(grad, lin, gain_ref, rotation):
        back = rotation.back(grad)
        scale = lax.rsqrt(jnp.mean(lin * lin, axis=-1, keepdims=True) + EPS)
        normal = lin * scale
        gained = back * gain_ref[...]
        d = scale * (gained - normal * jnp.mean(gained * normal, axis=-1, keepdims=True))
        return d.astype(BF16), jnp.sum(back * normal, axis=0, keepdims=True)

    def rotation_of(unit):
        return Turn(ca_ref, sa_ref, cb_ref, sb_ref, unit)

    def prepare_queries(unit, carry):
        rotation = rotation_of(unit)
        here = pl.ds(pl.multiple_of(unit * UNIT, UNIT), UNIT)
        for h in range(2):
            lanes = slice(h * HEAD_SIZE, (h + 1) * HEAD_SIZE)
            d, gain = head_back(dq_ref[here, lanes].astype(F32) * HEAD_SIZE**-0.5, lin_ref[here, lanes], qg_ref, rotation)
            d_lin[here, lanes] = d
            gains_ref[0:1, :] += gain
        return carry

    def prepare_keys(block):
        line.arrived(block)
        for i in range(units):
            unit = block * units + i
            here = pl.ds(pl.multiple_of(unit * UNIT, UNIT), UNIT)
            d_kv = dkv_ref[here, :].astype(F32) + from_lo[here, :].astype(F32) + from_hi[here, :].astype(F32)
            lanes = slice(2 * HEAD_SIZE, 3 * HEAD_SIZE)
            d, gain = head_back(d_kv[:, :HEAD_SIZE], lin_ref[here, lanes], kg_ref, rotation_of(unit))
            d_lin[here, lanes] = d
            gains_ref[1:2, :] += gain
            d_lin[here, 3 * HEAD_SIZE :] = d_kv[:, HEAD_SIZE:].astype(BF16)

    def tile_to(part, n, device):
        return send(
            tiles.at[part, device],
            tiles_in.at[part, me],
            t_sends.at[part, n],
            t_recvs.at[part, me],
            on_ctx(device),
        )

    def tile_from(part, device):
        return send(
            tiles.at[part, device],
            tiles_in.at[part, device],
            t_sends.at[part, 0],
            t_recvs.at[part, device],
            on_ctx(device),
        )

    def grads(part):
        def grad(n, carry):
            c = pick(n, order)
            slot = lax.rem(n, 2)
            columns(all_ref, slices, slice_sems, c, slot).wait()

            @pl.when((n < 7) | (part == 0))
            def _():
                columns(all_ref, slices, slice_sems, pick(lax.rem(n + 1, 8), order), 1 - slot).start()

            lanes = slice(part * wide, (part + 1) * wide)
            value = tn(slices[slot].reshape(plane_rows, deep), d_lin[:, lanes]).astype(BF16)

            @pl.when(n < 7)
            def _():
                tiles[part, c] = value
                tile_to(part, n, c).start()

            @pl.when(n == 7)
            def _():
                tiles_in[part, me] = value

            return carry

        lax.fori_loop(0, 8, grad, 0)

    def pair(part, p):
        return tiles_in.at[part, pl.ds(2 * p, 2)]

    def to_plane(part, n):
        return send(
            pair(part, far[n]),
            planes_in.at[part, plane],
            p_sends.at[part, n],
            p_recvs.at[part, plane],
            on_plane(far[n]),
        )

    def from_plane(part, p):
        return send(pair(part, p), planes_in.at[part, p], p_sends.at[part, 0], p_recvs.at[part, p], on_plane(p))

    def spread(part):
        for device in away:
            tile_from(part, device).wait_recv()
        for n in range(len(far)):
            to_plane(part, n).start()

    def collect(part):
        total = tiles_in[part, pl.ds(2 * plane, 2)].astype(F32)
        for p in far:
            from_plane(part, p).wait_recv()
            total += planes_in[part, p].astype(F32)
        gw_ref[part] = total

    def product(block, out, n):
        left = d_lin[at_block(block), :]
        for c in range(0, width, 512):
            out[n, :, c : c + 512] = nt(left, w_ref[c : c + 512, :]).astype(BF16)

    def turn(step, carry):
        prepare_keys(rs.block(step))
        rs.step(step, product, late=True)
        return carry

    def out_to(n):
        return send(
            wo_ref.at[far[n]], wo_planes_ref.at[plane], o_sends.at[n], o_recvs.at[plane], on_plane(far[n])
        )

    out_own = pltpu.make_async_copy(wo_ref.at[plane], wo_planes_ref.at[plane], o_local)
    lax.fori_loop(0, plane_rows // UNIT, prepare_queries, 0)
    grads(0)
    lax.fori_loop(0, 8, turn, 0)
    out_own.start()
    for n in range(len(far)):
        out_to(n).start()
    grads(1)
    rs.second_wave()
    swap = ChipSwap(swap_ref, swapped_ref, *c_sems)
    swap.start()
    spread(0)
    rs.finish(o_ref)
    spread(1)
    collect(0)
    collect(1)
    swap.finish()
    out_own.wait()
    for n, p in enumerate(far):
        send(
            wo_ref.at[p], wo_planes_ref.at[p], o_sends.at[n], o_recvs.at[p], on_plane(p)
        ).wait_recv()
        out_to(n).wait_send()
    for part in range(2):
        for n, device in enumerate(order[:7]):
            tile_to(part, n, device).wait_send()
        for n in range(len(far)):
            to_plane(part, n).wait_send()

    def settle(block, carry):
        line.sent(block)
        return carry

    lax.fori_loop(0, 8, settle, 0)


def scatter_normed(d_queries, d_kv, to_lo, to_hi, lin, w_qkv, normed_all, swap, wo, q_gain, k_gain, tables):
    _, rows, width = normed_all.shape
    deep = width // 8
    cols = w_qkv.shape[1]
    half = pltpu.VMEM(to_lo.shape, BF16)
    tiles = pltpu.VMEM((2, 8, deep, cols // 2), BF16)
    dma = pltpu.SemaphoreType.DMA
    return pl.pallas_call(
        normed_back_kernel,
        out_shape=(
            jax.ShapeDtypeStruct((rows, width), F32),
            jax.ShapeDtypeStruct((2, 2, deep, cols // 2), F32),
            jax.ShapeDtypeStruct((8, HEAD_SIZE), F32),
            jax.ShapeDtypeStruct(swap.shape, BF16),
            jax.ShapeDtypeStruct(wo.shape, BF16),
        ),
        in_specs=[spec_vmem()] * 2
        + [spec_any()] * 2
        + [spec_vmem()] * 2
        + [spec_any()] * 3
        + [spec_vmem()] * 6,
        out_specs=(spec_vmem(),) * 3 + (spec_any(),) * 2,
        scratch_shapes=scatter_scratch(rows, width)
        + [
            half,
            half,
            pltpu.VMEM((8 * rows, cols), BF16),
            pltpu.VMEM((2, 8, rows, deep), BF16),
            dma((2,)),
            tiles,
            tiles,
            pltpu.VMEM((2, 4, 2, deep, cols // 2), BF16),
            dma((2, 8 * rows // UNIT)),
            dma((2, 8 * rows // UNIT)),
            dma((2, 7)),
            dma((2, 8)),
            dma((2, 3)),
            dma((2, 4)),
            dma,
            dma((3,)),
            dma((4,)),
        ]
        + SWAP_SCRATCH,
        compiler_params=comm_params(8),
        cost_estimate=busy(110),
        name="scatter_normed",
    )(
        d_queries,
        d_kv,
        to_lo,
        to_hi,
        lin,
        w_qkv,
        normed_all,
        swap,
        wo,
        q_gain.reshape(1, -1),
        k_gain.reshape(1, -1),
        *tables,
    )


def total_kernel(v_ref, o_ref, held, held_planes, sends, recvs):
    me = lax.axis_index("ctx")
    plane, planes = lax.axis_index("tp"), lax.axis_size("tp")
    away = others(me)
    far = [lax.rem(plane + step, planes) for step in range(1, planes)]
    barrier = pltpu.get_barrier_semaphore()
    for where in [on_ctx(c) for c in away] + [on_plane(p) for p in far]:
        pl.semaphore_signal(barrier, inc=1, device_id=where, device_id_type=MESH)
    pl.semaphore_wait(barrier, len(away) + len(far))
    held[me] = v_ref[...]
    for n, c in enumerate(away):
        send(held.at[me], held.at[me], sends.at[n], recvs.at[me], on_ctx(c)).start()
    for c in away:
        send(held.at[c], held.at[c], sends.at[0], recvs.at[c], on_ctx(c)).wait_recv()
    value = held[0]
    for c in range(1, 8):
        value += held[c]
    held_planes[plane] = value
    for n, p in enumerate(far):
        send(
            held_planes.at[plane], held_planes.at[plane], sends.at[7 + n], recvs.at[8 + plane], on_plane(p)
        ).start()
    for p in far:
        send(held_planes.at[p], held_planes.at[p], sends.at[0], recvs.at[8 + p], on_plane(p)).wait_recv()
    value = held_planes[0]
    for p in range(1, 4):
        value += held_planes[p]
    o_ref[...] = value
    for n, c in enumerate(away):
        send(held.at[me], held.at[me], sends.at[n], recvs.at[me], on_ctx(c)).wait_send()
    for n, p in enumerate(far):
        send(
            held_planes.at[plane], held_planes.at[plane], sends.at[7 + n], recvs.at[8 + plane], on_plane(p)
        ).wait_send()


def total_of(values):
    return pl.pallas_call(
        total_kernel,
        out_shape=jax.ShapeDtypeStruct(values.shape, F32),
        in_specs=[spec_vmem()],
        out_specs=spec_vmem(),
        scratch_shapes=[
            pltpu.VMEM((8,) + values.shape, F32),
            pltpu.VMEM((4,) + values.shape, F32),
            pltpu.SemaphoreType.DMA((10,)),
            pltpu.SemaphoreType.DMA((12,)),
        ],
        compiler_params=pltpu.CompilerParams(collective_id=9, has_side_effects=True),
        cost_estimate=busy(12),
        name="total_of",
    )(values)


def finish_kernel(
    d_ref, tokens_ref, middle_ref, gain_ref, gu_ref, down_ref, qkv_ref, out_ref,
    dt_ref, gin_ref, gate_ref, up_ref, dw_ref, wq_ref, wk_ref, wv_ref, wo_ref,
):
    width = d_ref.shape[1]

    @pl.when(pl.program_id(0) == 0)
    def _():
        gin_ref[...] = jnp.zeros_like(gin_ref)

    stream = tokens_ref[...].astype(F32)
    scale = lax.rsqrt(jnp.mean(stream * stream, axis=-1, keepdims=True) + EPS)
    grad = d_ref[...]
    gin_ref[...] += jnp.sum(grad * (stream * scale), axis=0, keepdims=True)
    gained = grad * gain_ref[...]
    pull = scale * scale * scale * jnp.mean(gained * stream, axis=-1, keepdims=True)
    dt_ref[...] = (middle_ref[...] + (scale * gained - stream * pull)).astype(BF16)
    cols = gu_ref.shape[2] // 2
    for p in range(4):
        here = slice(p * cols, (p + 1) * cols)
        gate_ref[:, here] = gu_ref[p, :, :cols].astype(F32)
        up_ref[:, here] = gu_ref[p, :, cols:].astype(F32)
    dw_ref[...] = down_ref[...].astype(F32)
    wide = 2 * HEAD_SIZE
    for k in range(2):
        wq_ref[:, k * wide : (k + 1) * wide] = qkv_ref[0, k]
        wk_ref[:, k * HEAD_SIZE : (k + 1) * HEAD_SIZE] = qkv_ref[1, k, :, :HEAD_SIZE]
        wv_ref[:, k * HEAD_SIZE : (k + 1) * HEAD_SIZE] = qkv_ref[1, k, :, HEAD_SIZE:]
    wo_ref[...] = sum(out_ref[p].astype(F32) for p in range(4))


def finish(d_normed, tokens, d_middle, in_gain, gu, down, qkv, out):
    steps = 8

    def piece(shape, axis):
        block = list(shape)
        block[axis] //= steps
        return pl.BlockSpec(
            tuple(block), lambda i, axis=axis, n=len(shape): tuple(i if d == axis else 0 for d in range(n))
        )

    rows, width = tokens.shape
    deep, ff = gu.shape[1], 2 * gu.shape[2]
    one = (1, width)
    whole = pl.BlockSpec(one, lambda i: (0, 0))
    flat, square = (rows, width), (deep, 2 * HEAD_SIZE)
    ins = [(flat, 0), (flat, 0), (flat, 0), None, (gu.shape, 1), (down.shape, 1), (qkv.shape, 2), (out.shape, 1)]
    outs = [
        (flat, 0, BF16),
        None,
        ((deep, ff), 0, F32),
        ((deep, ff), 0, F32),
        (down.shape, 1, F32),
        ((deep, 4 * HEAD_SIZE), 0, F32),
        (square, 0, F32),
        (square, 0, F32),
        (out.shape[1:], 0, F32),
    ]
    return pl.pallas_call(
        finish_kernel,
        grid=(steps,),
        out_shape=tuple(jax.ShapeDtypeStruct(o[0], o[2]) if o else jax.ShapeDtypeStruct(one, F32) for o in outs),
        in_specs=[piece(*i) if i else whole for i in ins],
        out_specs=tuple(piece(o[0], o[1]) if o else whole for o in outs),
        compiler_params=pltpu.CompilerParams(vmem_limit_bytes=VMEM_LIMIT),
        cost_estimate=busy(8),
        name="finish",
    )(d_normed, tokens, d_middle, in_gain.reshape(1, -1), gu, down, qkv, out)


class Places:
    def __init__(self, order_ref, lens_ref):
        self.order, self.lens = order_ref, lens_ref
        self.plane = lax.axis_index("tp")
        self.seq0 = (3 * self.plane) // 4
        self.seq1 = (3 * self.plane + 2) // 4

    def position(self, seq, quarter, c):
        return 2 * self.order[seq, 2 * c + quarter // 2] + lax.rem(quarter, 2)

    def unit(self, u):
        c = u // 3
        g = 3 * self.plane + lax.rem(u, 3)
        seq = g // 4
        return seq, seq - self.seq0, self.position(seq, lax.rem(g, 4), c)

    def each(self, visit):
        for slot, seq in ((0, self.seq0), (1, self.seq1)):

            @pl.when((slot == 0) | (self.seq1 != self.seq0))
            def _():
                def one(i, carry):
                    quarter, c = i // 8, lax.rem(i, 8)
                    g = 4 * seq + quarter
                    away = g // 3 - self.plane
                    row = pl.multiple_of((c * 3 + lax.rem(g, 3)) * UNIT, UNIT)
                    visit(slot, self.position(seq, quarter, c), away, row)
                    return carry

                lax.fori_loop(0, 32, one, 0)

    def fetch(self, sources, keys, values, key_sem, value_sem):
        def visit(slot, position, away, row):
            at = pl.ds(pl.multiple_of(position * UNIT, UNIT), UNIT)
            for n, source in enumerate(sources):

                @pl.when(away == n - 1)
                def _():
                    pltpu.make_async_copy(
                        source.at[pl.ds(row, UNIT), pl.ds(0, HEAD_SIZE)], keys.at[slot, at], key_sem.at[slot]
                    ).start()
                    pltpu.make_async_copy(
                        source.at[pl.ds(row, UNIT), pl.ds(HEAD_SIZE, HEAD_SIZE)],
                        values.at[slot, at, pl.ds(0, HEAD_SIZE)],
                        value_sem.at[slot],
                    ).start()

        self.each(visit)
        for slot in range(2):

            @pl.when((slot == 0) | (self.seq1 != self.seq0))
            def _():
                pltpu.make_async_copy(keys.at[slot], keys.at[slot], key_sem.at[slot]).wait()
                pltpu.make_async_copy(keys.at[slot], keys.at[slot], value_sem.at[slot]).wait()


def sweep(clear, part):
    def four(i, carry):
        part(i * 4 * KEYS, 4 * KEYS, False)
        return carry

    lax.fori_loop(0, clear // 4, four, 0)

    @pl.when(lax.rem(clear, 4) >= 2)
    def _():
        part(clear // 4 * 4 * KEYS, 2 * KEYS, False)


    odd = lax.rem(clear, 2)

    @pl.when(odd == 1)
    def _():
        part((clear - 1) * KEYS, 2 * KEYS, True)

    @pl.when(odd == 0)
    def _():
        part(clear * KEYS, KEYS, True)


def attend_kernel(
    order_ref, lens_ref, q_ref, lo_ref, own_ref, hi_ref, o_ref, lse_ref, keys, values, acc, key_sem, value_sem
):
    places = Places(order_ref, lens_ref)
    values[:, :, HEAD_SIZE:] = jnp.ones((2, values.shape[1], HEAD_SIZE), BF16)
    places.fetch((lo_ref, own_ref, hi_ref), keys, values, key_sem, value_sem)

    def one_unit(u, carry):
        seq, slot, position = places.unit(u)
        length = lens_ref[seq]
        rows = pl.ds(pl.multiple_of(u * UNIT, UNIT), UNIT)
        both = q_ref[rows, :]
        queries = jnp.concatenate([both[:, :HEAD_SIZE], both[:, HEAD_SIZE:]], axis=0)
        clear = jnp.minimum(position * UNIT, length) // KEYS
        acc[...] = jnp.zeros_like(acc)
        row = lax.rem(lax.broadcasted_iota(jnp.int32, (2 * UNIT, 1), 0), UNIT)

        def part(start, size, masked):
            at = pl.ds(pl.multiple_of(start, KEYS), size)
            weights = jnp.exp2(nt(queries, keys[slot, at, :]))
            if masked:
                last = jnp.minimum(row + (position * UNIT - start), length - 1 - start)
                weights = jnp.where(lax.broadcasted_iota(jnp.int32, weights.shape, 1) <= last, weights, 0.0)
            acc[:, :HEAD_SIZE] += nn(weights.astype(BF16), values[slot, at, :HEAD_SIZE])
            part_sum = weights[:, :HEAD_SIZE]
            for n in range(HEAD_SIZE, size, HEAD_SIZE):
                part_sum += weights[:, n : n + HEAD_SIZE]
            acc[:, HEAD_SIZE:] += part_sum

        sweep(clear, part)
        total = jnp.sum(acc[:, HEAD_SIZE:], axis=-1, keepdims=True)
        mixed = (acc[:, :HEAD_SIZE] / total).astype(BF16)
        o_ref[rows, :] = jnp.concatenate([mixed[:UNIT], mixed[UNIT:]], axis=1)
        lse_ref[u] = jnp.transpose(jnp.broadcast_to(jnp.log2(total), (2 * UNIT, HEAD_SIZE)))[:8, :]
        return carry

    lax.fori_loop(0, q_ref.shape[0] // UNIT, one_unit, 0)


def attend(order, lens, q, lo, own, hi, seq_len):
    rows = q.shape[0]
    return pl.pallas_call(
        attend_kernel,
        out_shape=(
            jax.ShapeDtypeStruct(q.shape, BF16),
            jax.ShapeDtypeStruct((rows // UNIT, 8, 2 * UNIT), F32),
        ),
        in_specs=[spec_smem(), spec_smem(), spec_vmem(), spec_any(), spec_any(), spec_any()],
        out_specs=(spec_vmem(), spec_vmem()),
        scratch_shapes=[
            pltpu.VMEM((2, seq_len, HEAD_SIZE), BF16),
            pltpu.VMEM((2, seq_len, 2 * HEAD_SIZE), BF16),
            pltpu.VMEM((2 * UNIT, 2 * HEAD_SIZE), F32),
            pltpu.SemaphoreType.DMA((2,)),
            pltpu.SemaphoreType.DMA((2,)),
        ],
        compiler_params=pltpu.CompilerParams(vmem_limit_bytes=VMEM_LIMIT),
        cost_estimate=busy(50),
        name="attend",
    )(order, lens, q, lo, own, hi)


def attend_back_kernel(
    order_ref,
    lens_ref,
    q_ref,
    do_ref,
    o_ref,
    lse_ref,
    lo_ref,
    own_ref,
    hi_ref,
    dq_ref,
    dlo_ref,
    down_ref,
    dhi_ref,
    keys,
    values,
    dkeys,
    dvalues,
    dq_acc,
    key_sem,
    value_sem,
):
    places = Places(order_ref, lens_ref)
    dkeys[...] = jnp.zeros_like(dkeys)
    dvalues[...] = jnp.zeros_like(dvalues)
    places.fetch((lo_ref, own_ref, hi_ref), keys, values, key_sem, value_sem)

    def stacked(ref, rows):
        both = ref[rows, :]
        return jnp.concatenate([both[:, :HEAD_SIZE], both[:, HEAD_SIZE:]], axis=0)

    def one_unit(u, carry):
        seq, slot, position = places.unit(u)
        length = lens_ref[seq]
        rows = pl.ds(pl.multiple_of(u * UNIT, UNIT), UNIT)
        queries = stacked(q_ref, rows)
        grads = stacked(do_ref, rows)
        product = grads.astype(F32) * stacked(o_ref, rows).astype(F32)
        delta = jnp.sum(jnp.transpose(product), axis=0, keepdims=True)
        lse = lse_ref[u][:1, :]
        clear = jnp.minimum(position * UNIT, length) // KEYS
        dq_acc[...] = jnp.zeros_like(dq_acc)
        row = lax.rem(lax.broadcasted_iota(jnp.int32, (1, 2 * UNIT), 1), UNIT)

        def part(start, size, masked):
            at = pl.ds(pl.multiple_of(start, KEYS), size)
            key = keys[slot, at, :]
            probs = jnp.exp2(nt(key, queries) - lse)
            if masked:
                last = jnp.minimum(row + (position * UNIT - start), length - 1 - start)
                probs = jnp.where(lax.broadcasted_iota(jnp.int32, probs.shape, 0) <= last, probs, 0.0)
            d_scores = (probs * (nt(values[slot, at, :], grads) - delta)).astype(BF16)
            dvalues[slot, at, :] += nn(probs.astype(BF16), grads)
            dkeys[slot, at, :] += nn(d_scores, queries)
            dq_acc[...] += tn(d_scores, key)

        sweep(clear, part)
        dq_ref[rows, :] = jnp.concatenate([dq_acc[:UNIT, :], dq_acc[UNIT:, :]], axis=1).astype(BF16)
        return carry

    lax.fori_loop(0, q_ref.shape[0] // UNIT, one_unit, 0)
    dlo_ref[...] = jnp.zeros_like(dlo_ref)
    dhi_ref[...] = jnp.zeros_like(dhi_ref)

    def spread(slot, position, away, row):
        at = pl.ds(pl.multiple_of(position * UNIT, UNIT), UNIT)
        for n, out in enumerate((dlo_ref, down_ref, dhi_ref)):

            @pl.when(away == n - 1)
            def _():
                out[pl.ds(row, UNIT), :HEAD_SIZE] = (dkeys[slot, at, :] * (1.0 / LOG2E)).astype(out.dtype)
                out[pl.ds(row, UNIT), HEAD_SIZE:] = dvalues[slot, at, :].astype(out.dtype)

    places.each(spread)


def attend_back(order, lens, q, d_mixed, mixed, lse, lo, own, hi, seq_len):
    flat = jax.ShapeDtypeStruct(q.shape, BF16)
    held = pltpu.VMEM((2, seq_len, HEAD_SIZE), BF16)
    summed = pltpu.VMEM((2, seq_len, HEAD_SIZE), F32)
    return pl.pallas_call(
        attend_back_kernel,
        out_shape=(flat,) * 4,
        in_specs=[spec_smem(), spec_smem()] + [spec_vmem()] * 4 + [spec_any()] * 3,
        out_specs=(spec_vmem(),) * 4,
        scratch_shapes=[
            held,
            held,
            summed,
            summed,
            pltpu.VMEM((2 * UNIT, HEAD_SIZE), F32),
            pltpu.SemaphoreType.DMA((2,)),
            pltpu.SemaphoreType.DMA((2,)),
        ],
        compiler_params=pltpu.CompilerParams(vmem_limit_bytes=VMEM_LIMIT),
        cost_estimate=busy(75),
        name="attend_back",
    )(order, lens, q, d_mixed, mixed, lse, lo, own, hi)


def angles(block_order, tok_rows):
    inverse = THETA ** (-jnp.arange(0, HEAD_SIZE, 2, dtype=F32) / HEAD_SIZE)
    inverse = jnp.concatenate([inverse, inverse])
    units = tok_rows // UNIT
    g = lax.axis_index("tp") * units + jnp.arange(units, dtype=jnp.int32)
    seq, quarter = g // 4, g % 4
    c = jnp.arange(lax.axis_size("ctx"), dtype=jnp.int32)
    where = 2 * block_order[seq[None, :], 2 * c[:, None] + (quarter // 2)[None, :]] + (quarter % 2)[None, :]
    starts = (where.reshape(-1) * UNIT).astype(F32)
    coarse = starts[:, None] * inverse[None, :]
    fine = jnp.arange(UNIT, dtype=F32)[:, None] * inverse[None, :]
    return jnp.cos(coarse), jnp.sin(coarse), jnp.cos(fine), jnp.sin(fine)


def after(value, *earlier):
    return lax.optimization_barrier((value,) + earlier)[0]


def local_plane(
    tokens,
    teacher,
    seq_lens,
    block_order,
    in_gain,
    w_query,
    key_weight_matrix,
    value_weight_matrix,
    q_gain,
    k_gain,
    w_out,
    post_gain,
    w_gate,
    w_up,
    w_down,
):
    me = lax.axis_index("ctx")
    core = me % 2
    plane = lax.axis_index("tp")
    tok_rows, width = tokens.shape
    plane_rows = 8 * tok_rows
    seq_len = 2 * 8 * BLK
    deep = width // 8
    cols = w_gate.shape[1] // 4
    stream = tokens.astype(F32)
    normed_rows = (stream * rms_scale(stream) * in_gain).astype(BF16)
    unit = plane * (tok_rows // UNIT) + jnp.arange(tok_rows // UNIT, dtype=jnp.int32)
    seq, quarter = unit // 4, unit % 4
    start = block_order[seq, 2 * me + quarter // 2] * BLK + (quarter % 2) * UNIT
    position = start[:, None] + jnp.arange(UNIT, dtype=jnp.int32)
    valid = (position < seq_lens[seq][:, None]).astype(F32).reshape(tok_rows, 1)

    qkv_home = jnp.concatenate(
        [
            w_query.reshape(deep, 2, 2 * HEAD_SIZE),
            key_weight_matrix.reshape(deep, 2, HEAD_SIZE),
            value_weight_matrix.reshape(deep, 2, HEAD_SIZE),
        ],
        axis=2,
    )
    qkv_slab = lax.all_gather(jnp.transpose(qkv_home, (1, 0, 2)), "tp", axis=0, tiled=True)

    def to_chips(home):
        return lax.all_to_all(home, "ctx", 0, 0, axis_index_groups=CORE_GROUPS, tiled=True)

    gate_part = to_chips(jnp.transpose(w_gate.reshape(deep, 4, cols), (1, 0, 2)))
    up_part = to_chips(jnp.transpose(w_up.reshape(deep, 4, cols), (1, 0, 2)))
    down_part = to_chips(w_down.reshape(4, cols, deep))
    tables = angles(block_order, tok_rows)
    normed_all, w_qkv, queries, kv, kv_lo, kv_hi, lin, gate_parts, out_part = gather_qkv(
        normed_rows,
        after(qkv_slab, up_part, down_part),
        q_gain,
        k_gain,
        tables,
        gate_part,
        w_out.reshape(2, 2 * HEAD_SIZE, deep),
    )
    out_part = out_part.reshape(width, deep)
    out_parts = [out_part] + [lax.ppermute(out_part, "ctx", [(i, i ^ n) for i in range(8)]) for n in (2, 4, 6)]
    up_parts = lax.all_gather(after(up_part, kv[:8]), "tp", axis=0)
    mixed, lse = attend(block_order, seq_lens, queries, kv_lo, kv, kv_hi, seq_len)
    down_parts = lax.all_gather(after(down_part, kv[:8]), "tp", axis=0)
    middle, post_rows, mixed_rows, w_o = mix(mixed, tokens, post_gain, out_parts)
    post_all, w_gu, slope, active, hidden = gather_up(post_rows, gate_parts, up_parts)
    output, diff_low, diff, error, w_d = scatter_down(hidden, down_parts, middle, teacher, valid)
    d_gu, grad_wd = gather_down_back(diff_low, w_d, slope, active, hidden)
    d_post, grad_gu = scatter_post(d_gu, w_gu, post_all)

    def home_sum(parts):
        return lax.psum_scatter(parts, "tp", scatter_dimension=0, tiled=True)[0]

    grad_down = home_sum(grad_wd)
    grad_gu = home_sum(grad_gu)
    d_mixed, d_middle, grad_post, *grad_wo, grad_down = mix_back(
        d_post, middle, diff, post_gain, w_o, mixed_rows, grad_down
    )
    grad_wo = [grad_wo[0]] + [
        lax.ppermute(grad_wo[m], "ctx", [(i, i ^ n) for i in range(8)]) for m, n in ((1, 2), (2, 4), (3, 6))
    ]

    d_queries, to_lo, d_kv, to_hi = attend_back(
        block_order,
        seq_lens,
        queries,
        d_mixed,
        mixed,
        lse,
        kv_lo,
        kv,
        kv_hi,
        seq_len,
    )
    out_sum = sum(after(g, d_queries[:8]).astype(F32) for g in grad_wo).astype(BF16)
    d_normed, grad_qkv, grad_gains, gu_sum, grad_out = scatter_normed(
        d_queries,
        d_kv,
        to_lo,
        to_hi,
        lin,
        w_qkv,
        normed_all,
        grad_gu,
        out_sum.reshape(4, 4 * HEAD_SIZE, deep),
        q_gain,
        k_gain,
        tables,
    )
    d_tokens, grad_in, grad_gate, grad_up, grad_down, grad_query, grad_key, grad_value, grad_out = finish(
        d_normed, tokens, d_middle, in_gain, gu_sum, grad_down, grad_qkv, grad_out
    )
    lanes = width // HEAD_SIZE
    totals = total_of(
        jnp.concatenate(
            [
                grad_in.reshape(lanes, HEAD_SIZE),
                grad_post.reshape(lanes, HEAD_SIZE),
                grad_gains[:2],
                jnp.broadcast_to(error, (6, HEAD_SIZE)),
            ],
            axis=0,
        )
    )
    count_valid = jnp.sum(seq_lens).astype(F32)
    loss = 0.5 * jnp.sum(totals[2 * lanes + 2]) / (count_valid * MODEL_WIDTH)
    return (
        output,
        loss,
        d_tokens,
        totals[:lanes].reshape(width),
        grad_query,
        grad_key,
        grad_value,
        totals[2 * lanes],
        totals[2 * lanes + 1],
        grad_out,
        totals[lanes : 2 * lanes].reshape(width),
        grad_gate,
        grad_up,
        grad_down.reshape(4 * cols, deep),
    )


def solution(mesh):
    in_specs = (
        P(("ctx", "tp"), None),
        P(("ctx", "tp"), None),
        P(),
        P(),
        P(),
        P("ctx", "tp"),
        P("ctx", "tp"),
        P("ctx", "tp"),
        P(),
        P(),
        P("tp", "ctx"),
        P(),
        P("ctx", "tp"),
        P("ctx", "tp"),
        P("tp", "ctx"),
    )
    out_specs = (
        P(("ctx", "tp"), None),
        P(),
        P(("ctx", "tp"), None),
        P(),
        P("ctx", "tp"),
        P("ctx", "tp"),
        P("ctx", "tp"),
        P(),
        P(),
        P("tp", "ctx"),
        P(),
        P("ctx", "tp"),
        P("ctx", "tp"),
        P("tp", "ctx"),
    )
    body = local_plane if (mesh.shape["ctx"], mesh.shape["tp"]) == (8, 4) else local
    return jax.shard_map(body, mesh=mesh, in_specs=in_specs, out_specs=out_specs, check_vma=False)
```

```python
import functools

import jax
import jax.numpy as jnp
from jax import lax
from jax.experimental import pallas as pl
from jax.experimental.pallas import tpu as pltpu
from jax.sharding import PartitionSpec as P

MODEL_WIDTH = 2048
HEAD_SIZE = 128
SEQS = 3
BLK = 256


EPS = 1e-06
THETA = 1000000.0
FLOOR = -1e30


def from_behind(x, axis, by):
    count = lax.axis_size(axis)
    return lax.ppermute(x, axis, [(i, (i + by) % count) for i in range(count)])


def rms_scale(value):
    return lax.rsqrt(jnp.mean(value * value, axis=-1, keepdims=True) + EPS)


def rms_back(value, scale, grad_normed):
    return scale * grad_normed - value * scale**3 * jnp.mean(
        grad_normed * value, axis=-1, keepdims=True
    )


def rotate(value, cosine, sine):
    half = value.shape[-1] // 2
    first = value[..., :half]
    second = value[..., half:]
    return jnp.concatenate(
        [first * cosine - second * sine, second * cosine + first * sine], axis=-1
    )


def rotate_back(grad, cosine, sine):
    half = grad.shape[-1] // 2
    first = grad[..., :half]
    second = grad[..., half:]
    return jnp.concatenate(
        [first * cosine + second * sine, second * cosine - first * sine], axis=-1
    )


def matmul(left, right):
    return jnp.dot(left, right, preferred_element_type=jnp.float32)


def matmul_tn(left, right):
    return lax.dot_general(
        left, right, (((0,), (0,)), ((), ())), preferred_element_type=jnp.float32
    )


def matmul_nt(left, right):
    return lax.dot_general(
        left, right, (((1,), (1,)), ((), ())), preferred_element_type=jnp.float32
    )


def row_slice(value, start, count):
    return lax.dynamic_slice_in_dim(value, start, count, 0)


def local(
    tokens,
    teacher,
    seq_lens,
    block_order,
    in_gain,
    w_query,
    key_weight_matrix,
    value_weight_matrix,
    q_gain,
    k_gain,
    w_out,
    post_gain,
    w_gate,
    w_up,
    w_down,
):
    ctx_count = lax.axis_size("ctx")
    ctx_index = lax.axis_index("ctx")
    tp_index = lax.axis_index("tp")
    tok_rows = tokens.shape[0]
    ctx_rows = tok_rows * lax.axis_size("tp")
    block_span = 2 * BLK
    q_heads = w_query.shape[1] // HEAD_SIZE
    kv_heads = key_weight_matrix.shape[1] // HEAD_SIZE
    group_width = q_heads // kv_heads
    scale_qk = HEAD_SIZE ** (-0.5)
    weights = (
        lax.all_gather(w_query, "ctx", axis=0, tiled=True),
        lax.all_gather(key_weight_matrix, "ctx", axis=0, tiled=True),
        lax.all_gather(value_weight_matrix, "ctx", axis=0, tiled=True),
        lax.all_gather(w_out, "ctx", axis=1, tiled=True),
        lax.all_gather(w_gate, "ctx", axis=0, tiled=True),
        lax.all_gather(w_up, "ctx", axis=0, tiled=True),
        lax.all_gather(w_down, "ctx", axis=1, tiled=True),
    )
    wq_full, wk_full, wv_full, wo_full, wg_full, wu_full, wd_full = weights
    offsets = jnp.arange(BLK, dtype=jnp.int32)

    def block_positions(owner):
        columns = lax.dynamic_slice_in_dim(block_order, 2 * owner, 2, 1)
        return (columns[:, :, None] * BLK + offsets).reshape(SEQS, block_span)

    query_pos = block_positions(ctx_index)
    flat_pos = query_pos.reshape(-1)
    inverse = THETA ** (-jnp.arange(0, HEAD_SIZE, 2, dtype=jnp.float32) / HEAD_SIZE)
    angle = flat_pos.astype(jnp.float32)[:, None] * inverse[None, :]
    cosine = jnp.cos(angle)[:, None, :]
    sine = jnp.sin(angle)[:, None, :]
    stream = tokens.astype(jnp.float32)
    scale_in = rms_scale(stream)
    unit_in = stream * scale_in
    normed_rows = (unit_in * in_gain).astype(jnp.bfloat16)
    normed_all = lax.all_gather(normed_rows, "tp", axis=0, tiled=True)
    query_lin = matmul(normed_all, wq_full).reshape(ctx_rows, q_heads, HEAD_SIZE)
    key_linear = matmul(normed_all, wk_full).reshape(ctx_rows, kv_heads, HEAD_SIZE)
    value_low = (
        matmul(normed_all, wv_full)
        .astype(jnp.bfloat16)
        .reshape(SEQS, block_span, kv_heads, HEAD_SIZE)
    )
    query_scale = rms_scale(query_lin)
    query_unit = query_lin * query_scale
    query_low = (
        rotate(query_unit * q_gain, cosine, sine)
        .astype(jnp.bfloat16)
        .reshape(SEQS, block_span, kv_heads, group_width, HEAD_SIZE)
    )
    key_scale = rms_scale(key_linear)
    key_unit = key_linear * key_scale
    key_low = (
        rotate(key_unit * k_gain, cosine, sine)
        .astype(jnp.bfloat16)
        .reshape(SEQS, block_span, kv_heads, HEAD_SIZE)
    )

    def scores_of(keys, key_pos):
        raw = (
            jnp.einsum("sqkgd,slkd->skgql", query_low, keys, preferred_element_type=jnp.float32)
            * scale_qk
        )
        allowed = (key_pos[:, None, :] <= query_pos[:, :, None]) & (
            key_pos[:, None, :] < seq_lens[:, None, None]
        )
        allowed = allowed[:, None, None, :, :]
        return (jnp.where(allowed, raw, FLOOR), allowed)

    def absorb(state, keys, value_rows, owner):
        running_top, running_total, running_acc = state
        scores, allowed = scores_of(keys, block_positions(owner))
        new_top = jnp.maximum(running_top, jnp.max(scores, axis=-1))
        weights_now = jnp.where(allowed, jnp.exp(scores - new_top[..., None]), 0.0)
        shrink = jnp.exp(running_top - new_top)
        running_total = running_total * shrink + jnp.sum(weights_now, axis=-1)
        running_acc = running_acc * shrink[..., None] + jnp.einsum(
            "skgql,slkd->skgqd",
            weights_now.astype(jnp.bfloat16),
            value_rows,
            preferred_element_type=jnp.float32,
        )
        return (new_top, running_total, running_acc)

    stat_shape = (SEQS, kv_heads, group_width, block_span)
    initial = (
        jnp.full(stat_shape, FLOOR, jnp.float32),
        jnp.zeros(stat_shape, jnp.float32),
        jnp.zeros(stat_shape + (HEAD_SIZE,), jnp.float32),
    )
    first_state = absorb(initial, key_low, value_low, ctx_index)

    def cycle_turn(carry, turn):
        keys, value_rows, state = carry
        keys, value_rows = from_behind((keys, value_rows), "ctx", 1)
        owner = (ctx_index - turn) % ctx_count
        state = absorb(state, keys, value_rows, owner)
        return ((keys, value_rows, state), (keys, value_rows))

    (unused_keys, unused_values, final_state), (kept_keys, kept_values) = lax.scan(
        cycle_turn, (key_low, value_low, first_state), jnp.arange(1, ctx_count, dtype=jnp.int32)
    )
    all_keys = jnp.concatenate([key_low[None], kept_keys], axis=0)
    all_values = jnp.concatenate([value_low[None], kept_values], axis=0)
    top_final, total_final, acc_final = final_state
    log_total = top_final + jnp.log(total_final)
    attn_exact = acc_final / total_final[..., None]
    mixed_low = (
        jnp.transpose(attn_exact, (0, 3, 1, 2, 4))
        .reshape(ctx_rows, q_heads * HEAD_SIZE)
        .astype(jnp.bfloat16)
    )
    middle = stream + lax.psum_scatter(
        matmul(row_slice(mixed_low, jnp.int32(0), lax.axis_size("tp") * tok_rows), wo_full).astype(
            jnp.bfloat16
        ),
        "tp",
        scatter_dimension=0,
        tiled=True,
    ).astype(jnp.float32)
    scale_post = rms_scale(middle)
    unit_post = middle * scale_post
    post_rows = (unit_post * post_gain).astype(jnp.bfloat16)
    post_all = lax.all_gather(post_rows, "tp", axis=0, tiled=True)
    gate = matmul(post_all, wg_full)
    up_val = matmul(post_all, wu_full)
    sigma = jax.nn.sigmoid(gate)
    active = gate * sigma
    hidden_low = (active * up_val).astype(jnp.bfloat16)
    result = middle + lax.psum_scatter(
        matmul(row_slice(hidden_low, jnp.int32(0), lax.axis_size("tp") * tok_rows), wd_full).astype(
            jnp.bfloat16
        ),
        "tp",
        scatter_dimension=0,
        tiled=True,
    ).astype(jnp.float32)
    output = result.astype(jnp.bfloat16)
    valid_all = (query_pos < seq_lens[:, None]).reshape(-1).astype(jnp.float32)
    valid_rows = row_slice(valid_all, tp_index * tok_rows, tok_rows)
    diff = (result - teacher.astype(jnp.float32)) * valid_rows[:, None]
    error_local = jnp.sum(diff * diff)
    diff_low = diff.astype(jnp.bfloat16)
    diff_all = lax.all_gather(diff_low, "tp", axis=0, tiled=True)
    weights_two = (
        lax.all_gather(w_query, "ctx", axis=0, tiled=True),
        lax.all_gather(key_weight_matrix, "ctx", axis=0, tiled=True),
        lax.all_gather(value_weight_matrix, "ctx", axis=0, tiled=True),
        lax.all_gather(w_out, "ctx", axis=1, tiled=True),
        lax.all_gather(w_gate, "ctx", axis=0, tiled=True),
        lax.all_gather(w_up, "ctx", axis=0, tiled=True),
        lax.all_gather(w_down, "ctx", axis=1, tiled=True),
    )
    bq_full, bk_full, bv_full, bo_full, bg_full, bu_full, bd_full = weights_two
    grad_wd = matmul_tn(hidden_low, diff_all)
    d_hidden = matmul_nt(diff_all, bd_full)
    d_gate = (d_hidden * up_val * sigma * (1.0 + gate * (1.0 - sigma))).astype(jnp.bfloat16)
    d_up = (d_hidden * active).astype(jnp.bfloat16)
    grad_wg = matmul_tn(post_all, d_gate)
    grad_wu = matmul_tn(post_all, d_up)
    start = jnp.int32(0)
    d_post = lax.psum_scatter(
        (
            matmul_nt(row_slice(d_gate, start, lax.axis_size("tp") * tok_rows), bg_full)
            + matmul_nt(row_slice(d_up, start, lax.axis_size("tp") * tok_rows), bu_full)
        ).astype(jnp.bfloat16),
        "tp",
        scatter_dimension=0,
        tiled=True,
    ).astype(jnp.float32)
    grad_post_local = jnp.sum(d_post * unit_post, axis=0)
    d_middle = diff + rms_back(middle, scale_post, d_post * post_gain)
    d_mid_low = d_middle.astype(jnp.bfloat16)
    d_mid_all = lax.all_gather(d_mid_low, "tp", axis=0, tiled=True)
    grad_wo = matmul_tn(mixed_low, d_mid_all)
    d_mixed = matmul_nt(d_mid_all, bo_full).astype(jnp.bfloat16)
    d_mixed_grid = jnp.transpose(
        d_mixed.reshape(SEQS, block_span, kv_heads, group_width, HEAD_SIZE), (0, 2, 3, 1, 4)
    )
    delta = jnp.sum(d_mixed_grid.astype(jnp.float32) * attn_exact, axis=-1)

    def revisit(carry, turn):
        grad_queries, grad_keys, grad_values = carry
        owner = (ctx_index - turn) % ctx_count
        keys = all_keys[turn]
        value_rows = all_values[turn]
        scores, allowed = scores_of(keys, block_positions(owner))
        probs = jnp.where(allowed, jnp.exp(scores - log_total[..., None]), 0.0)
        probs_low = probs.astype(jnp.bfloat16)
        d_probs = jnp.einsum(
            "skgqd,slkd->skgql", d_mixed_grid, value_rows, preferred_element_type=jnp.float32
        )
        d_scores = (probs * (d_probs - delta[..., None])).astype(jnp.bfloat16)
        grad_queries = grad_queries + jnp.einsum(
            "skgql,slkd->skgqd", d_scores, keys, preferred_element_type=jnp.float32
        )
        grad_keys = grad_keys + jnp.einsum(
            "skgql,sqkgd->slkd", d_scores, query_low, preferred_element_type=jnp.float32
        )
        grad_values = grad_values + jnp.einsum(
            "skgql,skgqd->slkd", probs_low, d_mixed_grid, preferred_element_type=jnp.float32
        )
        grad_keys, grad_values = (
            from_behind(grad_keys.astype(jnp.bfloat16), "ctx", 1).astype(grad_keys.dtype),
            from_behind(grad_values.astype(jnp.bfloat16), "ctx", 1).astype(grad_values.dtype),
        )
        return ((grad_queries, grad_keys, grad_values), None)

    kv_shape = (SEQS, block_span, kv_heads, HEAD_SIZE)
    start_carry = (
        jnp.zeros(stat_shape + (HEAD_SIZE,), jnp.float32),
        jnp.zeros(kv_shape, jnp.float32),
        jnp.zeros(kv_shape, jnp.float32),
    )
    (grad_queries, grad_keys, grad_values), unused_out = lax.scan(
        revisit, start_carry, jnp.arange(ctx_count, dtype=jnp.int32)
    )
    grad_queries = (
        jnp.transpose(grad_queries, (0, 3, 1, 2, 4)).reshape(ctx_rows, q_heads, HEAD_SIZE)
        * scale_qk
    )
    grad_keys = grad_keys.reshape(ctx_rows, kv_heads, HEAD_SIZE) * scale_qk
    d_values = grad_values.reshape(ctx_rows, kv_heads * HEAD_SIZE).astype(jnp.bfloat16)
    query_back = rotate_back(grad_queries, cosine, sine)
    grad_q_local = jnp.sum(query_back * query_unit, axis=(0, 1))
    d_query_lin = (
        rms_back(query_lin, query_scale, query_back * q_gain)
        .reshape(ctx_rows, q_heads * HEAD_SIZE)
        .astype(jnp.bfloat16)
    )
    key_back = rotate_back(grad_keys, cosine, sine)
    grad_k_local = jnp.sum(key_back * key_unit, axis=(0, 1))
    d_key_lin = (
        rms_back(key_linear, key_scale, key_back * k_gain)
        .reshape(ctx_rows, kv_heads * HEAD_SIZE)
        .astype(jnp.bfloat16)
    )
    grad_wq = matmul_tn(normed_all, d_query_lin)
    grad_wk = matmul_tn(normed_all, d_key_lin)
    grad_wv = matmul_tn(normed_all, d_values)
    start = jnp.int32(0)
    part_query = matmul_nt(row_slice(d_query_lin, start, lax.axis_size("tp") * tok_rows), bq_full)
    part_key = matmul_nt(row_slice(d_key_lin, start, lax.axis_size("tp") * tok_rows), bk_full)
    part_value = matmul_nt(row_slice(d_values, start, lax.axis_size("tp") * tok_rows), bv_full)
    d_normed = lax.psum_scatter(
        (part_query + part_key + part_value).astype(jnp.bfloat16),
        "tp",
        scatter_dimension=0,
        tiled=True,
    ).astype(jnp.float32)
    grad_in_local = jnp.sum(d_normed * unit_in, axis=0)
    d_tokens = (d_middle + rms_back(stream, scale_in, d_normed * in_gain)).astype(jnp.bfloat16)
    summed = (
        lax.psum_scatter(
            grad_wq.astype(jnp.bfloat16), "ctx", scatter_dimension=0, tiled=True
        ).astype(jnp.float32),
        lax.psum_scatter(
            grad_wk.astype(jnp.bfloat16), "ctx", scatter_dimension=0, tiled=True
        ).astype(jnp.float32),
        lax.psum_scatter(
            grad_wv.astype(jnp.bfloat16), "ctx", scatter_dimension=0, tiled=True
        ).astype(jnp.float32),
        lax.psum_scatter(
            grad_wo.astype(jnp.bfloat16), "ctx", scatter_dimension=1, tiled=True
        ).astype(jnp.float32),
        lax.psum_scatter(
            grad_wg.astype(jnp.bfloat16), "ctx", scatter_dimension=0, tiled=True
        ).astype(jnp.float32),
        lax.psum_scatter(
            grad_wu.astype(jnp.bfloat16), "ctx", scatter_dimension=0, tiled=True
        ).astype(jnp.float32),
        lax.psum_scatter(
            grad_wd.astype(jnp.bfloat16), "ctx", scatter_dimension=1, tiled=True
        ).astype(jnp.float32),
    )
    totals = lax.psum(
        (grad_in_local, grad_q_local, grad_k_local, grad_post_local, error_local), ("ctx", "tp")
    )
    count_valid = jnp.sum(seq_lens).astype(jnp.float32)
    loss = 0.5 * totals[4] / (count_valid * MODEL_WIDTH)
    return (
        output,
        loss,
        d_tokens,
        totals[0],
        summed[0],
        summed[1],
        summed[2],
        totals[1],
        totals[2],
        summed[3],
        totals[3],
        summed[4],
        summed[5],
        summed[6],
    )


F32 = jnp.float32
BF16 = jnp.bfloat16
MESH = pl.DeviceIdType.MESH
VMEM_LIMIT = 62 << 20


def busy(us):
    return pl.CostEstimate(flops=0, bytes_accessed=us * 3_000_000, transcendentals=0)

LOG2E = 1.4426950408889634
UNIT = 128
KEYS = 512
CORE_GROUPS = [[0, 2, 4, 6], [1, 3, 5, 7]]
SIBLING = [(i, i ^ 1) for i in range(8)]


def spec_vmem():
    return pl.BlockSpec(memory_space=pltpu.VMEM)


def spec_any():
    return pl.BlockSpec(memory_space=pl.ANY)


def spec_smem():
    return pl.BlockSpec(memory_space=pltpu.SMEM)


def plane_neighbours():
    me = lax.axis_index("ctx")
    core = lax.rem(me, 2)
    x = lax.rem(me // 2, 2)
    y = me // 4
    sib = me + 1 - 2 * core
    nx = me + 2 - 4 * x
    ny = me + 4 - 8 * y
    dg = nx + 4 - 8 * y
    return me, sib, nx, ny, dg


def greet(devices):
    barrier = pltpu.get_barrier_semaphore()
    for device in devices:
        pl.semaphore_signal(barrier, inc=1, device_id={"ctx": device}, device_id_type=MESH)
    pl.semaphore_wait(barrier, len(devices))


def pick(step, options):
    value = options[0]
    for i in range(1, len(options)):
        value = jnp.where(step == i, options[i], value)
    return value


SUBS = 4


def on_ctx(device):
    return {"ctx": device}


def on_plane(plane):
    return {"tp": plane}


def send(src, dst, send_sem, recv_sem, where):
    return pltpu.make_async_remote_copy(
        src_ref=src,
        dst_ref=dst,
        send_sem=send_sem,
        recv_sem=recv_sem,
        device_id=where,
        device_id_type=MESH,
    )


class Gather:
    def __init__(self, x_ref, xs, local_sem, send_sems, recv_sems):
        self.x_ref, self.xs = x_ref, xs
        self.local_sem, self.send_sems, self.recv_sems = local_sem, send_sems, recv_sems
        self.me, self.sib, self.nx, self.ny, self.dg = plane_neighbours()
        self.shift = self.sib - self.me
        self.piece = x_ref.shape[0] // SUBS

    def part(self, block, s):
        return self.xs.at[block, pl.ds(s * self.piece, self.piece)]

    def remote(self, src, kind, block, s, device):
        return send(
            src, self.part(block, s), self.send_sems.at[kind, s], self.recv_sems.at[block, s], on_ctx(device)
        )

    def own(self, s):
        return self.x_ref.at[pl.ds(s * self.piece, self.piece)]

    def start(self):
        for s in range(SUBS):
            t = (s + SUBS // 2) % SUBS
            self.remote(self.own(s), 0, self.me, s, self.nx).start()
            self.remote(self.own(t), 1, self.me, t, self.ny).start()
        for s in range(SUBS):
            self.remote(self.own(s), 2, self.me, s, self.sib).start()
        keep = pltpu.make_async_copy(self.x_ref, self.xs.at[self.me], self.local_sem)
        keep.start()
        keep.wait()

    def arrived(self, block, s):
        self.remote(self.part(block, s), 0, block, s, self.sib).wait_recv()

    def relay(self, kind, block, s, device):
        self.remote(self.part(block, s), kind, block, s, device).start()

    def pass_on(self, i):
        half = SUBS // 2
        s, t = i, (i + half) % SUBS
        self.arrived(self.nx, s)
        if s < half:
            self.relay(3, self.nx, s, self.ny)
        self.relay(4, self.nx, s, self.sib)
        self.arrived(self.ny, t)
        if t >= half:
            self.relay(3, self.ny, t, self.nx)
        self.relay(5, self.ny, t, self.sib)

    def before(self, step, passing=True):
        half = SUBS // 2

        @pl.when(step == 1)
        def _():
            for s in range(SUBS):
                self.arrived(self.sib, s)

        if passing:

            @pl.when(step == 2)
            def _():
                for i in range(SUBS):
                    self.pass_on(i)

        @pl.when(step == 3)
        def _():
            for s in range(SUBS):
                self.arrived(self.nx + self.shift, s)

        @pl.when(step == 4)
        def _():
            for s in (0, half):
                self.arrived(self.dg, s)
                self.relay(6, self.dg, s, self.sib)

        @pl.when(step == 5)
        def _():
            for s in range(SUBS):
                self.arrived(self.ny + self.shift, s)

        @pl.when(step == 6)
        def _():
            for s in range(SUBS):
                if s % half:
                    self.arrived(self.dg, s)
                    self.relay(6, self.dg, s, self.sib)

        @pl.when(step == 7)
        def _():
            for s in range(SUBS):
                self.arrived(self.dg + self.shift, s)

    def block(self, step):
        near = (self.me, self.nx, self.ny, self.dg)
        return pick(step, [b + o for b in near for o in (0, self.shift)])

    def finish(self):
        for s in range(SUBS):
            for kind in range(7):
                self.remote(self.part(self.me, s), kind, self.me, s, self.sib).wait_send()


def gather_scratch(rows, width):
    return [
        pltpu.VMEM((8, rows, width), BF16),
        pltpu.SemaphoreType.DMA,
        pltpu.SemaphoreType.DMA((7, SUBS)),
        pltpu.SemaphoreType.DMA((8, SUBS)),
    ]


class Scatter:
    def __init__(self, to_sib, from_sib, own, diag_out, diag_in, x_out, y_out, x_in, y_in, sends, recvs):
        self.to_sib, self.from_sib, self.own = to_sib, from_sib, own
        self.diag_out, self.diag_in = diag_out, diag_in
        self.x_out, self.y_out, self.x_in, self.y_in = x_out, y_out, x_in, y_in
        self.sends, self.recvs = sends, recvs
        self.me, self.sib, self.nx, self.ny, self.dg = plane_neighbours()
        self.rows = diag_out.shape[0]

    def round(self, i):
        return pl.ds(i * (self.rows // 2), self.rows // 2)

    def piece(self, i, half):
        quarter = self.rows // 4
        return pl.ds((2 * i + half) * quarter, quarter)

    def remote(self, src, dst, kind, i, device):
        return send(src, dst, self.sends.at[kind, i], self.recvs.at[kind, i], on_ctx(device))

    def sibling(self, n, i):
        at = self.round(i)
        return self.remote(self.to_sib.at[n, at], self.from_sib.at[n, at], n, i, self.sib)

    def hop(self, kind, i):
        out, into, half, device = (
            (self.diag_out, self.diag_in, 0, self.nx),
            (self.diag_out, self.diag_in, 1, self.ny),
            (self.x_out, self.x_in, 0, self.nx),
            (self.x_out, self.x_in, 1, self.nx),
            (self.y_out, self.y_in, 0, self.ny),
            (self.y_out, self.y_in, 1, self.ny),
        )[kind]
        at = self.piece(i, half)
        return self.remote(out.at[at], into.at[at], 4 + kind, i, device)

    def blocks(self):
        shift = self.sib - self.me
        return [b + o for b in (self.dg, self.nx, self.ny, self.me) for o in (shift, 0)]

    def block(self, step):
        return pick(2 * (step // 4) + lax.rem(step, 2), self.blocks())

    def chip_sum(self, n, at):
        return self.own[n, at].astype(F32) + self.from_sib[n, at].astype(F32)

    def step(self, step, product, late=False):
        block = self.block(step)
        n = step // 4
        i = lax.rem(step, 4) // 2
        at = self.round(pl.multiple_of(i, 1))

        @pl.when(lax.rem(step, 2) == 0)
        def _():
            product(block, at, self.to_sib, n)
            self.sibling(n, i).start()

        @pl.when(lax.rem(step, 2) == 1)
        def _():
            product(block, at, self.own, n)
            self.sibling(n, i).wait_recv()

        for r in range(2):
            first, second = self.piece(r, 0), self.piece(r, 1)

            @pl.when(step == 1 + 2 * r)
            def _():
                self.diag_out[first] = self.chip_sum(0, first).astype(BF16)
                self.hop(0, r).start()
                self.diag_out[second] = self.chip_sum(0, second).astype(BF16)
                self.hop(1, r).start()

            @pl.when(step == 5 + 2 * r)
            def _():
                self.x_out[first] = self.chip_sum(1, first).astype(BF16)
                self.hop(2, r).start()

            @pl.when(step == 9 + 2 * r)
            def _():
                self.y_out[second] = self.chip_sum(2, second).astype(BF16)
                self.hop(5, r).start()

        if not late:

            @pl.when(step == 11)
            def _():
                self.second_wave()

    def second_wave(self):
        for i in range(2):
            first, second = self.piece(i, 0), self.piece(i, 1)
            self.hop(0, i).wait_recv()
            self.y_out[first] = (self.chip_sum(2, first) + self.diag_in[first].astype(F32)).astype(BF16)
            self.hop(4, i).start()
            self.hop(1, i).wait_recv()
            self.x_out[second] = (self.chip_sum(1, second) + self.diag_in[second].astype(F32)).astype(BF16)
            self.hop(3, i).start()

    def finish(self, o_ref):
        for i in range(2):
            for kind in range(2, 6):
                self.hop(kind, i).wait_recv()
            at = self.round(i)
            o_ref[at] = (
                self.chip_sum(3, at) + self.x_in[at].astype(F32) + self.y_in[at].astype(F32)
            ).astype(o_ref.dtype)
        for i in range(2):
            for n in range(4):
                self.sibling(n, i).wait_send()
            for kind in range(6):
                self.hop(kind, i).wait_send()


def scatter_scratch(rows, width):
    four = pltpu.VMEM((4, rows, width), BF16)
    one = pltpu.VMEM((rows, width), BF16)
    return [four] * 3 + [one] * 6 + [pltpu.SemaphoreType.DMA((10, 2)), pltpu.SemaphoreType.DMA((10, 2))]


N_SCATTER = 11


def nn(left, right):
    return lax.dot_general(left, right, (((1,), (0,)), ((), ())), preferred_element_type=F32)


def nt(left, right):
    return lax.dot_general(left, right, (((1,), (1,)), ((), ())), preferred_element_type=F32)


def tn(left, right):
    return lax.dot_general(left, right, (((0,), (0,)), ((), ())), preferred_element_type=F32)


def comm_params(collective_id):
    return pltpu.CompilerParams(
        collective_id=collective_id, has_side_effects=True, vmem_limit_bytes=VMEM_LIMIT
    )


def greet_column(devices):
    barrier = pltpu.get_barrier_semaphore()
    plane, planes = lax.axis_index("tp"), lax.axis_size("tp")
    for device in devices:
        pl.semaphore_signal(barrier, inc=1, device_id=on_ctx(device), device_id_type=MESH)
    for step in (1, planes - 1):
        where = on_plane(lax.rem(plane + step, planes))
        pl.semaphore_signal(barrier, inc=1, device_id=where, device_id_type=MESH)
    pl.semaphore_wait(barrier, len(devices) + 2)


class Line:
    def __init__(self, up_src, down_src, from_lo, from_hi, sends, recvs, rows, back):
        self.up_src, self.down_src, self.from_lo, self.from_hi = up_src, down_src, from_lo, from_hi
        self.sends, self.recvs = sends, recvs
        self.units = rows // UNIT
        self.back = back
        self.plane, self.planes = lax.axis_index("tp"), lax.axis_size("tp")

    def at(self, block, i):
        return pl.ds(pl.multiple_of((block * self.units + i) * UNIT, UNIT), UNIT)

    def up(self, block, i):
        at, n = self.at(block, i), block * self.units + i
        return send(self.up_src.at[at], self.from_lo.at[at], self.sends.at[0, n], self.recvs.at[0, n], on_plane(self.plane + 1))

    def down(self, block, i):
        at, n = self.at(block, i), block * self.units + i
        return send(self.down_src.at[at], self.from_hi.at[at], self.sends.at[1, n], self.recvs.at[1, n], on_plane(self.plane - 1))

    def each(self, block, ups, downs):
        for i in range(self.units):
            up = i < self.plane + 1 if self.back else i >= self.plane
            down = i >= self.plane - 1 if self.back else i < self.plane

            @pl.when(up & (self.plane < self.planes - 1))
            def _():
                ups(self.up(block, i))

            @pl.when(down & (self.plane > 0))
            def _():
                downs(self.down(block, i))

    def start(self, block):
        self.each(block, lambda copy: copy.start(), lambda copy: copy.start())

    def sent(self, block):
        self.each(block, lambda copy: copy.wait_send(), lambda copy: copy.wait_send())

    def arrived(self, block):
        for i in range(self.units):
            below = i < self.plane if self.back else i >= self.plane - 1
            above = i >= self.plane if self.back else i < self.plane + 1

            @pl.when(below & (self.plane > 0))
            def _():
                self.up(block, i).wait_recv()

            @pl.when(above & (self.plane < self.planes - 1))
            def _():
                self.down(block, i).wait_recv()


class ChipSwap:
    def __init__(self, src, dst, local_sem, send_sems, recv_sems):
        self.src, self.dst = src, dst
        self.local_sem, self.send_sems, self.recv_sems = local_sem, send_sems, recv_sems
        me, _, nx, ny, dg = plane_neighbours()
        self.chip, self.away = me // 2, (dg, nx, ny)

    def own(self):
        return pltpu.make_async_copy(self.src.at[self.chip], self.dst.at[self.chip], self.local_sem)

    def to(self, n):
        there = self.away[n]
        return send(
            self.src.at[there // 2], self.dst.at[self.chip], self.send_sems.at[n], self.recv_sems.at[self.chip], on_ctx(there)
        )

    def start(self):
        self.own().start()
        for n in range(3):
            self.to(n).start()

    def arrive(self):
        self.own().wait()
        for n in range(3):
            there = self.away[n] // 2
            send(
                self.src.at[there], self.dst.at[there], self.send_sems.at[n], self.recv_sems.at[there], on_ctx(self.away[n])
            ).wait_recv()

    def sent(self):
        for n in range(3):
            self.to(n).wait_send()

    def finish(self):
        self.arrive()
        self.sent()


SWAP_SCRATCH = [pltpu.SemaphoreType.DMA, pltpu.SemaphoreType.DMA((3,)), pltpu.SemaphoreType.DMA((4,))]


class LineGather:
    def __init__(self, src, dst, local_sem, send_sems, recv_sems):
        self.src, self.dst = src, dst
        self.local_sem, self.send_sems, self.recv_sems = local_sem, send_sems, recv_sems
        self.plane, self.planes = lax.axis_index("tp"), lax.axis_size("tp")
        self.pieces = src.shape[0]

    def own(self):
        return pltpu.make_async_copy(self.src, self.dst.at[self.plane], self.local_sem)

    def copy(self, way, hop, n, origin):
        src = self.src.at[n] if hop == 0 else self.dst.at[origin, n]
        return send(
            src,
            self.dst.at[origin, n],
            self.send_sems.at[way, hop, n],
            self.recv_sems.at[origin, n],
            on_plane(self.plane + 1 - 2 * way),
        )

    def ways(self, hop):
        up, down = self.plane - hop, self.plane + hop
        yield 0, up, up >= 0, self.plane < self.planes - 1
        yield 1, down, down < self.planes, self.plane > 0

    def start(self):
        self.own().start()
        for way, origin, _, goes_on in self.ways(0):

            @pl.when(goes_on)
            def _():
                for n in range(self.pieces):
                    self.copy(way, 0, n, origin).start()

    def arrive(self, hop, then=None):
        for way, origin, there, goes_on in self.ways(hop):

            @pl.when(there)
            def _():
                for n in range(self.pieces):
                    self.copy(way, 0, n, origin).wait_recv()
                    if hop == self.planes - 1:
                        continue

                    @pl.when(goes_on)
                    def _():
                        self.copy(way, hop, n, origin).start()

                if then is not None:
                    then(origin)

    def finish(self):
        self.own().wait()
        self.sent()

    def sent(self):
        for hop in range(self.planes - 1):
            for way, origin, there, goes_on in self.ways(hop):

                @pl.when(there & goes_on)
                def _():
                    for n in range(self.pieces):
                        self.copy(way, hop, n, origin).wait_send()


def line_scratch(pieces):
    dma = pltpu.SemaphoreType.DMA
    return [dma, dma((2, 3, pieces)), dma((4, pieces))]


class LineSum:
    def __init__(self, own, up_in, down_in, send_sems, recv_sems):
        self.own, self.into = own, (up_in, down_in)
        self.send_sems, self.recv_sems = send_sems, recv_sems
        self.plane, self.planes = lax.axis_index("tp"), lax.axis_size("tp")

    def copy(self, way, p, first):
        into = self.into[way]
        return send(
            self.own(p) if first else into.at[p],
            into.at[p],
            self.send_sems.at[way, p],
            self.recv_sems.at[way, p],
            on_plane(self.plane + 1 - 2 * way),
        )

    def moves(self, k):
        last = self.planes - 1
        for way in range(2):
            z = last - k if way else k
            yield way, z, (range(z) if way else range(last, z, -1))

    def stage(self, k):
        for way, z, ends in self.moves(k):

            @pl.when(self.plane == z)
            def _():
                for p in ends:
                    copy = self.copy(way, p, k == 0)
                    if k > 0:
                        copy.wait_recv()
                        into = self.into[way]
                        into[p] = (self.own(p)[...].astype(F32) + into[p].astype(F32)).astype(BF16)
                    copy.start()

    def collect(self, out):
        out[...] = self.own(self.plane)[...].astype(F32)
        for way in range(2):

            @pl.when(self.plane < self.planes - 1 if way else self.plane > 0)
            def _():
                self.copy(way, self.plane, False).wait_recv()
                out[...] += self.into[way][self.plane].astype(F32)

    def finish(self):
        for k in range(self.planes - 1):
            for way, z, ends in self.moves(k):

                @pl.when(self.plane == z)
                def _():
                    for p in ends:
                        self.copy(way, p, k == 0).wait_send()


class Turn:
    def __init__(self, ca_ref, sa_ref, cb_ref, sb_ref, unit):
        ca, sa = ca_ref[pl.ds(unit, 1), :], sa_ref[pl.ds(unit, 1), :]
        cb, sb = cb_ref[...], sb_ref[...]
        self.cosine = ca * cb - sa * sb
        sine = sa * cb + ca * sb
        lane = lax.broadcasted_iota(jnp.int32, sine.shape, 1)
        self.sine = jnp.where(lane < HEAD_SIZE // 2, -sine, sine)

    def forth(self, v):
        return v * self.cosine + pltpu.roll(v, HEAD_SIZE // 2, 1) * self.sine

    def back(self, v):
        return v * self.cosine - pltpu.roll(v, HEAD_SIZE // 2, 1) * self.sine


def others(me):
    _, sib, nx, ny, dg = plane_neighbours()
    shift = sib - me
    return (dg, dg + shift, nx, nx + shift, ny, ny + shift, sib)


def qkv_kernel(
    x_ref,
    home_ref,
    qg_ref,
    kg_ref,
    ca_ref,
    sa_ref,
    cb_ref,
    sb_ref,
    gate_ref,
    up_ref,
    down_ref,
    out_ref,
    all_ref,
    w_out_ref,
    q_ref,
    kv_ref,
    lo_ref,
    hi_ref,
    lin_ref,
    gates_ref,
    ups_ref,
    downs_ref,
    outs_ref,
    xs,
    local_sem,
    send_sems,
    recv_sems,
    keep_sems,
    w,
    w_local,
    w_sends,
    w_recvs,
    slab,
    gate_part,
    kv_sends,
    kv_recvs,
    *sems,
):
    ring = Gather(x_ref, xs, local_sem, send_sems, recv_sems)
    me = ring.me
    rows = x_ref.shape[0]
    deep = home_ref.shape[1]
    slabs = LineGather(home_ref, slab, *sems[0:3])
    outs = LineGather(out_ref, outs_ref, *sems[3:6])
    gates = LineGather(gate_part, gates_ref, *sems[6:9])
    gate_swap = ChipSwap(gate_ref, gate_part, *sems[9:12])
    late_swaps = (ChipSwap(up_ref, ups_ref, *sems[12:15]), ChipSwap(down_ref, downs_ref, *sems[15:18]))
    line = Line(kv_ref, kv_ref, lo_ref, hi_ref, kv_sends, kv_recvs, rows, False)

    def weight(source, origin, k):
        return send(
            slab.at[origin, k],
            w.at[pl.ds(source * deep, deep)],
            w_sends.at[2 * origin + k],
            w_recvs.at[source],
            on_ctx(2 * origin + k),
        )

    own_weight = pltpu.make_async_copy(
        slab.at[me // 2, lax.rem(me, 2)], w.at[pl.ds(me * deep, deep)], w_local
    )

    def hand_out(origin):
        for k in range(2):

            @pl.when(2 * origin + k == me)
            def _():
                own_weight.start()

            @pl.when(2 * origin + k != me)
            def _():
                weight(me, origin, k).start()

    greet_column(others(me))
    gate_swap.start()
    slabs.start()
    ring.start()
    outs.start()
    slabs.own().wait()
    hand_out(slabs.plane)
    slabs.arrive(1, hand_out)
    gate_swap.arrive()
    gates.start()
    ring.pass_on(0)
    ring.pass_on(1)
    slabs.arrive(2, hand_out)
    ring.pass_on(2)
    ring.pass_on(3)
    slabs.arrive(3, hand_out)
    for swap in late_swaps:
        swap.start()
    outs.arrive(1)
    gates.arrive(1)
    own_weight.wait()
    for device in others(me):
        weight(device, 0, 0).wait_recv()
    keep_w = pltpu.make_async_copy(w, w_out_ref, w_local)
    keep_w.start()

    def keep(block):
        return pltpu.make_async_copy(xs.at[block], all_ref.at[block], keep_sems.at[block])

    def head(v, gain_ref, turn):
        scale = lax.rsqrt(jnp.mean(v * v, axis=-1, keepdims=True) + EPS)
        return turn.forth(v * scale * gain_ref[...])

    def turn(step, carry):
        @pl.when(step == 4)
        def _():
            outs.arrive(2)
            gates.arrive(2)

        ring.before(step, passing=False)
        block = ring.block(step)
        keep(block).start()
        lin = nn(xs[block], w[...])
        lin_ref[pl.ds(pl.multiple_of(block * rows, rows), rows), :] = lin[:, : 3 * HEAD_SIZE]
        for i in range(rows // UNIT):
            unit = block * (rows // UNIT) + i
            rotation = Turn(ca_ref, sa_ref, cb_ref, sb_ref, unit)
            here = pl.ds(pl.multiple_of(unit * UNIT, UNIT), UNIT)
            part = lin[i * UNIT : (i + 1) * UNIT]
            for h in range(2):
                lanes = slice(h * HEAD_SIZE, (h + 1) * HEAD_SIZE)
                query = head(part[:, lanes], qg_ref, rotation)
                q_ref[here, lanes] = (query * (HEAD_SIZE**-0.5 * LOG2E)).astype(BF16)
            key = head(part[:, 2 * HEAD_SIZE : 3 * HEAD_SIZE], kg_ref, rotation)
            kv_ref[here, :HEAD_SIZE] = key.astype(BF16)
            kv_ref[here, HEAD_SIZE:] = part[:, 3 * HEAD_SIZE :].astype(BF16)

        line.start(block)
        return carry

    lax.fori_loop(0, 8, turn, 0)
    ring.finish()
    keep_w.wait()
    for origin in range(4):
        for k in range(2):

            @pl.when(2 * origin + k != me)
            def _():
                weight(me, origin, k).wait_send()

    for block in range(8):
        keep(block).wait()

    def settle(block, carry):
        line.sent(block)
        line.arrived(block)
        return carry

    lax.fori_loop(0, 8, settle, 0)
    for gather in (outs, gates):
        gather.arrive(3)
    for gather in (slabs, outs, gates):
        gather.finish() if gather is not slabs else gather.sent()
    gate_swap.sent()
    for swap in late_swaps:
        swap.finish()


def gather_qkv(normed, home, q_gain, k_gain, tables, gate, up, down, out):
    rows, width = normed.shape
    _, deep, cols = home.shape
    flat = jax.ShapeDtypeStruct((8 * rows, 2 * HEAD_SIZE), BF16)
    dma = pltpu.SemaphoreType.DMA
    return pl.pallas_call(
        qkv_kernel,
        out_shape=(
            jax.ShapeDtypeStruct((8, rows, width), BF16),
            jax.ShapeDtypeStruct((8 * deep, cols), BF16),
            flat,
            flat,
            flat,
            flat,
            jax.ShapeDtypeStruct((8 * rows, 3 * HEAD_SIZE), F32),
            jax.ShapeDtypeStruct((4,) + gate.shape, BF16),
            jax.ShapeDtypeStruct(up.shape, BF16),
            jax.ShapeDtypeStruct(down.shape, BF16),
            jax.ShapeDtypeStruct((4,) + out.shape, BF16),
        ),
        in_specs=[spec_any()] * 2 + [spec_vmem()] * 6 + [spec_any()] * 4,
        out_specs=(spec_any(), spec_any(), spec_vmem(), spec_vmem(), spec_any(), spec_any(), spec_vmem())
        + (spec_any(),) * 4,
        scratch_shapes=gather_scratch(rows, width)
        + [
            dma((8,)),
            pltpu.VMEM((8 * deep, cols), BF16),
            dma,
            dma((8,)),
            dma((8,)),
            pltpu.VMEM((4,) + home.shape, BF16),
            pltpu.VMEM(gate.shape, BF16),
            dma((2, 8 * rows // UNIT)),
            dma((2, 8 * rows // UNIT)),
        ]
        + line_scratch(home.shape[0])
        + line_scratch(out.shape[0])
        + line_scratch(gate.shape[0])
        + SWAP_SCRATCH * 3,
        compiler_params=comm_params(1),
        cost_estimate=busy(100),
        name="gather_qkv",
    )(normed, home, q_gain.reshape(1, -1), k_gain.reshape(1, -1), *tables, gate, up, down, out)


class Halves:
    def __init__(self, parts, at, local_sems, send_sems, recv_sems):
        self.parts, self.at = parts, at
        self.local_sems, self.send_sems, self.recv_sems = local_sems, send_sems, recv_sems
        self.me, self.sib = plane_neighbours()[:2]
        self.core = lax.rem(self.me, 2)

    def own(self, z, p):
        n = 4 * z + p
        return pltpu.make_async_copy(
            self.parts.at[2 * self.core + z, p], self.at(z, 2 * p + self.core), self.local_sems.at[n]
        )

    def swap(self, z, p):
        n = 4 * z + p
        return send(
            self.parts.at[2 - 2 * self.core + z, p],
            self.at(z, 2 * p + self.core),
            self.send_sems.at[n],
            self.recv_sems.at[n],
            on_ctx(self.sib),
        )

    def each(self):
        return [(z, p) for z in range(2) for p in range(4)]

    def start(self):
        for z, p in self.each():
            self.swap(z, p).start()
            self.own(z, p).start()

    def ready(self):
        for z, p in self.each():
            self.own(z, p).wait()
            n = 4 * z + p
            send(
                self.parts.at[2 * self.core + z, p],
                self.at(z, 2 * p + 1 - self.core),
                self.send_sems.at[n],
                self.recv_sems.at[n],
                on_ctx(self.sib),
            ).wait_recv()

    def finish(self):
        for z, p in self.each():
            self.swap(z, p).wait_send()


class Shares:
    def __init__(self, out, local_sems, send_sems, recv_sems):
        self.out = out
        self.local_sems, self.send_sems, self.recv_sems = local_sems, send_sems, recv_sems
        self.me, self.sib = plane_neighbours()[:2]
        self.core = lax.rem(self.me, 2)

    def own(self, tile, z, p):
        return pltpu.make_async_copy(tile, self.out.at[2 * self.core + z, p], self.local_sems.at[z, p])

    def other(self, tile, z, p):
        return send(
            tile,
            self.out.at[2 * self.core + z, p],
            self.send_sems.at[z, p],
            self.recv_sems.at[z, p],
            on_ctx(self.sib),
        )

    def arrive(self):
        for z in range(2):
            for p in range(4):
                there = self.out.at[2 - 2 * self.core + z, p]
                send(
                    there, there, self.send_sems.at[z, p], self.recv_sems.at[z, p], on_ctx(self.sib)
                ).wait_recv()


SHARES_SCRATCH = [pltpu.SemaphoreType.DMA((2, 4))] * 3
HALVES_SCRATCH = [pltpu.SemaphoreType.DMA((8,))] * 3


def up_kernel(
    x_ref,
    gate_ref,
    up_ref,
    all_ref,
    w_out_ref,
    a_ref,
    b_ref,
    h_ref,
    xs,
    local_sem,
    send_sems,
    recv_sems,
    keep_sems,
    stage,
    stage_sems,
    w,
    w_sem,
    *w_sems,
):
    ring = Gather(x_ref, xs, local_sem, send_sems, recv_sems)
    rows = x_ref.shape[0]
    halves, width, wide = w.shape
    deep = width // 8
    cols = wide // 2
    outs = (a_ref, b_ref, h_ref)
    greet((ring.sib, ring.nx, ring.ny))
    ring.start()
    gates = Halves(gate_ref, lambda z, c: w.at[z, pl.ds(c * deep, deep), pl.ds(0, cols)], *w_sems[:3])
    ups = Halves(up_ref, lambda z, c: w.at[z, pl.ds(c * deep, deep), pl.ds(cols, cols)], *w_sems[3:])
    gates.start()
    ups.start()
    gates.ready()
    ups.ready()
    keep_w = pltpu.make_async_copy(w, w_out_ref, w_sem)
    keep_w.start()

    def keep(block):
        return pltpu.make_async_copy(xs.at[block], all_ref.at[block], keep_sems.at[block])

    def put(slot, n, block):
        return pltpu.make_async_copy(
            stage.at[slot, n], outs[n].at[pl.ds(block * rows, rows)], stage_sems.at[slot, n]
        )

    def turn(step, carry):
        ring.before(step)
        block = ring.block(step)
        keep(block).start()
        slot = lax.rem(step, 2)

        @pl.when(step >= 2)
        def _():
            for n in range(3):
                put(slot, n, block).wait()

        for z in range(halves):
            both = nn(xs[block], w[z])
            gate, up = both[:, :cols], both[:, cols:]
            sigma = jax.nn.sigmoid(gate)
            active = gate * sigma
            here = slice(z * cols, (z + 1) * cols)
            stage[slot, 0, :, here] = (up * sigma * (1.0 + gate * (1.0 - sigma))).astype(BF16)
            stage[slot, 1, :, here] = active.astype(BF16)
            stage[slot, 2, :, here] = (active * up).astype(BF16)
        for n in range(3):
            put(slot, n, block).start()
        return carry

    lax.fori_loop(0, 8, turn, 0)
    ring.finish()
    gates.finish()
    ups.finish()
    keep_w.wait()
    for block in range(8):
        keep(block).wait()
    for slot in range(2):
        for n in range(3):
            put(slot, n, 0).wait()


def gather_up(post, gate_parts, up_parts):
    rows, width = post.shape
    wide = 2 * gate_parts.shape[-1]
    flat = jax.ShapeDtypeStruct((8 * rows, wide), BF16)
    return pl.pallas_call(
        up_kernel,
        out_shape=(
            jax.ShapeDtypeStruct((8, rows, width), BF16),
            jax.ShapeDtypeStruct((2, width, wide), BF16),
            flat,
            flat,
            flat,
        ),
        in_specs=[spec_any()] * 3,
        out_specs=(spec_any(),) * 5,
        scratch_shapes=gather_scratch(rows, width)
        + [
            pltpu.SemaphoreType.DMA((8,)),
            pltpu.VMEM((2, 3, rows, wide), BF16),
            pltpu.SemaphoreType.DMA((2, 3)),
            pltpu.VMEM((2, width, wide), BF16),
            pltpu.SemaphoreType.DMA,
        ]
        + HALVES_SCRATCH * 2,
        compiler_params=comm_params(2),
        cost_estimate=busy(62),
        name="gather_up",
    )(post, gate_parts, up_parts)


def down_kernel(h_any, parts_ref, middle_any, teacher_any, valid_ref, o_ref, low_ref, diff_ref, error_ref, w_out_ref, *scratch):
    rs = Scatter(*scratch[:N_SCATTER])
    (w, w_sem, h_ref, h_sems, middle_ref, teacher_ref, row_sems, w_local, w_sends, w_recvs) = scratch[N_SCATTER:]
    rows = o_ref.shape[0]
    _, _, cols, deep = parts_ref.shape
    weight = Halves(
        parts_ref,
        lambda z, c: w.at[pl.ds(z * cols, cols), pl.ds(pl.multiple_of(c * deep, deep), deep)],
        w_local,
        w_sends,
        w_recvs,
    )
    def fetch(block):
        here = pl.ds(pl.multiple_of(block * rows, rows), rows)
        return pltpu.make_async_copy(h_any.at[here], h_ref.at[here], h_sems.at[block])

    for block in rs.blocks():
        fetch(block).start()
    late = (
        pltpu.make_async_copy(middle_any, middle_ref, row_sems.at[0]),
        pltpu.make_async_copy(teacher_any, teacher_ref, row_sems.at[1]),
    )
    greet((rs.sib, rs.nx, rs.ny))
    weight.start()
    for copy in late:
        copy.start()
    weight.ready()
    keep_w = pltpu.make_async_copy(w, w_out_ref, w_sem)
    keep_w.start()

    def product(block, at, out, n):
        left = h_ref[pl.ds(pl.multiple_of(block * rows + at.start, rows // 2), rows // 2), :]
        for c in range(0, w.shape[1], 512):
            out[n, at, c : c + 512] = nn(left, w[:, c : c + 512]).astype(BF16)

    def turn(step, carry):
        @pl.when(lax.rem(step, 4) < 2)
        def _():
            fetch(rs.block(step)).wait()

        rs.step(step, product)
        return carry

    lax.fori_loop(0, 16, turn, 0)
    for copy in late:
        copy.wait()
    rs.finish(diff_ref)
    error = jnp.zeros((rows, HEAD_SIZE), F32)
    for n in range(0, diff_ref.shape[1], HEAD_SIZE):
        at = slice(n, n + HEAD_SIZE)
        result = middle_ref[:, at] + diff_ref[:, at]
        o_ref[:, at] = result.astype(BF16)
        diff = (result - teacher_ref[:, at].astype(F32)) * valid_ref[...]
        diff_ref[:, at] = diff
        low_ref[:, at] = diff.astype(BF16)
        error += diff * diff
    error_ref[...] = jnp.sum(error, axis=0, keepdims=True)
    weight.finish()
    keep_w.wait()


def scatter_down(hidden, parts, middle, teacher, valid):
    rows, width = middle.shape
    ff = hidden.shape[1]
    low = jax.ShapeDtypeStruct((rows, width), BF16)
    return pl.pallas_call(
        down_kernel,
        out_shape=(
            low,
            low,
            jax.ShapeDtypeStruct((rows, width), F32),
            jax.ShapeDtypeStruct((1, HEAD_SIZE), F32),
            jax.ShapeDtypeStruct((ff, width), BF16),
        ),
        in_specs=[spec_any()] * 4 + [spec_vmem()],
        out_specs=(spec_vmem(),) * 4 + (spec_any(),),
        scratch_shapes=scatter_scratch(rows, width)
        + [
            pltpu.VMEM((ff, width), BF16),
            pltpu.SemaphoreType.DMA,
            pltpu.VMEM(hidden.shape, BF16),
            pltpu.SemaphoreType.DMA((8,)),
            pltpu.VMEM((rows, width), F32),
            pltpu.VMEM((rows, width), BF16),
            pltpu.SemaphoreType.DMA((2,)),
        ]
        + HALVES_SCRATCH,
        compiler_params=comm_params(6),
        cost_estimate=busy(62),
        name="scatter_down",
    )(hidden, parts, middle, teacher, valid)


def down_back_kernel(
    x_ref,
    w_ref,
    a_ref,
    b_ref,
    h_ref,
    d_ref,
    gw_ref,
    xs,
    local_sem,
    send_sems,
    recv_sems,
    stage,
    stage_sems,
    total,
    low,
    w,
    w_sem,
    factors,
    factor_sems,
    hidden,
    hidden_sems,
    s_local,
    s_sends,
    s_recvs,
):
    ring = Gather(x_ref, xs, local_sem, send_sems, recv_sems)
    rows, width = x_ref.shape
    ff = w_ref.shape[0]
    cols = ff // 2
    fetch_w = pltpu.make_async_copy(w_ref, w, w_sem)
    fetch_w.start()
    shares = Shares(gw_ref, s_local, s_sends, s_recvs)
    core = shares.core
    deep = width // 8

    def tile(z, c):
        return low.at[pl.ds(z * cols, cols), pl.ds(pl.multiple_of(c * deep, deep), deep)]

    def put(slot, block):
        return pltpu.make_async_copy(
            stage.at[slot], d_ref.at[pl.ds(block * rows, rows)], stage_sems.at[slot]
        )

    def factor(n, slot, block):
        ref = (a_ref, b_ref)[n]
        return pltpu.make_async_copy(
            ref.at[pl.ds(block * rows, rows)], factors.at[slot, n], factor_sems.at[slot, n]
        )

    def chip_hidden(slot, block):
        return pltpu.make_async_copy(
            h_ref.at[pl.ds(block // 2 * 2 * rows, 2 * rows)], hidden.at[slot], hidden_sems.at[slot]
        )

    def fetch(step):
        block = ring.block(step)
        for n in range(2):
            factor(n, lax.rem(step, 2), block).start()

        @pl.when(lax.rem(step, 2) == 0)
        def _():
            chip_hidden(lax.rem(step // 2, 2), block).start()

    fetch(jnp.int32(0))
    greet((ring.sib, ring.nx, ring.ny))
    ring.start()
    total[...] = jnp.zeros_like(total)
    fetch_w.wait()

    def turn(step, carry):
        ring.before(step)
        block = ring.block(step)
        slot = lax.rem(step, 2)
        pair_slot = lax.rem(step // 2, 2)

        @pl.when(step >= 2)
        def _():
            put(slot, block).wait()

        for n in range(2):
            factor(n, slot, block).wait()

        @pl.when(step < 7)
        def _():
            fetch(step + 1)

        for z in range(2):
            part = slice(z * cols, (z + 1) * cols)
            grad = nt(xs[block], w[part, :])
            for n in range(2):
                stage[slot, :, (2 * z + n) * cols : (2 * z + n + 1) * cols] = (
                    grad * factors[slot, n, :, part].astype(F32)
                ).astype(BF16)
        put(slot, block).start()

        @pl.when(slot == 1)
        def _():
            chip_hidden(pair_slot, block).wait()
            pair = block // 2
            for p in range(4):
                at = slice(p * 2 * deep, (p + 1) * 2 * deep)
                seen = xs[pl.ds(pair * 2, 2), :, at].reshape(2 * rows, 2 * deep)
                total[:, at] += tn(hidden[pair_slot], seen)

                @pl.when(step == 7)
                def _():
                    low[:, at] = total[:, at].astype(BF16)
                    for z in range(2):
                        shares.other(tile(z, 2 * p + 1 - core), z, p).start()
                        shares.own(tile(z, 2 * p + core), z, p).start()

        return carry

    lax.fori_loop(0, 8, turn, 0)
    ring.finish()
    for slot in range(2):
        put(slot, 0).wait()
    shares.arrive()
    for z in range(2):
        for p in range(4):
            shares.other(tile(z, 2 * p + 1 - core), z, p).wait_send()
            shares.own(tile(z, 2 * p + core), z, p).wait()


def gather_down_back(diff, w_down, a, b, hidden):
    rows, width = diff.shape
    ff = w_down.shape[0]
    dma = pltpu.SemaphoreType.DMA
    return pl.pallas_call(
        down_back_kernel,
        out_shape=(
            jax.ShapeDtypeStruct((8 * rows, 2 * ff), BF16),
            jax.ShapeDtypeStruct((4, 4, ff // 2, width // 8), BF16),
        ),
        in_specs=[spec_any()] * 5,
        out_specs=(spec_any(), spec_any()),
        scratch_shapes=gather_scratch(rows, width)
        + [
            pltpu.VMEM((2, rows, 2 * ff), BF16),
            dma((2,)),
            pltpu.VMEM((ff, width), F32),
            pltpu.VMEM((ff, width), BF16),
            pltpu.VMEM((ff, width), BF16),
            dma,
            pltpu.VMEM((2, 2, rows, ff), BF16),
            dma((2, 2)),
            pltpu.VMEM((2, 2 * rows, ff), BF16),
            dma((2,)),
        ]
        + SHARES_SCRATCH,
        compiler_params=comm_params(3),
        cost_estimate=busy(66),
        name="gather_down_back",
    )(diff, w_down, a, b, hidden)


def mix_kernel(
    mixed_ref,
    tokens_ref,
    gain_ref,
    w0_ref,
    w1_ref,
    w2_ref,
    w3_ref,
    middle_ref,
    post_ref,
    rows_ref,
    w_ref,
    held,
    w,
    m_sems,
    m_sends,
    m_recvs,
    w_local,
    w_sends,
    w_recvs,
    keep_sems,
):
    me, sib, nx, ny, dg = plane_neighbours()
    shift = sib - me
    away = others(me)
    rows, width = held.shape
    deep = width // 8
    greet(away)

    def block(c):
        return pl.ds(pl.multiple_of(c * rows, rows), rows)

    def lanes(c):
        return pl.ds(pl.multiple_of(c * deep, deep), deep)

    def give(n, c):
        return send(mixed_ref.at[block(c)], held.at[:, lanes(me)], m_sends.at[n], m_recvs.at[me], on_ctx(c))

    def take(c):
        return send(mixed_ref.at[block(c)], held.at[:, lanes(c)], m_sends.at[0], m_recvs.at[c], on_ctx(c))

    for n, c in enumerate(away):
        give(n, c).start()
    own = pltpu.make_async_copy(mixed_ref.at[block(me)], held.at[:, lanes(me)], m_sems)
    own.start()
    parts = ((w0_ref, me), (w1_ref, nx), (w2_ref, ny), (w3_ref, dg))

    def swap(n):
        part, c = parts[n]
        return send(part, w.at[:, lanes(c)], w_sends.at[n], w_recvs.at[n], on_ctx(sib))

    def place(n):
        part, c = parts[n]
        return pltpu.make_async_copy(part, w.at[:, lanes(c)], w_local.at[n])

    for n in range(4):
        swap(n).start()
        place(n).start()
    for n in range(4):
        place(n).wait()
        there = w.at[:, lanes(parts[n][1] + shift)]
        send(there, there, w_sends.at[n], w_recvs.at[n], on_ctx(sib)).wait_recv()
    own.wait()
    for c in away:
        take(c).wait_recv()
    keep_rows = pltpu.make_async_copy(held, rows_ref, keep_sems.at[0])
    keep_rows.start()
    keep_w = pltpu.make_async_copy(w, w_ref, keep_sems.at[1])
    keep_w.start()
    total = jnp.zeros((rows, 1), F32)
    for n in range(0, width, 512):
        at = slice(n, n + 512)
        middle = tokens_ref[:, at].astype(F32) + nn(held[...], w[:, at])
        middle_ref[:, at] = middle
        total += jnp.sum(middle * middle, axis=-1, keepdims=True)
    scale = lax.rsqrt(total / width + EPS)
    for n in range(0, width, 512):
        at = slice(n, n + 512)
        post_ref[:, at] = (middle_ref[:, at] * scale * gain_ref[:, at]).astype(BF16)
    for n, c in enumerate(away):
        give(n, c).wait_send()
    for n in range(4):
        swap(n).wait_send()
    keep_rows.wait()
    keep_w.wait()


def mix(mixed, tokens, post_gain, parts):
    rows, width = tokens.shape
    dma = pltpu.SemaphoreType.DMA
    return pl.pallas_call(
        mix_kernel,
        out_shape=(
            jax.ShapeDtypeStruct((rows, width), F32),
            jax.ShapeDtypeStruct((rows, width), BF16),
            jax.ShapeDtypeStruct((rows, width), BF16),
            jax.ShapeDtypeStruct((width, width), BF16),
        ),
        in_specs=[spec_any(), spec_vmem(), spec_vmem()] + [spec_any()] * 4,
        out_specs=(spec_vmem(), spec_vmem(), spec_any(), spec_any()),
        scratch_shapes=[
            pltpu.VMEM((rows, width), BF16),
            pltpu.VMEM((width, width), BF16),
            dma,
            dma((7,)),
            dma((8,)),
            dma((4,)),
            dma((4,)),
            dma((4,)),
            dma((2,)),
        ],
        compiler_params=comm_params(5),
        cost_estimate=busy(28),
        name="mix",
    )(mixed, tokens, post_gain.reshape(1, -1), *parts)


def mix_back_kernel(
    post_ref,
    middle_ref,
    diff_ref,
    gain_ref,
    w_any,
    rows_any,
    swap_ref,
    dm_ref,
    d_middle_ref,
    gp_ref,
    g0_ref,
    g1_ref,
    g2_ref,
    g3_ref,
    swapped_ref,
    w_ref,
    rows_ref,
    fetch_sems,
    d_ref,
    stage,
    to_sib,
    from_sib,
    own,
    out_sem,
    out_sends,
    out_recvs,
    s_sends,
    s_recvs,
    g_sems,
    *c_sems,
):
    me, sib, nx, ny, dg = plane_neighbours()
    shift = sib - me
    away = others(me)
    rows, width = d_ref.shape
    deep = width // 8
    fetch_w = pltpu.make_async_copy(w_any, w_ref, fetch_sems.at[0])
    fetch_w.start()
    fetch_rows = pltpu.make_async_copy(rows_any, rows_ref, fetch_sems.at[1])
    fetch_rows.start()
    greet(away)
    weight_swap = ChipSwap(swap_ref, swapped_ref, *c_sems)
    weight_swap.start()
    squares = jnp.zeros((rows, HEAD_SIZE), F32)
    dots = jnp.zeros((rows, HEAD_SIZE), F32)
    cuts = [slice(n, n + HEAD_SIZE) for n in range(0, width, HEAD_SIZE)]
    for at in cuts:
        middle = middle_ref[:, at]
        squares += middle * middle
        dots += post_ref[:, at] * gain_ref[:, at] * middle
    scale = lax.rsqrt(jnp.sum(squares, axis=-1, keepdims=True) / width + EPS)
    pull = scale * scale * scale * (jnp.sum(dots, axis=-1, keepdims=True) / width)
    for at in cuts:
        middle, post = middle_ref[:, at], post_ref[:, at]
        gp_ref[:, at] = jnp.sum(post * (middle * scale), axis=0, keepdims=True)
        d_middle = diff_ref[:, at] + scale * (post * gain_ref[:, at]) - middle * pull
        d_middle_ref[:, at] = d_middle
        d_ref[:, at] = d_middle.astype(BF16)
    outs = (g0_ref, g1_ref, g2_ref, g3_ref)
    chips = (me, nx, ny, dg)
    fetch_w.wait()
    fetch_rows.wait()

    def block(c):
        return pl.ds(pl.multiple_of(c * rows, rows), rows)

    def give(n, c):
        return send(stage.at[c], dm_ref.at[block(me)], out_sends.at[n], out_recvs.at[me], on_ctx(c))

    def take(c):
        return send(stage.at[c], dm_ref.at[block(c)], out_sends.at[0], out_recvs.at[c], on_ctx(c))

    def heads(n, carry):
        c = pick(n, away + (me,))
        at = pl.ds(pl.multiple_of(c * deep, deep), deep)
        stage[c] = nt(d_ref[...], w_ref[at, :]).astype(BF16)

        @pl.when(n < 7)
        def _():
            give(n, c).start()

        return carry

    lax.fori_loop(0, 8, heads, 0)
    keep = pltpu.make_async_copy(stage.at[me], dm_ref.at[block(me)], out_sem)
    keep.start()

    def swap(n):
        return send(to_sib.at[n], from_sib.at[n], s_sends.at[n], s_recvs.at[n], on_ctx(sib))

    def grad(n, out, c):
        at = pl.ds(pl.multiple_of(c * deep, deep), deep)
        out[n] = tn(rows_ref[...], d_ref[:, at]).astype(BF16)

    def theirs(n, carry):
        grad(n, to_sib, pick(n, chips) + shift)
        swap(n).start()
        return carry

    def ours(n, carry):
        grad(n, own, pick(n, chips))
        return carry

    lax.fori_loop(0, 4, theirs, 0)
    lax.fori_loop(0, 4, ours, 0)
    for n in range(4):
        swap(n).wait_recv()
        own[n] = (own[n].astype(F32) + from_sib[n].astype(F32)).astype(BF16)
        pltpu.make_async_copy(own.at[n], outs[n], g_sems.at[n]).start()
    for c in away:
        take(c).wait_recv()
    keep.wait()
    for n, c in enumerate(away):
        give(n, c).wait_send()
    for n in range(4):
        swap(n).wait_send()
        pltpu.make_async_copy(own.at[n], outs[n], g_sems.at[n]).wait()
    weight_swap.finish()


def mix_back(d_post, middle, diff, post_gain, w, mixed_rows, swap):
    rows, width = middle.shape
    deep = width // 8
    dma = pltpu.SemaphoreType.DMA
    four = pltpu.VMEM((4, width, deep), BF16)
    return pl.pallas_call(
        mix_back_kernel,
        out_shape=(
            jax.ShapeDtypeStruct((8 * rows, deep), BF16),
            jax.ShapeDtypeStruct((rows, width), F32),
            jax.ShapeDtypeStruct((1, width), F32),
        )
        + (jax.ShapeDtypeStruct((width, deep), BF16),) * 4
        + (jax.ShapeDtypeStruct(swap.shape, BF16),),
        in_specs=[spec_vmem()] * 4 + [spec_any()] * 3,
        out_specs=(spec_any(), spec_vmem(), spec_vmem()) + (spec_any(),) * 5,
        scratch_shapes=[
            pltpu.VMEM((width, width), BF16),
            pltpu.VMEM((rows, width), BF16),
            dma((2,)),
            pltpu.VMEM((rows, width), BF16),
            pltpu.VMEM((8, rows, deep), BF16),
            four,
            four,
            four,
            dma,
            dma((7,)),
            dma((8,)),
            dma((4,)),
            dma((4,)),
            dma((4,)),
        ]
        + SWAP_SCRATCH,
        compiler_params=comm_params(4),
        cost_estimate=busy(26),
        name="mix_back",
    )(d_post, middle, diff, post_gain.reshape(1, -1), w, mixed_rows, swap)


def columns(all_ref, slices, sems, c, slot):
    deep = slices.shape[-1]
    return pltpu.make_async_copy(
        all_ref.at[:, :, pl.ds(pl.multiple_of(c * deep, deep), deep)], slices.at[slot], sems.at[slot]
    )


EARLY = 1


def post_back_kernel(d_any, w_any, all_ref, o_ref, gw_ref, *scratch):
    rs = Scatter(*scratch[:N_SCATTER])
    slices, slice_sems, tile, d_ref, d_sems, w_ref, w_sems, s_local, s_sends, s_recvs = scratch[N_SCATTER:]
    shares = Shares(gw_ref, s_local, s_sends, s_recvs)
    rows = o_ref.shape[0]
    _, width, wide = w_ref.shape
    plane_rows = d_ref.shape[0]
    deep = width // 8
    fetch_w = [pltpu.make_async_copy(w_any.at[z], w_ref.at[z], w_sems.at[z]) for z in range(2)]

    def fetch(block):
        here = pl.ds(pl.multiple_of(block * rows, rows), rows)
        return pltpu.make_async_copy(d_any.at[here], d_ref.at[here], d_sems.at[block])

    order = rs.blocks()
    fetch(order[0]).start()
    for copy in fetch_w:
        copy.start()
    for block in order[1:]:
        fetch(block).start()
    columns(all_ref, slices, slice_sems, 0, 0).start()
    greet((rs.sib, rs.nx, rs.ny))
    for copy in fetch_w:
        copy.wait()

    def product(block, at, out, n):
        here = pl.ds(pl.multiple_of(block * rows + at.start, rows // 2), rows // 2)
        for c in range(0, width, 512):
            total = nt(d_ref[here, :wide], w_ref[0, c : c + 512, :])
            total += nt(d_ref[here, wide:], w_ref[1, c : c + 512, :])
            out[n, at, c : c + 512] = total.astype(BF16)

    def put(slot, p, act):
        @pl.when(slot == shares.core)
        def _():
            for z in range(2):
                copy = shares.own(tile.at[slot, z], z, p)
                copy.start() if act == "start" else copy.wait()

        @pl.when(slot != shares.core)
        def _():
            for z in range(2):
                copy = shares.other(tile.at[slot, z], z, p)
                copy.start() if act == "start" else copy.wait_send()

    def grad(c):
        slot = lax.rem(c, 2)
        columns(all_ref, slices, slice_sems, c, slot).wait()

        @pl.when(c < 7)
        def _():
            columns(all_ref, slices, slice_sems, c + 1, 1 - slot).start()

        @pl.when(c >= 2)
        def _():
            put(slot, c // 2 - 1, "wait")

        seen = slices[slot].reshape(plane_rows, deep)
        for z in range(2):
            tile[slot, z] = tn(seen, d_ref[:, z * wide : (z + 1) * wide]).astype(BF16)
        put(slot, c // 2, "start")

    def turn(t, carry):
        is_grad = ((t >= 10) & (t < 10 + EARLY)) | (t >= 16 + EARLY)

        for n in range(2):

            @pl.when(t == n)
            def _():
                fetch(order[n]).wait()

        @pl.when(t == 4)
        def _():
            for block in order[2:]:
                fetch(block).wait()

        @pl.when(is_grad)
        def _():
            grad(jnp.where(t < 10 + EARLY, t - 10, t - 16))

        @pl.when(jnp.logical_not(is_grad))
        def _():
            rs.step(jnp.where(t < 10, t, t - EARLY), product)

        return carry

    lax.fori_loop(0, 24, turn, 0)
    rs.finish(o_ref)
    for slot in range(2):
        put(slot, 3, "wait")
    shares.arrive()


def scatter_post(d_gu, w_gu, post_all):
    _, rows, width = post_all.shape
    wide = w_gu.shape[-1]
    deep = width // 8
    return pl.pallas_call(
        post_back_kernel,
        out_shape=(
            jax.ShapeDtypeStruct((rows, width), F32),
            jax.ShapeDtypeStruct((4, 4, deep, wide), BF16),
        ),
        in_specs=[spec_any()] * 3,
        out_specs=(spec_vmem(), spec_any()),
        scratch_shapes=scatter_scratch(rows, width)
        + [
            pltpu.VMEM((2, 8, rows, deep), BF16),
            pltpu.SemaphoreType.DMA((2,)),
            pltpu.VMEM((2, 2, deep, wide), BF16),
            pltpu.VMEM(d_gu.shape, BF16),
            pltpu.SemaphoreType.DMA((8,)),
            pltpu.VMEM(w_gu.shape, BF16),
            pltpu.SemaphoreType.DMA((2,)),
        ]
        + SHARES_SCRATCH,
        compiler_params=comm_params(7),
        cost_estimate=busy(66),
        name="scatter_post",
    )(d_gu, w_gu, post_all)


def normed_back_kernel(
    dq_ref,
    dkv_ref,
    to_lo_ref,
    to_hi_ref,
    lin_ref,
    w_ref,
    all_ref,
    swap_ref,
    wo_ref,
    qg_ref,
    kg_ref,
    ca_ref,
    sa_ref,
    cb_ref,
    sb_ref,
    o_ref,
    gw_ref,
    gains_ref,
    swapped_ref,
    wo_sum_ref,
    *scratch,
):
    rs = Scatter(*scratch[:N_SCATTER])
    (
        from_lo,
        from_hi,
        d_lin,
        slices,
        slice_sems,
        tiles,
        tiles_in,
        up_in,
        down_in,
        wo_up,
        wo_down,
        z_sends,
        z_recvs,
        t_sends,
        t_recvs,
        p_sends,
        p_recvs,
        o_sends,
        o_recvs,
        *c_sems,
    ) = scratch[N_SCATTER:]
    me = rs.me
    plane, planes = lax.axis_index("tp"), lax.axis_size("tp")
    rows, width = o_ref.shape
    deep = width // 8
    plane_rows = dq_ref.shape[0]
    units = rows // UNIT
    wide = 2 * HEAD_SIZE
    away = others(me)
    order = rs.blocks()

    from_lo[...] = jnp.zeros_like(from_lo)
    from_hi[...] = jnp.zeros_like(from_hi)
    line = Line(to_hi_ref, to_lo_ref, from_lo, from_hi, z_sends, z_recvs, rows, True)
    greet_column(away)
    for block in order:
        line.start(block)
    columns(all_ref, slices, slice_sems, order[0], 0).start()
    gains_ref[...] = jnp.zeros_like(gains_ref)

    def head_back(grad, lin, gain_ref, rotation):
        back = rotation.back(grad)
        scale = lax.rsqrt(jnp.mean(lin * lin, axis=-1, keepdims=True) + EPS)
        normal = lin * scale
        gained = back * gain_ref[...]
        d = scale * (gained - normal * jnp.mean(gained * normal, axis=-1, keepdims=True))
        return d.astype(BF16), jnp.sum(back * normal, axis=0, keepdims=True)

    def rotation_of(unit):
        return Turn(ca_ref, sa_ref, cb_ref, sb_ref, unit)

    def prepare_queries(unit, carry):
        rotation = rotation_of(unit)
        here = pl.ds(pl.multiple_of(unit * UNIT, UNIT), UNIT)
        for h in range(2):
            lanes = slice(h * HEAD_SIZE, (h + 1) * HEAD_SIZE)
            d, gain = head_back(dq_ref[here, lanes].astype(F32) * HEAD_SIZE**-0.5, lin_ref[here, lanes], qg_ref, rotation)
            d_lin[here, lanes] = d
            gains_ref[0:1, :] += gain
        return carry

    def prepare_keys(block):
        line.arrived(block)
        for i in range(units):
            unit = block * units + i
            here = pl.ds(pl.multiple_of(unit * UNIT, UNIT), UNIT)
            d_kv = dkv_ref[here, :].astype(F32) + from_lo[here, :].astype(F32) + from_hi[here, :].astype(F32)
            lanes = slice(2 * HEAD_SIZE, 3 * HEAD_SIZE)
            d, gain = head_back(d_kv[:, :HEAD_SIZE], lin_ref[here, lanes], kg_ref, rotation_of(unit))
            d_lin[here, lanes] = d
            gains_ref[1:2, :] += gain
            d_lin[here, 3 * HEAD_SIZE :] = d_kv[:, HEAD_SIZE:].astype(BF16)

    def tile_to(part, n, device):
        return send(
            tiles.at[part, device],
            tiles_in.at[part, me],
            t_sends.at[part, n],
            t_recvs.at[part, me],
            on_ctx(device),
        )

    def tile_from(part, device):
        return send(
            tiles.at[part, device],
            tiles_in.at[part, device],
            t_sends.at[part, 0],
            t_recvs.at[part, device],
            on_ctx(device),
        )

    def grads(part):
        def grad(n, carry):
            c = pick(n, order)
            slot = lax.rem(n, 2)
            columns(all_ref, slices, slice_sems, c, slot).wait()

            @pl.when((n < 7) | (part == 0))
            def _():
                columns(all_ref, slices, slice_sems, pick(lax.rem(n + 1, 8), order), 1 - slot).start()

            lanes = slice(part * wide, (part + 1) * wide)
            value = tn(slices[slot].reshape(plane_rows, deep), d_lin[:, lanes]).astype(BF16)

            @pl.when(n < 7)
            def _():
                tiles[part, c] = value
                tile_to(part, n, c).start()

            @pl.when(n == 7)
            def _():
                tiles_in[part, me] = value

            return carry

        lax.fori_loop(0, 8, grad, 0)

    sums = [
        LineSum(
            lambda p, part=part: tiles_in.at[part, pl.ds(2 * p, 2)],
            up_in.at[part],
            down_in.at[part],
            p_sends.at[part],
            p_recvs.at[part],
        )
        for part in range(2)
    ]
    out_sum = LineSum(lambda p: wo_ref.at[p], wo_up, wo_down, o_sends, o_recvs)

    def tiles_there(part):
        for device in away:
            tile_from(part, device).wait_recv()

    def product(block, at, out, n):
        left = d_lin[pl.ds(pl.multiple_of(block * rows + at.start, rows // 2), rows // 2), :]
        for c in range(0, width, 512):
            out[n, at, c : c + 512] = nt(left, w_ref[c : c + 512, :]).astype(BF16)

    def turn(step, carry):
        @pl.when(lax.rem(step, 4) < 2)
        def _():
            prepare_keys(rs.block(step))

        rs.step(step, product, late=True)

        @pl.when(step == 4)
        def _():
            out_sum.stage(1)

        @pl.when(step == 7)
        def _():
            tiles_there(0)
            sums[0].stage(0)

        @pl.when(step == 9)
        def _():
            out_sum.stage(2)

        @pl.when(step == 12)
        def _():
            sums[0].stage(1)

        return carry

    swap = ChipSwap(swap_ref, swapped_ref, *c_sems)
    swap.start()
    out_sum.stage(0)
    lax.fori_loop(0, plane_rows // UNIT, prepare_queries, 0)
    grads(0)
    lax.fori_loop(0, 16, turn, 0)
    grads(1)
    rs.second_wave()
    sums[0].stage(2)
    tiles_there(1)
    for k in range(3):
        sums[1].stage(k)
    rs.finish(o_ref)
    out_sum.collect(wo_sum_ref)
    for part in range(2):
        sums[part].collect(gw_ref.at[part])
    swap.finish()
    for line_sum in (out_sum, *sums):
        line_sum.finish()
    for part in range(2):
        for n, device in enumerate(order[:7]):
            tile_to(part, n, device).wait_send()

    def settle(block, carry):
        line.sent(block)
        return carry

    lax.fori_loop(0, 8, settle, 0)


def scatter_normed(d_queries, d_kv, to_lo, to_hi, lin, w_qkv, normed_all, swap, wo, q_gain, k_gain, tables):
    _, rows, width = normed_all.shape
    deep = width // 8
    cols = w_qkv.shape[1]
    half = pltpu.VMEM(to_lo.shape, BF16)
    tiles = pltpu.VMEM((2, 8, deep, cols // 2), BF16)
    dma = pltpu.SemaphoreType.DMA
    return pl.pallas_call(
        normed_back_kernel,
        out_shape=(
            jax.ShapeDtypeStruct((rows, width), F32),
            jax.ShapeDtypeStruct((2, 2, deep, cols // 2), F32),
            jax.ShapeDtypeStruct((8, HEAD_SIZE), F32),
            jax.ShapeDtypeStruct(swap.shape, BF16),
            jax.ShapeDtypeStruct(wo.shape[1:], F32),
        ),
        in_specs=[spec_vmem()] * 2
        + [spec_any()] * 2
        + [spec_vmem()] * 2
        + [spec_any()] * 2
        + [spec_vmem()] * 7,
        out_specs=(spec_vmem(),) * 3 + (spec_any(), spec_vmem()),
        scratch_shapes=scatter_scratch(rows, width)
        + [
            half,
            half,
            pltpu.VMEM((8 * rows, cols), BF16),
            pltpu.VMEM((2, 8, rows, deep), BF16),
            dma((2,)),
            tiles,
            tiles,
            pltpu.VMEM((2, 4, 2, deep, cols // 2), BF16),
            pltpu.VMEM((2, 4, 2, deep, cols // 2), BF16),
            pltpu.VMEM(wo.shape, BF16),
            pltpu.VMEM(wo.shape, BF16),
            dma((2, 8 * rows // UNIT)),
            dma((2, 8 * rows // UNIT)),
            dma((2, 7)),
            dma((2, 8)),
            dma((2, 2, 4)),
            dma((2, 2, 4)),
            dma((2, 4)),
            dma((2, 4)),
        ]
        + SWAP_SCRATCH,
        compiler_params=comm_params(8),
        cost_estimate=busy(110),
        name="scatter_normed",
    )(
        d_queries,
        d_kv,
        to_lo,
        to_hi,
        lin,
        w_qkv,
        normed_all,
        swap,
        wo,
        q_gain.reshape(1, -1),
        k_gain.reshape(1, -1),
        *tables,
    )


def total_kernel(v_ref, o_ref, held, held_planes, sends, recvs):
    me = lax.axis_index("ctx")
    plane, planes = lax.axis_index("tp"), lax.axis_size("tp")
    away = others(me)
    far = [lax.rem(plane + step, planes) for step in range(1, planes)]
    barrier = pltpu.get_barrier_semaphore()
    for where in [on_ctx(c) for c in away] + [on_plane(p) for p in far]:
        pl.semaphore_signal(barrier, inc=1, device_id=where, device_id_type=MESH)
    pl.semaphore_wait(barrier, len(away) + len(far))
    held[me] = v_ref[...]
    for n, c in enumerate(away):
        send(held.at[me], held.at[me], sends.at[n], recvs.at[me], on_ctx(c)).start()
    for c in away:
        send(held.at[c], held.at[c], sends.at[0], recvs.at[c], on_ctx(c)).wait_recv()
    value = held[0]
    for c in range(1, 8):
        value += held[c]
    held_planes[plane] = value
    for n, p in enumerate(far):
        send(
            held_planes.at[plane], held_planes.at[plane], sends.at[7 + n], recvs.at[8 + plane], on_plane(p)
        ).start()
    for p in far:
        send(held_planes.at[p], held_planes.at[p], sends.at[0], recvs.at[8 + p], on_plane(p)).wait_recv()
    value = held_planes[0]
    for p in range(1, 4):
        value += held_planes[p]
    o_ref[...] = value
    for n, c in enumerate(away):
        send(held.at[me], held.at[me], sends.at[n], recvs.at[me], on_ctx(c)).wait_send()
    for n, p in enumerate(far):
        send(
            held_planes.at[plane], held_planes.at[plane], sends.at[7 + n], recvs.at[8 + plane], on_plane(p)
        ).wait_send()


def total_of(values):
    return pl.pallas_call(
        total_kernel,
        out_shape=jax.ShapeDtypeStruct(values.shape, F32),
        in_specs=[spec_vmem()],
        out_specs=spec_vmem(),
        scratch_shapes=[
            pltpu.VMEM((8,) + values.shape, F32),
            pltpu.VMEM((4,) + values.shape, F32),
            pltpu.SemaphoreType.DMA((10,)),
            pltpu.SemaphoreType.DMA((12,)),
        ],
        compiler_params=pltpu.CompilerParams(collective_id=9, has_side_effects=True),
        cost_estimate=busy(12),
        name="total_of",
    )(values)


def finish_kernel(
    d_ref, tokens_ref, middle_ref, gain_ref, gu_ref, down_ref, qkv_ref, out_ref,
    dt_ref, gin_ref, gate_ref, up_ref, dw_ref, wq_ref, wk_ref, wv_ref, wo_ref,
):
    width = d_ref.shape[1]

    @pl.when(pl.program_id(0) == 0)
    def _():
        gin_ref[...] = jnp.zeros_like(gin_ref)

    stream = tokens_ref[...].astype(F32)
    scale = lax.rsqrt(jnp.mean(stream * stream, axis=-1, keepdims=True) + EPS)
    grad = d_ref[...]
    gin_ref[...] += jnp.sum(grad * (stream * scale), axis=0, keepdims=True)
    gained = grad * gain_ref[...]
    pull = scale * scale * scale * jnp.mean(gained * stream, axis=-1, keepdims=True)
    dt_ref[...] = (middle_ref[...] + (scale * gained - stream * pull)).astype(BF16)
    cols = gu_ref.shape[2] // 2
    for p in range(4):
        here = slice(p * cols, (p + 1) * cols)
        gate_ref[:, here] = gu_ref[p, :, :cols].astype(F32)
        up_ref[:, here] = gu_ref[p, :, cols:].astype(F32)
    dw_ref[...] = down_ref[...].astype(F32)
    wide = 2 * HEAD_SIZE
    for k in range(2):
        wq_ref[:, k * wide : (k + 1) * wide] = qkv_ref[0, k]
        wk_ref[:, k * HEAD_SIZE : (k + 1) * HEAD_SIZE] = qkv_ref[1, k, :, :HEAD_SIZE]
        wv_ref[:, k * HEAD_SIZE : (k + 1) * HEAD_SIZE] = qkv_ref[1, k, :, HEAD_SIZE:]
    wo_ref[...] = out_ref[...]


def finish(d_normed, tokens, d_middle, in_gain, gu, down, qkv, out):
    steps = 8

    def piece(shape, axis):
        block = list(shape)
        block[axis] //= steps
        return pl.BlockSpec(
            tuple(block), lambda i, axis=axis, n=len(shape): tuple(i if d == axis else 0 for d in range(n))
        )

    rows, width = tokens.shape
    deep, ff = gu.shape[1], 2 * gu.shape[2]
    one = (1, width)
    whole = pl.BlockSpec(one, lambda i: (0, 0))
    flat, square = (rows, width), (deep, 2 * HEAD_SIZE)
    ins = [(flat, 0), (flat, 0), (flat, 0), None, (gu.shape, 1), (down.shape, 1), (qkv.shape, 2), (out.shape, 0)]
    outs = [
        (flat, 0, BF16),
        None,
        ((deep, ff), 0, F32),
        ((deep, ff), 0, F32),
        (down.shape, 1, F32),
        ((deep, 4 * HEAD_SIZE), 0, F32),
        (square, 0, F32),
        (square, 0, F32),
        (out.shape, 0, F32),
    ]
    return pl.pallas_call(
        finish_kernel,
        grid=(steps,),
        out_shape=tuple(jax.ShapeDtypeStruct(o[0], o[2]) if o else jax.ShapeDtypeStruct(one, F32) for o in outs),
        in_specs=[piece(*i) if i else whole for i in ins],
        out_specs=tuple(piece(o[0], o[1]) if o else whole for o in outs),
        compiler_params=pltpu.CompilerParams(vmem_limit_bytes=VMEM_LIMIT),
        cost_estimate=busy(8),
        name="finish",
    )(d_normed, tokens, d_middle, in_gain.reshape(1, -1), gu, down, qkv, out)


class Places:
    def __init__(self, order_ref, lens_ref):
        self.order, self.lens = order_ref, lens_ref
        self.plane = lax.axis_index("tp")
        self.seq0 = (3 * self.plane) // 4
        self.seq1 = (3 * self.plane + 2) // 4

    def position(self, seq, quarter, c):
        return 2 * self.order[seq, 2 * c + quarter // 2] + lax.rem(quarter, 2)

    def unit(self, u):
        c = u // 3
        g = 3 * self.plane + lax.rem(u, 3)
        seq = g // 4
        return seq, seq - self.seq0, self.position(seq, lax.rem(g, 4), c)

    def each(self, visit):
        for slot, seq in ((0, self.seq0), (1, self.seq1)):

            @pl.when((slot == 0) | (self.seq1 != self.seq0))
            def _():
                def one(i, carry):
                    quarter, c = i // 8, lax.rem(i, 8)
                    g = 4 * seq + quarter
                    away = g // 3 - self.plane
                    row = pl.multiple_of((c * 3 + lax.rem(g, 3)) * UNIT, UNIT)
                    visit(slot, self.position(seq, quarter, c), away, row)
                    return carry

                lax.fori_loop(0, 32, one, 0)

    def fetch(self, sources, keys, values, key_sem, value_sem):
        def visit(slot, position, away, row):
            at = pl.ds(pl.multiple_of(position * UNIT, UNIT), UNIT)
            for n, source in enumerate(sources):

                @pl.when(away == n - 1)
                def _():
                    pltpu.make_async_copy(
                        source.at[pl.ds(row, UNIT), pl.ds(0, HEAD_SIZE)], keys.at[slot, at], key_sem.at[slot]
                    ).start()
                    pltpu.make_async_copy(
                        source.at[pl.ds(row, UNIT), pl.ds(HEAD_SIZE, HEAD_SIZE)],
                        values.at[slot, at, pl.ds(0, HEAD_SIZE)],
                        value_sem.at[slot],
                    ).start()

        self.each(visit)
        for slot in range(2):

            @pl.when((slot == 0) | (self.seq1 != self.seq0))
            def _():
                pltpu.make_async_copy(keys.at[slot], keys.at[slot], key_sem.at[slot]).wait()
                pltpu.make_async_copy(keys.at[slot], keys.at[slot], value_sem.at[slot]).wait()


def sweep(clear, part):
    def four(i, carry):
        part(i * 4 * KEYS, 4 * KEYS, False)
        return carry

    lax.fori_loop(0, clear // 4, four, 0)

    @pl.when(lax.rem(clear, 4) >= 2)
    def _():
        part(clear // 4 * 4 * KEYS, 2 * KEYS, False)


    odd = lax.rem(clear, 2)

    @pl.when(odd == 1)
    def _():
        part((clear - 1) * KEYS, 2 * KEYS, True)

    @pl.when(odd == 0)
    def _():
        part(clear * KEYS, KEYS, True)


def attend_kernel(
    order_ref, lens_ref, q_ref, lo_ref, own_ref, hi_ref, o_ref, lse_ref, keys, values, acc, key_sem, value_sem
):
    places = Places(order_ref, lens_ref)
    values[:, :, HEAD_SIZE:] = jnp.ones((2, values.shape[1], HEAD_SIZE), BF16)
    places.fetch((lo_ref, own_ref, hi_ref), keys, values, key_sem, value_sem)

    def one_unit(u, carry):
        seq, slot, position = places.unit(u)
        length = lens_ref[seq]
        rows = pl.ds(pl.multiple_of(u * UNIT, UNIT), UNIT)
        both = q_ref[rows, :]
        queries = jnp.concatenate([both[:, :HEAD_SIZE], both[:, HEAD_SIZE:]], axis=0)
        clear = jnp.minimum(position * UNIT, length) // KEYS
        acc[...] = jnp.zeros_like(acc)
        row = lax.rem(lax.broadcasted_iota(jnp.int32, (2 * UNIT, 1), 0), UNIT)

        def part(start, size, masked):
            at = pl.ds(pl.multiple_of(start, KEYS), size)
            weights = jnp.exp2(nt(queries, keys[slot, at, :]))
            if masked:
                last = jnp.minimum(row + (position * UNIT - start), length - 1 - start)
                weights = jnp.where(lax.broadcasted_iota(jnp.int32, weights.shape, 1) <= last, weights, 0.0)
            acc[:, :HEAD_SIZE] += nn(weights.astype(BF16), values[slot, at, :HEAD_SIZE])
            part_sum = weights[:, :HEAD_SIZE]
            for n in range(HEAD_SIZE, size, HEAD_SIZE):
                part_sum += weights[:, n : n + HEAD_SIZE]
            acc[:, HEAD_SIZE:] += part_sum

        sweep(clear, part)
        total = jnp.sum(acc[:, HEAD_SIZE:], axis=-1, keepdims=True)
        mixed = (acc[:, :HEAD_SIZE] / total).astype(BF16)
        o_ref[rows, :] = jnp.concatenate([mixed[:UNIT], mixed[UNIT:]], axis=1)
        lse_ref[u] = jnp.transpose(jnp.broadcast_to(jnp.log2(total), (2 * UNIT, HEAD_SIZE)))[:8, :]
        return carry

    lax.fori_loop(0, q_ref.shape[0] // UNIT, one_unit, 0)


def attend(order, lens, q, lo, own, hi, seq_len):
    rows = q.shape[0]
    return pl.pallas_call(
        attend_kernel,
        out_shape=(
            jax.ShapeDtypeStruct(q.shape, BF16),
            jax.ShapeDtypeStruct((rows // UNIT, 8, 2 * UNIT), F32),
        ),
        in_specs=[spec_smem(), spec_smem(), spec_vmem(), spec_any(), spec_any(), spec_any()],
        out_specs=(spec_vmem(), spec_vmem()),
        scratch_shapes=[
            pltpu.VMEM((2, seq_len, HEAD_SIZE), BF16),
            pltpu.VMEM((2, seq_len, 2 * HEAD_SIZE), BF16),
            pltpu.VMEM((2 * UNIT, 2 * HEAD_SIZE), F32),
            pltpu.SemaphoreType.DMA((2,)),
            pltpu.SemaphoreType.DMA((2,)),
        ],
        compiler_params=pltpu.CompilerParams(vmem_limit_bytes=VMEM_LIMIT),
        cost_estimate=busy(50),
        name="attend",
    )(order, lens, q, lo, own, hi)


def attend_back_kernel(
    order_ref,
    lens_ref,
    q_ref,
    do_ref,
    o_ref,
    lse_ref,
    lo_ref,
    own_ref,
    hi_ref,
    dq_ref,
    dlo_ref,
    down_ref,
    dhi_ref,
    keys,
    values,
    dkeys,
    dvalues,
    dq_acc,
    key_sem,
    value_sem,
):
    places = Places(order_ref, lens_ref)
    dkeys[...] = jnp.zeros_like(dkeys)
    dvalues[...] = jnp.zeros_like(dvalues)
    places.fetch((lo_ref, own_ref, hi_ref), keys, values, key_sem, value_sem)

    def stacked(ref, rows):
        both = ref[rows, :]
        return jnp.concatenate([both[:, :HEAD_SIZE], both[:, HEAD_SIZE:]], axis=0)

    def one_unit(u, carry):
        seq, slot, position = places.unit(u)
        length = lens_ref[seq]
        rows = pl.ds(pl.multiple_of(u * UNIT, UNIT), UNIT)
        queries = stacked(q_ref, rows)
        grads = stacked(do_ref, rows)
        product = grads.astype(F32) * stacked(o_ref, rows).astype(F32)
        delta = jnp.sum(jnp.transpose(product), axis=0, keepdims=True)
        lse = lse_ref[u][:1, :]
        clear = jnp.minimum(position * UNIT, length) // KEYS
        dq_acc[...] = jnp.zeros_like(dq_acc)
        row = lax.rem(lax.broadcasted_iota(jnp.int32, (1, 2 * UNIT), 1), UNIT)

        def part(start, size, masked):
            at = pl.ds(pl.multiple_of(start, KEYS), size)
            key = keys[slot, at, :]
            probs = jnp.exp2(nt(key, queries) - lse)
            if masked:
                last = jnp.minimum(row + (position * UNIT - start), length - 1 - start)
                probs = jnp.where(lax.broadcasted_iota(jnp.int32, probs.shape, 0) <= last, probs, 0.0)
            d_scores = (probs * (nt(values[slot, at, :], grads) - delta)).astype(BF16)
            dvalues[slot, at, :] += nn(probs.astype(BF16), grads)
            dkeys[slot, at, :] += nn(d_scores, queries)
            dq_acc[...] += tn(d_scores, key)

        sweep(clear, part)
        dq_ref[rows, :] = jnp.concatenate([dq_acc[:UNIT, :], dq_acc[UNIT:, :]], axis=1).astype(BF16)
        return carry

    lax.fori_loop(0, q_ref.shape[0] // UNIT, one_unit, 0)
    dlo_ref[...] = jnp.zeros_like(dlo_ref)
    dhi_ref[...] = jnp.zeros_like(dhi_ref)

    def spread(slot, position, away, row):
        at = pl.ds(pl.multiple_of(position * UNIT, UNIT), UNIT)
        for n, out in enumerate((dlo_ref, down_ref, dhi_ref)):

            @pl.when(away == n - 1)
            def _():
                out[pl.ds(row, UNIT), :HEAD_SIZE] = (dkeys[slot, at, :] * (1.0 / LOG2E)).astype(out.dtype)
                out[pl.ds(row, UNIT), HEAD_SIZE:] = dvalues[slot, at, :].astype(out.dtype)

    places.each(spread)


def attend_back(order, lens, q, d_mixed, mixed, lse, lo, own, hi, seq_len):
    flat = jax.ShapeDtypeStruct(q.shape, BF16)
    held = pltpu.VMEM((2, seq_len, HEAD_SIZE), BF16)
    summed = pltpu.VMEM((2, seq_len, HEAD_SIZE), F32)
    return pl.pallas_call(
        attend_back_kernel,
        out_shape=(flat,) * 4,
        in_specs=[spec_smem(), spec_smem()] + [spec_vmem()] * 4 + [spec_any()] * 3,
        out_specs=(spec_vmem(),) * 4,
        scratch_shapes=[
            held,
            held,
            summed,
            summed,
            pltpu.VMEM((2 * UNIT, HEAD_SIZE), F32),
            pltpu.SemaphoreType.DMA((2,)),
            pltpu.SemaphoreType.DMA((2,)),
        ],
        compiler_params=pltpu.CompilerParams(vmem_limit_bytes=VMEM_LIMIT),
        cost_estimate=busy(75),
        name="attend_back",
    )(order, lens, q, d_mixed, mixed, lse, lo, own, hi)


def angles(block_order, tok_rows):
    inverse = THETA ** (-jnp.arange(0, HEAD_SIZE, 2, dtype=F32) / HEAD_SIZE)
    inverse = jnp.concatenate([inverse, inverse])
    units = tok_rows // UNIT
    g = lax.axis_index("tp") * units + jnp.arange(units, dtype=jnp.int32)
    seq, quarter = g // 4, g % 4
    c = jnp.arange(lax.axis_size("ctx"), dtype=jnp.int32)
    where = 2 * block_order[seq[None, :], 2 * c[:, None] + (quarter // 2)[None, :]] + (quarter % 2)[None, :]
    starts = (where.reshape(-1) * UNIT).astype(F32)
    coarse = starts[:, None] * inverse[None, :]
    fine = jnp.arange(UNIT, dtype=F32)[:, None] * inverse[None, :]
    return jnp.cos(coarse), jnp.sin(coarse), jnp.cos(fine), jnp.sin(fine)


def after(value, *earlier):
    return lax.optimization_barrier((value,) + earlier)[0]


def local_plane(
    tokens,
    teacher,
    seq_lens,
    block_order,
    in_gain,
    w_query,
    key_weight_matrix,
    value_weight_matrix,
    q_gain,
    k_gain,
    w_out,
    post_gain,
    w_gate,
    w_up,
    w_down,
):
    me = lax.axis_index("ctx")
    core = me % 2
    plane = lax.axis_index("tp")
    tok_rows, width = tokens.shape
    plane_rows = 8 * tok_rows
    seq_len = 2 * 8 * BLK
    deep = width // 8
    cols = w_gate.shape[1] // 4
    stream = tokens.astype(F32)
    normed_rows = (stream * rms_scale(stream) * in_gain).astype(BF16)
    unit = plane * (tok_rows // UNIT) + jnp.arange(tok_rows // UNIT, dtype=jnp.int32)
    seq, quarter = unit // 4, unit % 4
    start = block_order[seq, 2 * me + quarter // 2] * BLK + (quarter % 2) * UNIT
    position = start[:, None] + jnp.arange(UNIT, dtype=jnp.int32)
    valid = (position < seq_lens[seq][:, None]).astype(F32).reshape(tok_rows, 1)

    qkv_home = jnp.concatenate(
        [
            w_query.reshape(deep, 2, 2 * HEAD_SIZE),
            key_weight_matrix.reshape(deep, 2, HEAD_SIZE),
            value_weight_matrix.reshape(deep, 2, HEAD_SIZE),
        ],
        axis=2,
    )
    tables = angles(block_order, tok_rows)
    normed_all, w_qkv, queries, kv, kv_lo, kv_hi, lin, gate_parts, up_part, down_part, out_part = gather_qkv(
        normed_rows,
        jnp.transpose(qkv_home, (1, 0, 2)),
        q_gain,
        k_gain,
        tables,
        jnp.transpose(w_gate.reshape(deep, 4, cols), (1, 0, 2)),
        jnp.transpose(w_up.reshape(deep, 4, cols), (1, 0, 2)),
        w_down.reshape(4, cols, deep),
        w_out.reshape(2, 2 * HEAD_SIZE, deep),
    )
    out_part = out_part.reshape(width, deep)
    out_parts = [out_part] + [lax.ppermute(out_part, "ctx", [(i, i ^ n) for i in range(8)]) for n in (2, 4, 6)]
    up_parts = lax.all_gather(up_part, "tp", axis=0)
    mixed, lse = attend(block_order, seq_lens, queries, kv_lo, kv, kv_hi, seq_len)
    down_parts = lax.all_gather(down_part, "tp", axis=0)
    middle, post_rows, mixed_rows, w_o = mix(mixed, tokens, post_gain, out_parts)
    post_all, w_gu, slope, active, hidden = gather_up(post_rows, gate_parts, up_parts)
    output, diff_low, diff, error, w_d = scatter_down(hidden, down_parts, middle, teacher, valid)
    d_gu, grad_wd = gather_down_back(diff_low, w_d, slope, active, hidden)
    d_post, grad_gu = scatter_post(d_gu, w_gu, post_all)

    def home_sum(parts):
        return lax.psum_scatter(parts, "tp", scatter_dimension=0, tiled=True)[0]

    grad_down = home_sum(grad_wd)
    grad_gu = home_sum(grad_gu)
    d_mixed, d_middle, grad_post, *grad_wo, grad_down = mix_back(
        d_post, middle, diff, post_gain, w_o, mixed_rows, grad_down
    )
    grad_wo = [grad_wo[0]] + [
        lax.ppermute(grad_wo[m], "ctx", [(i, i ^ n) for i in range(8)]) for m, n in ((1, 2), (2, 4), (3, 6))
    ]

    d_queries, to_lo, d_kv, to_hi = attend_back(
        block_order,
        seq_lens,
        queries,
        d_mixed,
        mixed,
        lse,
        kv_lo,
        kv,
        kv_hi,
        seq_len,
    )
    out_sum = sum(after(g, d_queries[:8]).astype(F32) for g in grad_wo).astype(BF16)
    d_normed, grad_qkv, grad_gains, gu_sum, grad_out = scatter_normed(
        d_queries,
        d_kv,
        to_lo,
        to_hi,
        lin,
        w_qkv,
        normed_all,
        grad_gu,
        out_sum.reshape(4, 4 * HEAD_SIZE, deep),
        q_gain,
        k_gain,
        tables,
    )
    d_tokens, grad_in, grad_gate, grad_up, grad_down, grad_query, grad_key, grad_value, grad_out = finish(
        d_normed, tokens, d_middle, in_gain, gu_sum, grad_down, grad_qkv, grad_out
    )
    lanes = width // HEAD_SIZE
    totals = total_of(
        jnp.concatenate(
            [
                grad_in.reshape(lanes, HEAD_SIZE),
                grad_post.reshape(lanes, HEAD_SIZE),
                grad_gains[:2],
                jnp.broadcast_to(error, (6, HEAD_SIZE)),
            ],
            axis=0,
        )
    )
    count_valid = jnp.sum(seq_lens).astype(F32)
    loss = 0.5 * jnp.sum(totals[2 * lanes + 2]) / (count_valid * MODEL_WIDTH)
    return (
        output,
        loss,
        d_tokens,
        totals[:lanes].reshape(width),
        grad_query,
        grad_key,
        grad_value,
        totals[2 * lanes],
        totals[2 * lanes + 1],
        grad_out,
        totals[lanes : 2 * lanes].reshape(width),
        grad_gate,
        grad_up,
        grad_down.reshape(4 * cols, deep),
    )


def solution(mesh):
    in_specs = (
        P(("ctx", "tp"), None),
        P(("ctx", "tp"), None),
        P(),
        P(),
        P(),
        P("ctx", "tp"),
        P("ctx", "tp"),
        P("ctx", "tp"),
        P(),
        P(),
        P("tp", "ctx"),
        P(),
        P("ctx", "tp"),
        P("ctx", "tp"),
        P("tp", "ctx"),
    )
    out_specs = (
        P(("ctx", "tp"), None),
        P(),
        P(("ctx", "tp"), None),
        P(),
        P("ctx", "tp"),
        P("ctx", "tp"),
        P("ctx", "tp"),
        P(),
        P(),
        P("tp", "ctx"),
        P(),
        P("ctx", "tp"),
        P("ctx", "tp"),
        P("tp", "ctx"),
    )
    body = local_plane if (mesh.shape["ctx"], mesh.shape["tp"]) == (8, 4) else local
    return jax.shard_map(body, mesh=mesh, in_specs=in_specs, out_specs=out_specs, check_vma=False)
```

```python
import functools

import jax
import jax.numpy as jnp
from jax import lax
from jax.experimental import pallas as pl
from jax.experimental.pallas import tpu as pltpu
from jax.sharding import PartitionSpec as P

MODEL_WIDTH = 2048
HEAD_SIZE = 128
SEQS = 3
BLK = 256


EPS = 1e-06
THETA = 1000000.0
FLOOR = -1e30


def from_behind(x, axis, by):
    count = lax.axis_size(axis)
    return lax.ppermute(x, axis, [(i, (i + by) % count) for i in range(count)])


def rms_scale(value):
    return lax.rsqrt(jnp.mean(value * value, axis=-1, keepdims=True) + EPS)


def rms_back(value, scale, grad_normed):
    return scale * grad_normed - value * scale**3 * jnp.mean(
        grad_normed * value, axis=-1, keepdims=True
    )


def rotate(value, cosine, sine):
    half = value.shape[-1] // 2
    first = value[..., :half]
    second = value[..., half:]
    return jnp.concatenate(
        [first * cosine - second * sine, second * cosine + first * sine], axis=-1
    )


def rotate_back(grad, cosine, sine):
    half = grad.shape[-1] // 2
    first = grad[..., :half]
    second = grad[..., half:]
    return jnp.concatenate(
        [first * cosine + second * sine, second * cosine - first * sine], axis=-1
    )


def matmul(left, right):
    return jnp.dot(left, right, preferred_element_type=jnp.float32)


def matmul_tn(left, right):
    return lax.dot_general(
        left, right, (((0,), (0,)), ((), ())), preferred_element_type=jnp.float32
    )


def matmul_nt(left, right):
    return lax.dot_general(
        left, right, (((1,), (1,)), ((), ())), preferred_element_type=jnp.float32
    )


def row_slice(value, start, count):
    return lax.dynamic_slice_in_dim(value, start, count, 0)


def local(
    tokens,
    teacher,
    seq_lens,
    block_order,
    in_gain,
    w_query,
    key_weight_matrix,
    value_weight_matrix,
    q_gain,
    k_gain,
    w_out,
    post_gain,
    w_gate,
    w_up,
    w_down,
):
    ctx_count = lax.axis_size("ctx")
    ctx_index = lax.axis_index("ctx")
    tp_index = lax.axis_index("tp")
    tok_rows = tokens.shape[0]
    ctx_rows = tok_rows * lax.axis_size("tp")
    block_span = 2 * BLK
    q_heads = w_query.shape[1] // HEAD_SIZE
    kv_heads = key_weight_matrix.shape[1] // HEAD_SIZE
    group_width = q_heads // kv_heads
    scale_qk = HEAD_SIZE ** (-0.5)
    weights = (
        lax.all_gather(w_query, "ctx", axis=0, tiled=True),
        lax.all_gather(key_weight_matrix, "ctx", axis=0, tiled=True),
        lax.all_gather(value_weight_matrix, "ctx", axis=0, tiled=True),
        lax.all_gather(w_out, "ctx", axis=1, tiled=True),
        lax.all_gather(w_gate, "ctx", axis=0, tiled=True),
        lax.all_gather(w_up, "ctx", axis=0, tiled=True),
        lax.all_gather(w_down, "ctx", axis=1, tiled=True),
    )
    wq_full, wk_full, wv_full, wo_full, wg_full, wu_full, wd_full = weights
    offsets = jnp.arange(BLK, dtype=jnp.int32)

    def block_positions(owner):
        columns = lax.dynamic_slice_in_dim(block_order, 2 * owner, 2, 1)
        return (columns[:, :, None] * BLK + offsets).reshape(SEQS, block_span)

    query_pos = block_positions(ctx_index)
    flat_pos = query_pos.reshape(-1)
    inverse = THETA ** (-jnp.arange(0, HEAD_SIZE, 2, dtype=jnp.float32) / HEAD_SIZE)
    angle = flat_pos.astype(jnp.float32)[:, None] * inverse[None, :]
    cosine = jnp.cos(angle)[:, None, :]
    sine = jnp.sin(angle)[:, None, :]
    stream = tokens.astype(jnp.float32)
    scale_in = rms_scale(stream)
    unit_in = stream * scale_in
    normed_rows = (unit_in * in_gain).astype(jnp.bfloat16)
    normed_all = lax.all_gather(normed_rows, "tp", axis=0, tiled=True)
    query_lin = matmul(normed_all, wq_full).reshape(ctx_rows, q_heads, HEAD_SIZE)
    key_linear = matmul(normed_all, wk_full).reshape(ctx_rows, kv_heads, HEAD_SIZE)
    value_low = (
        matmul(normed_all, wv_full)
        .astype(jnp.bfloat16)
        .reshape(SEQS, block_span, kv_heads, HEAD_SIZE)
    )
    query_scale = rms_scale(query_lin)
    query_unit = query_lin * query_scale
    query_low = (
        rotate(query_unit * q_gain, cosine, sine)
        .astype(jnp.bfloat16)
        .reshape(SEQS, block_span, kv_heads, group_width, HEAD_SIZE)
    )
    key_scale = rms_scale(key_linear)
    key_unit = key_linear * key_scale
    key_low = (
        rotate(key_unit * k_gain, cosine, sine)
        .astype(jnp.bfloat16)
        .reshape(SEQS, block_span, kv_heads, HEAD_SIZE)
    )

    def scores_of(keys, key_pos):
        raw = (
            jnp.einsum("sqkgd,slkd->skgql", query_low, keys, preferred_element_type=jnp.float32)
            * scale_qk
        )
        allowed = (key_pos[:, None, :] <= query_pos[:, :, None]) & (
            key_pos[:, None, :] < seq_lens[:, None, None]
        )
        allowed = allowed[:, None, None, :, :]
        return (jnp.where(allowed, raw, FLOOR), allowed)

    def absorb(state, keys, value_rows, owner):
        running_top, running_total, running_acc = state
        scores, allowed = scores_of(keys, block_positions(owner))
        new_top = jnp.maximum(running_top, jnp.max(scores, axis=-1))
        weights_now = jnp.where(allowed, jnp.exp(scores - new_top[..., None]), 0.0)
        shrink = jnp.exp(running_top - new_top)
        running_total = running_total * shrink + jnp.sum(weights_now, axis=-1)
        running_acc = running_acc * shrink[..., None] + jnp.einsum(
            "skgql,slkd->skgqd",
            weights_now.astype(jnp.bfloat16),
            value_rows,
            preferred_element_type=jnp.float32,
        )
        return (new_top, running_total, running_acc)

    stat_shape = (SEQS, kv_heads, group_width, block_span)
    initial = (
        jnp.full(stat_shape, FLOOR, jnp.float32),
        jnp.zeros(stat_shape, jnp.float32),
        jnp.zeros(stat_shape + (HEAD_SIZE,), jnp.float32),
    )
    first_state = absorb(initial, key_low, value_low, ctx_index)

    def cycle_turn(carry, turn):
        keys, value_rows, state = carry
        keys, value_rows = from_behind((keys, value_rows), "ctx", 1)
        owner = (ctx_index - turn) % ctx_count
        state = absorb(state, keys, value_rows, owner)
        return ((keys, value_rows, state), (keys, value_rows))

    (unused_keys, unused_values, final_state), (kept_keys, kept_values) = lax.scan(
        cycle_turn, (key_low, value_low, first_state), jnp.arange(1, ctx_count, dtype=jnp.int32)
    )
    all_keys = jnp.concatenate([key_low[None], kept_keys], axis=0)
    all_values = jnp.concatenate([value_low[None], kept_values], axis=0)
    top_final, total_final, acc_final = final_state
    log_total = top_final + jnp.log(total_final)
    attn_exact = acc_final / total_final[..., None]
    mixed_low = (
        jnp.transpose(attn_exact, (0, 3, 1, 2, 4))
        .reshape(ctx_rows, q_heads * HEAD_SIZE)
        .astype(jnp.bfloat16)
    )
    middle = stream + lax.psum_scatter(
        matmul(row_slice(mixed_low, jnp.int32(0), lax.axis_size("tp") * tok_rows), wo_full).astype(
            jnp.bfloat16
        ),
        "tp",
        scatter_dimension=0,
        tiled=True,
    ).astype(jnp.float32)
    scale_post = rms_scale(middle)
    unit_post = middle * scale_post
    post_rows = (unit_post * post_gain).astype(jnp.bfloat16)
    post_all = lax.all_gather(post_rows, "tp", axis=0, tiled=True)
    gate = matmul(post_all, wg_full)
    up_val = matmul(post_all, wu_full)
    sigma = jax.nn.sigmoid(gate)
    active = gate * sigma
    hidden_low = (active * up_val).astype(jnp.bfloat16)
    result = middle + lax.psum_scatter(
        matmul(row_slice(hidden_low, jnp.int32(0), lax.axis_size("tp") * tok_rows), wd_full).astype(
            jnp.bfloat16
        ),
        "tp",
        scatter_dimension=0,
        tiled=True,
    ).astype(jnp.float32)
    output = result.astype(jnp.bfloat16)
    valid_all = (query_pos < seq_lens[:, None]).reshape(-1).astype(jnp.float32)
    valid_rows = row_slice(valid_all, tp_index * tok_rows, tok_rows)
    diff = (result - teacher.astype(jnp.float32)) * valid_rows[:, None]
    error_local = jnp.sum(diff * diff)
    diff_low = diff.astype(jnp.bfloat16)
    diff_all = lax.all_gather(diff_low, "tp", axis=0, tiled=True)
    weights_two = (
        lax.all_gather(w_query, "ctx", axis=0, tiled=True),
        lax.all_gather(key_weight_matrix, "ctx", axis=0, tiled=True),
        lax.all_gather(value_weight_matrix, "ctx", axis=0, tiled=True),
        lax.all_gather(w_out, "ctx", axis=1, tiled=True),
        lax.all_gather(w_gate, "ctx", axis=0, tiled=True),
        lax.all_gather(w_up, "ctx", axis=0, tiled=True),
        lax.all_gather(w_down, "ctx", axis=1, tiled=True),
    )
    bq_full, bk_full, bv_full, bo_full, bg_full, bu_full, bd_full = weights_two
    grad_wd = matmul_tn(hidden_low, diff_all)
    d_hidden = matmul_nt(diff_all, bd_full)
    d_gate = (d_hidden * up_val * sigma * (1.0 + gate * (1.0 - sigma))).astype(jnp.bfloat16)
    d_up = (d_hidden * active).astype(jnp.bfloat16)
    grad_wg = matmul_tn(post_all, d_gate)
    grad_wu = matmul_tn(post_all, d_up)
    start = jnp.int32(0)
    d_post = lax.psum_scatter(
        (
            matmul_nt(row_slice(d_gate, start, lax.axis_size("tp") * tok_rows), bg_full)
            + matmul_nt(row_slice(d_up, start, lax.axis_size("tp") * tok_rows), bu_full)
        ).astype(jnp.bfloat16),
        "tp",
        scatter_dimension=0,
        tiled=True,
    ).astype(jnp.float32)
    grad_post_local = jnp.sum(d_post * unit_post, axis=0)
    d_middle = diff + rms_back(middle, scale_post, d_post * post_gain)
    d_mid_low = d_middle.astype(jnp.bfloat16)
    d_mid_all = lax.all_gather(d_mid_low, "tp", axis=0, tiled=True)
    grad_wo = matmul_tn(mixed_low, d_mid_all)
    d_mixed = matmul_nt(d_mid_all, bo_full).astype(jnp.bfloat16)
    d_mixed_grid = jnp.transpose(
        d_mixed.reshape(SEQS, block_span, kv_heads, group_width, HEAD_SIZE), (0, 2, 3, 1, 4)
    )
    delta = jnp.sum(d_mixed_grid.astype(jnp.float32) * attn_exact, axis=-1)

    def revisit(carry, turn):
        grad_queries, grad_keys, grad_values = carry
        owner = (ctx_index - turn) % ctx_count
        keys = all_keys[turn]
        value_rows = all_values[turn]
        scores, allowed = scores_of(keys, block_positions(owner))
        probs = jnp.where(allowed, jnp.exp(scores - log_total[..., None]), 0.0)
        probs_low = probs.astype(jnp.bfloat16)
        d_probs = jnp.einsum(
            "skgqd,slkd->skgql", d_mixed_grid, value_rows, preferred_element_type=jnp.float32
        )
        d_scores = (probs * (d_probs - delta[..., None])).astype(jnp.bfloat16)
        grad_queries = grad_queries + jnp.einsum(
            "skgql,slkd->skgqd", d_scores, keys, preferred_element_type=jnp.float32
        )
        grad_keys = grad_keys + jnp.einsum(
            "skgql,sqkgd->slkd", d_scores, query_low, preferred_element_type=jnp.float32
        )
        grad_values = grad_values + jnp.einsum(
            "skgql,skgqd->slkd", probs_low, d_mixed_grid, preferred_element_type=jnp.float32
        )
        grad_keys, grad_values = (
            from_behind(grad_keys.astype(jnp.bfloat16), "ctx", 1).astype(grad_keys.dtype),
            from_behind(grad_values.astype(jnp.bfloat16), "ctx", 1).astype(grad_values.dtype),
        )
        return ((grad_queries, grad_keys, grad_values), None)

    kv_shape = (SEQS, block_span, kv_heads, HEAD_SIZE)
    start_carry = (
        jnp.zeros(stat_shape + (HEAD_SIZE,), jnp.float32),
        jnp.zeros(kv_shape, jnp.float32),
        jnp.zeros(kv_shape, jnp.float32),
    )
    (grad_queries, grad_keys, grad_values), unused_out = lax.scan(
        revisit, start_carry, jnp.arange(ctx_count, dtype=jnp.int32)
    )
    grad_queries = (
        jnp.transpose(grad_queries, (0, 3, 1, 2, 4)).reshape(ctx_rows, q_heads, HEAD_SIZE)
        * scale_qk
    )
    grad_keys = grad_keys.reshape(ctx_rows, kv_heads, HEAD_SIZE) * scale_qk
    d_values = grad_values.reshape(ctx_rows, kv_heads * HEAD_SIZE).astype(jnp.bfloat16)
    query_back = rotate_back(grad_queries, cosine, sine)
    grad_q_local = jnp.sum(query_back * query_unit, axis=(0, 1))
    d_query_lin = (
        rms_back(query_lin, query_scale, query_back * q_gain)
        .reshape(ctx_rows, q_heads * HEAD_SIZE)
        .astype(jnp.bfloat16)
    )
    key_back = rotate_back(grad_keys, cosine, sine)
    grad_k_local = jnp.sum(key_back * key_unit, axis=(0, 1))
    d_key_lin = (
        rms_back(key_linear, key_scale, key_back * k_gain)
        .reshape(ctx_rows, kv_heads * HEAD_SIZE)
        .astype(jnp.bfloat16)
    )
    grad_wq = matmul_tn(normed_all, d_query_lin)
    grad_wk = matmul_tn(normed_all, d_key_lin)
    grad_wv = matmul_tn(normed_all, d_values)
    start = jnp.int32(0)
    part_query = matmul_nt(row_slice(d_query_lin, start, lax.axis_size("tp") * tok_rows), bq_full)
    part_key = matmul_nt(row_slice(d_key_lin, start, lax.axis_size("tp") * tok_rows), bk_full)
    part_value = matmul_nt(row_slice(d_values, start, lax.axis_size("tp") * tok_rows), bv_full)
    d_normed = lax.psum_scatter(
        (part_query + part_key + part_value).astype(jnp.bfloat16),
        "tp",
        scatter_dimension=0,
        tiled=True,
    ).astype(jnp.float32)
    grad_in_local = jnp.sum(d_normed * unit_in, axis=0)
    d_tokens = (d_middle + rms_back(stream, scale_in, d_normed * in_gain)).astype(jnp.bfloat16)
    summed = (
        lax.psum_scatter(
            grad_wq.astype(jnp.bfloat16), "ctx", scatter_dimension=0, tiled=True
        ).astype(jnp.float32),
        lax.psum_scatter(
            grad_wk.astype(jnp.bfloat16), "ctx", scatter_dimension=0, tiled=True
        ).astype(jnp.float32),
        lax.psum_scatter(
            grad_wv.astype(jnp.bfloat16), "ctx", scatter_dimension=0, tiled=True
        ).astype(jnp.float32),
        lax.psum_scatter(
            grad_wo.astype(jnp.bfloat16), "ctx", scatter_dimension=1, tiled=True
        ).astype(jnp.float32),
        lax.psum_scatter(
            grad_wg.astype(jnp.bfloat16), "ctx", scatter_dimension=0, tiled=True
        ).astype(jnp.float32),
        lax.psum_scatter(
            grad_wu.astype(jnp.bfloat16), "ctx", scatter_dimension=0, tiled=True
        ).astype(jnp.float32),
        lax.psum_scatter(
            grad_wd.astype(jnp.bfloat16), "ctx", scatter_dimension=1, tiled=True
        ).astype(jnp.float32),
    )
    totals = lax.psum(
        (grad_in_local, grad_q_local, grad_k_local, grad_post_local, error_local), ("ctx", "tp")
    )
    count_valid = jnp.sum(seq_lens).astype(jnp.float32)
    loss = 0.5 * totals[4] / (count_valid * MODEL_WIDTH)
    return (
        output,
        loss,
        d_tokens,
        totals[0],
        summed[0],
        summed[1],
        summed[2],
        totals[1],
        totals[2],
        summed[3],
        totals[3],
        summed[4],
        summed[5],
        summed[6],
    )


F32 = jnp.float32
BF16 = jnp.bfloat16
MESH = pl.DeviceIdType.MESH
VMEM_LIMIT = 62 << 20


def busy(us):
    return pl.CostEstimate(flops=0, bytes_accessed=us * 3_000_000, transcendentals=0)

LOG2E = 1.4426950408889634
UNIT = 128
KEYS = 512
CORE_GROUPS = [[0, 2, 4, 6], [1, 3, 5, 7]]
SIBLING = [(i, i ^ 1) for i in range(8)]


def spec_vmem():
    return pl.BlockSpec(memory_space=pltpu.VMEM)


def spec_any():
    return pl.BlockSpec(memory_space=pl.ANY)


def spec_smem():
    return pl.BlockSpec(memory_space=pltpu.SMEM)


def plane_neighbours():
    me = lax.axis_index("ctx")
    core = lax.rem(me, 2)
    x = lax.rem(me // 2, 2)
    y = me // 4
    sib = me + 1 - 2 * core
    nx = me + 2 - 4 * x
    ny = me + 4 - 8 * y
    dg = nx + 4 - 8 * y
    return me, sib, nx, ny, dg


def greet(devices):
    barrier = pltpu.get_barrier_semaphore()
    for device in devices:
        pl.semaphore_signal(barrier, inc=1, device_id={"ctx": device}, device_id_type=MESH)
    pl.semaphore_wait(barrier, len(devices))


def pick(step, options):
    value = options[0]
    for i in range(1, len(options)):
        value = jnp.where(step == i, options[i], value)
    return value


SUBS = 4
BY_X, BY_Y = (0, 2, 1, 3), (1, 3, 0, 2)


def on_ctx(device):
    return {"ctx": device}


def on_plane(plane):
    return {"tp": plane}


def send(src, dst, send_sem, recv_sem, where):
    return pltpu.make_async_remote_copy(
        src_ref=src,
        dst_ref=dst,
        send_sem=send_sem,
        recv_sem=recv_sem,
        device_id=where,
        device_id_type=MESH,
    )


class Gather:
    def __init__(self, x_ref, xs, local_sem, send_sems, recv_sems):
        self.x_ref, self.xs = x_ref, xs
        self.local_sem, self.send_sems, self.recv_sems = local_sem, send_sems, recv_sems
        self.me, self.sib, self.nx, self.ny, self.dg = plane_neighbours()
        self.shift = self.sib - self.me
        self.piece = x_ref.shape[0] // SUBS

    def part(self, block, s):
        return self.xs.at[block, pl.ds(s * self.piece, self.piece)]

    def remote(self, src, kind, block, s, device):
        return send(
            src, self.part(block, s), self.send_sems.at[kind, s], self.recv_sems.at[block, s], on_ctx(device)
        )

    def own(self, s):
        return self.x_ref.at[pl.ds(s * self.piece, self.piece)]

    def start(self):
        for s, t in zip(BY_X, BY_Y):
            self.remote(self.own(s), 0, self.me, s, self.nx).start()
            self.remote(self.own(t), 1, self.me, t, self.ny).start()
        for s in range(SUBS):
            self.remote(self.own(s), 2, self.me, s, self.sib).start()
        keep = pltpu.make_async_copy(self.x_ref, self.xs.at[self.me], self.local_sem)
        keep.start()
        keep.wait()

    def arrived(self, block, s):
        self.remote(self.part(block, s), 0, block, s, self.sib).wait_recv()

    def relay(self, kind, block, s, device):
        self.remote(self.part(block, s), kind, block, s, device).start()

    def pass_on(self, i):
        s, t = BY_X[i], BY_Y[i]
        self.arrived(self.nx, s)
        if s % 2 == 0:
            self.relay(3, self.nx, s, self.ny)
        self.relay(4, self.nx, s, self.sib)
        self.arrived(self.ny, t)
        if t % 2 == 1:
            self.relay(3, self.ny, t, self.nx)
        self.relay(5, self.ny, t, self.sib)

    def far_half(self, h):
        for s in (2 * h, 2 * h + 1):
            self.arrived(self.dg, s)
            self.relay(6, self.dg, s, self.sib)

    def all_of(self, block, pieces=range(SUBS)):
        for s in pieces:
            self.arrived(block, s)

    def pass_all(self):
        for i in range(SUBS):
            self.pass_on(i)

    def before(self, step, passing=True):
        for at, act in (
            (1, lambda: self.all_of(self.sib)),
            (2, self.pass_all if passing else lambda: None),
            (3, lambda: self.all_of(self.nx + self.shift)),
            (4, lambda: self.far_half(0)),
            (5, lambda: self.all_of(self.ny + self.shift)),
            (6, lambda: self.far_half(1)),
            (7, lambda: self.all_of(self.dg + self.shift)),
        ):
            pl.when(step == at)(act)

    def before_half(self, step):
        for at, act in (
            (2, lambda: self.all_of(self.sib)),
            (4, self.pass_all),
            (6, lambda: self.all_of(self.nx + self.shift)),
            (8, lambda: self.far_half(0)),
            (10, lambda: self.all_of(self.ny + self.shift)),
            (13, lambda: self.all_of(self.dg + self.shift, (0, 1))),
            (14, lambda: self.far_half(1)),
            (15, lambda: self.all_of(self.dg + self.shift, (2, 3))),
        ):
            pl.when(step == at)(act)

    def block(self, step):
        near = (self.me, self.nx, self.ny, self.dg)
        return pick(step, [b + o for b in near for o in (0, self.shift)])

    def half_block(self, step):
        last = step >= 12
        n = jnp.where(last, 6 + lax.rem(step, 2), step // 2)
        return self.block(n), jnp.where(last, (step - 12) // 2, lax.rem(step, 2))

    def finish(self):
        for s in range(SUBS):
            for kind in range(7):
                self.remote(self.part(self.me, s), kind, self.me, s, self.sib).wait_send()


def gather_scratch(rows, width):
    return [
        pltpu.VMEM((8, rows, width), BF16),
        pltpu.SemaphoreType.DMA,
        pltpu.SemaphoreType.DMA((7, SUBS)),
        pltpu.SemaphoreType.DMA((8, SUBS)),
    ]


class Scatter:
    def __init__(self, to_sib, from_sib, own, diag_out, diag_in, x_out, y_out, x_in, y_in, sends, recvs):
        self.to_sib, self.from_sib, self.own = to_sib, from_sib, own
        self.diag_out, self.diag_in = diag_out, diag_in
        self.x_out, self.y_out, self.x_in, self.y_in = x_out, y_out, x_in, y_in
        self.sends, self.recvs = sends, recvs
        self.me, self.sib, self.nx, self.ny, self.dg = plane_neighbours()
        self.rows = diag_out.shape[0]

    def round(self, i):
        return pl.ds(i * (self.rows // 2), self.rows // 2)

    def piece(self, i, half):
        quarter = self.rows // 4
        return pl.ds((2 * i + half) * quarter, quarter)

    def remote(self, src, dst, kind, i, device):
        return send(src, dst, self.sends.at[kind, i], self.recvs.at[kind, i], on_ctx(device))

    def sibling(self, n, i):
        at = self.round(i)
        return self.remote(self.to_sib.at[n, at], self.from_sib.at[n, at], n, i, self.sib)

    def hop(self, kind, i):
        out, into, half, device = (
            (self.diag_out, self.diag_in, 0, self.nx),
            (self.diag_out, self.diag_in, 1, self.ny),
            (self.x_out, self.x_in, 0, self.nx),
            (self.x_out, self.x_in, 1, self.nx),
            (self.y_out, self.y_in, 0, self.ny),
            (self.y_out, self.y_in, 1, self.ny),
        )[kind]
        at = self.piece(i, half)
        return self.remote(out.at[at], into.at[at], 4 + kind, i, device)

    def blocks(self):
        shift = self.sib - self.me
        return [b + o for b in (self.dg, self.nx, self.ny, self.me) for o in (shift, 0)]

    def block(self, step):
        return pick(2 * (step // 4) + lax.rem(step, 2), self.blocks())

    def chip_sum(self, n, at):
        return self.own[n, at].astype(F32) + self.from_sib[n, at].astype(F32)

    def step(self, step, product, late=False):
        block = self.block(step)
        n = step // 4
        i = lax.rem(step, 4) // 2
        at = self.round(pl.multiple_of(i, 1))

        @pl.when(lax.rem(step, 2) == 0)
        def _():
            product(block, at, self.to_sib, n)
            self.sibling(n, i).start()

        @pl.when(lax.rem(step, 2) == 1)
        def _():
            product(block, at, self.own, n)
            self.sibling(n, i).wait_recv()

        for r in range(2):
            first, second = self.piece(r, 0), self.piece(r, 1)

            @pl.when(step == 1 + 2 * r)
            def _():
                self.diag_out[first] = self.chip_sum(0, first).astype(BF16)
                self.hop(0, r).start()
                self.diag_out[second] = self.chip_sum(0, second).astype(BF16)
                self.hop(1, r).start()

            @pl.when(step == 5 + 2 * r)
            def _():
                self.x_out[first] = self.chip_sum(1, first).astype(BF16)
                self.hop(2, r).start()

            @pl.when(step == 9 + 2 * r)
            def _():
                self.y_out[second] = self.chip_sum(2, second).astype(BF16)
                self.hop(5, r).start()

        if not late:

            @pl.when(step == 11)
            def _():
                self.second_wave()

    def second_wave(self):
        for i in range(2):
            first, second = self.piece(i, 0), self.piece(i, 1)
            self.hop(0, i).wait_recv()
            self.y_out[first] = (self.chip_sum(2, first) + self.diag_in[first].astype(F32)).astype(BF16)
            self.hop(4, i).start()
            self.hop(1, i).wait_recv()
            self.x_out[second] = (self.chip_sum(1, second) + self.diag_in[second].astype(F32)).astype(BF16)
            self.hop(3, i).start()

    def finish(self, o_ref):
        for i in range(2):
            for kind in range(2, 6):
                self.hop(kind, i).wait_recv()
            at = self.round(i)
            o_ref[at] = (
                self.chip_sum(3, at) + self.x_in[at].astype(F32) + self.y_in[at].astype(F32)
            ).astype(o_ref.dtype)
        for i in range(2):
            for n in range(4):
                self.sibling(n, i).wait_send()
            for kind in range(6):
                self.hop(kind, i).wait_send()


def scatter_scratch(rows, width):
    four = pltpu.VMEM((4, rows, width), BF16)
    one = pltpu.VMEM((rows, width), BF16)
    return [four] * 3 + [one] * 6 + [pltpu.SemaphoreType.DMA((10, 2)), pltpu.SemaphoreType.DMA((10, 2))]


N_SCATTER = 11


def nn(left, right):
    return lax.dot_general(left, right, (((1,), (0,)), ((), ())), preferred_element_type=F32)


def nt(left, right):
    return lax.dot_general(left, right, (((1,), (1,)), ((), ())), preferred_element_type=F32)


def tn(left, right):
    return lax.dot_general(left, right, (((0,), (0,)), ((), ())), preferred_element_type=F32)


def comm_params(collective_id):
    return pltpu.CompilerParams(
        collective_id=collective_id, has_side_effects=True, vmem_limit_bytes=VMEM_LIMIT
    )


def greet_column(devices):
    barrier = pltpu.get_barrier_semaphore()
    plane, planes = lax.axis_index("tp"), lax.axis_size("tp")
    for device in devices:
        pl.semaphore_signal(barrier, inc=1, device_id=on_ctx(device), device_id_type=MESH)
    for step in (1, planes - 1):
        where = on_plane(lax.rem(plane + step, planes))
        pl.semaphore_signal(barrier, inc=1, device_id=where, device_id_type=MESH)
    pl.semaphore_wait(barrier, len(devices) + 2)


class Line:
    def __init__(self, up_src, down_src, from_lo, from_hi, sends, recvs, rows, back):
        self.up_src, self.down_src, self.from_lo, self.from_hi = up_src, down_src, from_lo, from_hi
        self.sends, self.recvs = sends, recvs
        self.units = rows // UNIT
        self.back = back
        self.plane, self.planes = lax.axis_index("tp"), lax.axis_size("tp")

    def at(self, block, i):
        return pl.ds(pl.multiple_of((block * self.units + i) * UNIT, UNIT), UNIT)

    def up(self, block, i):
        at, n = self.at(block, i), block * self.units + i
        return send(self.up_src.at[at], self.from_lo.at[at], self.sends.at[0, n], self.recvs.at[0, n], on_plane(self.plane + 1))

    def down(self, block, i):
        at, n = self.at(block, i), block * self.units + i
        return send(self.down_src.at[at], self.from_hi.at[at], self.sends.at[1, n], self.recvs.at[1, n], on_plane(self.plane - 1))

    def each(self, block, ups, downs):
        for i in range(self.units):
            up = i < self.plane + 1 if self.back else i >= self.plane
            down = i >= self.plane - 1 if self.back else i < self.plane

            @pl.when(up & (self.plane < self.planes - 1))
            def _():
                ups(self.up(block, i))

            @pl.when(down & (self.plane > 0))
            def _():
                downs(self.down(block, i))

    def start(self, block):
        self.each(block, lambda copy: copy.start(), lambda copy: copy.start())

    def sent(self, block):
        self.each(block, lambda copy: copy.wait_send(), lambda copy: copy.wait_send())

    def arrived(self, block):
        for i in range(self.units):
            below = i < self.plane if self.back else i >= self.plane - 1
            above = i >= self.plane if self.back else i < self.plane + 1

            @pl.when(below & (self.plane > 0))
            def _():
                self.up(block, i).wait_recv()

            @pl.when(above & (self.plane < self.planes - 1))
            def _():
                self.down(block, i).wait_recv()


class ChipSwap:
    def __init__(self, src, dst, local_sem, send_sems, recv_sems):
        self.src, self.dst = src, dst
        self.local_sem, self.send_sems, self.recv_sems = local_sem, send_sems, recv_sems
        me, _, nx, ny, dg = plane_neighbours()
        self.chip, self.away = me // 2, (dg, nx, ny)

    def part(self, chip):
        if len(self.src.shape) == 3:
            return self.src.at[chip]
        cols = self.src.shape[1] // 4
        return self.src.at[:, pl.ds(pl.multiple_of(chip * cols, HEAD_SIZE), cols)]

    def own(self):
        return pltpu.make_async_copy(self.part(self.chip), self.dst.at[self.chip], self.local_sem)

    def to(self, n):
        there = self.away[n]
        return send(
            self.part(there // 2), self.dst.at[self.chip], self.send_sems.at[n], self.recv_sems.at[self.chip], on_ctx(there)
        )

    def start(self):
        self.own().start()
        for n in range(3):
            self.to(n).start()

    def arrive(self):
        self.own().wait()
        for n in range(3):
            there = self.away[n] // 2
            send(
                self.part(there), self.dst.at[there], self.send_sems.at[n], self.recv_sems.at[there], on_ctx(self.away[n])
            ).wait_recv()

    def sent(self):
        for n in range(3):
            self.to(n).wait_send()

    def finish(self):
        self.arrive()
        self.sent()


SWAP_SCRATCH = [pltpu.SemaphoreType.DMA, pltpu.SemaphoreType.DMA((3,)), pltpu.SemaphoreType.DMA((4,))]


class LineGather:
    def __init__(self, src, dst, local_sem, send_sems, recv_sems):
        self.src, self.dst = src, dst
        self.local_sem, self.send_sems, self.recv_sems = local_sem, send_sems, recv_sems
        self.plane, self.planes = lax.axis_index("tp"), lax.axis_size("tp")
        self.pieces = src.shape[0]

    def own(self):
        return pltpu.make_async_copy(self.src, self.dst.at[self.plane], self.local_sem)

    def copy(self, way, hop, n, origin):
        src = self.src.at[n] if hop == 0 else self.dst.at[origin, n]
        return send(
            src,
            self.dst.at[origin, n],
            self.send_sems.at[way, hop, n],
            self.recv_sems.at[origin, n],
            on_plane(self.plane + 1 - 2 * way),
        )

    def ways(self, hop):
        up, down = self.plane - hop, self.plane + hop
        yield 0, up, up >= 0, self.plane < self.planes - 1
        yield 1, down, down < self.planes, self.plane > 0

    def start(self):
        self.own().start()
        for way, origin, _, goes_on in self.ways(0):

            @pl.when(goes_on)
            def _():
                for n in range(self.pieces):
                    self.copy(way, 0, n, origin).start()

    def arrive(self, hop, then=None):
        for way, origin, there, goes_on in self.ways(hop):

            @pl.when(there)
            def _():
                for n in range(self.pieces):
                    self.copy(way, 0, n, origin).wait_recv()
                    if hop == self.planes - 1:
                        continue

                    @pl.when(goes_on)
                    def _():
                        self.copy(way, hop, n, origin).start()

                if then is not None:
                    then(origin)

    def finish(self):
        self.own().wait()
        self.sent()

    def sent(self):
        for hop in range(self.planes - 1):
            for way, origin, there, goes_on in self.ways(hop):

                @pl.when(there & goes_on)
                def _():
                    for n in range(self.pieces):
                        self.copy(way, hop, n, origin).wait_send()


def line_scratch(pieces):
    dma = pltpu.SemaphoreType.DMA
    return [dma, dma((2, 3, pieces)), dma((4, pieces))]


class LineSum:
    def __init__(self, own, up_in, down_in, send_sems, recv_sems):
        self.own, self.into = own, (up_in, down_in)
        self.send_sems, self.recv_sems = send_sems, recv_sems
        self.plane, self.planes = lax.axis_index("tp"), lax.axis_size("tp")

    def copy(self, way, p, first):
        into = self.into[way]
        return send(
            self.own(p) if first else into.at[p],
            into.at[p],
            self.send_sems.at[way, p],
            self.recv_sems.at[way, p],
            on_plane(self.plane + 1 - 2 * way),
        )

    def moves(self, k):
        last = self.planes - 1
        for way in range(2):
            z = last - k if way else k
            yield way, z, (range(z) if way else range(last, z, -1))

    def stage(self, k):
        for way, z, ends in self.moves(k):

            @pl.when(self.plane == z)
            def _():
                for p in ends:
                    copy = self.copy(way, p, k == 0)
                    if k > 0:
                        copy.wait_recv()
                        into = self.into[way]
                        into[p] = (self.own(p)[...].astype(F32) + into[p].astype(F32)).astype(BF16)
                    copy.start()

    def collect(self, out):
        out[...] = self.own(self.plane)[...].astype(F32)
        for way in range(2):

            @pl.when(self.plane < self.planes - 1 if way else self.plane > 0)
            def _():
                self.copy(way, self.plane, False).wait_recv()
                out[...] += self.into[way][self.plane].astype(F32)

    def finish(self):
        for k in range(self.planes - 1):
            for way, z, ends in self.moves(k):

                @pl.when(self.plane == z)
                def _():
                    for p in ends:
                        self.copy(way, p, k == 0).wait_send()


class Total:
    def __init__(self, held, held_planes, sends, recvs):
        self.held, self.held_planes, self.sends, self.recvs = held, held_planes, sends, recvs
        self.me = lax.axis_index("ctx")
        self.plane, self.planes = lax.axis_index("tp"), lax.axis_size("tp")
        self.away = others(self.me)
        self.far = [lax.rem(self.plane + step, self.planes) for step in range(1, self.planes)]

    def here(self, c, n):
        ref = self.held.at[c]
        return send(ref, ref, self.sends.at[n], self.recvs.at[c], on_ctx(self.away[n]))

    def there(self, p, n):
        ref = self.held_planes.at[p]
        return send(ref, ref, self.sends.at[7 + n], self.recvs.at[8 + p], on_plane(self.far[n]))

    def start(self):
        for n in range(7):
            self.here(self.me, n).start()

    def middle(self):
        for n, c in enumerate(self.away):
            self.here(c, n).wait_recv()
        value = self.held[0]
        for c in range(1, 8):
            value += self.held[c]
        self.held_planes[self.plane] = value
        for n in range(len(self.far)):
            self.there(self.plane, n).start()

    def finish(self, out):
        for n, p in enumerate(self.far):
            self.there(p, n).wait_recv()
        value = self.held_planes[0]
        for p in range(1, 4):
            value += self.held_planes[p]
        out[...] = value
        for n in range(7):
            self.here(self.me, n).wait_send()
        for n in range(len(self.far)):
            self.there(self.plane, n).wait_send()


class Turn:
    def __init__(self, ca_ref, sa_ref, cb_ref, sb_ref, unit):
        ca, sa = ca_ref[pl.ds(unit, 1), :], sa_ref[pl.ds(unit, 1), :]
        cb, sb = cb_ref[...], sb_ref[...]
        self.cosine = ca * cb - sa * sb
        sine = sa * cb + ca * sb
        lane = lax.broadcasted_iota(jnp.int32, sine.shape, 1)
        self.sine = jnp.where(lane < HEAD_SIZE // 2, -sine, sine)

    def forth(self, v):
        return v * self.cosine + pltpu.roll(v, HEAD_SIZE // 2, 1) * self.sine

    def back(self, v):
        return v * self.cosine - pltpu.roll(v, HEAD_SIZE // 2, 1) * self.sine


def others(me):
    _, sib, nx, ny, dg = plane_neighbours()
    shift = sib - me
    return (dg, dg + shift, nx, nx + shift, ny, ny + shift, sib)


def qkv_kernel(
    x_ref,
    home_ref,
    qg_ref,
    kg_ref,
    ca_ref,
    sa_ref,
    cb_ref,
    sb_ref,
    gate_ref,
    up_ref,
    down_ref,
    out_ref,
    all_ref,
    w_out_ref,
    q_ref,
    kv_ref,
    lo_ref,
    hi_ref,
    lin_ref,
    gates_ref,
    ups_ref,
    downs_ref,
    outs_ref,
    xs,
    local_sem,
    send_sems,
    recv_sems,
    keep_sems,
    w,
    w_local,
    w_sends,
    w_recvs,
    slab,
    gate_part,
    kv_sends,
    kv_recvs,
    *sems,
):
    ring = Gather(x_ref, xs, local_sem, send_sems, recv_sems)
    me = ring.me
    rows = x_ref.shape[0]
    deep = home_ref.shape[1]
    slabs = LineGather(home_ref, slab, *sems[0:3])
    outs = LineGather(out_ref, outs_ref, *sems[3:6])
    gates = LineGather(gate_part.at[pl.ds(0, 3)], gates_ref, *sems[6:9])
    gate_swap = ChipSwap(gate_ref, gate_part, *sems[9:12])
    late_swaps = (ChipSwap(up_ref, ups_ref.at[pl.ds(0, 4)], *sems[12:15]), ChipSwap(down_ref, downs_ref, *sems[15:18]))
    line = Line(kv_ref, kv_ref, lo_ref, hi_ref, kv_sends, kv_recvs, rows, False)

    def weight(source, origin, k):
        return send(
            slab.at[origin, k],
            w.at[pl.ds(source * deep, deep)],
            w_sends.at[2 * origin + k],
            w_recvs.at[source],
            on_ctx(2 * origin + k),
        )

    own_weight = pltpu.make_async_copy(
        slab.at[me // 2, lax.rem(me, 2)], w.at[pl.ds(me * deep, deep)], w_local
    )

    def hand_out(origin):
        for k in range(2):

            @pl.when(2 * origin + k == me)
            def _():
                own_weight.start()

            @pl.when(2 * origin + k != me)
            def _():
                weight(me, origin, k).start()

    greet_column(others(me))
    gate_swap.start()
    slabs.start()
    ring.start()
    outs.start()
    slabs.own().wait()
    hand_out(slabs.plane)
    slabs.arrive(1, hand_out)
    gate_swap.arrive()
    gates.start()
    keep_last = pltpu.make_async_copy(gate_part.at[3], ups_ref.at[4], sems[18])
    keep_last.start()
    ring.pass_on(0)
    ring.pass_on(1)
    slabs.arrive(2, hand_out)
    ring.pass_on(2)
    ring.pass_on(3)
    slabs.arrive(3, hand_out)
    for swap in late_swaps:
        swap.start()
    outs.arrive(1)
    gates.arrive(1)
    own_weight.wait()
    for device in others(me):
        weight(device, 0, 0).wait_recv()
    keep_w = pltpu.make_async_copy(w, w_out_ref, w_local)
    keep_w.start()

    def keep(block):
        return pltpu.make_async_copy(xs.at[block], all_ref.at[block], keep_sems.at[block])

    def head(v, gain_ref, turn):
        scale = lax.rsqrt(jnp.mean(v * v, axis=-1, keepdims=True) + EPS)
        return turn.forth(v * scale * gain_ref[...])

    def turn(step, carry):
        @pl.when(step == 4)
        def _():
            outs.arrive(2)
            gates.arrive(2)

        ring.before(step, passing=False)
        block = ring.block(step)
        keep(block).start()
        lin = nn(xs[block], w[...])
        lin_ref[pl.ds(pl.multiple_of(block * rows, rows), rows), :] = lin[:, : 3 * HEAD_SIZE]
        for i in range(rows // UNIT):
            unit = block * (rows // UNIT) + i
            rotation = Turn(ca_ref, sa_ref, cb_ref, sb_ref, unit)
            here = pl.ds(pl.multiple_of(unit * UNIT, UNIT), UNIT)
            part = lin[i * UNIT : (i + 1) * UNIT]
            for h in range(2):
                lanes = slice(h * HEAD_SIZE, (h + 1) * HEAD_SIZE)
                query = head(part[:, lanes], qg_ref, rotation)
                q_ref[here, lanes] = (query * (HEAD_SIZE**-0.5 * LOG2E)).astype(BF16)
            key = head(part[:, 2 * HEAD_SIZE : 3 * HEAD_SIZE], kg_ref, rotation)
            kv_ref[here, :HEAD_SIZE] = key.astype(BF16)
            kv_ref[here, HEAD_SIZE:] = part[:, 3 * HEAD_SIZE :].astype(BF16)

        line.start(block)
        return carry

    lax.fori_loop(0, 8, turn, 0)
    ring.finish()
    keep_w.wait()
    for origin in range(4):
        for k in range(2):

            @pl.when(2 * origin + k != me)
            def _():
                weight(me, origin, k).wait_send()

    for block in range(8):
        keep(block).wait()

    def settle(block, carry):
        line.sent(block)
        line.arrived(block)
        return carry

    lax.fori_loop(0, 8, settle, 0)
    for gather in (outs, gates):
        gather.arrive(3)
    for gather in (slabs, outs, gates):
        gather.finish() if gather is not slabs else gather.sent()
    gate_swap.sent()
    keep_last.wait()
    for swap in late_swaps:
        swap.finish()


def gather_qkv(normed, home, q_gain, k_gain, tables, gate, up, down, out):
    rows, width = normed.shape
    _, deep, cols = home.shape
    part = (4, gate.shape[0], gate.shape[1] // 4)
    flat = jax.ShapeDtypeStruct((8 * rows, 2 * HEAD_SIZE), BF16)
    dma = pltpu.SemaphoreType.DMA
    return pl.pallas_call(
        qkv_kernel,
        out_shape=(
            jax.ShapeDtypeStruct((8, rows, width), BF16),
            jax.ShapeDtypeStruct((8 * deep, cols), BF16),
            flat,
            flat,
            flat,
            flat,
            jax.ShapeDtypeStruct((8 * rows, 3 * HEAD_SIZE), F32),
            jax.ShapeDtypeStruct((4, 3) + part[1:], BF16),
            jax.ShapeDtypeStruct((5,) + part[1:], BF16),
            jax.ShapeDtypeStruct(down.shape, BF16),
            jax.ShapeDtypeStruct((4,) + out.shape, BF16),
        ),
        in_specs=[spec_any()] * 2 + [spec_vmem()] * 6 + [spec_any()] * 4,
        out_specs=(spec_any(), spec_any(), spec_vmem(), spec_vmem(), spec_any(), spec_any(), spec_vmem())
        + (spec_any(),) * 4,
        scratch_shapes=gather_scratch(rows, width)
        + [
            dma((8,)),
            pltpu.VMEM((8 * deep, cols), BF16),
            dma,
            dma((8,)),
            dma((8,)),
            pltpu.VMEM((4,) + home.shape, BF16),
            pltpu.VMEM(part, BF16),
            dma((2, 8 * rows // UNIT)),
            dma((2, 8 * rows // UNIT)),
        ]
        + line_scratch(home.shape[0])
        + line_scratch(out.shape[0])
        + line_scratch(3)
        + SWAP_SCRATCH * 3
        + [dma],
        compiler_params=comm_params(1),
        cost_estimate=busy(100),
        name="gather_qkv",
    )(normed, home, q_gain.reshape(1, -1), k_gain.reshape(1, -1), *tables, gate, up, down, out)


class Halves:
    def __init__(self, parts, at, local_sems, send_sems, recv_sems):
        self.parts, self.at = parts, at
        self.local_sems, self.send_sems, self.recv_sems = local_sems, send_sems, recv_sems
        self.me, self.sib = plane_neighbours()[:2]
        self.core = lax.rem(self.me, 2)

    def own(self, z, p):
        n = 4 * z + p
        return pltpu.make_async_copy(
            self.parts(2 * self.core + z, p), self.at(z, 2 * p + self.core), self.local_sems.at[n]
        )

    def swap(self, z, p):
        n = 4 * z + p
        return send(
            self.parts(2 - 2 * self.core + z, p),
            self.at(z, 2 * p + self.core),
            self.send_sems.at[n],
            self.recv_sems.at[n],
            on_ctx(self.sib),
        )

    def each(self):
        return [(z, p) for z in range(2) for p in range(4)]

    def start(self):
        for z, p in self.each():
            self.swap(z, p).start()
            self.own(z, p).start()

    def ready(self):
        for z, p in self.each():
            self.own(z, p).wait()
            n = 4 * z + p
            send(
                self.parts(2 * self.core + z, p),
                self.at(z, 2 * p + 1 - self.core),
                self.send_sems.at[n],
                self.recv_sems.at[n],
                on_ctx(self.sib),
            ).wait_recv()

    def finish(self):
        for z, p in self.each():
            self.swap(z, p).wait_send()


class Shares:
    def __init__(self, out, local_sems, send_sems, recv_sems):
        self.out = out
        self.local_sems, self.send_sems, self.recv_sems = local_sems, send_sems, recv_sems
        self.me, self.sib = plane_neighbours()[:2]
        self.core = lax.rem(self.me, 2)

    def own(self, tile, z, p):
        return pltpu.make_async_copy(tile, self.out.at[2 * self.core + z, p], self.local_sems.at[z, p])

    def other(self, tile, z, p):
        return send(
            tile,
            self.out.at[2 * self.core + z, p],
            self.send_sems.at[z, p],
            self.recv_sems.at[z, p],
            on_ctx(self.sib),
        )

    def arrive(self):
        for z in range(2):
            for p in range(4):
                there = self.out.at[2 - 2 * self.core + z, p]
                send(
                    there, there, self.send_sems.at[z, p], self.recv_sems.at[z, p], on_ctx(self.sib)
                ).wait_recv()


SHARES_SCRATCH = [pltpu.SemaphoreType.DMA((2, 4))] * 3
HALVES_SCRATCH = [pltpu.SemaphoreType.DMA((8,))] * 3


def up_kernel(
    x_ref,
    gate_ref,
    up_ref,
    all_ref,
    w_out_ref,
    a_ref,
    b_ref,
    h_ref,
    xs,
    local_sem,
    send_sems,
    recv_sems,
    keep_sems,
    stage,
    stage_sems,
    w,
    w_sem,
    *w_sems,
):
    ring = Gather(x_ref, xs, local_sem, send_sems, recv_sems)
    rows = x_ref.shape[0]
    halves, width, wide = w.shape
    deep = width // 8
    cols = wide // 2
    outs = (a_ref, b_ref, h_ref)
    greet((ring.sib, ring.nx, ring.ny))
    ring.start()
    gates = Halves(
        lambda plane, p: gate_ref.at[plane, p] if p < 3 else up_ref.at[plane, 4],
        lambda z, c: w.at[z, pl.ds(c * deep, deep), pl.ds(0, cols)],
        *w_sems[:3],
    )
    ups = Halves(
        lambda plane, p: up_ref.at[plane, p],
        lambda z, c: w.at[z, pl.ds(c * deep, deep), pl.ds(cols, cols)],
        *w_sems[3:],
    )
    gates.start()
    ups.start()
    gates.ready()
    ups.ready()
    keep_w = pltpu.make_async_copy(w, w_out_ref, w_sem)
    keep_w.start()

    def keep(block):
        return pltpu.make_async_copy(xs.at[block], all_ref.at[block], keep_sems.at[block])

    part = rows // 2

    def put(slot, n, at):
        return pltpu.make_async_copy(stage.at[slot, n], outs[n].at[at], stage_sems.at[slot, n])

    def turn(step, carry):
        ring.before_half(step)
        block, h = ring.half_block(step)
        seen = xs[block, pl.ds(pl.multiple_of(h * part, part), part), :]
        at = pl.ds(pl.multiple_of(block * rows + h * part, part), part)

        @pl.when(h == 1)
        def _():
            keep(block).start()

        slot = lax.rem(step, 2)

        @pl.when(step >= 2)
        def _():
            for n in range(3):
                put(slot, n, at).wait()

        for z in range(halves):
            both = nn(seen, w[z])
            gate, up = both[:, :cols], both[:, cols:]
            sigma = jax.nn.sigmoid(gate)
            active = gate * sigma
            here = slice(z * cols, (z + 1) * cols)
            stage[slot, 0, :, here] = (up * sigma * (1.0 + gate * (1.0 - sigma))).astype(BF16)
            stage[slot, 1, :, here] = active.astype(BF16)
            stage[slot, 2, :, here] = (active * up).astype(BF16)
        for n in range(3):
            put(slot, n, at).start()
        return carry

    lax.fori_loop(0, 16, turn, 0)
    ring.finish()
    gates.finish()
    ups.finish()
    keep_w.wait()
    for block in range(8):
        keep(block).wait()
    for slot in range(2):
        for n in range(3):
            put(slot, n, pl.ds(0, part)).wait()


def gather_up(post, gate_parts, up_parts):
    rows, width = post.shape
    wide = 2 * gate_parts.shape[-1]
    flat = jax.ShapeDtypeStruct((8 * rows, wide), BF16)
    return pl.pallas_call(
        up_kernel,
        out_shape=(
            jax.ShapeDtypeStruct((8, rows, width), BF16),
            jax.ShapeDtypeStruct((2, width, wide), BF16),
            flat,
            flat,
            flat,
        ),
        in_specs=[spec_any()] * 3,
        out_specs=(spec_any(),) * 5,
        scratch_shapes=gather_scratch(rows, width)
        + [
            pltpu.SemaphoreType.DMA((8,)),
            pltpu.VMEM((2, 3, rows // 2, wide), BF16),
            pltpu.SemaphoreType.DMA((2, 3)),
            pltpu.VMEM((2, width, wide), BF16),
            pltpu.SemaphoreType.DMA,
        ]
        + HALVES_SCRATCH * 2,
        compiler_params=comm_params(2),
        cost_estimate=busy(62),
        name="gather_up",
    )(post, gate_parts, up_parts)


def down_kernel(h_any, parts_ref, middle_any, teacher_any, valid_ref, o_ref, low_ref, diff_ref, error_ref, w_out_ref, *scratch):
    rs = Scatter(*scratch[:N_SCATTER])
    (w, w_sem, h_ref, h_sems, middle_ref, teacher_ref, row_sems, w_local, w_sends, w_recvs) = scratch[N_SCATTER:]
    rows = o_ref.shape[0]
    _, _, cols, deep = parts_ref.shape
    weight = Halves(
        lambda plane, p: parts_ref.at[plane, p],
        lambda z, c: w.at[pl.ds(z * cols, cols), pl.ds(pl.multiple_of(c * deep, deep), deep)],
        w_local,
        w_sends,
        w_recvs,
    )
    def fetch(block):
        here = pl.ds(pl.multiple_of(block * rows, rows), rows)
        return pltpu.make_async_copy(h_any.at[here], h_ref.at[here], h_sems.at[block])

    for block in rs.blocks():
        fetch(block).start()
    late = (
        pltpu.make_async_copy(middle_any, middle_ref, row_sems.at[0]),
        pltpu.make_async_copy(teacher_any, teacher_ref, row_sems.at[1]),
    )
    greet((rs.sib, rs.nx, rs.ny))
    weight.start()
    for copy in late:
        copy.start()
    weight.ready()
    keep_w = pltpu.make_async_copy(w, w_out_ref, w_sem)
    keep_w.start()

    def product(block, at, out, n):
        left = h_ref[pl.ds(pl.multiple_of(block * rows + at.start, rows // 2), rows // 2), :]
        for c in range(0, w.shape[1], 512):
            out[n, at, c : c + 512] = nn(left, w[:, c : c + 512]).astype(BF16)

    def turn(step, carry):
        @pl.when(lax.rem(step, 4) < 2)
        def _():
            fetch(rs.block(step)).wait()

        rs.step(step, product)
        return carry

    lax.fori_loop(0, 16, turn, 0)
    for copy in late:
        copy.wait()
    rs.finish(diff_ref)
    error = jnp.zeros((rows, HEAD_SIZE), F32)
    for n in range(0, diff_ref.shape[1], HEAD_SIZE):
        at = slice(n, n + HEAD_SIZE)
        result = middle_ref[:, at] + diff_ref[:, at]
        o_ref[:, at] = result.astype(BF16)
        diff = (result - teacher_ref[:, at].astype(F32)) * valid_ref[...]
        diff_ref[:, at] = diff
        low_ref[:, at] = diff.astype(BF16)
        error += diff * diff
    error_ref[...] = jnp.sum(error, axis=0, keepdims=True)
    weight.finish()
    keep_w.wait()


def scatter_down(hidden, parts, middle, teacher, valid):
    rows, width = middle.shape
    ff = hidden.shape[1]
    low = jax.ShapeDtypeStruct((rows, width), BF16)
    return pl.pallas_call(
        down_kernel,
        out_shape=(
            low,
            low,
            jax.ShapeDtypeStruct((rows, width), F32),
            jax.ShapeDtypeStruct((1, HEAD_SIZE), F32),
            jax.ShapeDtypeStruct((ff, width), BF16),
        ),
        in_specs=[spec_any()] * 4 + [spec_vmem()],
        out_specs=(spec_vmem(),) * 4 + (spec_any(),),
        scratch_shapes=scatter_scratch(rows, width)
        + [
            pltpu.VMEM((ff, width), BF16),
            pltpu.SemaphoreType.DMA,
            pltpu.VMEM(hidden.shape, BF16),
            pltpu.SemaphoreType.DMA((8,)),
            pltpu.VMEM((rows, width), F32),
            pltpu.VMEM((rows, width), BF16),
            pltpu.SemaphoreType.DMA((2,)),
        ]
        + HALVES_SCRATCH,
        compiler_params=comm_params(6),
        cost_estimate=busy(62),
        name="scatter_down",
    )(hidden, parts, middle, teacher, valid)


def down_back_kernel(
    x_ref,
    w_ref,
    a_ref,
    b_ref,
    h_ref,
    d_ref,
    gw_ref,
    xs,
    local_sem,
    send_sems,
    recv_sems,
    stage,
    stage_sems,
    total,
    low,
    w,
    w_sem,
    factors,
    factor_sems,
    hidden,
    hidden_sems,
    s_local,
    s_sends,
    s_recvs,
):
    ring = Gather(x_ref, xs, local_sem, send_sems, recv_sems)
    rows, width = x_ref.shape
    ff = w_ref.shape[0]
    cols = ff // 2
    fetch_w = pltpu.make_async_copy(w_ref, w, w_sem)
    fetch_w.start()
    shares = Shares(gw_ref, s_local, s_sends, s_recvs)
    core = shares.core
    deep = width // 8

    def tile(z, c):
        return low.at[pl.ds(z * cols, cols), pl.ds(pl.multiple_of(c * deep, deep), deep)]

    def put(slot, block):
        return pltpu.make_async_copy(
            stage.at[slot], d_ref.at[pl.ds(block * rows, rows)], stage_sems.at[slot]
        )

    def factor(n, slot, block):
        ref = (a_ref, b_ref)[n]
        return pltpu.make_async_copy(
            ref.at[pl.ds(block * rows, rows)], factors.at[slot, n], factor_sems.at[slot, n]
        )

    def chip_hidden(slot, block):
        return pltpu.make_async_copy(
            h_ref.at[pl.ds(block // 2 * 2 * rows, 2 * rows)], hidden.at[slot], hidden_sems.at[slot]
        )

    def fetch(step):
        block = ring.block(step)
        for n in range(2):
            factor(n, lax.rem(step, 2), block).start()

        @pl.when(lax.rem(step, 2) == 0)
        def _():
            chip_hidden(lax.rem(step // 2, 2), block).start()

    fetch(jnp.int32(0))
    greet((ring.sib, ring.nx, ring.ny))
    ring.start()
    total[...] = jnp.zeros_like(total)
    fetch_w.wait()

    def turn(step, carry):
        ring.before(step)
        block = ring.block(step)
        slot = lax.rem(step, 2)
        pair_slot = lax.rem(step // 2, 2)

        @pl.when(step >= 2)
        def _():
            put(slot, block).wait()

        for n in range(2):
            factor(n, slot, block).wait()

        @pl.when(step < 7)
        def _():
            fetch(step + 1)

        for z in range(2):
            part = slice(z * cols, (z + 1) * cols)
            grad = nt(xs[block], w[part, :])
            for n in range(2):
                stage[slot, :, (2 * z + n) * cols : (2 * z + n + 1) * cols] = (
                    grad * factors[slot, n, :, part].astype(F32)
                ).astype(BF16)
        put(slot, block).start()

        @pl.when(slot == 1)
        def _():
            chip_hidden(pair_slot, block).wait()
            pair = block // 2
            for p in range(4):
                at = slice(p * 2 * deep, (p + 1) * 2 * deep)
                seen = xs[pl.ds(pair * 2, 2), :, at].reshape(2 * rows, 2 * deep)
                total[:, at] += tn(hidden[pair_slot], seen)

                @pl.when(step == 7)
                def _():
                    low[:, at] = total[:, at].astype(BF16)
                    for z in range(2):
                        shares.other(tile(z, 2 * p + 1 - core), z, p).start()
                        shares.own(tile(z, 2 * p + core), z, p).start()

        return carry

    lax.fori_loop(0, 8, turn, 0)
    ring.finish()
    for slot in range(2):
        put(slot, 0).wait()
    shares.arrive()
    for z in range(2):
        for p in range(4):
            shares.other(tile(z, 2 * p + 1 - core), z, p).wait_send()
            shares.own(tile(z, 2 * p + core), z, p).wait()


def gather_down_back(diff, w_down, a, b, hidden):
    rows, width = diff.shape
    ff = w_down.shape[0]
    dma = pltpu.SemaphoreType.DMA
    return pl.pallas_call(
        down_back_kernel,
        out_shape=(
            jax.ShapeDtypeStruct((8 * rows, 2 * ff), BF16),
            jax.ShapeDtypeStruct((4, 4, ff // 2, width // 8), BF16),
        ),
        in_specs=[spec_any()] * 5,
        out_specs=(spec_any(), spec_any()),
        scratch_shapes=gather_scratch(rows, width)
        + [
            pltpu.VMEM((2, rows, 2 * ff), BF16),
            dma((2,)),
            pltpu.VMEM((ff, width), F32),
            pltpu.VMEM((ff, width), BF16),
            pltpu.VMEM((ff, width), BF16),
            dma,
            pltpu.VMEM((2, 2, rows, ff), BF16),
            dma((2, 2)),
            pltpu.VMEM((2, 2 * rows, ff), BF16),
            dma((2,)),
        ]
        + SHARES_SCRATCH,
        compiler_params=comm_params(3),
        cost_estimate=busy(66),
        name="gather_down_back",
    )(diff, w_down, a, b, hidden)


def mix_kernel(
    mixed_ref,
    tokens_ref,
    gain_ref,
    w0_ref,
    w1_ref,
    w2_ref,
    w3_ref,
    middle_ref,
    post_ref,
    rows_ref,
    w_ref,
    held,
    w,
    m_sems,
    m_sends,
    m_recvs,
    w_local,
    w_sends,
    w_recvs,
    keep_sems,
):
    me, sib, nx, ny, dg = plane_neighbours()
    shift = sib - me
    away = others(me)
    rows, width = held.shape
    deep = width // 8
    greet(away)

    def block(c):
        return pl.ds(pl.multiple_of(c * rows, rows), rows)

    def lanes(c):
        return pl.ds(pl.multiple_of(c * deep, deep), deep)

    def give(n, c):
        return send(mixed_ref.at[block(c)], held.at[:, lanes(me)], m_sends.at[n], m_recvs.at[me], on_ctx(c))

    def take(c):
        return send(mixed_ref.at[block(c)], held.at[:, lanes(c)], m_sends.at[0], m_recvs.at[c], on_ctx(c))

    for n, c in enumerate(away):
        give(n, c).start()
    own = pltpu.make_async_copy(mixed_ref.at[block(me)], held.at[:, lanes(me)], m_sems)
    own.start()
    parts = ((w0_ref, me), (w1_ref, nx), (w2_ref, ny), (w3_ref, dg))

    def swap(n):
        part, c = parts[n]
        return send(part, w.at[:, lanes(c)], w_sends.at[n], w_recvs.at[n], on_ctx(sib))

    def place(n):
        part, c = parts[n]
        return pltpu.make_async_copy(part, w.at[:, lanes(c)], w_local.at[n])

    for n in range(4):
        swap(n).start()
        place(n).start()
    for n in range(4):
        place(n).wait()
        there = w.at[:, lanes(parts[n][1] + shift)]
        send(there, there, w_sends.at[n], w_recvs.at[n], on_ctx(sib)).wait_recv()
    own.wait()
    for c in away:
        take(c).wait_recv()
    keep_rows = pltpu.make_async_copy(held, rows_ref, keep_sems.at[0])
    keep_rows.start()
    keep_w = pltpu.make_async_copy(w, w_ref, keep_sems.at[1])
    keep_w.start()
    total = jnp.zeros((rows, 1), F32)
    for n in range(0, width, 512):
        at = slice(n, n + 512)
        middle = tokens_ref[:, at].astype(F32) + nn(held[...], w[:, at])
        middle_ref[:, at] = middle
        total += jnp.sum(middle * middle, axis=-1, keepdims=True)
    scale = lax.rsqrt(total / width + EPS)
    for n in range(0, width, 512):
        at = slice(n, n + 512)
        post_ref[:, at] = (middle_ref[:, at] * scale * gain_ref[:, at]).astype(BF16)
    for n, c in enumerate(away):
        give(n, c).wait_send()
    for n in range(4):
        swap(n).wait_send()
    keep_rows.wait()
    keep_w.wait()


def mix(mixed, tokens, post_gain, parts):
    rows, width = tokens.shape
    dma = pltpu.SemaphoreType.DMA
    return pl.pallas_call(
        mix_kernel,
        out_shape=(
            jax.ShapeDtypeStruct((rows, width), F32),
            jax.ShapeDtypeStruct((rows, width), BF16),
            jax.ShapeDtypeStruct((rows, width), BF16),
            jax.ShapeDtypeStruct((width, width), BF16),
        ),
        in_specs=[spec_any(), spec_vmem(), spec_vmem()] + [spec_any()] * 4,
        out_specs=(spec_vmem(), spec_vmem(), spec_any(), spec_any()),
        scratch_shapes=[
            pltpu.VMEM((rows, width), BF16),
            pltpu.VMEM((width, width), BF16),
            dma,
            dma((7,)),
            dma((8,)),
            dma((4,)),
            dma((4,)),
            dma((4,)),
            dma((2,)),
        ],
        compiler_params=comm_params(5),
        cost_estimate=busy(28),
        name="mix",
    )(mixed, tokens, post_gain.reshape(1, -1), *parts)


def mix_back_kernel(
    post_ref,
    middle_ref,
    diff_ref,
    gain_ref,
    w_any,
    rows_any,
    swap_ref,
    dm_ref,
    d_middle_ref,
    gp_ref,
    g0_ref,
    g1_ref,
    g2_ref,
    g3_ref,
    swapped_ref,
    w_ref,
    rows_ref,
    fetch_sems,
    d_ref,
    stage,
    to_sib,
    from_sib,
    own,
    out_sem,
    out_sends,
    out_recvs,
    s_sends,
    s_recvs,
    g_sems,
    *c_sems,
):
    me, sib, nx, ny, dg = plane_neighbours()
    shift = sib - me
    away = others(me)
    rows, width = d_ref.shape
    deep = width // 8
    fetch_w = pltpu.make_async_copy(w_any, w_ref, fetch_sems.at[0])
    fetch_w.start()
    fetch_rows = pltpu.make_async_copy(rows_any, rows_ref, fetch_sems.at[1])
    fetch_rows.start()
    greet(away)
    weight_swap = ChipSwap(swap_ref, swapped_ref, *c_sems)
    weight_swap.start()
    squares = jnp.zeros((rows, HEAD_SIZE), F32)
    dots = jnp.zeros((rows, HEAD_SIZE), F32)
    cuts = [slice(n, n + HEAD_SIZE) for n in range(0, width, HEAD_SIZE)]
    for at in cuts:
        middle = middle_ref[:, at]
        squares += middle * middle
        dots += post_ref[:, at] * gain_ref[:, at] * middle
    scale = lax.rsqrt(jnp.sum(squares, axis=-1, keepdims=True) / width + EPS)
    pull = scale * scale * scale * (jnp.sum(dots, axis=-1, keepdims=True) / width)
    for at in cuts:
        middle, post = middle_ref[:, at], post_ref[:, at]
        gp_ref[:, at] = jnp.sum(post * (middle * scale), axis=0, keepdims=True)
        d_middle = diff_ref[:, at] + scale * (post * gain_ref[:, at]) - middle * pull
        d_middle_ref[:, at] = d_middle
        d_ref[:, at] = d_middle.astype(BF16)
    outs = (g0_ref, g1_ref, g2_ref, g3_ref)
    chips = (me, nx, ny, dg)
    fetch_w.wait()
    fetch_rows.wait()

    def block(c):
        return pl.ds(pl.multiple_of(c * rows, rows), rows)

    def give(n, c):
        return send(stage.at[c], dm_ref.at[block(me)], out_sends.at[n], out_recvs.at[me], on_ctx(c))

    def take(c):
        return send(stage.at[c], dm_ref.at[block(c)], out_sends.at[0], out_recvs.at[c], on_ctx(c))

    def heads(n, carry):
        c = pick(n, away + (me,))
        at = pl.ds(pl.multiple_of(c * deep, deep), deep)
        stage[c] = nt(d_ref[...], w_ref[at, :]).astype(BF16)

        @pl.when(n < 7)
        def _():
            give(n, c).start()

        return carry

    lax.fori_loop(0, 8, heads, 0)
    keep = pltpu.make_async_copy(stage.at[me], dm_ref.at[block(me)], out_sem)
    keep.start()

    def swap(n):
        return send(to_sib.at[n], from_sib.at[n], s_sends.at[n], s_recvs.at[n], on_ctx(sib))

    def grad(n, out, c):
        at = pl.ds(pl.multiple_of(c * deep, deep), deep)
        out[n] = tn(rows_ref[...], d_ref[:, at]).astype(BF16)

    def theirs(n, carry):
        grad(n, to_sib, pick(n, chips) + shift)
        swap(n).start()
        return carry

    def ours(n, carry):
        grad(n, own, pick(n, chips))
        return carry

    lax.fori_loop(0, 4, theirs, 0)
    lax.fori_loop(0, 4, ours, 0)
    for n in range(4):
        swap(n).wait_recv()
        own[n] = (own[n].astype(F32) + from_sib[n].astype(F32)).astype(BF16)
        pltpu.make_async_copy(own.at[n], outs[n], g_sems.at[n]).start()
    for c in away:
        take(c).wait_recv()
    keep.wait()
    for n, c in enumerate(away):
        give(n, c).wait_send()
    for n in range(4):
        swap(n).wait_send()
        pltpu.make_async_copy(own.at[n], outs[n], g_sems.at[n]).wait()
    weight_swap.finish()


def mix_back(d_post, middle, diff, post_gain, w, mixed_rows, swap):
    rows, width = middle.shape
    deep = width // 8
    dma = pltpu.SemaphoreType.DMA
    four = pltpu.VMEM((4, width, deep), BF16)
    return pl.pallas_call(
        mix_back_kernel,
        out_shape=(
            jax.ShapeDtypeStruct((8 * rows, deep), BF16),
            jax.ShapeDtypeStruct((rows, width), F32),
            jax.ShapeDtypeStruct((1, width), F32),
        )
        + (jax.ShapeDtypeStruct((width, deep), BF16),) * 4
        + (jax.ShapeDtypeStruct(swap.shape, BF16),),
        in_specs=[spec_vmem()] * 4 + [spec_any()] * 3,
        out_specs=(spec_any(), spec_vmem(), spec_vmem()) + (spec_any(),) * 5,
        scratch_shapes=[
            pltpu.VMEM((width, width), BF16),
            pltpu.VMEM((rows, width), BF16),
            dma((2,)),
            pltpu.VMEM((rows, width), BF16),
            pltpu.VMEM((8, rows, deep), BF16),
            four,
            four,
            four,
            dma,
            dma((7,)),
            dma((8,)),
            dma((4,)),
            dma((4,)),
            dma((4,)),
        ]
        + SWAP_SCRATCH,
        compiler_params=comm_params(4),
        cost_estimate=busy(26),
        name="mix_back",
    )(d_post, middle, diff, post_gain.reshape(1, -1), w, mixed_rows, swap)


def columns(all_ref, slices, sems, c, slot):
    deep = slices.shape[-1]
    return pltpu.make_async_copy(
        all_ref.at[:, :, pl.ds(pl.multiple_of(c * deep, deep), deep)], slices.at[slot], sems.at[slot]
    )


EARLY = 1


def post_back_kernel(d_any, w_any, all_ref, o_ref, gw_ref, *scratch):
    rs = Scatter(*scratch[:N_SCATTER])
    slices, slice_sems, tile, d_ref, d_sems, w_ref, w_sems, s_local, s_sends, s_recvs = scratch[N_SCATTER:]
    shares = Shares(gw_ref, s_local, s_sends, s_recvs)
    rows = o_ref.shape[0]
    _, width, wide = w_ref.shape
    plane_rows = d_ref.shape[0]
    deep = width // 8
    fetch_w = [pltpu.make_async_copy(w_any.at[z], w_ref.at[z], w_sems.at[z]) for z in range(2)]

    def fetch(block):
        here = pl.ds(pl.multiple_of(block * rows, rows), rows)
        return pltpu.make_async_copy(d_any.at[here], d_ref.at[here], d_sems.at[block])

    order = rs.blocks()
    fetch(order[0]).start()
    for copy in fetch_w:
        copy.start()
    for block in order[1:]:
        fetch(block).start()
    columns(all_ref, slices, slice_sems, 0, 0).start()
    greet((rs.sib, rs.nx, rs.ny))
    for copy in fetch_w:
        copy.wait()

    def product(block, at, out, n):
        here = pl.ds(pl.multiple_of(block * rows + at.start, rows // 2), rows // 2)
        for c in range(0, width, 512):
            total = nt(d_ref[here, :wide], w_ref[0, c : c + 512, :])
            total += nt(d_ref[here, wide:], w_ref[1, c : c + 512, :])
            out[n, at, c : c + 512] = total.astype(BF16)

    def put(slot, p, act):
        @pl.when(slot == shares.core)
        def _():
            for z in range(2):
                copy = shares.own(tile.at[slot, z], z, p)
                copy.start() if act == "start" else copy.wait()

        @pl.when(slot != shares.core)
        def _():
            for z in range(2):
                copy = shares.other(tile.at[slot, z], z, p)
                copy.start() if act == "start" else copy.wait_send()

    def grad(c):
        slot = lax.rem(c, 2)
        columns(all_ref, slices, slice_sems, c, slot).wait()

        @pl.when(c < 7)
        def _():
            columns(all_ref, slices, slice_sems, c + 1, 1 - slot).start()

        @pl.when(c >= 2)
        def _():
            put(slot, c // 2 - 1, "wait")

        seen = slices[slot].reshape(plane_rows, deep)
        for z in range(2):
            tile[slot, z] = tn(seen, d_ref[:, z * wide : (z + 1) * wide]).astype(BF16)
        put(slot, c // 2, "start")

    def turn(t, carry):
        is_grad = ((t >= 10) & (t < 10 + EARLY)) | (t >= 16 + EARLY)

        for n in range(2):

            @pl.when(t == n)
            def _():
                fetch(order[n]).wait()

        @pl.when(t == 4)
        def _():
            for block in order[2:]:
                fetch(block).wait()

        @pl.when(is_grad)
        def _():
            grad(jnp.where(t < 10 + EARLY, t - 10, t - 16))

        @pl.when(jnp.logical_not(is_grad))
        def _():
            rs.step(jnp.where(t < 10, t, t - EARLY), product)

        return carry

    lax.fori_loop(0, 24, turn, 0)
    rs.finish(o_ref)
    for slot in range(2):
        put(slot, 3, "wait")
    shares.arrive()


def scatter_post(d_gu, w_gu, post_all):
    _, rows, width = post_all.shape
    wide = w_gu.shape[-1]
    deep = width // 8
    return pl.pallas_call(
        post_back_kernel,
        out_shape=(
            jax.ShapeDtypeStruct((rows, width), F32),
            jax.ShapeDtypeStruct((4, 4, deep, wide), BF16),
        ),
        in_specs=[spec_any()] * 3,
        out_specs=(spec_vmem(), spec_any()),
        scratch_shapes=scatter_scratch(rows, width)
        + [
            pltpu.VMEM((2, 8, rows, deep), BF16),
            pltpu.SemaphoreType.DMA((2,)),
            pltpu.VMEM((2, 2, deep, wide), BF16),
            pltpu.VMEM(d_gu.shape, BF16),
            pltpu.SemaphoreType.DMA((8,)),
            pltpu.VMEM(w_gu.shape, BF16),
            pltpu.SemaphoreType.DMA((2,)),
        ]
        + SHARES_SCRATCH,
        compiler_params=comm_params(7),
        cost_estimate=busy(66),
        name="scatter_post",
    )(d_gu, w_gu, post_all)


def normed_back_kernel(
    dq_ref,
    dkv_ref,
    to_lo_ref,
    to_hi_ref,
    lin_ref,
    w_ref,
    all_ref,
    swap_ref,
    wo_ref,
    tokens_ref,
    gp_ref,
    error_ref,
    qg_ref,
    kg_ref,
    ca_ref,
    sa_ref,
    cb_ref,
    sb_ref,
    o_ref,
    gw_ref,
    totals_ref,
    swapped_ref,
    wo_sum_ref,
    *scratch,
):
    rs = Scatter(*scratch[:N_SCATTER])
    (
        from_lo,
        from_hi,
        d_lin,
        slices,
        slice_sems,
        tiles,
        tiles_in,
        up_in,
        down_in,
        wo_up,
        wo_down,
        z_sends,
        z_recvs,
        t_sends,
        t_recvs,
        p_sends,
        p_recvs,
        o_sends,
        o_recvs,
        gains_ref,
        held,
        held_planes,
        v_sends,
        v_recvs,
        *c_sems,
    ) = scratch[N_SCATTER:]
    me = rs.me
    plane, planes = lax.axis_index("tp"), lax.axis_size("tp")
    rows, width = o_ref.shape
    deep = width // 8
    plane_rows = dq_ref.shape[0]
    units = rows // UNIT
    wide = 2 * HEAD_SIZE
    away = others(me)
    order = rs.blocks()

    from_lo[...] = jnp.zeros_like(from_lo)
    from_hi[...] = jnp.zeros_like(from_hi)
    line = Line(to_hi_ref, to_lo_ref, from_lo, from_hi, z_sends, z_recvs, rows, True)
    barrier = pltpu.get_barrier_semaphore()
    far = [lax.rem(plane + step, planes) for step in range(1, planes)]
    for where in [on_ctx(c) for c in away] + [on_plane(p) for p in far]:
        pl.semaphore_signal(barrier, inc=1, device_id=where, device_id_type=MESH)
    pl.semaphore_wait(barrier, len(away) + len(far))
    for block in order:
        line.start(block)
    columns(all_ref, slices, slice_sems, order[0], 0).start()
    gains_ref[...] = jnp.zeros_like(gains_ref)

    def head_back(grad, lin, gain_ref, rotation):
        back = rotation.back(grad)
        scale = lax.rsqrt(jnp.mean(lin * lin, axis=-1, keepdims=True) + EPS)
        normal = lin * scale
        gained = back * gain_ref[...]
        d = scale * (gained - normal * jnp.mean(gained * normal, axis=-1, keepdims=True))
        return d.astype(BF16), jnp.sum(back * normal, axis=0, keepdims=True)

    def rotation_of(unit):
        return Turn(ca_ref, sa_ref, cb_ref, sb_ref, unit)

    def prepare_queries(unit, carry):
        rotation = rotation_of(unit)
        here = pl.ds(pl.multiple_of(unit * UNIT, UNIT), UNIT)
        for h in range(2):
            lanes = slice(h * HEAD_SIZE, (h + 1) * HEAD_SIZE)
            d, gain = head_back(dq_ref[here, lanes].astype(F32) * HEAD_SIZE**-0.5, lin_ref[here, lanes], qg_ref, rotation)
            d_lin[here, lanes] = d
            gains_ref[0:1, :] += gain
        return carry

    def prepare_keys(block):
        line.arrived(block)
        for i in range(units):
            unit = block * units + i
            here = pl.ds(pl.multiple_of(unit * UNIT, UNIT), UNIT)
            d_kv = dkv_ref[here, :].astype(F32) + from_lo[here, :].astype(F32) + from_hi[here, :].astype(F32)
            lanes = slice(2 * HEAD_SIZE, 3 * HEAD_SIZE)
            d, gain = head_back(d_kv[:, :HEAD_SIZE], lin_ref[here, lanes], kg_ref, rotation_of(unit))
            d_lin[here, lanes] = d
            gains_ref[1:2, :] += gain
            d_lin[here, 3 * HEAD_SIZE :] = d_kv[:, HEAD_SIZE:].astype(BF16)

    def tile_to(part, n, device):
        return send(
            tiles.at[part, device],
            tiles_in.at[part, me],
            t_sends.at[part, n],
            t_recvs.at[part, me],
            on_ctx(device),
        )

    def tile_from(part, device):
        return send(
            tiles.at[part, device],
            tiles_in.at[part, device],
            t_sends.at[part, 0],
            t_recvs.at[part, device],
            on_ctx(device),
        )

    def grads(part):
        def grad(n, carry):
            c = pick(n, order)
            slot = lax.rem(n, 2)
            columns(all_ref, slices, slice_sems, c, slot).wait()

            @pl.when((n < 7) | (part == 0))
            def _():
                columns(all_ref, slices, slice_sems, pick(lax.rem(n + 1, 8), order), 1 - slot).start()

            lanes = slice(part * wide, (part + 1) * wide)
            value = tn(slices[slot].reshape(plane_rows, deep), d_lin[:, lanes]).astype(BF16)

            @pl.when(n < 7)
            def _():
                tiles[part, c] = value
                tile_to(part, n, c).start()

            @pl.when(n == 7)
            def _():
                tiles_in[part, me] = value

            return carry

        lax.fori_loop(0, 8, grad, 0)

    sums = [
        LineSum(
            lambda p, part=part: tiles_in.at[part, pl.ds(2 * p, 2)],
            up_in.at[part],
            down_in.at[part],
            p_sends.at[part],
            p_recvs.at[part],
        )
        for part in range(2)
    ]
    out_sum = LineSum(lambda p: wo_ref.at[p], wo_up, wo_down, o_sends, o_recvs)

    def tiles_there(part):
        for device in away:
            tile_from(part, device).wait_recv()

    def product(block, at, out, n):
        left = d_lin[pl.ds(pl.multiple_of(block * rows + at.start, rows // 2), rows // 2), :]
        for c in range(0, width, 512):
            out[n, at, c : c + 512] = nt(left, w_ref[c : c + 512, :]).astype(BF16)

    def turn(step, carry):
        @pl.when(lax.rem(step, 4) < 2)
        def _():
            prepare_keys(rs.block(step))

        rs.step(step, product, late=True)

        @pl.when(step == 4)
        def _():
            out_sum.stage(1)

        @pl.when(step == 7)
        def _():
            tiles_there(0)
            sums[0].stage(0)

        @pl.when(step == 9)
        def _():
            out_sum.stage(2)

        @pl.when(step == 12)
        def _():
            sums[0].stage(1)

        return carry

    swap = ChipSwap(swap_ref, swapped_ref, *c_sems)
    swap.start()
    out_sum.stage(0)
    lax.fori_loop(0, plane_rows // UNIT, prepare_queries, 0)
    grads(0)
    lax.fori_loop(0, 16, turn, 0)
    grads(1)
    for c in range(8):
        pltpu.make_async_copy(
            tokens_ref.at[:, pl.ds(c * deep, deep)], slices.at[0, c], slice_sems.at[0]
        ).start()
    rs.second_wave()
    sums[0].stage(2)
    tiles_there(1)
    for k in range(3):
        sums[1].stage(k)
    rs.finish(o_ref)
    total = Total(held, held_planes, v_sends, v_recvs)
    vector = held.at[me]
    pltpu.make_async_copy(slices.at[0], slices.at[0], slice_sems.at[0]).wait()
    squares = jnp.zeros((rows, deep), F32)
    for c in range(8):
        stream = slices[0, c].astype(F32)
        squares += stream * stream
    scale = lax.rsqrt(jnp.sum(squares, axis=-1, keepdims=True) / width + EPS)
    lanes_of = width // HEAD_SIZE
    for c in range(8):
        at = slice(c * deep, (c + 1) * deep)
        unit_in = slices[0, c].astype(F32) * scale
        gain = jnp.sum(o_ref[:, at].astype(F32) * unit_in, axis=0, keepdims=True)
        for i in range(2):
            n, lanes = 2 * c + i, slice(i * HEAD_SIZE, (i + 1) * HEAD_SIZE)
            vector[n : n + 1, :] = gain[:, lanes]
            vector[lanes_of + n : lanes_of + n + 1, :] = gp_ref[:, n * HEAD_SIZE : (n + 1) * HEAD_SIZE]
    vector[2 * lanes_of : 2 * lanes_of + 2, :] = gains_ref[0:2, :]
    vector[2 * lanes_of + 2 : 2 * lanes_of + 8, :] = jnp.broadcast_to(error_ref[...], (6, HEAD_SIZE))
    total.start()
    out_sum.collect(wo_sum_ref)
    for part in range(2):
        sums[part].collect(gw_ref.at[part])
    total.middle()
    swap.finish()
    total.finish(totals_ref)
    for line_sum in (out_sum, *sums):
        line_sum.finish()
    for part in range(2):
        for n, device in enumerate(order[:7]):
            tile_to(part, n, device).wait_send()

    def settle(block, carry):
        line.sent(block)
        return carry

    lax.fori_loop(0, 8, settle, 0)


def scatter_normed(d_queries, d_kv, to_lo, to_hi, lin, w_qkv, normed_all, swap, wo, tokens, gp, error, q_gain, k_gain, tables):
    _, rows, width = normed_all.shape
    deep = width // 8
    cols = w_qkv.shape[1]
    half = pltpu.VMEM(to_lo.shape, BF16)
    tiles = pltpu.VMEM((2, 8, deep, cols // 2), BF16)
    dma = pltpu.SemaphoreType.DMA
    return pl.pallas_call(
        normed_back_kernel,
        out_shape=(
            jax.ShapeDtypeStruct((rows, width), BF16),
            jax.ShapeDtypeStruct((2, 2, deep, cols // 2), F32),
            jax.ShapeDtypeStruct((2 * width // HEAD_SIZE + 8, HEAD_SIZE), F32),
            jax.ShapeDtypeStruct(swap.shape, BF16),
            jax.ShapeDtypeStruct(wo.shape[1:], F32),
        ),
        in_specs=[spec_vmem()] * 2
        + [spec_any()] * 2
        + [spec_vmem()] * 2
        + [spec_any()] * 2
        + [spec_vmem(), spec_any()]
        + [spec_vmem()] * 8,
        out_specs=(spec_vmem(),) * 3 + (spec_any(), spec_vmem()),
        scratch_shapes=scatter_scratch(rows, width)
        + [
            half,
            half,
            pltpu.VMEM((8 * rows, cols), BF16),
            pltpu.VMEM((2, 8, rows, deep), BF16),
            dma((2,)),
            tiles,
            tiles,
            pltpu.VMEM((2, 4, 2, deep, cols // 2), BF16),
            pltpu.VMEM((2, 4, 2, deep, cols // 2), BF16),
            pltpu.VMEM(wo.shape, BF16),
            pltpu.VMEM(wo.shape, BF16),
            dma((2, 8 * rows // UNIT)),
            dma((2, 8 * rows // UNIT)),
            dma((2, 7)),
            dma((2, 8)),
            dma((2, 2, 4)),
            dma((2, 2, 4)),
            dma((2, 4)),
            dma((2, 4)),
            pltpu.VMEM((8, HEAD_SIZE), F32),
            pltpu.VMEM((8, 2 * width // HEAD_SIZE + 8, HEAD_SIZE), F32),
            pltpu.VMEM((4, 2 * width // HEAD_SIZE + 8, HEAD_SIZE), F32),
            dma((10,)),
            dma((12,)),
        ]
        + SWAP_SCRATCH,
        compiler_params=comm_params(8),
        cost_estimate=busy(110),
        name="scatter_normed",
    )(
        d_queries,
        d_kv,
        to_lo,
        to_hi,
        lin,
        w_qkv,
        normed_all,
        swap,
        wo,
        tokens,
        gp,
        error,
        q_gain.reshape(1, -1),
        k_gain.reshape(1, -1),
        *tables,
    )


def finish_kernel(
    d_ref, tokens_ref, middle_ref, gain_ref, gu_ref, down_ref, qkv_ref, out_ref,
    dt_ref, gate_ref, up_ref, dw_ref, wq_ref, wk_ref, wv_ref, wo_ref,
):
    stream = tokens_ref[...].astype(F32)
    scale = lax.rsqrt(jnp.mean(stream * stream, axis=-1, keepdims=True) + EPS)
    gained = d_ref[...].astype(F32) * gain_ref[...]
    pull = scale * scale * scale * jnp.mean(gained * stream, axis=-1, keepdims=True)
    dt_ref[...] = (middle_ref[...] + (scale * gained - stream * pull)).astype(BF16)
    cols = gu_ref.shape[2] // 2
    for p in range(4):
        here = slice(p * cols, (p + 1) * cols)
        gate_ref[:, here] = gu_ref[p, :, :cols].astype(F32)
        up_ref[:, here] = gu_ref[p, :, cols:].astype(F32)
    dw_ref[...] = down_ref[...].astype(F32)
    wide = 2 * HEAD_SIZE
    for k in range(2):
        wq_ref[:, k * wide : (k + 1) * wide] = qkv_ref[0, k]
        wk_ref[:, k * HEAD_SIZE : (k + 1) * HEAD_SIZE] = qkv_ref[1, k, :, :HEAD_SIZE]
        wv_ref[:, k * HEAD_SIZE : (k + 1) * HEAD_SIZE] = qkv_ref[1, k, :, HEAD_SIZE:]
    wo_ref[...] = out_ref[...]


def finish(d_normed, tokens, d_middle, in_gain, gu, down, qkv, out):
    steps = 8

    def piece(shape, axis):
        block = list(shape)
        block[axis] //= steps
        return pl.BlockSpec(
            tuple(block), lambda i, axis=axis, n=len(shape): tuple(i if d == axis else 0 for d in range(n))
        )

    rows, width = tokens.shape
    deep, ff = gu.shape[1], 2 * gu.shape[2]
    one = (1, width)
    whole = pl.BlockSpec(one, lambda i: (0, 0))
    flat, square = (rows, width), (deep, 2 * HEAD_SIZE)
    ins = [(flat, 0), (flat, 0), (flat, 0), None, (gu.shape, 1), (down.shape, 1), (qkv.shape, 2), (out.shape, 0)]
    outs = [
        (flat, 0, BF16),
        ((deep, ff), 0, F32),
        ((deep, ff), 0, F32),
        (down.shape, 1, F32),
        ((deep, 4 * HEAD_SIZE), 0, F32),
        (square, 0, F32),
        (square, 0, F32),
        (out.shape, 0, F32),
    ]
    return pl.pallas_call(
        finish_kernel,
        grid=(steps,),
        out_shape=tuple(jax.ShapeDtypeStruct(o[0], o[2]) for o in outs),
        in_specs=[piece(*i) if i else whole for i in ins],
        out_specs=tuple(piece(o[0], o[1]) for o in outs),
        compiler_params=pltpu.CompilerParams(vmem_limit_bytes=VMEM_LIMIT),
        cost_estimate=busy(8),
        name="finish",
    )(d_normed, tokens, d_middle, in_gain.reshape(1, -1), gu, down, qkv, out)


class Places:
    def __init__(self, order_ref, lens_ref):
        self.order, self.lens = order_ref, lens_ref
        self.plane = lax.axis_index("tp")
        self.seq0 = (3 * self.plane) // 4
        self.seq1 = (3 * self.plane + 2) // 4

    def position(self, seq, quarter, c):
        return 2 * self.order[seq, 2 * c + quarter // 2] + lax.rem(quarter, 2)

    def unit(self, u):
        c = u // 3
        g = 3 * self.plane + lax.rem(u, 3)
        seq = g // 4
        return seq, seq - self.seq0, self.position(seq, lax.rem(g, 4), c)

    def each(self, visit):
        for slot, seq in ((0, self.seq0), (1, self.seq1)):

            @pl.when((slot == 0) | (self.seq1 != self.seq0))
            def _():
                def one(i, carry):
                    quarter, c = i // 8, lax.rem(i, 8)
                    g = 4 * seq + quarter
                    away = g // 3 - self.plane
                    row = pl.multiple_of((c * 3 + lax.rem(g, 3)) * UNIT, UNIT)
                    visit(slot, self.position(seq, quarter, c), away, row)
                    return carry

                lax.fori_loop(0, 32, one, 0)

    def fetch(self, sources, keys, values, key_sem, value_sem):
        def visit(slot, position, away, row):
            at = pl.ds(pl.multiple_of(position * UNIT, UNIT), UNIT)
            for n, source in enumerate(sources):

                @pl.when(away == n - 1)
                def _():
                    pltpu.make_async_copy(
                        source.at[pl.ds(row, UNIT), pl.ds(0, HEAD_SIZE)], keys.at[slot, at], key_sem.at[slot]
                    ).start()
                    pltpu.make_async_copy(
                        source.at[pl.ds(row, UNIT), pl.ds(HEAD_SIZE, HEAD_SIZE)],
                        values.at[slot, at, pl.ds(0, HEAD_SIZE)],
                        value_sem.at[slot],
                    ).start()

        self.each(visit)
        for slot in range(2):

            @pl.when((slot == 0) | (self.seq1 != self.seq0))
            def _():
                pltpu.make_async_copy(keys.at[slot], keys.at[slot], key_sem.at[slot]).wait()
                pltpu.make_async_copy(keys.at[slot], keys.at[slot], value_sem.at[slot]).wait()


def sweep(clear, part):
    def four(i, carry):
        part(i * 4 * KEYS, 4 * KEYS, False)
        return carry

    lax.fori_loop(0, clear // 4, four, 0)

    @pl.when(lax.rem(clear, 4) >= 2)
    def _():
        part(clear // 4 * 4 * KEYS, 2 * KEYS, False)


    odd = lax.rem(clear, 2)

    @pl.when(odd == 1)
    def _():
        part((clear - 1) * KEYS, 2 * KEYS, True)

    @pl.when(odd == 0)
    def _():
        part(clear * KEYS, KEYS, True)


def attend_kernel(
    order_ref, lens_ref, q_ref, lo_ref, own_ref, hi_ref, o_ref, lse_ref, keys, values, acc, key_sem, value_sem
):
    places = Places(order_ref, lens_ref)
    values[:, :, HEAD_SIZE:] = jnp.ones((2, values.shape[1], HEAD_SIZE), BF16)
    places.fetch((lo_ref, own_ref, hi_ref), keys, values, key_sem, value_sem)

    def one_unit(u, carry):
        seq, slot, position = places.unit(u)
        length = lens_ref[seq]
        rows = pl.ds(pl.multiple_of(u * UNIT, UNIT), UNIT)
        both = q_ref[rows, :]
        queries = jnp.concatenate([both[:, :HEAD_SIZE], both[:, HEAD_SIZE:]], axis=0)
        clear = jnp.minimum(position * UNIT, length) // KEYS
        acc[...] = jnp.zeros_like(acc)
        row = lax.rem(lax.broadcasted_iota(jnp.int32, (2 * UNIT, 1), 0), UNIT)

        def part(start, size, masked):
            at = pl.ds(pl.multiple_of(start, KEYS), size)
            weights = jnp.exp2(nt(queries, keys[slot, at, :]))
            if masked:
                last = jnp.minimum(row + (position * UNIT - start), length - 1 - start)
                weights = jnp.where(lax.broadcasted_iota(jnp.int32, weights.shape, 1) <= last, weights, 0.0)
            acc[:, :HEAD_SIZE] += nn(weights.astype(BF16), values[slot, at, :HEAD_SIZE])
            part_sum = weights[:, :HEAD_SIZE]
            for n in range(HEAD_SIZE, size, HEAD_SIZE):
                part_sum += weights[:, n : n + HEAD_SIZE]
            acc[:, HEAD_SIZE:] += part_sum

        sweep(clear, part)
        total = jnp.sum(acc[:, HEAD_SIZE:], axis=-1, keepdims=True)
        mixed = (acc[:, :HEAD_SIZE] / total).astype(BF16)
        o_ref[rows, :] = jnp.concatenate([mixed[:UNIT], mixed[UNIT:]], axis=1)
        lse_ref[u] = jnp.transpose(jnp.broadcast_to(jnp.log2(total), (2 * UNIT, HEAD_SIZE)))[:8, :]
        return carry

    lax.fori_loop(0, q_ref.shape[0] // UNIT, one_unit, 0)


def attend(order, lens, q, lo, own, hi, seq_len):
    rows = q.shape[0]
    return pl.pallas_call(
        attend_kernel,
        out_shape=(
            jax.ShapeDtypeStruct(q.shape, BF16),
            jax.ShapeDtypeStruct((rows // UNIT, 8, 2 * UNIT), F32),
        ),
        in_specs=[spec_smem(), spec_smem(), spec_vmem(), spec_any(), spec_any(), spec_any()],
        out_specs=(spec_vmem(), spec_vmem()),
        scratch_shapes=[
            pltpu.VMEM((2, seq_len, HEAD_SIZE), BF16),
            pltpu.VMEM((2, seq_len, 2 * HEAD_SIZE), BF16),
            pltpu.VMEM((2 * UNIT, 2 * HEAD_SIZE), F32),
            pltpu.SemaphoreType.DMA((2,)),
            pltpu.SemaphoreType.DMA((2,)),
        ],
        compiler_params=pltpu.CompilerParams(vmem_limit_bytes=VMEM_LIMIT),
        cost_estimate=busy(50),
        name="attend",
    )(order, lens, q, lo, own, hi)


def attend_back_kernel(
    order_ref,
    lens_ref,
    q_ref,
    do_ref,
    o_ref,
    lse_ref,
    lo_ref,
    own_ref,
    hi_ref,
    dq_ref,
    dlo_ref,
    down_ref,
    dhi_ref,
    keys,
    values,
    dkeys,
    dvalues,
    dq_acc,
    key_sem,
    value_sem,
):
    places = Places(order_ref, lens_ref)
    dkeys[...] = jnp.zeros_like(dkeys)
    dvalues[...] = jnp.zeros_like(dvalues)
    places.fetch((lo_ref, own_ref, hi_ref), keys, values, key_sem, value_sem)

    def stacked(ref, rows):
        both = ref[rows, :]
        return jnp.concatenate([both[:, :HEAD_SIZE], both[:, HEAD_SIZE:]], axis=0)

    def one_unit(u, carry):
        seq, slot, position = places.unit(u)
        length = lens_ref[seq]
        rows = pl.ds(pl.multiple_of(u * UNIT, UNIT), UNIT)
        queries = stacked(q_ref, rows)
        grads = stacked(do_ref, rows)
        product = grads.astype(F32) * stacked(o_ref, rows).astype(F32)
        delta = jnp.sum(jnp.transpose(product), axis=0, keepdims=True)
        lse = lse_ref[u][:1, :]
        clear = jnp.minimum(position * UNIT, length) // KEYS
        dq_acc[...] = jnp.zeros_like(dq_acc)
        row = lax.rem(lax.broadcasted_iota(jnp.int32, (1, 2 * UNIT), 1), UNIT)

        def part(start, size, masked):
            at = pl.ds(pl.multiple_of(start, KEYS), size)
            key = keys[slot, at, :]
            probs = jnp.exp2(nt(key, queries) - lse)
            if masked:
                last = jnp.minimum(row + (position * UNIT - start), length - 1 - start)
                probs = jnp.where(lax.broadcasted_iota(jnp.int32, probs.shape, 0) <= last, probs, 0.0)
            d_scores = (probs * (nt(values[slot, at, :], grads) - delta)).astype(BF16)
            dvalues[slot, at, :] += nn(probs.astype(BF16), grads)
            dkeys[slot, at, :] += nn(d_scores, queries)
            dq_acc[...] += tn(d_scores, key)

        sweep(clear, part)
        dq_ref[rows, :] = jnp.concatenate([dq_acc[:UNIT, :], dq_acc[UNIT:, :]], axis=1).astype(BF16)
        return carry

    lax.fori_loop(0, q_ref.shape[0] // UNIT, one_unit, 0)
    dlo_ref[...] = jnp.zeros_like(dlo_ref)
    dhi_ref[...] = jnp.zeros_like(dhi_ref)

    def spread(slot, position, away, row):
        at = pl.ds(pl.multiple_of(position * UNIT, UNIT), UNIT)
        for n, out in enumerate((dlo_ref, down_ref, dhi_ref)):

            @pl.when(away == n - 1)
            def _():
                out[pl.ds(row, UNIT), :HEAD_SIZE] = (dkeys[slot, at, :] * (1.0 / LOG2E)).astype(out.dtype)
                out[pl.ds(row, UNIT), HEAD_SIZE:] = dvalues[slot, at, :].astype(out.dtype)

    places.each(spread)


def attend_back(order, lens, q, d_mixed, mixed, lse, lo, own, hi, seq_len):
    flat = jax.ShapeDtypeStruct(q.shape, BF16)
    held = pltpu.VMEM((2, seq_len, HEAD_SIZE), BF16)
    summed = pltpu.VMEM((2, seq_len, HEAD_SIZE), F32)
    return pl.pallas_call(
        attend_back_kernel,
        out_shape=(flat,) * 4,
        in_specs=[spec_smem(), spec_smem()] + [spec_vmem()] * 4 + [spec_any()] * 3,
        out_specs=(spec_vmem(),) * 4,
        scratch_shapes=[
            held,
            held,
            summed,
            summed,
            pltpu.VMEM((2 * UNIT, HEAD_SIZE), F32),
            pltpu.SemaphoreType.DMA((2,)),
            pltpu.SemaphoreType.DMA((2,)),
        ],
        compiler_params=pltpu.CompilerParams(vmem_limit_bytes=VMEM_LIMIT),
        cost_estimate=busy(75),
        name="attend_back",
    )(order, lens, q, d_mixed, mixed, lse, lo, own, hi)


def angles(block_order, tok_rows):
    inverse = THETA ** (-jnp.arange(0, HEAD_SIZE, 2, dtype=F32) / HEAD_SIZE)
    inverse = jnp.concatenate([inverse, inverse])
    units = tok_rows // UNIT
    g = lax.axis_index("tp") * units + jnp.arange(units, dtype=jnp.int32)
    seq, quarter = g // 4, g % 4
    c = jnp.arange(lax.axis_size("ctx"), dtype=jnp.int32)
    where = 2 * block_order[seq[None, :], 2 * c[:, None] + (quarter // 2)[None, :]] + (quarter % 2)[None, :]
    starts = (where.reshape(-1) * UNIT).astype(F32)
    coarse = starts[:, None] * inverse[None, :]
    fine = jnp.arange(UNIT, dtype=F32)[:, None] * inverse[None, :]
    return jnp.cos(coarse), jnp.sin(coarse), jnp.cos(fine), jnp.sin(fine)


def after(value, *earlier):
    return lax.optimization_barrier((value,) + earlier)[0]


def local_plane(
    tokens,
    teacher,
    seq_lens,
    block_order,
    in_gain,
    w_query,
    key_weight_matrix,
    value_weight_matrix,
    q_gain,
    k_gain,
    w_out,
    post_gain,
    w_gate,
    w_up,
    w_down,
):
    me = lax.axis_index("ctx")
    core = me % 2
    plane = lax.axis_index("tp")
    tok_rows, width = tokens.shape
    plane_rows = 8 * tok_rows
    seq_len = 2 * 8 * BLK
    deep = width // 8
    cols = w_gate.shape[1] // 4
    stream = tokens.astype(F32)
    normed_rows = (stream * rms_scale(stream) * in_gain).astype(BF16)
    unit = plane * (tok_rows // UNIT) + jnp.arange(tok_rows // UNIT, dtype=jnp.int32)
    seq, quarter = unit // 4, unit % 4
    start = block_order[seq, 2 * me + quarter // 2] * BLK + (quarter % 2) * UNIT
    position = start[:, None] + jnp.arange(UNIT, dtype=jnp.int32)
    valid = (position < seq_lens[seq][:, None]).astype(F32).reshape(tok_rows, 1)

    qkv_home = jnp.concatenate(
        [
            w_query.reshape(deep, 2, 2 * HEAD_SIZE),
            key_weight_matrix.reshape(deep, 2, HEAD_SIZE),
            value_weight_matrix.reshape(deep, 2, HEAD_SIZE),
        ],
        axis=2,
    )
    tables = angles(block_order, tok_rows)
    normed_all, w_qkv, queries, kv, kv_lo, kv_hi, lin, gate_parts, *parts = gather_qkv(
        normed_rows,
        jnp.transpose(qkv_home, (1, 0, 2)),
        q_gain,
        k_gain,
        tables,
        w_gate,
        w_up,
        w_down.reshape(4, cols, deep),
        w_out.reshape(2, 2 * HEAD_SIZE, deep),
    )
    up_part, down_part, out_part = parts
    out_part = out_part.reshape(width, deep)
    out_parts = [out_part] + [lax.ppermute(out_part, "ctx", [(i, i ^ n) for i in range(8)]) for n in (2, 4, 6)]
    up_parts = lax.all_gather(up_part, "tp", axis=0)
    mixed, lse = attend(block_order, seq_lens, queries, kv_lo, kv, kv_hi, seq_len)
    down_parts = lax.all_gather(down_part, "tp", axis=0)
    middle, post_rows, mixed_rows, w_o = mix(mixed, tokens, post_gain, out_parts)
    post_all, w_gu, slope, active, hidden = gather_up(post_rows, gate_parts, up_parts)
    output, diff_low, diff, error, w_d = scatter_down(hidden, down_parts, middle, teacher, valid)
    d_gu, grad_wd = gather_down_back(diff_low, w_d, slope, active, hidden)
    d_post, grad_gu = scatter_post(d_gu, w_gu, post_all)

    def home_sum(parts):
        return lax.psum_scatter(parts, "tp", scatter_dimension=0, tiled=True)[0]

    grad_down = home_sum(grad_wd)
    grad_gu = home_sum(grad_gu)
    d_mixed, d_middle, grad_post, *grad_wo, grad_down = mix_back(
        d_post, middle, diff, post_gain, w_o, mixed_rows, grad_down
    )
    grad_wo = [grad_wo[0]] + [
        lax.ppermute(grad_wo[m], "ctx", [(i, i ^ n) for i in range(8)]) for m, n in ((1, 2), (2, 4), (3, 6))
    ]

    d_queries, to_lo, d_kv, to_hi = attend_back(
        block_order,
        seq_lens,
        queries,
        d_mixed,
        mixed,
        lse,
        kv_lo,
        kv,
        kv_hi,
        seq_len,
    )
    out_sum = sum(after(g, d_queries[:8]).astype(F32) for g in grad_wo).astype(BF16)
    d_normed, grad_qkv, totals, gu_sum, grad_out = scatter_normed(
        d_queries,
        d_kv,
        to_lo,
        to_hi,
        lin,
        w_qkv,
        normed_all,
        grad_gu,
        out_sum.reshape(4, 4 * HEAD_SIZE, deep),
        tokens,
        grad_post,
        error,
        q_gain,
        k_gain,
        tables,
    )
    d_tokens, grad_gate, grad_up, grad_down, grad_query, grad_key, grad_value, grad_out = finish(
        d_normed, tokens, d_middle, in_gain, gu_sum, grad_down, grad_qkv, grad_out
    )
    lanes = width // HEAD_SIZE
    count_valid = jnp.sum(seq_lens).astype(F32)
    loss = 0.5 * jnp.sum(totals[2 * lanes + 2]) / (count_valid * MODEL_WIDTH)
    return (
        output,
        loss,
        d_tokens,
        totals[:lanes].reshape(width),
        grad_query,
        grad_key,
        grad_value,
        totals[2 * lanes],
        totals[2 * lanes + 1],
        grad_out,
        totals[lanes : 2 * lanes].reshape(width),
        grad_gate,
        grad_up,
        grad_down.reshape(4 * cols, deep),
    )


def solution(mesh):
    in_specs = (
        P(("ctx", "tp"), None),
        P(("ctx", "tp"), None),
        P(),
        P(),
        P(),
        P("ctx", "tp"),
        P("ctx", "tp"),
        P("ctx", "tp"),
        P(),
        P(),
        P("tp", "ctx"),
        P(),
        P("ctx", "tp"),
        P("ctx", "tp"),
        P("tp", "ctx"),
    )
    out_specs = (
        P(("ctx", "tp"), None),
        P(),
        P(("ctx", "tp"), None),
        P(),
        P("ctx", "tp"),
        P("ctx", "tp"),
        P("ctx", "tp"),
        P(),
        P(),
        P("tp", "ctx"),
        P(),
        P("ctx", "tp"),
        P("ctx", "tp"),
        P("tp", "ctx"),
    )
    body = local_plane if (mesh.shape["ctx"], mesh.shape["tp"]) == (8, 4) else local
    return jax.shard_map(body, mesh=mesh, in_specs=in_specs, out_specs=out_specs, check_vma=False)
```

```python
import functools

import jax
import jax.numpy as jnp
from jax import lax
from jax.experimental import pallas as pl
from jax.experimental.pallas import tpu as pltpu
from jax.sharding import PartitionSpec as P

MODEL_WIDTH = 2048
HEAD_SIZE = 128
SEQS = 3
BLK = 256


EPS = 1e-06
THETA = 1000000.0
FLOOR = -1e30


def from_behind(x, axis, by):
    count = lax.axis_size(axis)
    return lax.ppermute(x, axis, [(i, (i + by) % count) for i in range(count)])


def rms_scale(value):
    return lax.rsqrt(jnp.mean(value * value, axis=-1, keepdims=True) + EPS)


def rms_back(value, scale, grad_normed):
    return scale * grad_normed - value * scale**3 * jnp.mean(
        grad_normed * value, axis=-1, keepdims=True
    )


def rotate(value, cosine, sine):
    half = value.shape[-1] // 2
    first = value[..., :half]
    second = value[..., half:]
    return jnp.concatenate(
        [first * cosine - second * sine, second * cosine + first * sine], axis=-1
    )


def rotate_back(grad, cosine, sine):
    half = grad.shape[-1] // 2
    first = grad[..., :half]
    second = grad[..., half:]
    return jnp.concatenate(
        [first * cosine + second * sine, second * cosine - first * sine], axis=-1
    )


def matmul(left, right):
    return jnp.dot(left, right, preferred_element_type=jnp.float32)


def matmul_tn(left, right):
    return lax.dot_general(
        left, right, (((0,), (0,)), ((), ())), preferred_element_type=jnp.float32
    )


def matmul_nt(left, right):
    return lax.dot_general(
        left, right, (((1,), (1,)), ((), ())), preferred_element_type=jnp.float32
    )


def row_slice(value, start, count):
    return lax.dynamic_slice_in_dim(value, start, count, 0)


def local(
    tokens,
    teacher,
    seq_lens,
    block_order,
    in_gain,
    w_query,
    key_weight_matrix,
    value_weight_matrix,
    q_gain,
    k_gain,
    w_out,
    post_gain,
    w_gate,
    w_up,
    w_down,
):
    ctx_count = lax.axis_size("ctx")
    ctx_index = lax.axis_index("ctx")
    tp_index = lax.axis_index("tp")
    tok_rows = tokens.shape[0]
    ctx_rows = tok_rows * lax.axis_size("tp")
    block_span = 2 * BLK
    q_heads = w_query.shape[1] // HEAD_SIZE
    kv_heads = key_weight_matrix.shape[1] // HEAD_SIZE
    group_width = q_heads // kv_heads
    scale_qk = HEAD_SIZE ** (-0.5)
    weights = (
        lax.all_gather(w_query, "ctx", axis=0, tiled=True),
        lax.all_gather(key_weight_matrix, "ctx", axis=0, tiled=True),
        lax.all_gather(value_weight_matrix, "ctx", axis=0, tiled=True),
        lax.all_gather(w_out, "ctx", axis=1, tiled=True),
        lax.all_gather(w_gate, "ctx", axis=0, tiled=True),
        lax.all_gather(w_up, "ctx", axis=0, tiled=True),
        lax.all_gather(w_down, "ctx", axis=1, tiled=True),
    )
    wq_full, wk_full, wv_full, wo_full, wg_full, wu_full, wd_full = weights
    offsets = jnp.arange(BLK, dtype=jnp.int32)

    def block_positions(owner):
        columns = lax.dynamic_slice_in_dim(block_order, 2 * owner, 2, 1)
        return (columns[:, :, None] * BLK + offsets).reshape(SEQS, block_span)

    query_pos = block_positions(ctx_index)
    flat_pos = query_pos.reshape(-1)
    inverse = THETA ** (-jnp.arange(0, HEAD_SIZE, 2, dtype=jnp.float32) / HEAD_SIZE)
    angle = flat_pos.astype(jnp.float32)[:, None] * inverse[None, :]
    cosine = jnp.cos(angle)[:, None, :]
    sine = jnp.sin(angle)[:, None, :]
    stream = tokens.astype(jnp.float32)
    scale_in = rms_scale(stream)
    unit_in = stream * scale_in
    normed_rows = (unit_in * in_gain).astype(jnp.bfloat16)
    normed_all = lax.all_gather(normed_rows, "tp", axis=0, tiled=True)
    query_lin = matmul(normed_all, wq_full).reshape(ctx_rows, q_heads, HEAD_SIZE)
    key_linear = matmul(normed_all, wk_full).reshape(ctx_rows, kv_heads, HEAD_SIZE)
    value_low = (
        matmul(normed_all, wv_full)
        .astype(jnp.bfloat16)
        .reshape(SEQS, block_span, kv_heads, HEAD_SIZE)
    )
    query_scale = rms_scale(query_lin)
    query_unit = query_lin * query_scale
    query_low = (
        rotate(query_unit * q_gain, cosine, sine)
        .astype(jnp.bfloat16)
        .reshape(SEQS, block_span, kv_heads, group_width, HEAD_SIZE)
    )
    key_scale = rms_scale(key_linear)
    key_unit = key_linear * key_scale
    key_low = (
        rotate(key_unit * k_gain, cosine, sine)
        .astype(jnp.bfloat16)
        .reshape(SEQS, block_span, kv_heads, HEAD_SIZE)
    )

    def scores_of(keys, key_pos):
        raw = (
            jnp.einsum("sqkgd,slkd->skgql", query_low, keys, preferred_element_type=jnp.float32)
            * scale_qk
        )
        allowed = (key_pos[:, None, :] <= query_pos[:, :, None]) & (
            key_pos[:, None, :] < seq_lens[:, None, None]
        )
        allowed = allowed[:, None, None, :, :]
        return (jnp.where(allowed, raw, FLOOR), allowed)

    def absorb(state, keys, value_rows, owner):
        running_top, running_total, running_acc = state
        scores, allowed = scores_of(keys, block_positions(owner))
        new_top = jnp.maximum(running_top, jnp.max(scores, axis=-1))
        weights_now = jnp.where(allowed, jnp.exp(scores - new_top[..., None]), 0.0)
        shrink = jnp.exp(running_top - new_top)
        running_total = running_total * shrink + jnp.sum(weights_now, axis=-1)
        running_acc = running_acc * shrink[..., None] + jnp.einsum(
            "skgql,slkd->skgqd",
            weights_now.astype(jnp.bfloat16),
            value_rows,
            preferred_element_type=jnp.float32,
        )
        return (new_top, running_total, running_acc)

    stat_shape = (SEQS, kv_heads, group_width, block_span)
    initial = (
        jnp.full(stat_shape, FLOOR, jnp.float32),
        jnp.zeros(stat_shape, jnp.float32),
        jnp.zeros(stat_shape + (HEAD_SIZE,), jnp.float32),
    )
    first_state = absorb(initial, key_low, value_low, ctx_index)

    def cycle_turn(carry, turn):
        keys, value_rows, state = carry
        keys, value_rows = from_behind((keys, value_rows), "ctx", 1)
        owner = (ctx_index - turn) % ctx_count
        state = absorb(state, keys, value_rows, owner)
        return ((keys, value_rows, state), (keys, value_rows))

    (unused_keys, unused_values, final_state), (kept_keys, kept_values) = lax.scan(
        cycle_turn, (key_low, value_low, first_state), jnp.arange(1, ctx_count, dtype=jnp.int32)
    )
    all_keys = jnp.concatenate([key_low[None], kept_keys], axis=0)
    all_values = jnp.concatenate([value_low[None], kept_values], axis=0)
    top_final, total_final, acc_final = final_state
    log_total = top_final + jnp.log(total_final)
    attn_exact = acc_final / total_final[..., None]
    mixed_low = (
        jnp.transpose(attn_exact, (0, 3, 1, 2, 4))
        .reshape(ctx_rows, q_heads * HEAD_SIZE)
        .astype(jnp.bfloat16)
    )
    middle = stream + lax.psum_scatter(
        matmul(row_slice(mixed_low, jnp.int32(0), lax.axis_size("tp") * tok_rows), wo_full).astype(
            jnp.bfloat16
        ),
        "tp",
        scatter_dimension=0,
        tiled=True,
    ).astype(jnp.float32)
    scale_post = rms_scale(middle)
    unit_post = middle * scale_post
    post_rows = (unit_post * post_gain).astype(jnp.bfloat16)
    post_all = lax.all_gather(post_rows, "tp", axis=0, tiled=True)
    gate = matmul(post_all, wg_full)
    up_val = matmul(post_all, wu_full)
    sigma = jax.nn.sigmoid(gate)
    active = gate * sigma
    hidden_low = (active * up_val).astype(jnp.bfloat16)
    result = middle + lax.psum_scatter(
        matmul(row_slice(hidden_low, jnp.int32(0), lax.axis_size("tp") * tok_rows), wd_full).astype(
            jnp.bfloat16
        ),
        "tp",
        scatter_dimension=0,
        tiled=True,
    ).astype(jnp.float32)
    output = result.astype(jnp.bfloat16)
    valid_all = (query_pos < seq_lens[:, None]).reshape(-1).astype(jnp.float32)
    valid_rows = row_slice(valid_all, tp_index * tok_rows, tok_rows)
    diff = (result - teacher.astype(jnp.float32)) * valid_rows[:, None]
    error_local = jnp.sum(diff * diff)
    diff_low = diff.astype(jnp.bfloat16)
    diff_all = lax.all_gather(diff_low, "tp", axis=0, tiled=True)
    weights_two = (
        lax.all_gather(w_query, "ctx", axis=0, tiled=True),
        lax.all_gather(key_weight_matrix, "ctx", axis=0, tiled=True),
        lax.all_gather(value_weight_matrix, "ctx", axis=0, tiled=True),
        lax.all_gather(w_out, "ctx", axis=1, tiled=True),
        lax.all_gather(w_gate, "ctx", axis=0, tiled=True),
        lax.all_gather(w_up, "ctx", axis=0, tiled=True),
        lax.all_gather(w_down, "ctx", axis=1, tiled=True),
    )
    bq_full, bk_full, bv_full, bo_full, bg_full, bu_full, bd_full = weights_two
    grad_wd = matmul_tn(hidden_low, diff_all)
    d_hidden = matmul_nt(diff_all, bd_full)
    d_gate = (d_hidden * up_val * sigma * (1.0 + gate * (1.0 - sigma))).astype(jnp.bfloat16)
    d_up = (d_hidden * active).astype(jnp.bfloat16)
    grad_wg = matmul_tn(post_all, d_gate)
    grad_wu = matmul_tn(post_all, d_up)
    start = jnp.int32(0)
    d_post = lax.psum_scatter(
        (
            matmul_nt(row_slice(d_gate, start, lax.axis_size("tp") * tok_rows), bg_full)
            + matmul_nt(row_slice(d_up, start, lax.axis_size("tp") * tok_rows), bu_full)
        ).astype(jnp.bfloat16),
        "tp",
        scatter_dimension=0,
        tiled=True,
    ).astype(jnp.float32)
    grad_post_local = jnp.sum(d_post * unit_post, axis=0)
    d_middle = diff + rms_back(middle, scale_post, d_post * post_gain)
    d_mid_low = d_middle.astype(jnp.bfloat16)
    d_mid_all = lax.all_gather(d_mid_low, "tp", axis=0, tiled=True)
    grad_wo = matmul_tn(mixed_low, d_mid_all)
    d_mixed = matmul_nt(d_mid_all, bo_full).astype(jnp.bfloat16)
    d_mixed_grid = jnp.transpose(
        d_mixed.reshape(SEQS, block_span, kv_heads, group_width, HEAD_SIZE), (0, 2, 3, 1, 4)
    )
    delta = jnp.sum(d_mixed_grid.astype(jnp.float32) * attn_exact, axis=-1)

    def revisit(carry, turn):
        grad_queries, grad_keys, grad_values = carry
        owner = (ctx_index - turn) % ctx_count
        keys = all_keys[turn]
        value_rows = all_values[turn]
        scores, allowed = scores_of(keys, block_positions(owner))
        probs = jnp.where(allowed, jnp.exp(scores - log_total[..., None]), 0.0)
        probs_low = probs.astype(jnp.bfloat16)
        d_probs = jnp.einsum(
            "skgqd,slkd->skgql", d_mixed_grid, value_rows, preferred_element_type=jnp.float32
        )
        d_scores = (probs * (d_probs - delta[..., None])).astype(jnp.bfloat16)
        grad_queries = grad_queries + jnp.einsum(
            "skgql,slkd->skgqd", d_scores, keys, preferred_element_type=jnp.float32
        )
        grad_keys = grad_keys + jnp.einsum(
            "skgql,sqkgd->slkd", d_scores, query_low, preferred_element_type=jnp.float32
        )
        grad_values = grad_values + jnp.einsum(
            "skgql,skgqd->slkd", probs_low, d_mixed_grid, preferred_element_type=jnp.float32
        )
        grad_keys, grad_values = (
            from_behind(grad_keys.astype(jnp.bfloat16), "ctx", 1).astype(grad_keys.dtype),
            from_behind(grad_values.astype(jnp.bfloat16), "ctx", 1).astype(grad_values.dtype),
        )
        return ((grad_queries, grad_keys, grad_values), None)

    kv_shape = (SEQS, block_span, kv_heads, HEAD_SIZE)
    start_carry = (
        jnp.zeros(stat_shape + (HEAD_SIZE,), jnp.float32),
        jnp.zeros(kv_shape, jnp.float32),
        jnp.zeros(kv_shape, jnp.float32),
    )
    (grad_queries, grad_keys, grad_values), unused_out = lax.scan(
        revisit, start_carry, jnp.arange(ctx_count, dtype=jnp.int32)
    )
    grad_queries = (
        jnp.transpose(grad_queries, (0, 3, 1, 2, 4)).reshape(ctx_rows, q_heads, HEAD_SIZE)
        * scale_qk
    )
    grad_keys = grad_keys.reshape(ctx_rows, kv_heads, HEAD_SIZE) * scale_qk
    d_values = grad_values.reshape(ctx_rows, kv_heads * HEAD_SIZE).astype(jnp.bfloat16)
    query_back = rotate_back(grad_queries, cosine, sine)
    grad_q_local = jnp.sum(query_back * query_unit, axis=(0, 1))
    d_query_lin = (
        rms_back(query_lin, query_scale, query_back * q_gain)
        .reshape(ctx_rows, q_heads * HEAD_SIZE)
        .astype(jnp.bfloat16)
    )
    key_back = rotate_back(grad_keys, cosine, sine)
    grad_k_local = jnp.sum(key_back * key_unit, axis=(0, 1))
    d_key_lin = (
        rms_back(key_linear, key_scale, key_back * k_gain)
        .reshape(ctx_rows, kv_heads * HEAD_SIZE)
        .astype(jnp.bfloat16)
    )
    grad_wq = matmul_tn(normed_all, d_query_lin)
    grad_wk = matmul_tn(normed_all, d_key_lin)
    grad_wv = matmul_tn(normed_all, d_values)
    start = jnp.int32(0)
    part_query = matmul_nt(row_slice(d_query_lin, start, lax.axis_size("tp") * tok_rows), bq_full)
    part_key = matmul_nt(row_slice(d_key_lin, start, lax.axis_size("tp") * tok_rows), bk_full)
    part_value = matmul_nt(row_slice(d_values, start, lax.axis_size("tp") * tok_rows), bv_full)
    d_normed = lax.psum_scatter(
        (part_query + part_key + part_value).astype(jnp.bfloat16),
        "tp",
        scatter_dimension=0,
        tiled=True,
    ).astype(jnp.float32)
    grad_in_local = jnp.sum(d_normed * unit_in, axis=0)
    d_tokens = (d_middle + rms_back(stream, scale_in, d_normed * in_gain)).astype(jnp.bfloat16)
    summed = (
        lax.psum_scatter(
            grad_wq.astype(jnp.bfloat16), "ctx", scatter_dimension=0, tiled=True
        ).astype(jnp.float32),
        lax.psum_scatter(
            grad_wk.astype(jnp.bfloat16), "ctx", scatter_dimension=0, tiled=True
        ).astype(jnp.float32),
        lax.psum_scatter(
            grad_wv.astype(jnp.bfloat16), "ctx", scatter_dimension=0, tiled=True
        ).astype(jnp.float32),
        lax.psum_scatter(
            grad_wo.astype(jnp.bfloat16), "ctx", scatter_dimension=1, tiled=True
        ).astype(jnp.float32),
        lax.psum_scatter(
            grad_wg.astype(jnp.bfloat16), "ctx", scatter_dimension=0, tiled=True
        ).astype(jnp.float32),
        lax.psum_scatter(
            grad_wu.astype(jnp.bfloat16), "ctx", scatter_dimension=0, tiled=True
        ).astype(jnp.float32),
        lax.psum_scatter(
            grad_wd.astype(jnp.bfloat16), "ctx", scatter_dimension=1, tiled=True
        ).astype(jnp.float32),
    )
    totals = lax.psum(
        (grad_in_local, grad_q_local, grad_k_local, grad_post_local, error_local), ("ctx", "tp")
    )
    count_valid = jnp.sum(seq_lens).astype(jnp.float32)
    loss = 0.5 * totals[4] / (count_valid * MODEL_WIDTH)
    return (
        output,
        loss,
        d_tokens,
        totals[0],
        summed[0],
        summed[1],
        summed[2],
        totals[1],
        totals[2],
        summed[3],
        totals[3],
        summed[4],
        summed[5],
        summed[6],
    )


F32 = jnp.float32
BF16 = jnp.bfloat16
MESH = pl.DeviceIdType.MESH
VMEM_LIMIT = 62 << 20


def busy(us):
    return pl.CostEstimate(flops=0, bytes_accessed=us * 3_000_000, transcendentals=0)

LOG2E = 1.4426950408889634
UNIT = 128
KEYS = 512
CORE_GROUPS = [[0, 2, 4, 6], [1, 3, 5, 7]]
SIBLING = [(i, i ^ 1) for i in range(8)]


def spec_vmem():
    return pl.BlockSpec(memory_space=pltpu.VMEM)


def spec_any():
    return pl.BlockSpec(memory_space=pl.ANY)


def spec_smem():
    return pl.BlockSpec(memory_space=pltpu.SMEM)


def plane_neighbours():
    me = lax.axis_index("ctx")
    core = lax.rem(me, 2)
    x = lax.rem(me // 2, 2)
    y = me // 4
    sib = me + 1 - 2 * core
    nx = me + 2 - 4 * x
    ny = me + 4 - 8 * y
    dg = nx + 4 - 8 * y
    return me, sib, nx, ny, dg


def greet(devices):
    barrier = pltpu.get_barrier_semaphore()
    for device in devices:
        pl.semaphore_signal(barrier, inc=1, device_id={"ctx": device}, device_id_type=MESH)
    pl.semaphore_wait(barrier, len(devices))


def pick(step, options):
    value = options[0]
    for i in range(1, len(options)):
        value = jnp.where(step == i, options[i], value)
    return value


SUBS = 4
BY_X, BY_Y = (0, 2, 1, 3), (1, 3, 0, 2)


def on_ctx(device):
    return {"ctx": device}


def on_plane(plane):
    return {"tp": plane}


def send(src, dst, send_sem, recv_sem, where):
    return pltpu.make_async_remote_copy(
        src_ref=src,
        dst_ref=dst,
        send_sem=send_sem,
        recv_sem=recv_sem,
        device_id=where,
        device_id_type=MESH,
    )


class Gather:
    def __init__(self, x_ref, xs, local_sem, send_sems, recv_sems):
        self.x_ref, self.xs = x_ref, xs
        self.local_sem, self.send_sems, self.recv_sems = local_sem, send_sems, recv_sems
        self.me, self.sib, self.nx, self.ny, self.dg = plane_neighbours()
        self.shift = self.sib - self.me
        self.piece = x_ref.shape[0] // SUBS

    def part(self, block, s):
        return self.xs.at[block, pl.ds(s * self.piece, self.piece)]

    def remote(self, src, kind, block, s, device):
        return send(
            src, self.part(block, s), self.send_sems.at[kind, s], self.recv_sems.at[block, s], on_ctx(device)
        )

    def own(self, s):
        return self.x_ref.at[pl.ds(s * self.piece, self.piece)]

    def start(self):
        for s, t in zip(BY_X, BY_Y):
            self.remote(self.own(s), 0, self.me, s, self.nx).start()
            self.remote(self.own(t), 1, self.me, t, self.ny).start()
        for s in range(SUBS):
            self.remote(self.own(s), 2, self.me, s, self.sib).start()
        keep = pltpu.make_async_copy(self.x_ref, self.xs.at[self.me], self.local_sem)
        keep.start()
        keep.wait()

    def arrived(self, block, s):
        self.remote(self.part(block, s), 0, block, s, self.sib).wait_recv()

    def relay(self, kind, block, s, device):
        self.remote(self.part(block, s), kind, block, s, device).start()

    def pass_on(self, i):
        s, t = BY_X[i], BY_Y[i]
        self.arrived(self.nx, s)
        if s % 2 == 0:
            self.relay(3, self.nx, s, self.ny)
        self.relay(4, self.nx, s, self.sib)
        self.arrived(self.ny, t)
        if t % 2 == 1:
            self.relay(3, self.ny, t, self.nx)
        self.relay(5, self.ny, t, self.sib)

    def far_half(self, h):
        for s in (2 * h, 2 * h + 1):
            self.arrived(self.dg, s)
            self.relay(6, self.dg, s, self.sib)

    def all_of(self, block, pieces=range(SUBS)):
        for s in pieces:
            self.arrived(block, s)

    def pass_all(self):
        for i in range(SUBS):
            self.pass_on(i)

    def before(self, step, passing=True):
        for at, act in (
            (1, lambda: self.all_of(self.sib)),
            (2, self.pass_all if passing else lambda: None),
            (3, lambda: self.all_of(self.nx + self.shift)),
            (4, lambda: self.far_half(0)),
            (5, lambda: self.all_of(self.ny + self.shift)),
            (6, lambda: self.far_half(1)),
            (7, lambda: self.all_of(self.dg + self.shift)),
        ):
            pl.when(step == at)(act)

    def before_half(self, step):
        for at, act in (
            (2, lambda: self.all_of(self.sib)),
            (4, self.pass_all),
            (6, lambda: self.all_of(self.nx + self.shift)),
            (8, lambda: self.far_half(0)),
            (10, lambda: self.all_of(self.ny + self.shift)),
            (13, lambda: self.all_of(self.dg + self.shift, (0, 1))),
            (14, lambda: self.far_half(1)),
            (15, lambda: self.all_of(self.dg + self.shift, (2, 3))),
        ):
            pl.when(step == at)(act)

    def block(self, step):
        near = (self.me, self.nx, self.ny, self.dg)
        return pick(step, [b + o for b in near for o in (0, self.shift)])

    def half_block(self, step):
        last = step >= 12
        n = jnp.where(last, 6 + lax.rem(step, 2), step // 2)
        return self.block(n), jnp.where(last, (step - 12) // 2, lax.rem(step, 2))

    def finish(self):
        for s in range(SUBS):
            for kind in range(7):
                self.remote(self.part(self.me, s), kind, self.me, s, self.sib).wait_send()


def gather_scratch(rows, width):
    return [
        pltpu.VMEM((8, rows, width), BF16),
        pltpu.SemaphoreType.DMA,
        pltpu.SemaphoreType.DMA((7, SUBS)),
        pltpu.SemaphoreType.DMA((8, SUBS)),
    ]


class Scatter:
    def __init__(self, to_sib, from_sib, own, diag_out, diag_in, x_out, y_out, x_in, y_in, sends, recvs):
        self.to_sib, self.from_sib, self.own = to_sib, from_sib, own
        self.diag_out, self.diag_in = diag_out, diag_in
        self.x_out, self.y_out, self.x_in, self.y_in = x_out, y_out, x_in, y_in
        self.sends, self.recvs = sends, recvs
        self.me, self.sib, self.nx, self.ny, self.dg = plane_neighbours()
        self.rows = diag_out.shape[0]

    def round(self, i):
        return pl.ds(i * (self.rows // 2), self.rows // 2)

    def piece(self, i, half):
        quarter = self.rows // 4
        return pl.ds((2 * i + half) * quarter, quarter)

    def remote(self, src, dst, kind, i, device):
        return send(src, dst, self.sends.at[kind, i], self.recvs.at[kind, i], on_ctx(device))

    def sibling(self, n, i):
        at = self.round(i)
        return self.remote(self.to_sib.at[n, at], self.from_sib.at[n, at], n, i, self.sib)

    def hop(self, kind, i):
        out, into, half, device = (
            (self.diag_out, self.diag_in, 0, self.nx),
            (self.diag_out, self.diag_in, 1, self.ny),
            (self.x_out, self.x_in, 0, self.nx),
            (self.x_out, self.x_in, 1, self.nx),
            (self.y_out, self.y_in, 0, self.ny),
            (self.y_out, self.y_in, 1, self.ny),
        )[kind]
        at = self.piece(i, half)
        return self.remote(out.at[at], into.at[at], 4 + kind, i, device)

    def blocks(self):
        shift = self.sib - self.me
        return [b + o for b in (self.dg, self.nx, self.ny, self.me) for o in (shift, 0)]

    def block(self, step):
        return pick(2 * (step // 4) + lax.rem(step, 2), self.blocks())

    def chip_sum(self, n, at):
        return self.own[n, at].astype(F32) + self.from_sib[n, at].astype(F32)

    def step(self, step, product, late=False):
        block = self.block(step)
        n = step // 4
        i = lax.rem(step, 4) // 2
        at = self.round(pl.multiple_of(i, 1))

        @pl.when(lax.rem(step, 2) == 0)
        def _():
            product(block, at, self.to_sib, n)
            self.sibling(n, i).start()

        @pl.when(lax.rem(step, 2) == 1)
        def _():
            product(block, at, self.own, n)
            self.sibling(n, i).wait_recv()

        for r in range(2):
            first, second = self.piece(r, 0), self.piece(r, 1)

            @pl.when(step == 1 + 2 * r)
            def _():
                self.diag_out[first] = self.chip_sum(0, first).astype(BF16)
                self.hop(0, r).start()
                self.diag_out[second] = self.chip_sum(0, second).astype(BF16)
                self.hop(1, r).start()

            @pl.when(step == 5 + 2 * r)
            def _():
                self.x_out[first] = self.chip_sum(1, first).astype(BF16)
                self.hop(2, r).start()

            @pl.when(step == 9 + 2 * r)
            def _():
                self.y_out[second] = self.chip_sum(2, second).astype(BF16)
                self.hop(5, r).start()

        if not late:

            @pl.when(step == 11)
            def _():
                self.second_wave()

    def second_wave(self):
        for i in range(2):
            first, second = self.piece(i, 0), self.piece(i, 1)
            self.hop(0, i).wait_recv()
            self.y_out[first] = (self.chip_sum(2, first) + self.diag_in[first].astype(F32)).astype(BF16)
            self.hop(4, i).start()
            self.hop(1, i).wait_recv()
            self.x_out[second] = (self.chip_sum(1, second) + self.diag_in[second].astype(F32)).astype(BF16)
            self.hop(3, i).start()

    def finish(self, o_ref):
        for i in range(2):
            for kind in range(2, 6):
                self.hop(kind, i).wait_recv()
            at = self.round(i)
            o_ref[at] = (
                self.chip_sum(3, at) + self.x_in[at].astype(F32) + self.y_in[at].astype(F32)
            ).astype(o_ref.dtype)
        for i in range(2):
            for n in range(4):
                self.sibling(n, i).wait_send()
            for kind in range(6):
                self.hop(kind, i).wait_send()


def scatter_scratch(rows, width):
    four = pltpu.VMEM((4, rows, width), BF16)
    one = pltpu.VMEM((rows, width), BF16)
    return [four] * 3 + [one] * 6 + [pltpu.SemaphoreType.DMA((10, 2)), pltpu.SemaphoreType.DMA((10, 2))]


N_SCATTER = 11


def nn(left, right):
    return lax.dot_general(left, right, (((1,), (0,)), ((), ())), preferred_element_type=F32)


def nt(left, right):
    return lax.dot_general(left, right, (((1,), (1,)), ((), ())), preferred_element_type=F32)


def tn(left, right):
    return lax.dot_general(left, right, (((0,), (0,)), ((), ())), preferred_element_type=F32)


def comm_params(collective_id):
    return pltpu.CompilerParams(
        collective_id=collective_id, has_side_effects=True, vmem_limit_bytes=VMEM_LIMIT
    )


def greet_column(devices):
    barrier = pltpu.get_barrier_semaphore()
    plane, planes = lax.axis_index("tp"), lax.axis_size("tp")
    for device in devices:
        pl.semaphore_signal(barrier, inc=1, device_id=on_ctx(device), device_id_type=MESH)
    for step in (1, planes - 1):
        where = on_plane(lax.rem(plane + step, planes))
        pl.semaphore_signal(barrier, inc=1, device_id=where, device_id_type=MESH)
    pl.semaphore_wait(barrier, len(devices) + 2)


class Line:
    def __init__(self, up_src, down_src, from_lo, from_hi, sends, recvs, rows, back):
        self.up_src, self.down_src, self.from_lo, self.from_hi = up_src, down_src, from_lo, from_hi
        self.sends, self.recvs = sends, recvs
        self.units = rows // UNIT
        self.back = back
        self.plane, self.planes = lax.axis_index("tp"), lax.axis_size("tp")

    def at(self, block, i):
        return pl.ds(pl.multiple_of((block * self.units + i) * UNIT, UNIT), UNIT)

    def up(self, block, i):
        at, n = self.at(block, i), block * self.units + i
        return send(self.up_src.at[at], self.from_lo.at[at], self.sends.at[0, n], self.recvs.at[0, n], on_plane(self.plane + 1))

    def down(self, block, i):
        at, n = self.at(block, i), block * self.units + i
        return send(self.down_src.at[at], self.from_hi.at[at], self.sends.at[1, n], self.recvs.at[1, n], on_plane(self.plane - 1))

    def each(self, block, ups, downs):
        for i in range(self.units):
            up = i < self.plane + 1 if self.back else i >= self.plane
            down = i >= self.plane - 1 if self.back else i < self.plane

            @pl.when(up & (self.plane < self.planes - 1))
            def _():
                ups(self.up(block, i))

            @pl.when(down & (self.plane > 0))
            def _():
                downs(self.down(block, i))

    def start(self, block):
        self.each(block, lambda copy: copy.start(), lambda copy: copy.start())

    def sent(self, block):
        self.each(block, lambda copy: copy.wait_send(), lambda copy: copy.wait_send())

    def arrived(self, block):
        for i in range(self.units):
            below = i < self.plane if self.back else i >= self.plane - 1
            above = i >= self.plane if self.back else i < self.plane + 1

            @pl.when(below & (self.plane > 0))
            def _():
                self.up(block, i).wait_recv()

            @pl.when(above & (self.plane < self.planes - 1))
            def _():
                self.down(block, i).wait_recv()


class ChipSwap:
    def __init__(self, src, dst, local_sem, send_sems, recv_sems):
        self.src, self.dst = src, dst
        self.local_sem, self.send_sems, self.recv_sems = local_sem, send_sems, recv_sems
        me, _, nx, ny, dg = plane_neighbours()
        self.chip, self.away = me // 2, (dg, nx, ny)

    def part(self, chip):
        if len(self.src.shape) == 3:
            return self.src.at[chip]
        cols = self.src.shape[1] // 4
        return self.src.at[:, pl.ds(pl.multiple_of(chip * cols, HEAD_SIZE), cols)]

    def own(self):
        return pltpu.make_async_copy(self.part(self.chip), self.dst.at[self.chip], self.local_sem)

    def to(self, n):
        there = self.away[n]
        return send(
            self.part(there // 2), self.dst.at[self.chip], self.send_sems.at[n], self.recv_sems.at[self.chip], on_ctx(there)
        )

    def start(self):
        self.own().start()
        for n in range(3):
            self.to(n).start()

    def arrive(self):
        self.own().wait()
        for n in range(3):
            there = self.away[n] // 2
            send(
                self.part(there), self.dst.at[there], self.send_sems.at[n], self.recv_sems.at[there], on_ctx(self.away[n])
            ).wait_recv()

    def sent(self):
        for n in range(3):
            self.to(n).wait_send()

    def finish(self):
        self.arrive()
        self.sent()


SWAP_SCRATCH = [pltpu.SemaphoreType.DMA, pltpu.SemaphoreType.DMA((3,)), pltpu.SemaphoreType.DMA((4,))]


class LineGather:
    def __init__(self, src, dst, local_sem, send_sems, recv_sems):
        self.src, self.dst = src, dst
        self.local_sem, self.send_sems, self.recv_sems = local_sem, send_sems, recv_sems
        self.plane, self.planes = lax.axis_index("tp"), lax.axis_size("tp")
        self.pieces = src.shape[0]

    def own(self):
        return pltpu.make_async_copy(self.src, self.dst.at[self.plane], self.local_sem)

    def copy(self, way, hop, n, origin):
        src = self.src.at[n] if hop == 0 else self.dst.at[origin, n]
        return send(
            src,
            self.dst.at[origin, n],
            self.send_sems.at[way, hop, n],
            self.recv_sems.at[origin, n],
            on_plane(self.plane + 1 - 2 * way),
        )

    def ways(self, hop):
        up, down = self.plane - hop, self.plane + hop
        yield 0, up, up >= 0, self.plane < self.planes - 1
        yield 1, down, down < self.planes, self.plane > 0

    def start(self):
        self.own().start()
        for way, origin, _, goes_on in self.ways(0):

            @pl.when(goes_on)
            def _():
                for n in range(self.pieces):
                    self.copy(way, 0, n, origin).start()

    def arrive(self, hop, then=None):
        for way, origin, there, goes_on in self.ways(hop):

            @pl.when(there)
            def _():
                for n in range(self.pieces):
                    self.copy(way, 0, n, origin).wait_recv()
                    if hop == self.planes - 1:
                        continue

                    @pl.when(goes_on)
                    def _():
                        self.copy(way, hop, n, origin).start()

                if then is not None:
                    then(origin)

    def finish(self):
        self.own().wait()
        self.sent()

    def sent(self):
        for hop in range(self.planes - 1):
            for way, origin, there, goes_on in self.ways(hop):

                @pl.when(there & goes_on)
                def _():
                    for n in range(self.pieces):
                        self.copy(way, hop, n, origin).wait_send()


def line_scratch(pieces):
    dma = pltpu.SemaphoreType.DMA
    return [dma, dma((2, 3, pieces)), dma((4, pieces))]


class LineSum:
    def __init__(self, own, up_in, down_in, send_sems, recv_sems):
        self.own, self.into = own, (up_in, down_in)
        self.send_sems, self.recv_sems = send_sems, recv_sems
        self.plane, self.planes = lax.axis_index("tp"), lax.axis_size("tp")

    def copy(self, way, p, first):
        into = self.into[way]
        return send(
            self.own(p) if first else into.at[p],
            into.at[p],
            self.send_sems.at[way, p],
            self.recv_sems.at[way, p],
            on_plane(self.plane + 1 - 2 * way),
        )

    def moves(self, k):
        last = self.planes - 1
        for way in range(2):
            z = last - k if way else k
            yield way, z, (range(z) if way else range(last, z, -1))

    def stage(self, k):
        for way, z, ends in self.moves(k):

            @pl.when(self.plane == z)
            def _():
                for p in ends:
                    copy = self.copy(way, p, k == 0)
                    if k > 0:
                        copy.wait_recv()
                        into = self.into[way]
                        into[p] = (self.own(p)[...].astype(F32) + into[p].astype(F32)).astype(BF16)
                    copy.start()

    def collect(self, out):
        out[...] = self.own(self.plane)[...].astype(F32)
        for way in range(2):

            @pl.when(self.plane < self.planes - 1 if way else self.plane > 0)
            def _():
                self.copy(way, self.plane, False).wait_recv()
                out[...] += self.into[way][self.plane].astype(F32)

    def finish(self):
        for k in range(self.planes - 1):
            for way, z, ends in self.moves(k):

                @pl.when(self.plane == z)
                def _():
                    for p in ends:
                        self.copy(way, p, k == 0).wait_send()


class Total:
    def __init__(self, held, held_planes, sends, recvs):
        self.held, self.held_planes, self.sends, self.recvs = held, held_planes, sends, recvs
        self.me = lax.axis_index("ctx")
        self.plane, self.planes = lax.axis_index("tp"), lax.axis_size("tp")
        self.away = others(self.me)
        self.far = [lax.rem(self.plane + step, self.planes) for step in range(1, self.planes)]

    def here(self, c, n):
        ref = self.held.at[c]
        return send(ref, ref, self.sends.at[n], self.recvs.at[c], on_ctx(self.away[n]))

    def there(self, p, n):
        ref = self.held_planes.at[p]
        return send(ref, ref, self.sends.at[7 + n], self.recvs.at[8 + p], on_plane(self.far[n]))

    def start(self):
        for n in range(7):
            self.here(self.me, n).start()

    def middle(self):
        for n, c in enumerate(self.away):
            self.here(c, n).wait_recv()
        value = self.held[0]
        for c in range(1, 8):
            value += self.held[c]
        self.held_planes[self.plane] = value
        for n in range(len(self.far)):
            self.there(self.plane, n).start()

    def finish(self, out):
        for n, p in enumerate(self.far):
            self.there(p, n).wait_recv()
        value = self.held_planes[0]
        for p in range(1, 4):
            value += self.held_planes[p]
        out[...] = value
        for n in range(7):
            self.here(self.me, n).wait_send()
        for n in range(len(self.far)):
            self.there(self.plane, n).wait_send()


class Turn:
    def __init__(self, ca_ref, sa_ref, cb_ref, sb_ref, unit):
        ca, sa = ca_ref[pl.ds(unit, 1), :], sa_ref[pl.ds(unit, 1), :]
        cb, sb = cb_ref[...], sb_ref[...]
        self.cosine = ca * cb - sa * sb
        sine = sa * cb + ca * sb
        lane = lax.broadcasted_iota(jnp.int32, sine.shape, 1)
        self.sine = jnp.where(lane < HEAD_SIZE // 2, -sine, sine)

    def forth(self, v):
        return v * self.cosine + pltpu.roll(v, HEAD_SIZE // 2, 1) * self.sine

    def back(self, v):
        return v * self.cosine - pltpu.roll(v, HEAD_SIZE // 2, 1) * self.sine


def others(me):
    _, sib, nx, ny, dg = plane_neighbours()
    shift = sib - me
    return (dg, dg + shift, nx, nx + shift, ny, ny + shift, sib)


def qkv_kernel(
    x_ref,
    home_ref,
    qg_ref,
    kg_ref,
    ca_ref,
    sa_ref,
    cb_ref,
    sb_ref,
    gate_ref,
    up_ref,
    down_ref,
    out_ref,
    all_ref,
    w_out_ref,
    q_ref,
    kv_ref,
    lo_ref,
    hi_ref,
    lin_ref,
    gates_ref,
    ups_ref,
    downs_ref,
    outs_ref,
    xs,
    local_sem,
    send_sems,
    recv_sems,
    keep_sems,
    w,
    w_local,
    w_sends,
    w_recvs,
    slab,
    gate_part,
    kv_sends,
    kv_recvs,
    *sems,
):
    ring = Gather(x_ref, xs, local_sem, send_sems, recv_sems)
    me = ring.me
    rows = x_ref.shape[0]
    deep = home_ref.shape[1]
    slabs = LineGather(home_ref, slab, *sems[0:3])
    outs = LineGather(out_ref, outs_ref, *sems[3:6])
    gates = LineGather(gate_part.at[pl.ds(0, 3)], gates_ref, *sems[6:9])
    gate_swap = ChipSwap(gate_ref, gate_part, *sems[9:12])
    late_swaps = (ChipSwap(up_ref, ups_ref.at[pl.ds(0, 4)], *sems[12:15]), ChipSwap(down_ref, downs_ref, *sems[15:18]))
    line = Line(kv_ref, kv_ref, lo_ref, hi_ref, kv_sends, kv_recvs, rows, False)

    def weight(source, origin, k):
        return send(
            slab.at[origin, k],
            w.at[pl.ds(source * deep, deep)],
            w_sends.at[2 * origin + k],
            w_recvs.at[source],
            on_ctx(2 * origin + k),
        )

    own_weight = pltpu.make_async_copy(
        slab.at[me // 2, lax.rem(me, 2)], w.at[pl.ds(me * deep, deep)], w_local
    )

    def hand_out(origin):
        for k in range(2):

            @pl.when(2 * origin + k == me)
            def _():
                own_weight.start()

            @pl.when(2 * origin + k != me)
            def _():
                weight(me, origin, k).start()

    greet_column(others(me))
    gate_swap.start()
    slabs.start()
    ring.start()
    slabs.own().wait()
    hand_out(slabs.plane)
    slabs.arrive(1, hand_out)
    gate_swap.arrive()
    gates.start()
    keep_last = pltpu.make_async_copy(gate_part.at[3], ups_ref.at[4], sems[18])
    keep_last.start()
    slabs.arrive(2, hand_out)
    outs.start()
    ring.pass_on(0)
    slabs.arrive(3, hand_out)
    for i in range(1, SUBS):
        ring.pass_on(i)
    for swap in late_swaps:
        swap.start()
    outs.arrive(1)
    gates.arrive(1)
    own_weight.wait()
    for device in others(me):
        weight(device, 0, 0).wait_recv()
    keep_w = pltpu.make_async_copy(w, w_out_ref, w_local)
    keep_w.start()

    def keep(block):
        return pltpu.make_async_copy(xs.at[block], all_ref.at[block], keep_sems.at[block])

    def head(v, gain_ref, turn):
        scale = lax.rsqrt(jnp.mean(v * v, axis=-1, keepdims=True) + EPS)
        return turn.forth(v * scale * gain_ref[...])

    def turn(step, carry):
        @pl.when(step == 4)
        def _():
            outs.arrive(2)
            gates.arrive(2)

        ring.before(step, passing=False)
        block = ring.block(step)
        keep(block).start()
        lin = nn(xs[block], w[...])
        lin_ref[pl.ds(pl.multiple_of(block * rows, rows), rows), :] = lin[:, : 3 * HEAD_SIZE]
        for i in range(rows // UNIT):
            unit = block * (rows // UNIT) + i
            rotation = Turn(ca_ref, sa_ref, cb_ref, sb_ref, unit)
            here = pl.ds(pl.multiple_of(unit * UNIT, UNIT), UNIT)
            part = lin[i * UNIT : (i + 1) * UNIT]
            for h in range(2):
                lanes = slice(h * HEAD_SIZE, (h + 1) * HEAD_SIZE)
                query = head(part[:, lanes], qg_ref, rotation)
                q_ref[here, lanes] = (query * (HEAD_SIZE**-0.5 * LOG2E)).astype(BF16)
            key = head(part[:, 2 * HEAD_SIZE : 3 * HEAD_SIZE], kg_ref, rotation)
            kv_ref[here, :HEAD_SIZE] = key.astype(BF16)
            kv_ref[here, HEAD_SIZE:] = part[:, 3 * HEAD_SIZE :].astype(BF16)

        line.start(block)
        return carry

    lax.fori_loop(0, 8, turn, 0)
    ring.finish()
    keep_w.wait()
    for origin in range(4):
        for k in range(2):

            @pl.when(2 * origin + k != me)
            def _():
                weight(me, origin, k).wait_send()

    for block in range(8):
        keep(block).wait()

    def settle(block, carry):
        line.sent(block)
        line.arrived(block)
        return carry

    lax.fori_loop(0, 8, settle, 0)
    for gather in (outs, gates):
        gather.arrive(3)
    for gather in (slabs, outs, gates):
        gather.finish() if gather is not slabs else gather.sent()
    gate_swap.sent()
    keep_last.wait()
    for swap in late_swaps:
        swap.finish()


def gather_qkv(normed, home, q_gain, k_gain, tables, gate, up, down, out):
    rows, width = normed.shape
    _, deep, cols = home.shape
    part = (4, gate.shape[0], gate.shape[1] // 4)
    flat = jax.ShapeDtypeStruct((8 * rows, 2 * HEAD_SIZE), BF16)
    dma = pltpu.SemaphoreType.DMA
    return pl.pallas_call(
        qkv_kernel,
        out_shape=(
            jax.ShapeDtypeStruct((8, rows, width), BF16),
            jax.ShapeDtypeStruct((8 * deep, cols), BF16),
            flat,
            flat,
            flat,
            flat,
            jax.ShapeDtypeStruct((8 * rows, 3 * HEAD_SIZE), F32),
            jax.ShapeDtypeStruct((4, 3) + part[1:], BF16),
            jax.ShapeDtypeStruct((5,) + part[1:], BF16),
            jax.ShapeDtypeStruct(down.shape, BF16),
            jax.ShapeDtypeStruct((4,) + out.shape, BF16),
        ),
        in_specs=[spec_any()] * 2 + [spec_vmem()] * 6 + [spec_any()] * 4,
        out_specs=(spec_any(), spec_any(), spec_vmem(), spec_vmem(), spec_any(), spec_any(), spec_vmem())
        + (spec_any(),) * 4,
        scratch_shapes=gather_scratch(rows, width)
        + [
            dma((8,)),
            pltpu.VMEM((8 * deep, cols), BF16),
            dma,
            dma((8,)),
            dma((8,)),
            pltpu.VMEM((4,) + home.shape, BF16),
            pltpu.VMEM(part, BF16),
            dma((2, 8 * rows // UNIT)),
            dma((2, 8 * rows // UNIT)),
        ]
        + line_scratch(home.shape[0])
        + line_scratch(out.shape[0])
        + line_scratch(3)
        + SWAP_SCRATCH * 3
        + [dma],
        compiler_params=comm_params(1),
        cost_estimate=busy(100),
        name="gather_qkv",
    )(normed, home, q_gain.reshape(1, -1), k_gain.reshape(1, -1), *tables, gate, up, down, out)


class Halves:
    def __init__(self, parts, at, local_sems, send_sems, recv_sems):
        self.parts, self.at = parts, at
        self.local_sems, self.send_sems, self.recv_sems = local_sems, send_sems, recv_sems
        self.me, self.sib = plane_neighbours()[:2]
        self.core = lax.rem(self.me, 2)

    def own(self, z, p):
        n = 4 * z + p
        return pltpu.make_async_copy(
            self.parts(2 * self.core + z, p), self.at(z, 2 * p + self.core), self.local_sems.at[n]
        )

    def swap(self, z, p):
        n = 4 * z + p
        return send(
            self.parts(2 - 2 * self.core + z, p),
            self.at(z, 2 * p + self.core),
            self.send_sems.at[n],
            self.recv_sems.at[n],
            on_ctx(self.sib),
        )

    def each(self):
        return [(z, p) for z in range(2) for p in range(4)]

    def start(self):
        for z, p in self.each():
            self.swap(z, p).start()
            self.own(z, p).start()

    def ready(self):
        for z, p in self.each():
            self.own(z, p).wait()
            n = 4 * z + p
            send(
                self.parts(2 * self.core + z, p),
                self.at(z, 2 * p + 1 - self.core),
                self.send_sems.at[n],
                self.recv_sems.at[n],
                on_ctx(self.sib),
            ).wait_recv()

    def finish(self):
        for z, p in self.each():
            self.swap(z, p).wait_send()


class Shares:
    def __init__(self, out, local_sems, send_sems, recv_sems):
        self.out = out
        self.local_sems, self.send_sems, self.recv_sems = local_sems, send_sems, recv_sems
        self.me, self.sib = plane_neighbours()[:2]
        self.core = lax.rem(self.me, 2)

    def own(self, tile, z, p):
        return pltpu.make_async_copy(tile, self.out.at[2 * self.core + z, p], self.local_sems.at[z, p])

    def other(self, tile, z, p):
        return send(
            tile,
            self.out.at[2 * self.core + z, p],
            self.send_sems.at[z, p],
            self.recv_sems.at[z, p],
            on_ctx(self.sib),
        )

    def arrive(self):
        for z in range(2):
            for p in range(4):
                there = self.out.at[2 - 2 * self.core + z, p]
                send(
                    there, there, self.send_sems.at[z, p], self.recv_sems.at[z, p], on_ctx(self.sib)
                ).wait_recv()


SHARES_SCRATCH = [pltpu.SemaphoreType.DMA((2, 4))] * 3
HALVES_SCRATCH = [pltpu.SemaphoreType.DMA((8,))] * 3


def up_kernel(
    x_ref,
    gate_ref,
    up_ref,
    all_ref,
    w_out_ref,
    a_ref,
    b_ref,
    h_ref,
    xs,
    local_sem,
    send_sems,
    recv_sems,
    keep_sems,
    stage,
    stage_sems,
    w,
    w_sem,
    *w_sems,
):
    ring = Gather(x_ref, xs, local_sem, send_sems, recv_sems)
    rows = x_ref.shape[0]
    halves, width, wide = w.shape
    deep = width // 8
    cols = wide // 2
    outs = (a_ref, b_ref, h_ref)
    greet((ring.sib, ring.nx, ring.ny))
    ring.start()
    gates = Halves(
        lambda plane, p: gate_ref.at[plane, p] if p < 3 else up_ref.at[plane, 4],
        lambda z, c: w.at[z, pl.ds(c * deep, deep), pl.ds(0, cols)],
        *w_sems[:3],
    )
    ups = Halves(
        lambda plane, p: up_ref.at[plane, p],
        lambda z, c: w.at[z, pl.ds(c * deep, deep), pl.ds(cols, cols)],
        *w_sems[3:],
    )
    gates.start()
    ups.start()
    gates.ready()
    ups.ready()
    keep_w = pltpu.make_async_copy(w, w_out_ref, w_sem)
    keep_w.start()

    def keep(block):
        return pltpu.make_async_copy(xs.at[block], all_ref.at[block], keep_sems.at[block])

    part = rows // 2

    def put(slot, n, at):
        return pltpu.make_async_copy(stage.at[slot, n], outs[n].at[at], stage_sems.at[slot, n])

    def turn(step, carry):
        ring.before_half(step)
        block, h = ring.half_block(step)
        seen = xs[block, pl.ds(pl.multiple_of(h * part, part), part), :]
        at = pl.ds(pl.multiple_of(block * rows + h * part, part), part)

        @pl.when(h == 1)
        def _():
            keep(block).start()

        slot = lax.rem(step, 2)

        @pl.when(step >= 2)
        def _():
            for n in range(3):
                put(slot, n, at).wait()

        for z in range(halves):
            both = nn(seen, w[z])
            gate, up = both[:, :cols], both[:, cols:]
            sigma = jax.nn.sigmoid(gate)
            active = gate * sigma
            here = slice(z * cols, (z + 1) * cols)
            stage[slot, 0, :, here] = (up * sigma * (1.0 + gate * (1.0 - sigma))).astype(BF16)
            stage[slot, 1, :, here] = active.astype(BF16)
            stage[slot, 2, :, here] = (active * up).astype(BF16)
        for n in range(3):
            put(slot, n, at).start()
        return carry

    lax.fori_loop(0, 16, turn, 0)
    ring.finish()
    gates.finish()
    ups.finish()
    keep_w.wait()
    for block in range(8):
        keep(block).wait()
    for slot in range(2):
        for n in range(3):
            put(slot, n, pl.ds(0, part)).wait()


def gather_up(post, gate_parts, up_parts):
    rows, width = post.shape
    wide = 2 * gate_parts.shape[-1]
    flat = jax.ShapeDtypeStruct((8 * rows, wide), BF16)
    return pl.pallas_call(
        up_kernel,
        out_shape=(
            jax.ShapeDtypeStruct((8, rows, width), BF16),
            jax.ShapeDtypeStruct((2, width, wide), BF16),
            flat,
            flat,
            flat,
        ),
        in_specs=[spec_any()] * 3,
        out_specs=(spec_any(),) * 5,
        scratch_shapes=gather_scratch(rows, width)
        + [
            pltpu.SemaphoreType.DMA((8,)),
            pltpu.VMEM((2, 3, rows // 2, wide), BF16),
            pltpu.SemaphoreType.DMA((2, 3)),
            pltpu.VMEM((2, width, wide), BF16),
            pltpu.SemaphoreType.DMA,
        ]
        + HALVES_SCRATCH * 2,
        compiler_params=comm_params(2),
        cost_estimate=busy(62),
        name="gather_up",
    )(post, gate_parts, up_parts)


def down_kernel(h_any, parts_ref, middle_any, teacher_any, valid_ref, o_ref, low_ref, diff_ref, error_ref, w_out_ref, *scratch):
    rs = Scatter(*scratch[:N_SCATTER])
    (w, w_sem, h_ref, h_sems, middle_ref, teacher_ref, row_sems, w_local, w_sends, w_recvs) = scratch[N_SCATTER:]
    rows = o_ref.shape[0]
    _, _, cols, deep = parts_ref.shape
    weight = Halves(
        lambda plane, p: parts_ref.at[plane, p],
        lambda z, c: w.at[pl.ds(z * cols, cols), pl.ds(pl.multiple_of(c * deep, deep), deep)],
        w_local,
        w_sends,
        w_recvs,
    )
    def fetch(block):
        here = pl.ds(pl.multiple_of(block * rows, rows), rows)
        return pltpu.make_async_copy(h_any.at[here], h_ref.at[here], h_sems.at[block])

    for block in rs.blocks():
        fetch(block).start()
    late = (
        pltpu.make_async_copy(middle_any, middle_ref, row_sems.at[0]),
        pltpu.make_async_copy(teacher_any, teacher_ref, row_sems.at[1]),
    )
    greet((rs.sib, rs.nx, rs.ny))
    weight.start()
    for copy in late:
        copy.start()
    weight.ready()
    keep_w = pltpu.make_async_copy(w, w_out_ref, w_sem)
    keep_w.start()

    def product(block, at, out, n):
        left = h_ref[pl.ds(pl.multiple_of(block * rows + at.start, rows // 2), rows // 2), :]
        for c in range(0, w.shape[1], 512):
            out[n, at, c : c + 512] = nn(left, w[:, c : c + 512]).astype(BF16)

    def turn(step, carry):
        @pl.when(lax.rem(step, 4) < 2)
        def _():
            fetch(rs.block(step)).wait()

        rs.step(step, product)
        return carry

    lax.fori_loop(0, 16, turn, 0)
    for copy in late:
        copy.wait()
    rs.finish(diff_ref)
    error = jnp.zeros((rows, HEAD_SIZE), F32)
    for n in range(0, diff_ref.shape[1], HEAD_SIZE):
        at = slice(n, n + HEAD_SIZE)
        result = middle_ref[:, at] + diff_ref[:, at]
        o_ref[:, at] = result.astype(BF16)
        diff = (result - teacher_ref[:, at].astype(F32)) * valid_ref[...]
        diff_ref[:, at] = diff
        low_ref[:, at] = diff.astype(BF16)
        error += diff * diff
    error_ref[...] = jnp.sum(error, axis=0, keepdims=True)
    weight.finish()
    keep_w.wait()


def scatter_down(hidden, parts, middle, teacher, valid):
    rows, width = middle.shape
    ff = hidden.shape[1]
    low = jax.ShapeDtypeStruct((rows, width), BF16)
    return pl.pallas_call(
        down_kernel,
        out_shape=(
            low,
            low,
            jax.ShapeDtypeStruct((rows, width), F32),
            jax.ShapeDtypeStruct((1, HEAD_SIZE), F32),
            jax.ShapeDtypeStruct((ff, width), BF16),
        ),
        in_specs=[spec_any()] * 4 + [spec_vmem()],
        out_specs=(spec_vmem(),) * 4 + (spec_any(),),
        scratch_shapes=scatter_scratch(rows, width)
        + [
            pltpu.VMEM((ff, width), BF16),
            pltpu.SemaphoreType.DMA,
            pltpu.VMEM(hidden.shape, BF16),
            pltpu.SemaphoreType.DMA((8,)),
            pltpu.VMEM((rows, width), F32),
            pltpu.VMEM((rows, width), BF16),
            pltpu.SemaphoreType.DMA((2,)),
        ]
        + HALVES_SCRATCH,
        compiler_params=comm_params(6),
        cost_estimate=busy(62),
        name="scatter_down",
    )(hidden, parts, middle, teacher, valid)


def down_back_kernel(
    x_ref,
    w_ref,
    a_ref,
    b_ref,
    h_ref,
    d_ref,
    gw_ref,
    xs,
    local_sem,
    send_sems,
    recv_sems,
    stage,
    stage_sems,
    total,
    low,
    w,
    w_sem,
    factors,
    factor_sems,
    hidden,
    hidden_sems,
    s_local,
    s_sends,
    s_recvs,
):
    ring = Gather(x_ref, xs, local_sem, send_sems, recv_sems)
    rows, width = x_ref.shape
    ff = w_ref.shape[0]
    cols = ff // 2
    fetch_w = pltpu.make_async_copy(w_ref, w, w_sem)
    fetch_w.start()
    shares = Shares(gw_ref, s_local, s_sends, s_recvs)
    core = shares.core
    deep = width // 8

    def tile(z, c):
        return low.at[pl.ds(z * cols, cols), pl.ds(pl.multiple_of(c * deep, deep), deep)]

    def put(slot, block):
        return pltpu.make_async_copy(
            stage.at[slot], d_ref.at[pl.ds(block * rows, rows)], stage_sems.at[slot]
        )

    def factor(n, slot, block):
        ref = (a_ref, b_ref)[n]
        return pltpu.make_async_copy(
            ref.at[pl.ds(block * rows, rows)], factors.at[slot, n], factor_sems.at[slot, n]
        )

    def chip_hidden(slot, block):
        return pltpu.make_async_copy(
            h_ref.at[pl.ds(block // 2 * 2 * rows, 2 * rows)], hidden.at[slot], hidden_sems.at[slot]
        )

    def fetch(step):
        block = ring.block(step)
        for n in range(2):
            factor(n, lax.rem(step, 2), block).start()

        @pl.when(lax.rem(step, 2) == 0)
        def _():
            chip_hidden(lax.rem(step // 2, 2), block).start()

    fetch(jnp.int32(0))
    greet((ring.sib, ring.nx, ring.ny))
    ring.start()
    total[...] = jnp.zeros_like(total)
    fetch_w.wait()

    def turn(step, carry):
        ring.before(step)
        block = ring.block(step)
        slot = lax.rem(step, 2)
        pair_slot = lax.rem(step // 2, 2)

        @pl.when(step >= 2)
        def _():
            put(slot, block).wait()

        for n in range(2):
            factor(n, slot, block).wait()

        @pl.when(step < 7)
        def _():
            fetch(step + 1)

        for z in range(2):
            part = slice(z * cols, (z + 1) * cols)
            grad = nt(xs[block], w[part, :])
            for n in range(2):
                stage[slot, :, (2 * z + n) * cols : (2 * z + n + 1) * cols] = (
                    grad * factors[slot, n, :, part].astype(F32)
                ).astype(BF16)
        put(slot, block).start()

        @pl.when(slot == 1)
        def _():
            chip_hidden(pair_slot, block).wait()
            pair = block // 2
            for p in range(4):
                at = slice(p * 2 * deep, (p + 1) * 2 * deep)
                seen = xs[pl.ds(pair * 2, 2), :, at].reshape(2 * rows, 2 * deep)
                total[:, at] += tn(hidden[pair_slot], seen)

                @pl.when(step == 7)
                def _():
                    low[:, at] = total[:, at].astype(BF16)
                    for z in range(2):
                        shares.other(tile(z, 2 * p + 1 - core), z, p).start()
                        shares.own(tile(z, 2 * p + core), z, p).start()

        return carry

    lax.fori_loop(0, 8, turn, 0)
    ring.finish()
    for slot in range(2):
        put(slot, 0).wait()
    shares.arrive()
    for z in range(2):
        for p in range(4):
            shares.other(tile(z, 2 * p + 1 - core), z, p).wait_send()
            shares.own(tile(z, 2 * p + core), z, p).wait()


def gather_down_back(diff, w_down, a, b, hidden):
    rows, width = diff.shape
    ff = w_down.shape[0]
    dma = pltpu.SemaphoreType.DMA
    return pl.pallas_call(
        down_back_kernel,
        out_shape=(
            jax.ShapeDtypeStruct((8 * rows, 2 * ff), BF16),
            jax.ShapeDtypeStruct((4, 4, ff // 2, width // 8), BF16),
        ),
        in_specs=[spec_any()] * 5,
        out_specs=(spec_any(), spec_any()),
        scratch_shapes=gather_scratch(rows, width)
        + [
            pltpu.VMEM((2, rows, 2 * ff), BF16),
            dma((2,)),
            pltpu.VMEM((ff, width), F32),
            pltpu.VMEM((ff, width), BF16),
            pltpu.VMEM((ff, width), BF16),
            dma,
            pltpu.VMEM((2, 2, rows, ff), BF16),
            dma((2, 2)),
            pltpu.VMEM((2, 2 * rows, ff), BF16),
            dma((2,)),
        ]
        + SHARES_SCRATCH,
        compiler_params=comm_params(3),
        cost_estimate=busy(66),
        name="gather_down_back",
    )(diff, w_down, a, b, hidden)


def mix_kernel(
    mixed_ref,
    tokens_ref,
    gain_ref,
    w0_ref,
    w1_ref,
    w2_ref,
    w3_ref,
    middle_ref,
    post_ref,
    rows_ref,
    w_ref,
    held,
    w,
    m_sems,
    m_sends,
    m_recvs,
    w_local,
    w_sends,
    w_recvs,
    keep_sems,
):
    me, sib, nx, ny, dg = plane_neighbours()
    shift = sib - me
    away = others(me)
    rows, width = held.shape
    deep = width // 8
    greet(away)

    def block(c):
        return pl.ds(pl.multiple_of(c * rows, rows), rows)

    def lanes(c):
        return pl.ds(pl.multiple_of(c * deep, deep), deep)

    def give(n, c):
        return send(mixed_ref.at[block(c)], held.at[:, lanes(me)], m_sends.at[n], m_recvs.at[me], on_ctx(c))

    def take(c):
        return send(mixed_ref.at[block(c)], held.at[:, lanes(c)], m_sends.at[0], m_recvs.at[c], on_ctx(c))

    for n, c in enumerate(away):
        give(n, c).start()
    own = pltpu.make_async_copy(mixed_ref.at[block(me)], held.at[:, lanes(me)], m_sems)
    own.start()
    parts = ((w0_ref, me), (w1_ref, nx), (w2_ref, ny), (w3_ref, dg))

    def swap(n):
        part, c = parts[n]
        return send(part, w.at[:, lanes(c)], w_sends.at[n], w_recvs.at[n], on_ctx(sib))

    def place(n):
        part, c = parts[n]
        return pltpu.make_async_copy(part, w.at[:, lanes(c)], w_local.at[n])

    for n in range(4):
        swap(n).start()
        place(n).start()
    for n in range(4):
        place(n).wait()
        there = w.at[:, lanes(parts[n][1] + shift)]
        send(there, there, w_sends.at[n], w_recvs.at[n], on_ctx(sib)).wait_recv()
    own.wait()
    for c in away:
        take(c).wait_recv()
    keep_rows = pltpu.make_async_copy(held, rows_ref, keep_sems.at[0])
    keep_rows.start()
    keep_w = pltpu.make_async_copy(w, w_ref, keep_sems.at[1])
    keep_w.start()
    total = jnp.zeros((rows, 1), F32)
    for n in range(0, width, 512):
        at = slice(n, n + 512)
        middle = tokens_ref[:, at].astype(F32) + nn(held[...], w[:, at])
        middle_ref[:, at] = middle
        total += jnp.sum(middle * middle, axis=-1, keepdims=True)
    scale = lax.rsqrt(total / width + EPS)
    for n in range(0, width, 512):
        at = slice(n, n + 512)
        post_ref[:, at] = (middle_ref[:, at] * scale * gain_ref[:, at]).astype(BF16)
    for n, c in enumerate(away):
        give(n, c).wait_send()
    for n in range(4):
        swap(n).wait_send()
    keep_rows.wait()
    keep_w.wait()


def mix(mixed, tokens, post_gain, parts):
    rows, width = tokens.shape
    dma = pltpu.SemaphoreType.DMA
    return pl.pallas_call(
        mix_kernel,
        out_shape=(
            jax.ShapeDtypeStruct((rows, width), F32),
            jax.ShapeDtypeStruct((rows, width), BF16),
            jax.ShapeDtypeStruct((rows, width), BF16),
            jax.ShapeDtypeStruct((width, width), BF16),
        ),
        in_specs=[spec_any(), spec_vmem(), spec_vmem()] + [spec_any()] * 4,
        out_specs=(spec_vmem(), spec_vmem(), spec_any(), spec_any()),
        scratch_shapes=[
            pltpu.VMEM((rows, width), BF16),
            pltpu.VMEM((width, width), BF16),
            dma,
            dma((7,)),
            dma((8,)),
            dma((4,)),
            dma((4,)),
            dma((4,)),
            dma((2,)),
        ],
        compiler_params=comm_params(5),
        cost_estimate=busy(28),
        name="mix",
    )(mixed, tokens, post_gain.reshape(1, -1), *parts)


def mix_back_kernel(
    post_ref,
    middle_ref,
    diff_ref,
    gain_ref,
    w_any,
    rows_any,
    swap_ref,
    dm_ref,
    d_middle_ref,
    gp_ref,
    g0_ref,
    g1_ref,
    g2_ref,
    g3_ref,
    swapped_ref,
    w_ref,
    rows_ref,
    fetch_sems,
    d_ref,
    stage,
    to_sib,
    from_sib,
    own,
    out_sem,
    out_sends,
    out_recvs,
    s_sends,
    s_recvs,
    g_sems,
    *c_sems,
):
    me, sib, nx, ny, dg = plane_neighbours()
    shift = sib - me
    away = others(me)
    rows, width = d_ref.shape
    deep = width // 8
    fetch_w = pltpu.make_async_copy(w_any, w_ref, fetch_sems.at[0])
    fetch_w.start()
    fetch_rows = pltpu.make_async_copy(rows_any, rows_ref, fetch_sems.at[1])
    fetch_rows.start()
    greet(away)
    weight_swap = ChipSwap(swap_ref, swapped_ref, *c_sems)
    weight_swap.start()
    squares = jnp.zeros((rows, HEAD_SIZE), F32)
    dots = jnp.zeros((rows, HEAD_SIZE), F32)
    cuts = [slice(n, n + HEAD_SIZE) for n in range(0, width, HEAD_SIZE)]
    for at in cuts:
        middle = middle_ref[:, at]
        squares += middle * middle
        dots += post_ref[:, at] * gain_ref[:, at] * middle
    scale = lax.rsqrt(jnp.sum(squares, axis=-1, keepdims=True) / width + EPS)
    pull = scale * scale * scale * (jnp.sum(dots, axis=-1, keepdims=True) / width)
    for at in cuts:
        middle, post = middle_ref[:, at], post_ref[:, at]
        gp_ref[:, at] = jnp.sum(post * (middle * scale), axis=0, keepdims=True)
        d_middle = diff_ref[:, at] + scale * (post * gain_ref[:, at]) - middle * pull
        d_middle_ref[:, at] = d_middle
        d_ref[:, at] = d_middle.astype(BF16)
    outs = (g0_ref, g1_ref, g2_ref, g3_ref)
    chips = (me, nx, ny, dg)
    fetch_w.wait()
    fetch_rows.wait()

    def block(c):
        return pl.ds(pl.multiple_of(c * rows, rows), rows)

    def give(n, c):
        return send(stage.at[c], dm_ref.at[block(me)], out_sends.at[n], out_recvs.at[me], on_ctx(c))

    def take(c):
        return send(stage.at[c], dm_ref.at[block(c)], out_sends.at[0], out_recvs.at[c], on_ctx(c))

    def heads(n, carry):
        c = pick(n, away + (me,))
        at = pl.ds(pl.multiple_of(c * deep, deep), deep)
        stage[c] = nt(d_ref[...], w_ref[at, :]).astype(BF16)

        @pl.when(n < 7)
        def _():
            give(n, c).start()

        return carry

    lax.fori_loop(0, 8, heads, 0)
    keep = pltpu.make_async_copy(stage.at[me], dm_ref.at[block(me)], out_sem)
    keep.start()

    def swap(n):
        return send(to_sib.at[n], from_sib.at[n], s_sends.at[n], s_recvs.at[n], on_ctx(sib))

    def grad(n, out, c):
        at = pl.ds(pl.multiple_of(c * deep, deep), deep)
        out[n] = tn(rows_ref[...], d_ref[:, at]).astype(BF16)

    def theirs(n, carry):
        grad(n, to_sib, pick(n, chips) + shift)
        swap(n).start()
        return carry

    def ours(n, carry):
        grad(n, own, pick(n, chips))
        return carry

    lax.fori_loop(0, 4, theirs, 0)
    lax.fori_loop(0, 4, ours, 0)
    for n in range(4):
        swap(n).wait_recv()
        own[n] = (own[n].astype(F32) + from_sib[n].astype(F32)).astype(BF16)
        pltpu.make_async_copy(own.at[n], outs[n], g_sems.at[n]).start()
    for c in away:
        take(c).wait_recv()
    keep.wait()
    for n, c in enumerate(away):
        give(n, c).wait_send()
    for n in range(4):
        swap(n).wait_send()
        pltpu.make_async_copy(own.at[n], outs[n], g_sems.at[n]).wait()
    weight_swap.finish()


def mix_back(d_post, middle, diff, post_gain, w, mixed_rows, swap):
    rows, width = middle.shape
    deep = width // 8
    dma = pltpu.SemaphoreType.DMA
    four = pltpu.VMEM((4, width, deep), BF16)
    return pl.pallas_call(
        mix_back_kernel,
        out_shape=(
            jax.ShapeDtypeStruct((8 * rows, deep), BF16),
            jax.ShapeDtypeStruct((rows, width), F32),
            jax.ShapeDtypeStruct((1, width), F32),
        )
        + (jax.ShapeDtypeStruct((width, deep), BF16),) * 4
        + (jax.ShapeDtypeStruct(swap.shape, BF16),),
        in_specs=[spec_vmem()] * 4 + [spec_any()] * 3,
        out_specs=(spec_any(), spec_vmem(), spec_vmem()) + (spec_any(),) * 5,
        scratch_shapes=[
            pltpu.VMEM((width, width), BF16),
            pltpu.VMEM((rows, width), BF16),
            dma((2,)),
            pltpu.VMEM((rows, width), BF16),
            pltpu.VMEM((8, rows, deep), BF16),
            four,
            four,
            four,
            dma,
            dma((7,)),
            dma((8,)),
            dma((4,)),
            dma((4,)),
            dma((4,)),
        ]
        + SWAP_SCRATCH,
        compiler_params=comm_params(4),
        cost_estimate=busy(26),
        name="mix_back",
    )(d_post, middle, diff, post_gain.reshape(1, -1), w, mixed_rows, swap)


def columns(all_ref, slices, sems, c, slot):
    deep = slices.shape[-1]
    return pltpu.make_async_copy(
        all_ref.at[:, :, pl.ds(pl.multiple_of(c * deep, deep), deep)], slices.at[slot], sems.at[slot]
    )


EARLY = 1


def post_back_kernel(d_any, w_any, all_ref, o_ref, gw_ref, *scratch):
    rs = Scatter(*scratch[:N_SCATTER])
    slices, slice_sems, tile, d_ref, d_sems, w_ref, w_sems, s_local, s_sends, s_recvs = scratch[N_SCATTER:]
    shares = Shares(gw_ref, s_local, s_sends, s_recvs)
    rows = o_ref.shape[0]
    _, width, wide = w_ref.shape
    plane_rows = d_ref.shape[0]
    deep = width // 8
    fetch_w = [pltpu.make_async_copy(w_any.at[z], w_ref.at[z], w_sems.at[z]) for z in range(2)]

    def fetch(block):
        here = pl.ds(pl.multiple_of(block * rows, rows), rows)
        return pltpu.make_async_copy(d_any.at[here], d_ref.at[here], d_sems.at[block])

    order = rs.blocks()
    fetch(order[0]).start()
    for copy in fetch_w:
        copy.start()
    for block in order[1:]:
        fetch(block).start()
    columns(all_ref, slices, slice_sems, 0, 0).start()
    greet((rs.sib, rs.nx, rs.ny))
    for copy in fetch_w:
        copy.wait()

    def product(block, at, out, n):
        here = pl.ds(pl.multiple_of(block * rows + at.start, rows // 2), rows // 2)
        for c in range(0, width, 512):
            total = nt(d_ref[here, :wide], w_ref[0, c : c + 512, :])
            total += nt(d_ref[here, wide:], w_ref[1, c : c + 512, :])
            out[n, at, c : c + 512] = total.astype(BF16)

    def put(slot, p, act):
        @pl.when(slot == shares.core)
        def _():
            for z in range(2):
                copy = shares.own(tile.at[slot, z], z, p)
                copy.start() if act == "start" else copy.wait()

        @pl.when(slot != shares.core)
        def _():
            for z in range(2):
                copy = shares.other(tile.at[slot, z], z, p)
                copy.start() if act == "start" else copy.wait_send()

    def grad(c):
        slot = lax.rem(c, 2)
        columns(all_ref, slices, slice_sems, c, slot).wait()

        @pl.when(c < 7)
        def _():
            columns(all_ref, slices, slice_sems, c + 1, 1 - slot).start()

        @pl.when(c >= 2)
        def _():
            put(slot, c // 2 - 1, "wait")

        seen = slices[slot].reshape(plane_rows, deep)
        for z in range(2):
            tile[slot, z] = tn(seen, d_ref[:, z * wide : (z + 1) * wide]).astype(BF16)
        put(slot, c // 2, "start")

    def turn(t, carry):
        is_grad = ((t >= 10) & (t < 10 + EARLY)) | (t >= 16 + EARLY)

        for n in range(2):

            @pl.when(t == n)
            def _():
                fetch(order[n]).wait()

        @pl.when(t == 4)
        def _():
            for block in order[2:]:
                fetch(block).wait()

        @pl.when(is_grad)
        def _():
            grad(jnp.where(t < 10 + EARLY, t - 10, t - 16))

        @pl.when(jnp.logical_not(is_grad))
        def _():
            rs.step(jnp.where(t < 10, t, t - EARLY), product)

        return carry

    lax.fori_loop(0, 24, turn, 0)
    rs.finish(o_ref)
    for slot in range(2):
        put(slot, 3, "wait")
    shares.arrive()


def scatter_post(d_gu, w_gu, post_all):
    _, rows, width = post_all.shape
    wide = w_gu.shape[-1]
    deep = width // 8
    return pl.pallas_call(
        post_back_kernel,
        out_shape=(
            jax.ShapeDtypeStruct((rows, width), F32),
            jax.ShapeDtypeStruct((4, 4, deep, wide), BF16),
        ),
        in_specs=[spec_any()] * 3,
        out_specs=(spec_vmem(), spec_any()),
        scratch_shapes=scatter_scratch(rows, width)
        + [
            pltpu.VMEM((2, 8, rows, deep), BF16),
            pltpu.SemaphoreType.DMA((2,)),
            pltpu.VMEM((2, 2, deep, wide), BF16),
            pltpu.VMEM(d_gu.shape, BF16),
            pltpu.SemaphoreType.DMA((8,)),
            pltpu.VMEM(w_gu.shape, BF16),
            pltpu.SemaphoreType.DMA((2,)),
        ]
        + SHARES_SCRATCH,
        compiler_params=comm_params(7),
        cost_estimate=busy(66),
        name="scatter_post",
    )(d_gu, w_gu, post_all)


def normed_back_kernel(
    dq_ref,
    dkv_ref,
    to_lo_ref,
    to_hi_ref,
    lin_ref,
    w_ref,
    all_ref,
    swap_ref,
    wo_ref,
    tokens_ref,
    gp_ref,
    error_ref,
    qg_ref,
    kg_ref,
    ca_ref,
    sa_ref,
    cb_ref,
    sb_ref,
    o_ref,
    gw_ref,
    totals_ref,
    swapped_ref,
    wo_sum_ref,
    *scratch,
):
    rs = Scatter(*scratch[:N_SCATTER])
    (
        from_lo,
        from_hi,
        d_lin,
        slices,
        slice_sems,
        tiles,
        tiles_in,
        up_in,
        down_in,
        wo_up,
        wo_down,
        z_sends,
        z_recvs,
        t_sends,
        t_recvs,
        p_sends,
        p_recvs,
        o_sends,
        o_recvs,
        gains_ref,
        held,
        held_planes,
        v_sends,
        v_recvs,
        *c_sems,
    ) = scratch[N_SCATTER:]
    me = rs.me
    plane, planes = lax.axis_index("tp"), lax.axis_size("tp")
    rows, width = o_ref.shape
    deep = width // 8
    plane_rows = dq_ref.shape[0]
    units = rows // UNIT
    wide = 2 * HEAD_SIZE
    away = others(me)
    order = rs.blocks()

    from_lo[...] = jnp.zeros_like(from_lo)
    from_hi[...] = jnp.zeros_like(from_hi)
    line = Line(to_hi_ref, to_lo_ref, from_lo, from_hi, z_sends, z_recvs, rows, True)
    barrier = pltpu.get_barrier_semaphore()
    far = [lax.rem(plane + step, planes) for step in range(1, planes)]
    for where in [on_ctx(c) for c in away] + [on_plane(p) for p in far]:
        pl.semaphore_signal(barrier, inc=1, device_id=where, device_id_type=MESH)
    pl.semaphore_wait(barrier, len(away) + len(far))
    for block in order:
        line.start(block)
    columns(all_ref, slices, slice_sems, order[0], 0).start()
    gains_ref[...] = jnp.zeros_like(gains_ref)

    def head_back(grad, lin, gain_ref, rotation):
        back = rotation.back(grad)
        scale = lax.rsqrt(jnp.mean(lin * lin, axis=-1, keepdims=True) + EPS)
        normal = lin * scale
        gained = back * gain_ref[...]
        d = scale * (gained - normal * jnp.mean(gained * normal, axis=-1, keepdims=True))
        return d.astype(BF16), jnp.sum(back * normal, axis=0, keepdims=True)

    def rotation_of(unit):
        return Turn(ca_ref, sa_ref, cb_ref, sb_ref, unit)

    def prepare_queries(unit, carry):
        rotation = rotation_of(unit)
        here = pl.ds(pl.multiple_of(unit * UNIT, UNIT), UNIT)
        for h in range(2):
            lanes = slice(h * HEAD_SIZE, (h + 1) * HEAD_SIZE)
            d, gain = head_back(dq_ref[here, lanes].astype(F32) * HEAD_SIZE**-0.5, lin_ref[here, lanes], qg_ref, rotation)
            d_lin[here, lanes] = d
            gains_ref[0:1, :] += gain
        return carry

    def prepare_keys(block):
        line.arrived(block)
        for i in range(units):
            unit = block * units + i
            here = pl.ds(pl.multiple_of(unit * UNIT, UNIT), UNIT)
            d_kv = dkv_ref[here, :].astype(F32) + from_lo[here, :].astype(F32) + from_hi[here, :].astype(F32)
            lanes = slice(2 * HEAD_SIZE, 3 * HEAD_SIZE)
            d, gain = head_back(d_kv[:, :HEAD_SIZE], lin_ref[here, lanes], kg_ref, rotation_of(unit))
            d_lin[here, lanes] = d
            gains_ref[1:2, :] += gain
            d_lin[here, 3 * HEAD_SIZE :] = d_kv[:, HEAD_SIZE:].astype(BF16)

    def tile_to(part, n, device):
        return send(
            tiles.at[part, device],
            tiles_in.at[part, me],
            t_sends.at[part, n],
            t_recvs.at[part, me],
            on_ctx(device),
        )

    def tile_from(part, device):
        return send(
            tiles.at[part, device],
            tiles_in.at[part, device],
            t_sends.at[part, 0],
            t_recvs.at[part, device],
            on_ctx(device),
        )

    def grads(part):
        def grad(n, carry):
            c = pick(n, order)
            slot = lax.rem(n, 2)
            columns(all_ref, slices, slice_sems, c, slot).wait()

            @pl.when((n < 7) | (part == 0))
            def _():
                columns(all_ref, slices, slice_sems, pick(lax.rem(n + 1, 8), order), 1 - slot).start()

            lanes = slice(part * wide, (part + 1) * wide)
            value = tn(slices[slot].reshape(plane_rows, deep), d_lin[:, lanes]).astype(BF16)

            @pl.when(n < 7)
            def _():
                tiles[part, c] = value
                tile_to(part, n, c).start()

            @pl.when(n == 7)
            def _():
                tiles_in[part, me] = value

            return carry

        lax.fori_loop(0, 8, grad, 0)

    sums = [
        LineSum(
            lambda p, part=part: tiles_in.at[part, pl.ds(2 * p, 2)],
            up_in.at[part],
            down_in.at[part],
            p_sends.at[part],
            p_recvs.at[part],
        )
        for part in range(2)
    ]
    out_sum = LineSum(lambda p: wo_ref.at[p], wo_up, wo_down, o_sends, o_recvs)

    def tiles_there(part):
        for device in away:
            tile_from(part, device).wait_recv()

    def product(block, at, out, n):
        left = d_lin[pl.ds(pl.multiple_of(block * rows + at.start, rows // 2), rows // 2), :]
        for c in range(0, width, 512):
            out[n, at, c : c + 512] = nt(left, w_ref[c : c + 512, :]).astype(BF16)

    def turn(step, carry):
        @pl.when(lax.rem(step, 4) < 2)
        def _():
            prepare_keys(rs.block(step))

        rs.step(step, product, late=True)

        @pl.when(step == 4)
        def _():
            out_sum.stage(1)

        @pl.when(step == 7)
        def _():
            tiles_there(0)
            sums[0].stage(0)

        @pl.when(step == 9)
        def _():
            out_sum.stage(2)

        @pl.when(step == 12)
        def _():
            sums[0].stage(1)

        return carry

    swap = ChipSwap(swap_ref, swapped_ref, *c_sems)
    swap.start()
    out_sum.stage(0)
    lax.fori_loop(0, plane_rows // UNIT, prepare_queries, 0)
    grads(0)
    lax.fori_loop(0, 16, turn, 0)
    grads(1)
    for c in range(8):
        pltpu.make_async_copy(
            tokens_ref.at[:, pl.ds(c * deep, deep)], slices.at[0, c], slice_sems.at[0]
        ).start()
    rs.second_wave()
    sums[0].stage(2)
    tiles_there(1)
    for k in range(3):
        sums[1].stage(k)
    rs.finish(o_ref)
    total = Total(held, held_planes, v_sends, v_recvs)
    vector = held.at[me]
    pltpu.make_async_copy(slices.at[0], slices.at[0], slice_sems.at[0]).wait()
    squares = jnp.zeros((rows, deep), F32)
    for c in range(8):
        stream = slices[0, c].astype(F32)
        squares += stream * stream
    scale = lax.rsqrt(jnp.sum(squares, axis=-1, keepdims=True) / width + EPS)
    lanes_of = width // HEAD_SIZE
    for c in range(8):
        at = slice(c * deep, (c + 1) * deep)
        unit_in = slices[0, c].astype(F32) * scale
        gain = jnp.sum(o_ref[:, at].astype(F32) * unit_in, axis=0, keepdims=True)
        for i in range(2):
            n, lanes = 2 * c + i, slice(i * HEAD_SIZE, (i + 1) * HEAD_SIZE)
            vector[n : n + 1, :] = gain[:, lanes]
            vector[lanes_of + n : lanes_of + n + 1, :] = gp_ref[:, n * HEAD_SIZE : (n + 1) * HEAD_SIZE]
    vector[2 * lanes_of : 2 * lanes_of + 2, :] = gains_ref[0:2, :]
    vector[2 * lanes_of + 2 : 2 * lanes_of + 8, :] = jnp.broadcast_to(error_ref[...], (6, HEAD_SIZE))
    total.start()
    out_sum.collect(wo_sum_ref)
    for part in range(2):
        sums[part].collect(gw_ref.at[part])
    total.middle()
    swap.finish()
    total.finish(totals_ref)
    for line_sum in (out_sum, *sums):
        line_sum.finish()
    for part in range(2):
        for n, device in enumerate(order[:7]):
            tile_to(part, n, device).wait_send()

    def settle(block, carry):
        line.sent(block)
        return carry

    lax.fori_loop(0, 8, settle, 0)


def scatter_normed(d_queries, d_kv, to_lo, to_hi, lin, w_qkv, normed_all, swap, wo, tokens, gp, error, q_gain, k_gain, tables):
    _, rows, width = normed_all.shape
    deep = width // 8
    cols = w_qkv.shape[1]
    half = pltpu.VMEM(to_lo.shape, BF16)
    tiles = pltpu.VMEM((2, 8, deep, cols // 2), BF16)
    dma = pltpu.SemaphoreType.DMA
    return pl.pallas_call(
        normed_back_kernel,
        out_shape=(
            jax.ShapeDtypeStruct((rows, width), BF16),
            jax.ShapeDtypeStruct((2, 2, deep, cols // 2), F32),
            jax.ShapeDtypeStruct((2 * width // HEAD_SIZE + 8, HEAD_SIZE), F32),
            jax.ShapeDtypeStruct(swap.shape, BF16),
            jax.ShapeDtypeStruct(wo.shape[1:], F32),
        ),
        in_specs=[spec_vmem()] * 2
        + [spec_any()] * 2
        + [spec_vmem()] * 2
        + [spec_any()] * 2
        + [spec_vmem(), spec_any()]
        + [spec_vmem()] * 8,
        out_specs=(spec_vmem(),) * 3 + (spec_any(), spec_vmem()),
        scratch_shapes=scatter_scratch(rows, width)
        + [
            half,
            half,
            pltpu.VMEM((8 * rows, cols), BF16),
            pltpu.VMEM((2, 8, rows, deep), BF16),
            dma((2,)),
            tiles,
            tiles,
            pltpu.VMEM((2, 4, 2, deep, cols // 2), BF16),
            pltpu.VMEM((2, 4, 2, deep, cols // 2), BF16),
            pltpu.VMEM(wo.shape, BF16),
            pltpu.VMEM(wo.shape, BF16),
            dma((2, 8 * rows // UNIT)),
            dma((2, 8 * rows // UNIT)),
            dma((2, 7)),
            dma((2, 8)),
            dma((2, 2, 4)),
            dma((2, 2, 4)),
            dma((2, 4)),
            dma((2, 4)),
            pltpu.VMEM((8, HEAD_SIZE), F32),
            pltpu.VMEM((8, 2 * width // HEAD_SIZE + 8, HEAD_SIZE), F32),
            pltpu.VMEM((4, 2 * width // HEAD_SIZE + 8, HEAD_SIZE), F32),
            dma((10,)),
            dma((12,)),
        ]
        + SWAP_SCRATCH,
        compiler_params=comm_params(8),
        cost_estimate=busy(110),
        name="scatter_normed",
    )(
        d_queries,
        d_kv,
        to_lo,
        to_hi,
        lin,
        w_qkv,
        normed_all,
        swap,
        wo,
        tokens,
        gp,
        error,
        q_gain.reshape(1, -1),
        k_gain.reshape(1, -1),
        *tables,
    )


def finish_kernel(
    d_ref, tokens_ref, middle_ref, gain_ref, gu_ref, down_ref, qkv_ref, out_ref,
    dt_ref, gate_ref, up_ref, dw_ref, wq_ref, wk_ref, wv_ref, wo_ref,
):
    stream = tokens_ref[...].astype(F32)
    scale = lax.rsqrt(jnp.mean(stream * stream, axis=-1, keepdims=True) + EPS)
    gained = d_ref[...].astype(F32) * gain_ref[...]
    pull = scale * scale * scale * jnp.mean(gained * stream, axis=-1, keepdims=True)
    dt_ref[...] = (middle_ref[...] + (scale * gained - stream * pull)).astype(BF16)
    cols = gu_ref.shape[2] // 2
    for p in range(4):
        here = slice(p * cols, (p + 1) * cols)
        gate_ref[:, here] = gu_ref[p, :, :cols].astype(F32)
        up_ref[:, here] = gu_ref[p, :, cols:].astype(F32)
    dw_ref[...] = down_ref[...].astype(F32)
    wide = 2 * HEAD_SIZE
    for k in range(2):
        wq_ref[:, k * wide : (k + 1) * wide] = qkv_ref[0, k]
        wk_ref[:, k * HEAD_SIZE : (k + 1) * HEAD_SIZE] = qkv_ref[1, k, :, :HEAD_SIZE]
        wv_ref[:, k * HEAD_SIZE : (k + 1) * HEAD_SIZE] = qkv_ref[1, k, :, HEAD_SIZE:]
    wo_ref[...] = out_ref[...]


def finish(d_normed, tokens, d_middle, in_gain, gu, down, qkv, out):
    steps = 8

    def piece(shape, axis):
        block = list(shape)
        block[axis] //= steps
        return pl.BlockSpec(
            tuple(block), lambda i, axis=axis, n=len(shape): tuple(i if d == axis else 0 for d in range(n))
        )

    rows, width = tokens.shape
    deep, ff = gu.shape[1], 2 * gu.shape[2]
    one = (1, width)
    whole = pl.BlockSpec(one, lambda i: (0, 0))
    flat, square = (rows, width), (deep, 2 * HEAD_SIZE)
    ins = [(flat, 0), (flat, 0), (flat, 0), None, (gu.shape, 1), (down.shape, 1), (qkv.shape, 2), (out.shape, 0)]
    outs = [
        (flat, 0, BF16),
        ((deep, ff), 0, F32),
        ((deep, ff), 0, F32),
        (down.shape, 1, F32),
        ((deep, 4 * HEAD_SIZE), 0, F32),
        (square, 0, F32),
        (square, 0, F32),
        (out.shape, 0, F32),
    ]
    return pl.pallas_call(
        finish_kernel,
        grid=(steps,),
        out_shape=tuple(jax.ShapeDtypeStruct(o[0], o[2]) for o in outs),
        in_specs=[piece(*i) if i else whole for i in ins],
        out_specs=tuple(piece(o[0], o[1]) for o in outs),
        compiler_params=pltpu.CompilerParams(vmem_limit_bytes=VMEM_LIMIT),
        cost_estimate=busy(8),
        name="finish",
    )(d_normed, tokens, d_middle, in_gain.reshape(1, -1), gu, down, qkv, out)


class Places:
    def __init__(self, order_ref, lens_ref):
        self.order, self.lens = order_ref, lens_ref
        self.plane = lax.axis_index("tp")
        self.seq0 = (3 * self.plane) // 4
        self.seq1 = (3 * self.plane + 2) // 4

    def position(self, seq, quarter, c):
        return 2 * self.order[seq, 2 * c + quarter // 2] + lax.rem(quarter, 2)

    def unit(self, u):
        c = u // 3
        g = 3 * self.plane + lax.rem(u, 3)
        seq = g // 4
        return seq, seq - self.seq0, self.position(seq, lax.rem(g, 4), c)

    def each(self, visit):
        for slot, seq in ((0, self.seq0), (1, self.seq1)):

            @pl.when((slot == 0) | (self.seq1 != self.seq0))
            def _():
                def one(i, carry):
                    quarter, c = i // 8, lax.rem(i, 8)
                    g = 4 * seq + quarter
                    away = g // 3 - self.plane
                    row = pl.multiple_of((c * 3 + lax.rem(g, 3)) * UNIT, UNIT)
                    visit(slot, self.position(seq, quarter, c), away, row)
                    return carry

                lax.fori_loop(0, 32, one, 0)

    def fetch(self, sources, keys, values, key_sem, value_sem):
        def visit(slot, position, away, row):
            at = pl.ds(pl.multiple_of(position * UNIT, UNIT), UNIT)
            for n, source in enumerate(sources):

                @pl.when(away == n - 1)
                def _():
                    pltpu.make_async_copy(
                        source.at[pl.ds(row, UNIT), pl.ds(0, HEAD_SIZE)], keys.at[slot, at], key_sem.at[slot]
                    ).start()
                    pltpu.make_async_copy(
                        source.at[pl.ds(row, UNIT), pl.ds(HEAD_SIZE, HEAD_SIZE)],
                        values.at[slot, at, pl.ds(0, HEAD_SIZE)],
                        value_sem.at[slot],
                    ).start()

        self.each(visit)
        for slot in range(2):

            @pl.when((slot == 0) | (self.seq1 != self.seq0))
            def _():
                pltpu.make_async_copy(keys.at[slot], keys.at[slot], key_sem.at[slot]).wait()
                pltpu.make_async_copy(keys.at[slot], keys.at[slot], value_sem.at[slot]).wait()


def sweep(clear, part):
    def four(i, carry):
        part(i * 4 * KEYS, 4 * KEYS, False)
        return carry

    lax.fori_loop(0, clear // 4, four, 0)

    @pl.when(lax.rem(clear, 4) >= 2)
    def _():
        part(clear // 4 * 4 * KEYS, 2 * KEYS, False)


    odd = lax.rem(clear, 2)

    @pl.when(odd == 1)
    def _():
        part((clear - 1) * KEYS, 2 * KEYS, True)

    @pl.when(odd == 0)
    def _():
        part(clear * KEYS, KEYS, True)


def attend_kernel(
    order_ref, lens_ref, q_ref, lo_ref, own_ref, hi_ref, o_ref, lse_ref, keys, values, acc, key_sem, value_sem
):
    places = Places(order_ref, lens_ref)
    values[:, :, HEAD_SIZE:] = jnp.ones((2, values.shape[1], HEAD_SIZE), BF16)
    places.fetch((lo_ref, own_ref, hi_ref), keys, values, key_sem, value_sem)

    def one_unit(u, carry):
        seq, slot, position = places.unit(u)
        length = lens_ref[seq]
        rows = pl.ds(pl.multiple_of(u * UNIT, UNIT), UNIT)
        both = q_ref[rows, :]
        queries = jnp.concatenate([both[:, :HEAD_SIZE], both[:, HEAD_SIZE:]], axis=0)
        clear = jnp.minimum(position * UNIT, length) // KEYS
        acc[...] = jnp.zeros_like(acc)
        row = lax.rem(lax.broadcasted_iota(jnp.int32, (2 * UNIT, 1), 0), UNIT)

        def part(start, size, masked):
            at = pl.ds(pl.multiple_of(start, KEYS), size)
            weights = jnp.exp2(nt(queries, keys[slot, at, :]))
            if masked:
                last = jnp.minimum(row + (position * UNIT - start), length - 1 - start)
                weights = jnp.where(lax.broadcasted_iota(jnp.int32, weights.shape, 1) <= last, weights, 0.0)
            acc[:, :HEAD_SIZE] += nn(weights.astype(BF16), values[slot, at, :HEAD_SIZE])
            part_sum = weights[:, :HEAD_SIZE]
            for n in range(HEAD_SIZE, size, HEAD_SIZE):
                part_sum += weights[:, n : n + HEAD_SIZE]
            acc[:, HEAD_SIZE:] += part_sum

        sweep(clear, part)
        total = jnp.sum(acc[:, HEAD_SIZE:], axis=-1, keepdims=True)
        mixed = (acc[:, :HEAD_SIZE] / total).astype(BF16)
        o_ref[rows, :] = jnp.concatenate([mixed[:UNIT], mixed[UNIT:]], axis=1)
        lse_ref[u] = jnp.transpose(jnp.broadcast_to(jnp.log2(total), (2 * UNIT, HEAD_SIZE)))[:8, :]
        return carry

    lax.fori_loop(0, q_ref.shape[0] // UNIT, one_unit, 0)


def attend(order, lens, q, lo, own, hi, seq_len):
    rows = q.shape[0]
    return pl.pallas_call(
        attend_kernel,
        out_shape=(
            jax.ShapeDtypeStruct(q.shape, BF16),
            jax.ShapeDtypeStruct((rows // UNIT, 8, 2 * UNIT), F32),
        ),
        in_specs=[spec_smem(), spec_smem(), spec_vmem(), spec_any(), spec_any(), spec_any()],
        out_specs=(spec_vmem(), spec_vmem()),
        scratch_shapes=[
            pltpu.VMEM((2, seq_len, HEAD_SIZE), BF16),
            pltpu.VMEM((2, seq_len, 2 * HEAD_SIZE), BF16),
            pltpu.VMEM((2 * UNIT, 2 * HEAD_SIZE), F32),
            pltpu.SemaphoreType.DMA((2,)),
            pltpu.SemaphoreType.DMA((2,)),
        ],
        compiler_params=pltpu.CompilerParams(vmem_limit_bytes=VMEM_LIMIT),
        cost_estimate=busy(50),
        name="attend",
    )(order, lens, q, lo, own, hi)


def attend_back_kernel(
    order_ref,
    lens_ref,
    q_ref,
    do_ref,
    o_ref,
    lse_ref,
    lo_ref,
    own_ref,
    hi_ref,
    dq_ref,
    dlo_ref,
    down_ref,
    dhi_ref,
    keys,
    values,
    dkeys,
    dvalues,
    dq_acc,
    key_sem,
    value_sem,
):
    places = Places(order_ref, lens_ref)
    dkeys[...] = jnp.zeros_like(dkeys)
    dvalues[...] = jnp.zeros_like(dvalues)
    places.fetch((lo_ref, own_ref, hi_ref), keys, values, key_sem, value_sem)

    def stacked(ref, rows):
        both = ref[rows, :]
        return jnp.concatenate([both[:, :HEAD_SIZE], both[:, HEAD_SIZE:]], axis=0)

    def one_unit(u, carry):
        seq, slot, position = places.unit(u)
        length = lens_ref[seq]
        rows = pl.ds(pl.multiple_of(u * UNIT, UNIT), UNIT)
        queries = stacked(q_ref, rows)
        grads = stacked(do_ref, rows)
        product = grads.astype(F32) * stacked(o_ref, rows).astype(F32)
        delta = jnp.sum(jnp.transpose(product), axis=0, keepdims=True)
        lse = lse_ref[u][:1, :]
        clear = jnp.minimum(position * UNIT, length) // KEYS
        dq_acc[...] = jnp.zeros_like(dq_acc)
        row = lax.rem(lax.broadcasted_iota(jnp.int32, (1, 2 * UNIT), 1), UNIT)

        def part(start, size, masked):
            at = pl.ds(pl.multiple_of(start, KEYS), size)
            key = keys[slot, at, :]
            probs = jnp.exp2(nt(key, queries) - lse)
            if masked:
                last = jnp.minimum(row + (position * UNIT - start), length - 1 - start)
                probs = jnp.where(lax.broadcasted_iota(jnp.int32, probs.shape, 0) <= last, probs, 0.0)
            d_scores = (probs * (nt(values[slot, at, :], grads) - delta)).astype(BF16)
            dvalues[slot, at, :] += nn(probs.astype(BF16), grads)
            dkeys[slot, at, :] += nn(d_scores, queries)
            dq_acc[...] += tn(d_scores, key)

        sweep(clear, part)
        dq_ref[rows, :] = jnp.concatenate([dq_acc[:UNIT, :], dq_acc[UNIT:, :]], axis=1).astype(BF16)
        return carry

    lax.fori_loop(0, q_ref.shape[0] // UNIT, one_unit, 0)
    dlo_ref[...] = jnp.zeros_like(dlo_ref)
    dhi_ref[...] = jnp.zeros_like(dhi_ref)

    def spread(slot, position, away, row):
        at = pl.ds(pl.multiple_of(position * UNIT, UNIT), UNIT)
        for n, out in enumerate((dlo_ref, down_ref, dhi_ref)):

            @pl.when(away == n - 1)
            def _():
                out[pl.ds(row, UNIT), :HEAD_SIZE] = (dkeys[slot, at, :] * (1.0 / LOG2E)).astype(out.dtype)
                out[pl.ds(row, UNIT), HEAD_SIZE:] = dvalues[slot, at, :].astype(out.dtype)

    places.each(spread)


def attend_back(order, lens, q, d_mixed, mixed, lse, lo, own, hi, seq_len):
    flat = jax.ShapeDtypeStruct(q.shape, BF16)
    held = pltpu.VMEM((2, seq_len, HEAD_SIZE), BF16)
    summed = pltpu.VMEM((2, seq_len, HEAD_SIZE), F32)
    return pl.pallas_call(
        attend_back_kernel,
        out_shape=(flat,) * 4,
        in_specs=[spec_smem(), spec_smem()] + [spec_vmem()] * 4 + [spec_any()] * 3,
        out_specs=(spec_vmem(),) * 4,
        scratch_shapes=[
            held,
            held,
            summed,
            summed,
            pltpu.VMEM((2 * UNIT, HEAD_SIZE), F32),
            pltpu.SemaphoreType.DMA((2,)),
            pltpu.SemaphoreType.DMA((2,)),
        ],
        compiler_params=pltpu.CompilerParams(vmem_limit_bytes=VMEM_LIMIT),
        cost_estimate=busy(75),
        name="attend_back",
    )(order, lens, q, d_mixed, mixed, lse, lo, own, hi)


def angles(block_order, tok_rows):
    inverse = THETA ** (-jnp.arange(0, HEAD_SIZE, 2, dtype=F32) / HEAD_SIZE)
    inverse = jnp.concatenate([inverse, inverse])
    units = tok_rows // UNIT
    g = lax.axis_index("tp") * units + jnp.arange(units, dtype=jnp.int32)
    seq, quarter = g // 4, g % 4
    c = jnp.arange(lax.axis_size("ctx"), dtype=jnp.int32)
    where = 2 * block_order[seq[None, :], 2 * c[:, None] + (quarter // 2)[None, :]] + (quarter % 2)[None, :]
    starts = (where.reshape(-1) * UNIT).astype(F32)
    coarse = starts[:, None] * inverse[None, :]
    fine = jnp.arange(UNIT, dtype=F32)[:, None] * inverse[None, :]
    return jnp.cos(coarse), jnp.sin(coarse), jnp.cos(fine), jnp.sin(fine)


def after(value, *earlier):
    return lax.optimization_barrier((value,) + earlier)[0]


def local_plane(
    tokens,
    teacher,
    seq_lens,
    block_order,
    in_gain,
    w_query,
    key_weight_matrix,
    value_weight_matrix,
    q_gain,
    k_gain,
    w_out,
    post_gain,
    w_gate,
    w_up,
    w_down,
):
    me = lax.axis_index("ctx")
    core = me % 2
    plane = lax.axis_index("tp")
    tok_rows, width = tokens.shape
    plane_rows = 8 * tok_rows
    seq_len = 2 * 8 * BLK
    deep = width // 8
    cols = w_gate.shape[1] // 4
    stream = tokens.astype(F32)
    normed_rows = (stream * rms_scale(stream) * in_gain).astype(BF16)
    unit = plane * (tok_rows // UNIT) + jnp.arange(tok_rows // UNIT, dtype=jnp.int32)
    seq, quarter = unit // 4, unit % 4
    start = block_order[seq, 2 * me + quarter // 2] * BLK + (quarter % 2) * UNIT
    position = start[:, None] + jnp.arange(UNIT, dtype=jnp.int32)
    valid = (position < seq_lens[seq][:, None]).astype(F32).reshape(tok_rows, 1)

    qkv_home = jnp.concatenate(
        [
            w_query.reshape(deep, 2, 2 * HEAD_SIZE),
            key_weight_matrix.reshape(deep, 2, HEAD_SIZE),
            value_weight_matrix.reshape(deep, 2, HEAD_SIZE),
        ],
        axis=2,
    )
    tables = angles(block_order, tok_rows)
    normed_all, w_qkv, queries, kv, kv_lo, kv_hi, lin, gate_parts, *parts = gather_qkv(
        normed_rows,
        jnp.transpose(qkv_home, (1, 0, 2)),
        q_gain,
        k_gain,
        tables,
        w_gate,
        w_up,
        w_down.reshape(4, cols, deep),
        w_out.reshape(2, 2 * HEAD_SIZE, deep),
    )
    up_part, down_part, out_part = parts
    out_part = out_part.reshape(width, deep)
    out_parts = [out_part] + [lax.ppermute(out_part, "ctx", [(i, i ^ n) for i in range(8)]) for n in (2, 4, 6)]
    up_parts = lax.all_gather(up_part, "tp", axis=0)
    mixed, lse = attend(block_order, seq_lens, queries, kv_lo, kv, kv_hi, seq_len)
    down_parts = lax.all_gather(down_part, "tp", axis=0)
    middle, post_rows, mixed_rows, w_o = mix(mixed, tokens, post_gain, out_parts)
    post_all, w_gu, slope, active, hidden = gather_up(post_rows, gate_parts, up_parts)
    output, diff_low, diff, error, w_d = scatter_down(hidden, down_parts, middle, teacher, valid)
    d_gu, grad_wd = gather_down_back(diff_low, w_d, slope, active, hidden)
    d_post, grad_gu = scatter_post(d_gu, w_gu, post_all)

    def home_sum(parts):
        return lax.psum_scatter(parts, "tp", scatter_dimension=0, tiled=True)[0]

    grad_down = home_sum(grad_wd)
    grad_gu = home_sum(grad_gu)
    d_mixed, d_middle, grad_post, *grad_wo, grad_down = mix_back(
        d_post, middle, diff, post_gain, w_o, mixed_rows, grad_down
    )
    grad_wo = [grad_wo[0]] + [
        lax.ppermute(grad_wo[m], "ctx", [(i, i ^ n) for i in range(8)]) for m, n in ((1, 2), (2, 4), (3, 6))
    ]

    d_queries, to_lo, d_kv, to_hi = attend_back(
        block_order,
        seq_lens,
        queries,
        d_mixed,
        mixed,
        lse,
        kv_lo,
        kv,
        kv_hi,
        seq_len,
    )
    out_sum = sum(after(g, d_queries[:8]).astype(F32) for g in grad_wo).astype(BF16)
    d_normed, grad_qkv, totals, gu_sum, grad_out = scatter_normed(
        d_queries,
        d_kv,
        to_lo,
        to_hi,
        lin,
        w_qkv,
        normed_all,
        grad_gu,
        out_sum.reshape(4, 4 * HEAD_SIZE, deep),
        tokens,
        grad_post,
        error,
        q_gain,
        k_gain,
        tables,
    )
    d_tokens, grad_gate, grad_up, grad_down, grad_query, grad_key, grad_value, grad_out = finish(
        d_normed, tokens, d_middle, in_gain, gu_sum, grad_down, grad_qkv, grad_out
    )
    lanes = width // HEAD_SIZE
    count_valid = jnp.sum(seq_lens).astype(F32)
    loss = 0.5 * jnp.sum(totals[2 * lanes + 2]) / (count_valid * MODEL_WIDTH)
    return (
        output,
        loss,
        d_tokens,
        totals[:lanes].reshape(width),
        grad_query,
        grad_key,
        grad_value,
        totals[2 * lanes],
        totals[2 * lanes + 1],
        grad_out,
        totals[lanes : 2 * lanes].reshape(width),
        grad_gate,
        grad_up,
        grad_down.reshape(4 * cols, deep),
    )


def solution(mesh):
    in_specs = (
        P(("ctx", "tp"), None),
        P(("ctx", "tp"), None),
        P(),
        P(),
        P(),
        P("ctx", "tp"),
        P("ctx", "tp"),
        P("ctx", "tp"),
        P(),
        P(),
        P("tp", "ctx"),
        P(),
        P("ctx", "tp"),
        P("ctx", "tp"),
        P("tp", "ctx"),
    )
    out_specs = (
        P(("ctx", "tp"), None),
        P(),
        P(("ctx", "tp"), None),
        P(),
        P("ctx", "tp"),
        P("ctx", "tp"),
        P("ctx", "tp"),
        P(),
        P(),
        P("tp", "ctx"),
        P(),
        P("ctx", "tp"),
        P("ctx", "tp"),
        P("tp", "ctx"),
    )
    body = local_plane if (mesh.shape["ctx"], mesh.shape["tp"]) == (8, 4) else local
    return jax.shard_map(body, mesh=mesh, in_specs=in_specs, out_specs=out_specs, check_vma=False)
```

```python
import functools

import jax
import jax.numpy as jnp
from jax import lax
from jax.experimental import pallas as pl
from jax.experimental.pallas import tpu as pltpu
from jax.sharding import PartitionSpec as P

MODEL_WIDTH = 2048
HEAD_SIZE = 128
SEQS = 3
BLK = 256


EPS = 1e-06
THETA = 1000000.0
FLOOR = -1e30


def from_behind(x, axis, by):
    count = lax.axis_size(axis)
    return lax.ppermute(x, axis, [(i, (i + by) % count) for i in range(count)])


def rms_scale(value):
    return lax.rsqrt(jnp.mean(value * value, axis=-1, keepdims=True) + EPS)


def rms_back(value, scale, grad_normed):
    return scale * grad_normed - value * scale**3 * jnp.mean(
        grad_normed * value, axis=-1, keepdims=True
    )


def rotate(value, cosine, sine):
    half = value.shape[-1] // 2
    first = value[..., :half]
    second = value[..., half:]
    return jnp.concatenate(
        [first * cosine - second * sine, second * cosine + first * sine], axis=-1
    )


def rotate_back(grad, cosine, sine):
    half = grad.shape[-1] // 2
    first = grad[..., :half]
    second = grad[..., half:]
    return jnp.concatenate(
        [first * cosine + second * sine, second * cosine - first * sine], axis=-1
    )


def matmul(left, right):
    return jnp.dot(left, right, preferred_element_type=jnp.float32)


def matmul_tn(left, right):
    return lax.dot_general(
        left, right, (((0,), (0,)), ((), ())), preferred_element_type=jnp.float32
    )


def matmul_nt(left, right):
    return lax.dot_general(
        left, right, (((1,), (1,)), ((), ())), preferred_element_type=jnp.float32
    )


def row_slice(value, start, count):
    return lax.dynamic_slice_in_dim(value, start, count, 0)


def local(
    tokens,
    teacher,
    seq_lens,
    block_order,
    in_gain,
    w_query,
    key_weight_matrix,
    value_weight_matrix,
    q_gain,
    k_gain,
    w_out,
    post_gain,
    w_gate,
    w_up,
    w_down,
):
    ctx_count = lax.axis_size("ctx")
    ctx_index = lax.axis_index("ctx")
    tp_index = lax.axis_index("tp")
    tok_rows = tokens.shape[0]
    ctx_rows = tok_rows * lax.axis_size("tp")
    block_span = 2 * BLK
    q_heads = w_query.shape[1] // HEAD_SIZE
    kv_heads = key_weight_matrix.shape[1] // HEAD_SIZE
    group_width = q_heads // kv_heads
    scale_qk = HEAD_SIZE ** (-0.5)
    weights = (
        lax.all_gather(w_query, "ctx", axis=0, tiled=True),
        lax.all_gather(key_weight_matrix, "ctx", axis=0, tiled=True),
        lax.all_gather(value_weight_matrix, "ctx", axis=0, tiled=True),
        lax.all_gather(w_out, "ctx", axis=1, tiled=True),
        lax.all_gather(w_gate, "ctx", axis=0, tiled=True),
        lax.all_gather(w_up, "ctx", axis=0, tiled=True),
        lax.all_gather(w_down, "ctx", axis=1, tiled=True),
    )
    wq_full, wk_full, wv_full, wo_full, wg_full, wu_full, wd_full = weights
    offsets = jnp.arange(BLK, dtype=jnp.int32)

    def block_positions(owner):
        columns = lax.dynamic_slice_in_dim(block_order, 2 * owner, 2, 1)
        return (columns[:, :, None] * BLK + offsets).reshape(SEQS, block_span)

    query_pos = block_positions(ctx_index)
    flat_pos = query_pos.reshape(-1)
    inverse = THETA ** (-jnp.arange(0, HEAD_SIZE, 2, dtype=jnp.float32) / HEAD_SIZE)
    angle = flat_pos.astype(jnp.float32)[:, None] * inverse[None, :]
    cosine = jnp.cos(angle)[:, None, :]
    sine = jnp.sin(angle)[:, None, :]
    stream = tokens.astype(jnp.float32)
    scale_in = rms_scale(stream)
    unit_in = stream * scale_in
    normed_rows = (unit_in * in_gain).astype(jnp.bfloat16)
    normed_all = lax.all_gather(normed_rows, "tp", axis=0, tiled=True)
    query_lin = matmul(normed_all, wq_full).reshape(ctx_rows, q_heads, HEAD_SIZE)
    key_linear = matmul(normed_all, wk_full).reshape(ctx_rows, kv_heads, HEAD_SIZE)
    value_low = (
        matmul(normed_all, wv_full)
        .astype(jnp.bfloat16)
        .reshape(SEQS, block_span, kv_heads, HEAD_SIZE)
    )
    query_scale = rms_scale(query_lin)
    query_unit = query_lin * query_scale
    query_low = (
        rotate(query_unit * q_gain, cosine, sine)
        .astype(jnp.bfloat16)
        .reshape(SEQS, block_span, kv_heads, group_width, HEAD_SIZE)
    )
    key_scale = rms_scale(key_linear)
    key_unit = key_linear * key_scale
    key_low = (
        rotate(key_unit * k_gain, cosine, sine)
        .astype(jnp.bfloat16)
        .reshape(SEQS, block_span, kv_heads, HEAD_SIZE)
    )

    def scores_of(keys, key_pos):
        raw = (
            jnp.einsum("sqkgd,slkd->skgql", query_low, keys, preferred_element_type=jnp.float32)
            * scale_qk
        )
        allowed = (key_pos[:, None, :] <= query_pos[:, :, None]) & (
            key_pos[:, None, :] < seq_lens[:, None, None]
        )
        allowed = allowed[:, None, None, :, :]
        return (jnp.where(allowed, raw, FLOOR), allowed)

    def absorb(state, keys, value_rows, owner):
        running_top, running_total, running_acc = state
        scores, allowed = scores_of(keys, block_positions(owner))
        new_top = jnp.maximum(running_top, jnp.max(scores, axis=-1))
        weights_now = jnp.where(allowed, jnp.exp(scores - new_top[..., None]), 0.0)
        shrink = jnp.exp(running_top - new_top)
        running_total = running_total * shrink + jnp.sum(weights_now, axis=-1)
        running_acc = running_acc * shrink[..., None] + jnp.einsum(
            "skgql,slkd->skgqd",
            weights_now.astype(jnp.bfloat16),
            value_rows,
            preferred_element_type=jnp.float32,
        )
        return (new_top, running_total, running_acc)

    stat_shape = (SEQS, kv_heads, group_width, block_span)
    initial = (
        jnp.full(stat_shape, FLOOR, jnp.float32),
        jnp.zeros(stat_shape, jnp.float32),
        jnp.zeros(stat_shape + (HEAD_SIZE,), jnp.float32),
    )
    first_state = absorb(initial, key_low, value_low, ctx_index)

    def cycle_turn(carry, turn):
        keys, value_rows, state = carry
        keys, value_rows = from_behind((keys, value_rows), "ctx", 1)
        owner = (ctx_index - turn) % ctx_count
        state = absorb(state, keys, value_rows, owner)
        return ((keys, value_rows, state), (keys, value_rows))

    (unused_keys, unused_values, final_state), (kept_keys, kept_values) = lax.scan(
        cycle_turn, (key_low, value_low, first_state), jnp.arange(1, ctx_count, dtype=jnp.int32)
    )
    all_keys = jnp.concatenate([key_low[None], kept_keys], axis=0)
    all_values = jnp.concatenate([value_low[None], kept_values], axis=0)
    top_final, total_final, acc_final = final_state
    log_total = top_final + jnp.log(total_final)
    attn_exact = acc_final / total_final[..., None]
    mixed_low = (
        jnp.transpose(attn_exact, (0, 3, 1, 2, 4))
        .reshape(ctx_rows, q_heads * HEAD_SIZE)
        .astype(jnp.bfloat16)
    )
    middle = stream + lax.psum_scatter(
        matmul(row_slice(mixed_low, jnp.int32(0), lax.axis_size("tp") * tok_rows), wo_full).astype(
            jnp.bfloat16
        ),
        "tp",
        scatter_dimension=0,
        tiled=True,
    ).astype(jnp.float32)
    scale_post = rms_scale(middle)
    unit_post = middle * scale_post
    post_rows = (unit_post * post_gain).astype(jnp.bfloat16)
    post_all = lax.all_gather(post_rows, "tp", axis=0, tiled=True)
    gate = matmul(post_all, wg_full)
    up_val = matmul(post_all, wu_full)
    sigma = jax.nn.sigmoid(gate)
    active = gate * sigma
    hidden_low = (active * up_val).astype(jnp.bfloat16)
    result = middle + lax.psum_scatter(
        matmul(row_slice(hidden_low, jnp.int32(0), lax.axis_size("tp") * tok_rows), wd_full).astype(
            jnp.bfloat16
        ),
        "tp",
        scatter_dimension=0,
        tiled=True,
    ).astype(jnp.float32)
    output = result.astype(jnp.bfloat16)
    valid_all = (query_pos < seq_lens[:, None]).reshape(-1).astype(jnp.float32)
    valid_rows = row_slice(valid_all, tp_index * tok_rows, tok_rows)
    diff = (result - teacher.astype(jnp.float32)) * valid_rows[:, None]
    error_local = jnp.sum(diff * diff)
    diff_low = diff.astype(jnp.bfloat16)
    diff_all = lax.all_gather(diff_low, "tp", axis=0, tiled=True)
    weights_two = (
        lax.all_gather(w_query, "ctx", axis=0, tiled=True),
        lax.all_gather(key_weight_matrix, "ctx", axis=0, tiled=True),
        lax.all_gather(value_weight_matrix, "ctx", axis=0, tiled=True),
        lax.all_gather(w_out, "ctx", axis=1, tiled=True),
        lax.all_gather(w_gate, "ctx", axis=0, tiled=True),
        lax.all_gather(w_up, "ctx", axis=0, tiled=True),
        lax.all_gather(w_down, "ctx", axis=1, tiled=True),
    )
    bq_full, bk_full, bv_full, bo_full, bg_full, bu_full, bd_full = weights_two
    grad_wd = matmul_tn(hidden_low, diff_all)
    d_hidden = matmul_nt(diff_all, bd_full)
    d_gate = (d_hidden * up_val * sigma * (1.0 + gate * (1.0 - sigma))).astype(jnp.bfloat16)
    d_up = (d_hidden * active).astype(jnp.bfloat16)
    grad_wg = matmul_tn(post_all, d_gate)
    grad_wu = matmul_tn(post_all, d_up)
    start = jnp.int32(0)
    d_post = lax.psum_scatter(
        (
            matmul_nt(row_slice(d_gate, start, lax.axis_size("tp") * tok_rows), bg_full)
            + matmul_nt(row_slice(d_up, start, lax.axis_size("tp") * tok_rows), bu_full)
        ).astype(jnp.bfloat16),
        "tp",
        scatter_dimension=0,
        tiled=True,
    ).astype(jnp.float32)
    grad_post_local = jnp.sum(d_post * unit_post, axis=0)
    d_middle = diff + rms_back(middle, scale_post, d_post * post_gain)
    d_mid_low = d_middle.astype(jnp.bfloat16)
    d_mid_all = lax.all_gather(d_mid_low, "tp", axis=0, tiled=True)
    grad_wo = matmul_tn(mixed_low, d_mid_all)
    d_mixed = matmul_nt(d_mid_all, bo_full).astype(jnp.bfloat16)
    d_mixed_grid = jnp.transpose(
        d_mixed.reshape(SEQS, block_span, kv_heads, group_width, HEAD_SIZE), (0, 2, 3, 1, 4)
    )
    delta = jnp.sum(d_mixed_grid.astype(jnp.float32) * attn_exact, axis=-1)

    def revisit(carry, turn):
        grad_queries, grad_keys, grad_values = carry
        owner = (ctx_index - turn) % ctx_count
        keys = all_keys[turn]
        value_rows = all_values[turn]
        scores, allowed = scores_of(keys, block_positions(owner))
        probs = jnp.where(allowed, jnp.exp(scores - log_total[..., None]), 0.0)
        probs_low = probs.astype(jnp.bfloat16)
        d_probs = jnp.einsum(
            "skgqd,slkd->skgql", d_mixed_grid, value_rows, preferred_element_type=jnp.float32
        )
        d_scores = (probs * (d_probs - delta[..., None])).astype(jnp.bfloat16)
        grad_queries = grad_queries + jnp.einsum(
            "skgql,slkd->skgqd", d_scores, keys, preferred_element_type=jnp.float32
        )
        grad_keys = grad_keys + jnp.einsum(
            "skgql,sqkgd->slkd", d_scores, query_low, preferred_element_type=jnp.float32
        )
        grad_values = grad_values + jnp.einsum(
            "skgql,skgqd->slkd", probs_low, d_mixed_grid, preferred_element_type=jnp.float32
        )
        grad_keys, grad_values = (
            from_behind(grad_keys.astype(jnp.bfloat16), "ctx", 1).astype(grad_keys.dtype),
            from_behind(grad_values.astype(jnp.bfloat16), "ctx", 1).astype(grad_values.dtype),
        )
        return ((grad_queries, grad_keys, grad_values), None)

    kv_shape = (SEQS, block_span, kv_heads, HEAD_SIZE)
    start_carry = (
        jnp.zeros(stat_shape + (HEAD_SIZE,), jnp.float32),
        jnp.zeros(kv_shape, jnp.float32),
        jnp.zeros(kv_shape, jnp.float32),
    )
    (grad_queries, grad_keys, grad_values), unused_out = lax.scan(
        revisit, start_carry, jnp.arange(ctx_count, dtype=jnp.int32)
    )
    grad_queries = (
        jnp.transpose(grad_queries, (0, 3, 1, 2, 4)).reshape(ctx_rows, q_heads, HEAD_SIZE)
        * scale_qk
    )
    grad_keys = grad_keys.reshape(ctx_rows, kv_heads, HEAD_SIZE) * scale_qk
    d_values = grad_values.reshape(ctx_rows, kv_heads * HEAD_SIZE).astype(jnp.bfloat16)
    query_back = rotate_back(grad_queries, cosine, sine)
    grad_q_local = jnp.sum(query_back * query_unit, axis=(0, 1))
    d_query_lin = (
        rms_back(query_lin, query_scale, query_back * q_gain)
        .reshape(ctx_rows, q_heads * HEAD_SIZE)
        .astype(jnp.bfloat16)
    )
    key_back = rotate_back(grad_keys, cosine, sine)
    grad_k_local = jnp.sum(key_back * key_unit, axis=(0, 1))
    d_key_lin = (
        rms_back(key_linear, key_scale, key_back * k_gain)
        .reshape(ctx_rows, kv_heads * HEAD_SIZE)
        .astype(jnp.bfloat16)
    )
    grad_wq = matmul_tn(normed_all, d_query_lin)
    grad_wk = matmul_tn(normed_all, d_key_lin)
    grad_wv = matmul_tn(normed_all, d_values)
    start = jnp.int32(0)
    part_query = matmul_nt(row_slice(d_query_lin, start, lax.axis_size("tp") * tok_rows), bq_full)
    part_key = matmul_nt(row_slice(d_key_lin, start, lax.axis_size("tp") * tok_rows), bk_full)
    part_value = matmul_nt(row_slice(d_values, start, lax.axis_size("tp") * tok_rows), bv_full)
    d_normed = lax.psum_scatter(
        (part_query + part_key + part_value).astype(jnp.bfloat16),
        "tp",
        scatter_dimension=0,
        tiled=True,
    ).astype(jnp.float32)
    grad_in_local = jnp.sum(d_normed * unit_in, axis=0)
    d_tokens = (d_middle + rms_back(stream, scale_in, d_normed * in_gain)).astype(jnp.bfloat16)
    summed = (
        lax.psum_scatter(
            grad_wq.astype(jnp.bfloat16), "ctx", scatter_dimension=0, tiled=True
        ).astype(jnp.float32),
        lax.psum_scatter(
            grad_wk.astype(jnp.bfloat16), "ctx", scatter_dimension=0, tiled=True
        ).astype(jnp.float32),
        lax.psum_scatter(
            grad_wv.astype(jnp.bfloat16), "ctx", scatter_dimension=0, tiled=True
        ).astype(jnp.float32),
        lax.psum_scatter(
            grad_wo.astype(jnp.bfloat16), "ctx", scatter_dimension=1, tiled=True
        ).astype(jnp.float32),
        lax.psum_scatter(
            grad_wg.astype(jnp.bfloat16), "ctx", scatter_dimension=0, tiled=True
        ).astype(jnp.float32),
        lax.psum_scatter(
            grad_wu.astype(jnp.bfloat16), "ctx", scatter_dimension=0, tiled=True
        ).astype(jnp.float32),
        lax.psum_scatter(
            grad_wd.astype(jnp.bfloat16), "ctx", scatter_dimension=1, tiled=True
        ).astype(jnp.float32),
    )
    totals = lax.psum(
        (grad_in_local, grad_q_local, grad_k_local, grad_post_local, error_local), ("ctx", "tp")
    )
    count_valid = jnp.sum(seq_lens).astype(jnp.float32)
    loss = 0.5 * totals[4] / (count_valid * MODEL_WIDTH)
    return (
        output,
        loss,
        d_tokens,
        totals[0],
        summed[0],
        summed[1],
        summed[2],
        totals[1],
        totals[2],
        summed[3],
        totals[3],
        summed[4],
        summed[5],
        summed[6],
    )


F32 = jnp.float32
BF16 = jnp.bfloat16
MESH = pl.DeviceIdType.MESH
VMEM_LIMIT = 62 << 20


def busy(us):
    return pl.CostEstimate(flops=0, bytes_accessed=us * 3_000_000, transcendentals=0)

LOG2E = 1.4426950408889634
UNIT = 128
KEYS = 512
CORE_GROUPS = [[0, 2, 4, 6], [1, 3, 5, 7]]
SIBLING = [(i, i ^ 1) for i in range(8)]


def spec_vmem():
    return pl.BlockSpec(memory_space=pltpu.VMEM)


def spec_any():
    return pl.BlockSpec(memory_space=pl.ANY)


def spec_smem():
    return pl.BlockSpec(memory_space=pltpu.SMEM)


def plane_neighbours():
    me = lax.axis_index("ctx")
    core = lax.rem(me, 2)
    x = lax.rem(me // 2, 2)
    y = me // 4
    sib = me + 1 - 2 * core
    nx = me + 2 - 4 * x
    ny = me + 4 - 8 * y
    dg = nx + 4 - 8 * y
    return me, sib, nx, ny, dg


def greet(devices):
    barrier = pltpu.get_barrier_semaphore()
    for device in devices:
        pl.semaphore_signal(barrier, inc=1, device_id={"ctx": device}, device_id_type=MESH)
    pl.semaphore_wait(barrier, len(devices))


def pick(step, options):
    value = options[0]
    for i in range(1, len(options)):
        value = jnp.where(step == i, options[i], value)
    return value


SUBS = 4
BY_X, BY_Y = (0, 2, 1, 3), (1, 3, 0, 2)


def on_ctx(device):
    return {"ctx": device}


def on_plane(plane):
    return {"tp": plane}


def send(src, dst, send_sem, recv_sem, where):
    return pltpu.make_async_remote_copy(
        src_ref=src,
        dst_ref=dst,
        send_sem=send_sem,
        recv_sem=recv_sem,
        device_id=where,
        device_id_type=MESH,
    )


class Gather:
    def __init__(self, x_ref, xs, local_sem, send_sems, recv_sems):
        self.x_ref, self.xs = x_ref, xs
        self.local_sem, self.send_sems, self.recv_sems = local_sem, send_sems, recv_sems
        self.me, self.sib, self.nx, self.ny, self.dg = plane_neighbours()
        self.shift = self.sib - self.me
        self.piece = x_ref.shape[0] // SUBS

    def part(self, block, s):
        return self.xs.at[block, pl.ds(s * self.piece, self.piece)]

    def remote(self, src, kind, block, s, device):
        return send(
            src, self.part(block, s), self.send_sems.at[kind, s], self.recv_sems.at[block, s], on_ctx(device)
        )

    def own(self, s):
        return self.x_ref.at[pl.ds(s * self.piece, self.piece)]

    def start(self):
        for s, t in zip(BY_X, BY_Y):
            self.remote(self.own(s), 0, self.me, s, self.nx).start()
            self.remote(self.own(t), 1, self.me, t, self.ny).start()
        for s in range(SUBS):
            self.remote(self.own(s), 2, self.me, s, self.sib).start()
        keep = pltpu.make_async_copy(self.x_ref, self.xs.at[self.me], self.local_sem)
        keep.start()
        keep.wait()

    def arrived(self, block, s):
        self.remote(self.part(block, s), 0, block, s, self.sib).wait_recv()

    def relay(self, kind, block, s, device):
        self.remote(self.part(block, s), kind, block, s, device).start()

    def pass_on(self, i):
        s, t = BY_X[i], BY_Y[i]
        self.arrived(self.nx, s)
        if s % 2 == 0:
            self.relay(3, self.nx, s, self.ny)
        self.relay(4, self.nx, s, self.sib)
        self.arrived(self.ny, t)
        if t % 2 == 1:
            self.relay(3, self.ny, t, self.nx)
        self.relay(5, self.ny, t, self.sib)

    def far_half(self, h):
        for s in (2 * h, 2 * h + 1):
            self.arrived(self.dg, s)
            self.relay(6, self.dg, s, self.sib)

    def all_of(self, block, pieces=range(SUBS)):
        for s in pieces:
            self.arrived(block, s)

    def pass_all(self):
        for i in range(SUBS):
            self.pass_on(i)

    def before(self, step, passing=True):
        for at, act in (
            (1, lambda: self.all_of(self.sib)),
            (2, self.pass_all if passing else lambda: None),
            (3, lambda: self.all_of(self.nx + self.shift)),
            (4, lambda: self.far_half(0)),
            (5, lambda: self.all_of(self.ny + self.shift)),
            (6, lambda: self.far_half(1)),
            (7, lambda: self.all_of(self.dg + self.shift)),
        ):
            pl.when(step == at)(act)

    def before_half(self, step):
        for at, act in (
            (2, lambda: self.all_of(self.sib)),
            (4, self.pass_all),
            (6, lambda: self.all_of(self.nx + self.shift)),
            (8, lambda: self.far_half(0)),
            (10, lambda: self.all_of(self.ny + self.shift)),
            (13, lambda: self.all_of(self.dg + self.shift, (0, 1))),
            (14, lambda: self.far_half(1)),
            (15, lambda: self.all_of(self.dg + self.shift, (2, 3))),
        ):
            pl.when(step == at)(act)

    def block(self, step):
        near = (self.me, self.nx, self.ny, self.dg)
        return pick(step, [b + o for b in near for o in (0, self.shift)])

    def half_block(self, step):
        last = step >= 12
        n = jnp.where(last, 6 + lax.rem(step, 2), step // 2)
        return self.block(n), jnp.where(last, (step - 12) // 2, lax.rem(step, 2))

    def finish(self):
        for s in range(SUBS):
            for kind in range(7):
                self.remote(self.part(self.me, s), kind, self.me, s, self.sib).wait_send()


def gather_scratch(rows, width):
    return [
        pltpu.VMEM((8, rows, width), BF16),
        pltpu.SemaphoreType.DMA,
        pltpu.SemaphoreType.DMA((7, SUBS)),
        pltpu.SemaphoreType.DMA((8, SUBS)),
    ]


class Scatter:
    def __init__(self, to_sib, from_sib, own, diag_out, diag_in, x_out, y_out, x_in, y_in, sends, recvs):
        self.to_sib, self.from_sib, self.own = to_sib, from_sib, own
        self.diag_out, self.diag_in = diag_out, diag_in
        self.x_out, self.y_out, self.x_in, self.y_in = x_out, y_out, x_in, y_in
        self.sends, self.recvs = sends, recvs
        self.me, self.sib, self.nx, self.ny, self.dg = plane_neighbours()
        self.rows = diag_out.shape[0]

    def round(self, i):
        return pl.ds(i * (self.rows // 2), self.rows // 2)

    def piece(self, i, half):
        quarter = self.rows // 4
        return pl.ds((2 * i + half) * quarter, quarter)

    def remote(self, src, dst, kind, i, device):
        return send(src, dst, self.sends.at[kind, i], self.recvs.at[kind, i], on_ctx(device))

    def sibling(self, n, i):
        at = self.round(i)
        return self.remote(self.to_sib.at[n, at], self.from_sib.at[n, at], n, i, self.sib)

    def hop(self, kind, i):
        out, into, half, device = (
            (self.diag_out, self.diag_in, 0, self.nx),
            (self.diag_out, self.diag_in, 1, self.ny),
            (self.x_out, self.x_in, 0, self.nx),
            (self.x_out, self.x_in, 1, self.nx),
            (self.y_out, self.y_in, 0, self.ny),
            (self.y_out, self.y_in, 1, self.ny),
        )[kind]
        at = self.piece(i, half)
        return self.remote(out.at[at], into.at[at], 4 + kind, i, device)

    def blocks(self):
        shift = self.sib - self.me
        return [b + o for b in (self.dg, self.nx, self.ny, self.me) for o in (shift, 0)]

    def block(self, step):
        return pick(2 * (step // 4) + lax.rem(step, 2), self.blocks())

    def chip_sum(self, n, at):
        return self.own[n, at].astype(F32) + self.from_sib[n, at].astype(F32)

    def step(self, step, product, late=False):
        block = self.block(step)
        n = step // 4
        i = lax.rem(step, 4) // 2
        at = self.round(pl.multiple_of(i, 1))

        @pl.when(lax.rem(step, 2) == 0)
        def _():
            product(block, at, self.to_sib, n)
            self.sibling(n, i).start()

        @pl.when(lax.rem(step, 2) == 1)
        def _():
            product(block, at, self.own, n)
            self.sibling(n, i).wait_recv()

        for r in range(2):
            first, second = self.piece(r, 0), self.piece(r, 1)

            @pl.when(step == 1 + 2 * r)
            def _():
                self.diag_out[first] = self.chip_sum(0, first).astype(BF16)
                self.hop(0, r).start()
                self.diag_out[second] = self.chip_sum(0, second).astype(BF16)
                self.hop(1, r).start()

            @pl.when(step == 5 + 2 * r)
            def _():
                self.x_out[first] = self.chip_sum(1, first).astype(BF16)
                self.hop(2, r).start()

            @pl.when(step == 9 + 2 * r)
            def _():
                self.y_out[second] = self.chip_sum(2, second).astype(BF16)
                self.hop(5, r).start()

        if not late:

            @pl.when(step == 11)
            def _():
                self.second_wave()

    def second_wave(self):
        for i in range(2):
            first, second = self.piece(i, 0), self.piece(i, 1)
            self.hop(0, i).wait_recv()
            self.y_out[first] = (self.chip_sum(2, first) + self.diag_in[first].astype(F32)).astype(BF16)
            self.hop(4, i).start()
            self.hop(1, i).wait_recv()
            self.x_out[second] = (self.chip_sum(1, second) + self.diag_in[second].astype(F32)).astype(BF16)
            self.hop(3, i).start()

    def finish(self, o_ref):
        for i in range(2):
            for kind in range(2, 6):
                self.hop(kind, i).wait_recv()
            at = self.round(i)
            o_ref[at] = (
                self.chip_sum(3, at) + self.x_in[at].astype(F32) + self.y_in[at].astype(F32)
            ).astype(o_ref.dtype)
        for i in range(2):
            for n in range(4):
                self.sibling(n, i).wait_send()
            for kind in range(6):
                self.hop(kind, i).wait_send()


def scatter_scratch(rows, width):
    four = pltpu.VMEM((4, rows, width), BF16)
    one = pltpu.VMEM((rows, width), BF16)
    return [four] * 3 + [one] * 6 + [pltpu.SemaphoreType.DMA((10, 2)), pltpu.SemaphoreType.DMA((10, 2))]


N_SCATTER = 11


def nn(left, right):
    return lax.dot_general(left, right, (((1,), (0,)), ((), ())), preferred_element_type=F32)


def nt(left, right):
    return lax.dot_general(left, right, (((1,), (1,)), ((), ())), preferred_element_type=F32)


def tn(left, right):
    return lax.dot_general(left, right, (((0,), (0,)), ((), ())), preferred_element_type=F32)


def comm_params(collective_id):
    return pltpu.CompilerParams(
        collective_id=collective_id, has_side_effects=True, vmem_limit_bytes=VMEM_LIMIT
    )


def greet_column(devices):
    barrier = pltpu.get_barrier_semaphore()
    plane, planes = lax.axis_index("tp"), lax.axis_size("tp")
    for device in devices:
        pl.semaphore_signal(barrier, inc=1, device_id=on_ctx(device), device_id_type=MESH)
    for step in (1, planes - 1):
        where = on_plane(lax.rem(plane + step, planes))
        pl.semaphore_signal(barrier, inc=1, device_id=where, device_id_type=MESH)
    pl.semaphore_wait(barrier, len(devices) + 2)


class Line:
    def __init__(self, up_src, down_src, from_lo, from_hi, sends, recvs, rows, back):
        self.up_src, self.down_src, self.from_lo, self.from_hi = up_src, down_src, from_lo, from_hi
        self.sends, self.recvs = sends, recvs
        self.units = rows // UNIT
        self.back = back
        self.plane, self.planes = lax.axis_index("tp"), lax.axis_size("tp")

    def at(self, block, i):
        return pl.ds(pl.multiple_of((block * self.units + i) * UNIT, UNIT), UNIT)

    def up(self, block, i):
        at, n = self.at(block, i), block * self.units + i
        return send(self.up_src.at[at], self.from_lo.at[at], self.sends.at[0, n], self.recvs.at[0, n], on_plane(self.plane + 1))

    def down(self, block, i):
        at, n = self.at(block, i), block * self.units + i
        return send(self.down_src.at[at], self.from_hi.at[at], self.sends.at[1, n], self.recvs.at[1, n], on_plane(self.plane - 1))

    def each(self, block, ups, downs):
        for i in range(self.units):
            up = i < self.plane + 1 if self.back else i >= self.plane
            down = i >= self.plane - 1 if self.back else i < self.plane

            @pl.when(up & (self.plane < self.planes - 1))
            def _():
                ups(self.up(block, i))

            @pl.when(down & (self.plane > 0))
            def _():
                downs(self.down(block, i))

    def start(self, block):
        self.each(block, lambda copy: copy.start(), lambda copy: copy.start())

    def sent(self, block):
        self.each(block, lambda copy: copy.wait_send(), lambda copy: copy.wait_send())

    def arrived(self, block):
        for i in range(self.units):
            below = i < self.plane if self.back else i >= self.plane - 1
            above = i >= self.plane if self.back else i < self.plane + 1

            @pl.when(below & (self.plane > 0))
            def _():
                self.up(block, i).wait_recv()

            @pl.when(above & (self.plane < self.planes - 1))
            def _():
                self.down(block, i).wait_recv()


class ChipSwap:
    def __init__(self, src, dst, local_sem, send_sems, recv_sems):
        self.src, self.dst = src, dst
        self.local_sem, self.send_sems, self.recv_sems = local_sem, send_sems, recv_sems
        me, _, nx, ny, dg = plane_neighbours()
        self.chip, self.away = me // 2, (dg, nx, ny)

    def part(self, chip):
        if len(self.src.shape) == 3:
            return self.src.at[chip]
        cols = self.src.shape[1] // 4
        return self.src.at[:, pl.ds(pl.multiple_of(chip * cols, HEAD_SIZE), cols)]

    def own(self):
        return pltpu.make_async_copy(self.part(self.chip), self.dst.at[self.chip], self.local_sem)

    def to(self, n):
        there = self.away[n]
        return send(
            self.part(there // 2), self.dst.at[self.chip], self.send_sems.at[n], self.recv_sems.at[self.chip], on_ctx(there)
        )

    def start(self):
        self.own().start()
        for n in range(3):
            self.to(n).start()

    def arrive(self):
        self.own().wait()
        for n in range(3):
            there = self.away[n] // 2
            send(
                self.part(there), self.dst.at[there], self.send_sems.at[n], self.recv_sems.at[there], on_ctx(self.away[n])
            ).wait_recv()

    def sent(self):
        for n in range(3):
            self.to(n).wait_send()

    def finish(self):
        self.arrive()
        self.sent()


SWAP_SCRATCH = [pltpu.SemaphoreType.DMA, pltpu.SemaphoreType.DMA((3,)), pltpu.SemaphoreType.DMA((4,))]


class LineGather:
    def __init__(self, src, dst, local_sem, send_sems, recv_sems):
        self.src, self.dst = src, dst
        self.local_sem, self.send_sems, self.recv_sems = local_sem, send_sems, recv_sems
        self.plane, self.planes = lax.axis_index("tp"), lax.axis_size("tp")
        self.pieces = src.shape[0]

    def own(self):
        return pltpu.make_async_copy(self.src, self.dst.at[self.plane], self.local_sem)

    def copy(self, way, hop, n, origin):
        src = self.src.at[n] if hop == 0 else self.dst.at[origin, n]
        return send(
            src,
            self.dst.at[origin, n],
            self.send_sems.at[way, hop, n],
            self.recv_sems.at[origin, n],
            on_plane(self.plane + 1 - 2 * way),
        )

    def ways(self, hop):
        up, down = self.plane - hop, self.plane + hop
        yield 0, up, up >= 0, self.plane < self.planes - 1
        yield 1, down, down < self.planes, self.plane > 0

    def start(self):
        self.own().start()
        for way, origin, _, goes_on in self.ways(0):

            @pl.when(goes_on)
            def _():
                for n in range(self.pieces):
                    self.copy(way, 0, n, origin).start()

    def arrive(self, hop, then=None):
        for way, origin, there, goes_on in self.ways(hop):

            @pl.when(there)
            def _():
                for n in range(self.pieces):
                    self.copy(way, 0, n, origin).wait_recv()
                    if hop == self.planes - 1:
                        continue

                    @pl.when(goes_on)
                    def _():
                        self.copy(way, hop, n, origin).start()

                if then is not None:
                    then(origin)

    def finish(self):
        self.own().wait()
        self.sent()

    def sent(self):
        for hop in range(self.planes - 1):
            for way, origin, there, goes_on in self.ways(hop):

                @pl.when(there & goes_on)
                def _():
                    for n in range(self.pieces):
                        self.copy(way, hop, n, origin).wait_send()


def line_scratch(pieces):
    dma = pltpu.SemaphoreType.DMA
    return [dma, dma((2, 3, pieces)), dma((4, pieces))]


class LineSum:
    def __init__(self, own, up_in, down_in, send_sems, recv_sems):
        self.own, self.into = own, (up_in, down_in)
        self.send_sems, self.recv_sems = send_sems, recv_sems
        self.plane, self.planes = lax.axis_index("tp"), lax.axis_size("tp")

    def copy(self, way, p, first):
        into = self.into[way]
        return send(
            self.own(p) if first else into.at[p],
            into.at[p],
            self.send_sems.at[way, p],
            self.recv_sems.at[way, p],
            on_plane(self.plane + 1 - 2 * way),
        )

    def moves(self, k):
        last = self.planes - 1
        for way in range(2):
            z = last - k if way else k
            yield way, z, (range(z) if way else range(last, z, -1))

    def stage(self, k):
        for way, z, ends in self.moves(k):

            @pl.when(self.plane == z)
            def _():
                for p in ends:
                    copy = self.copy(way, p, k == 0)
                    if k > 0:
                        copy.wait_recv()
                        into = self.into[way]
                        into[p] = (self.own(p)[...].astype(F32) + into[p].astype(F32)).astype(BF16)
                    copy.start()

    def collect(self, out):
        out[...] = self.own(self.plane)[...].astype(F32)
        for way in range(2):

            @pl.when(self.plane < self.planes - 1 if way else self.plane > 0)
            def _():
                self.copy(way, self.plane, False).wait_recv()
                out[...] += self.into[way][self.plane].astype(F32)

    def finish(self):
        for k in range(self.planes - 1):
            for way, z, ends in self.moves(k):

                @pl.when(self.plane == z)
                def _():
                    for p in ends:
                        self.copy(way, p, k == 0).wait_send()


class Total:
    def __init__(self, held, held_planes, sends, recvs):
        self.held, self.held_planes, self.sends, self.recvs = held, held_planes, sends, recvs
        self.me = lax.axis_index("ctx")
        self.plane, self.planes = lax.axis_index("tp"), lax.axis_size("tp")
        self.away = others(self.me)
        self.far = [lax.rem(self.plane + step, self.planes) for step in range(1, self.planes)]

    def here(self, c, n):
        ref = self.held.at[c]
        return send(ref, ref, self.sends.at[n], self.recvs.at[c], on_ctx(self.away[n]))

    def there(self, p, n):
        ref = self.held_planes.at[p]
        return send(ref, ref, self.sends.at[7 + n], self.recvs.at[8 + p], on_plane(self.far[n]))

    def start(self):
        for n in range(7):
            self.here(self.me, n).start()

    def middle(self):
        for n, c in enumerate(self.away):
            self.here(c, n).wait_recv()
        value = self.held[0]
        for c in range(1, 8):
            value += self.held[c]
        self.held_planes[self.plane] = value
        for n in range(len(self.far)):
            self.there(self.plane, n).start()

    def finish(self, out):
        for n, p in enumerate(self.far):
            self.there(p, n).wait_recv()
        value = self.held_planes[0]
        for p in range(1, 4):
            value += self.held_planes[p]
        out[...] = value
        for n in range(7):
            self.here(self.me, n).wait_send()
        for n in range(len(self.far)):
            self.there(self.plane, n).wait_send()


class Turn:
    def __init__(self, ca_ref, sa_ref, cb_ref, sb_ref, unit):
        ca, sa = ca_ref[pl.ds(unit, 1), :], sa_ref[pl.ds(unit, 1), :]
        cb, sb = cb_ref[...], sb_ref[...]
        self.cosine = ca * cb - sa * sb
        sine = sa * cb + ca * sb
        lane = lax.broadcasted_iota(jnp.int32, sine.shape, 1)
        self.sine = jnp.where(lane < HEAD_SIZE // 2, -sine, sine)

    def forth(self, v):
        return v * self.cosine + pltpu.roll(v, HEAD_SIZE // 2, 1) * self.sine

    def back(self, v):
        return v * self.cosine - pltpu.roll(v, HEAD_SIZE // 2, 1) * self.sine


def others(me):
    _, sib, nx, ny, dg = plane_neighbours()
    shift = sib - me
    return (dg, dg + shift, nx, nx + shift, ny, ny + shift, sib)


def qkv_kernel(
    x_ref,
    home_ref,
    qg_ref,
    kg_ref,
    ca_ref,
    sa_ref,
    cb_ref,
    sb_ref,
    gate_ref,
    up_ref,
    down_ref,
    out_ref,
    all_ref,
    w_out_ref,
    q_ref,
    kv_ref,
    lo_ref,
    hi_ref,
    lin_ref,
    gates_ref,
    ups_ref,
    downs_ref,
    outs_ref,
    xs,
    local_sem,
    send_sems,
    recv_sems,
    keep_sems,
    w,
    w_local,
    w_sends,
    w_recvs,
    slab,
    gate_part,
    kv_sends,
    kv_recvs,
    *sems,
):
    ring = Gather(x_ref, xs, local_sem, send_sems, recv_sems)
    me = ring.me
    rows = x_ref.shape[0]
    deep = home_ref.shape[1]
    slabs = LineGather(home_ref, slab, *sems[0:3])
    outs = LineGather(out_ref, outs_ref, *sems[3:6])
    gates = LineGather(gate_part.at[pl.ds(0, 3)], gates_ref, *sems[6:9])
    gate_swap = ChipSwap(gate_ref, gate_part, *sems[9:12])
    late_swaps = (ChipSwap(up_ref, ups_ref.at[pl.ds(0, 4)], *sems[12:15]), ChipSwap(down_ref, downs_ref, *sems[15:18]))
    line = Line(kv_ref, kv_ref, lo_ref, hi_ref, kv_sends, kv_recvs, rows, False)

    def weight(source, origin, k):
        return send(
            slab.at[origin, k],
            w.at[pl.ds(source * deep, deep)],
            w_sends.at[2 * origin + k],
            w_recvs.at[source],
            on_ctx(2 * origin + k),
        )

    own_weight = pltpu.make_async_copy(
        slab.at[me // 2, lax.rem(me, 2)], w.at[pl.ds(me * deep, deep)], w_local
    )

    def hand_out(origin):
        for first in range(2):
            k = lax.rem(me + first, 2)

            @pl.when(2 * origin + k == me)
            def _():
                own_weight.start()

            @pl.when(2 * origin + k != me)
            def _():
                weight(me, origin, k).start()

    greet_column(others(me))
    gate_swap.start()
    slabs.start()
    ring.start()
    slabs.own().wait()
    hand_out(slabs.plane)
    slabs.arrive(1, hand_out)
    gate_swap.arrive()
    gates.start()
    keep_last = pltpu.make_async_copy(gate_part.at[3], ups_ref.at[4], sems[18])
    keep_last.start()
    slabs.arrive(2, hand_out)
    outs.start()
    ring.pass_on(0)
    slabs.arrive(3, hand_out)
    for i in range(1, SUBS):
        ring.pass_on(i)
    for swap in late_swaps:
        swap.start()
    outs.arrive(1)
    gates.arrive(1)
    own_weight.wait()
    for device in others(me):
        weight(device, 0, 0).wait_recv()
    keep_w = pltpu.make_async_copy(w, w_out_ref, w_local)
    keep_w.start()

    def keep(block):
        return pltpu.make_async_copy(xs.at[block], all_ref.at[block], keep_sems.at[block])

    def head(v, gain_ref, turn):
        scale = lax.rsqrt(jnp.mean(v * v, axis=-1, keepdims=True) + EPS)
        return turn.forth(v * scale * gain_ref[...])

    def turn(step, carry):
        @pl.when(step == 4)
        def _():
            outs.arrive(2)
            gates.arrive(2)

        ring.before(step, passing=False)
        block = ring.block(step)
        keep(block).start()
        lin = nn(xs[block], w[...])
        lin_ref[pl.ds(pl.multiple_of(block * rows, rows), rows), :] = lin[:, : 3 * HEAD_SIZE]
        for i in range(rows // UNIT):
            unit = block * (rows // UNIT) + i
            rotation = Turn(ca_ref, sa_ref, cb_ref, sb_ref, unit)
            here = pl.ds(pl.multiple_of(unit * UNIT, UNIT), UNIT)
            part = lin[i * UNIT : (i + 1) * UNIT]
            for h in range(2):
                lanes = slice(h * HEAD_SIZE, (h + 1) * HEAD_SIZE)
                query = head(part[:, lanes], qg_ref, rotation)
                q_ref[here, lanes] = (query * (HEAD_SIZE**-0.5 * LOG2E)).astype(BF16)
            key = head(part[:, 2 * HEAD_SIZE : 3 * HEAD_SIZE], kg_ref, rotation)
            kv_ref[here, :HEAD_SIZE] = key.astype(BF16)
            kv_ref[here, HEAD_SIZE:] = part[:, 3 * HEAD_SIZE :].astype(BF16)

        line.start(block)
        return carry

    lax.fori_loop(0, 8, turn, 0)
    ring.finish()
    keep_w.wait()
    for origin in range(4):
        for k in range(2):

            @pl.when(2 * origin + k != me)
            def _():
                weight(me, origin, k).wait_send()

    for block in range(8):
        keep(block).wait()

    def settle(block, carry):
        line.sent(block)
        line.arrived(block)
        return carry

    lax.fori_loop(0, 8, settle, 0)
    for gather in (outs, gates):
        gather.arrive(3)
    for gather in (slabs, outs, gates):
        gather.finish() if gather is not slabs else gather.sent()
    gate_swap.sent()
    keep_last.wait()
    for swap in late_swaps:
        swap.finish()


def gather_qkv(normed, home, q_gain, k_gain, tables, gate, up, down, out):
    rows, width = normed.shape
    _, deep, cols = home.shape
    part = (4, gate.shape[0], gate.shape[1] // 4)
    flat = jax.ShapeDtypeStruct((8 * rows, 2 * HEAD_SIZE), BF16)
    dma = pltpu.SemaphoreType.DMA
    return pl.pallas_call(
        qkv_kernel,
        out_shape=(
            jax.ShapeDtypeStruct((8, rows, width), BF16),
            jax.ShapeDtypeStruct((8 * deep, cols), BF16),
            flat,
            flat,
            flat,
            flat,
            jax.ShapeDtypeStruct((8 * rows, 3 * HEAD_SIZE), F32),
            jax.ShapeDtypeStruct((4, 3) + part[1:], BF16),
            jax.ShapeDtypeStruct((5,) + part[1:], BF16),
            jax.ShapeDtypeStruct(down.shape, BF16),
            jax.ShapeDtypeStruct((4,) + out.shape, BF16),
        ),
        in_specs=[spec_any()] * 2 + [spec_vmem()] * 6 + [spec_any()] * 4,
        out_specs=(spec_any(), spec_any(), spec_vmem(), spec_vmem(), spec_any(), spec_any(), spec_vmem())
        + (spec_any(),) * 4,
        scratch_shapes=gather_scratch(rows, width)
        + [
            dma((8,)),
            pltpu.VMEM((8 * deep, cols), BF16),
            dma,
            dma((8,)),
            dma((8,)),
            pltpu.VMEM((4,) + home.shape, BF16),
            pltpu.VMEM(part, BF16),
            dma((2, 8 * rows // UNIT)),
            dma((2, 8 * rows // UNIT)),
        ]
        + line_scratch(home.shape[0])
        + line_scratch(out.shape[0])
        + line_scratch(3)
        + SWAP_SCRATCH * 3
        + [dma],
        compiler_params=comm_params(1),
        cost_estimate=busy(100),
        name="gather_qkv",
    )(normed, home, q_gain.reshape(1, -1), k_gain.reshape(1, -1), *tables, gate, up, down, out)


class Halves:
    def __init__(self, parts, at, local_sems, send_sems, recv_sems):
        self.parts, self.at = parts, at
        self.local_sems, self.send_sems, self.recv_sems = local_sems, send_sems, recv_sems
        self.me, self.sib = plane_neighbours()[:2]
        self.core = lax.rem(self.me, 2)

    def own(self, z, p):
        n = 4 * z + p
        return pltpu.make_async_copy(
            self.parts(2 * self.core + z, p), self.at(z, 2 * p + self.core), self.local_sems.at[n]
        )

    def swap(self, z, p):
        n = 4 * z + p
        return send(
            self.parts(2 - 2 * self.core + z, p),
            self.at(z, 2 * p + self.core),
            self.send_sems.at[n],
            self.recv_sems.at[n],
            on_ctx(self.sib),
        )

    def each(self):
        return [(z, p) for z in range(2) for p in range(4)]

    def start(self):
        for z, p in self.each():
            self.swap(z, p).start()
            self.own(z, p).start()

    def ready(self):
        for z, p in self.each():
            self.own(z, p).wait()
            n = 4 * z + p
            send(
                self.parts(2 * self.core + z, p),
                self.at(z, 2 * p + 1 - self.core),
                self.send_sems.at[n],
                self.recv_sems.at[n],
                on_ctx(self.sib),
            ).wait_recv()

    def finish(self):
        for z, p in self.each():
            self.swap(z, p).wait_send()


class Shares:
    def __init__(self, out, local_sems, send_sems, recv_sems):
        self.out = out
        self.local_sems, self.send_sems, self.recv_sems = local_sems, send_sems, recv_sems
        self.me, self.sib = plane_neighbours()[:2]
        self.core = lax.rem(self.me, 2)

    def own(self, tile, z, p):
        return pltpu.make_async_copy(tile, self.out.at[2 * self.core + z, p], self.local_sems.at[z, p])

    def other(self, tile, z, p):
        return send(
            tile,
            self.out.at[2 * self.core + z, p],
            self.send_sems.at[z, p],
            self.recv_sems.at[z, p],
            on_ctx(self.sib),
        )

    def arrive(self):
        for z in range(2):
            for p in range(4):
                there = self.out.at[2 - 2 * self.core + z, p]
                send(
                    there, there, self.send_sems.at[z, p], self.recv_sems.at[z, p], on_ctx(self.sib)
                ).wait_recv()


SHARES_SCRATCH = [pltpu.SemaphoreType.DMA((2, 4))] * 3
HALVES_SCRATCH = [pltpu.SemaphoreType.DMA((8,))] * 3


def up_kernel(
    x_ref,
    gate_ref,
    up_ref,
    all_ref,
    w_out_ref,
    a_ref,
    b_ref,
    h_ref,
    xs,
    local_sem,
    send_sems,
    recv_sems,
    keep_sems,
    stage,
    stage_sems,
    w,
    w_sem,
    *w_sems,
):
    ring = Gather(x_ref, xs, local_sem, send_sems, recv_sems)
    rows = x_ref.shape[0]
    halves, width, wide = w.shape
    deep = width // 8
    cols = wide // 2
    outs = (a_ref, b_ref, h_ref)
    greet((ring.sib, ring.nx, ring.ny))
    ring.start()
    gates = Halves(
        lambda plane, p: gate_ref.at[plane, p] if p < 3 else up_ref.at[plane, 4],
        lambda z, c: w.at[z, pl.ds(c * deep, deep), pl.ds(0, cols)],
        *w_sems[:3],
    )
    ups = Halves(
        lambda plane, p: up_ref.at[plane, p],
        lambda z, c: w.at[z, pl.ds(c * deep, deep), pl.ds(cols, cols)],
        *w_sems[3:],
    )
    gates.start()
    ups.start()
    gates.ready()
    ups.ready()
    keep_w = pltpu.make_async_copy(w, w_out_ref, w_sem)
    keep_w.start()

    def keep(block):
        return pltpu.make_async_copy(xs.at[block], all_ref.at[block], keep_sems.at[block])

    part = rows // 2

    def put(slot, n, at):
        return pltpu.make_async_copy(stage.at[slot, n], outs[n].at[at], stage_sems.at[slot, n])

    def turn(step, carry):
        ring.before_half(step)
        block, h = ring.half_block(step)
        seen = xs[block, pl.ds(pl.multiple_of(h * part, part), part), :]
        at = pl.ds(pl.multiple_of(block * rows + h * part, part), part)

        @pl.when(h == 1)
        def _():
            keep(block).start()

        slot = lax.rem(step, 2)

        @pl.when(step >= 2)
        def _():
            for n in range(3):
                put(slot, n, at).wait()

        for z in range(halves):
            both = nn(seen, w[z])
            gate, up = both[:, :cols], both[:, cols:]
            sigma = jax.nn.sigmoid(gate)
            active = gate * sigma
            here = slice(z * cols, (z + 1) * cols)
            stage[slot, 0, :, here] = (up * sigma * (1.0 + gate * (1.0 - sigma))).astype(BF16)
            stage[slot, 1, :, here] = active.astype(BF16)
            stage[slot, 2, :, here] = (active * up).astype(BF16)
        for n in range(3):
            put(slot, n, at).start()
        return carry

    lax.fori_loop(0, 16, turn, 0)
    ring.finish()
    gates.finish()
    ups.finish()
    keep_w.wait()
    for block in range(8):
        keep(block).wait()
    for slot in range(2):
        for n in range(3):
            put(slot, n, pl.ds(0, part)).wait()


def gather_up(post, gate_parts, up_parts):
    rows, width = post.shape
    wide = 2 * gate_parts.shape[-1]
    flat = jax.ShapeDtypeStruct((8 * rows, wide), BF16)
    return pl.pallas_call(
        up_kernel,
        out_shape=(
            jax.ShapeDtypeStruct((8, rows, width), BF16),
            jax.ShapeDtypeStruct((2, width, wide), BF16),
            flat,
            flat,
            flat,
        ),
        in_specs=[spec_any()] * 3,
        out_specs=(spec_any(),) * 5,
        scratch_shapes=gather_scratch(rows, width)
        + [
            pltpu.SemaphoreType.DMA((8,)),
            pltpu.VMEM((2, 3, rows // 2, wide), BF16),
            pltpu.SemaphoreType.DMA((2, 3)),
            pltpu.VMEM((2, width, wide), BF16),
            pltpu.SemaphoreType.DMA,
        ]
        + HALVES_SCRATCH * 2,
        compiler_params=comm_params(2),
        cost_estimate=busy(62),
        name="gather_up",
    )(post, gate_parts, up_parts)


def down_kernel(h_any, parts_ref, middle_any, teacher_any, valid_ref, o_ref, low_ref, diff_ref, error_ref, w_out_ref, *scratch):
    rs = Scatter(*scratch[:N_SCATTER])
    (w, w_sem, h_ref, h_sems, middle_ref, teacher_ref, row_sems, w_local, w_sends, w_recvs) = scratch[N_SCATTER:]
    rows = o_ref.shape[0]
    _, _, cols, deep = parts_ref.shape
    weight = Halves(
        lambda plane, p: parts_ref.at[plane, p],
        lambda z, c: w.at[pl.ds(z * cols, cols), pl.ds(pl.multiple_of(c * deep, deep), deep)],
        w_local,
        w_sends,
        w_recvs,
    )
    def fetch(block):
        here = pl.ds(pl.multiple_of(block * rows, rows), rows)
        return pltpu.make_async_copy(h_any.at[here], h_ref.at[here], h_sems.at[block])

    for block in rs.blocks():
        fetch(block).start()
    late = (
        pltpu.make_async_copy(middle_any, middle_ref, row_sems.at[0]),
        pltpu.make_async_copy(teacher_any, teacher_ref, row_sems.at[1]),
    )
    greet((rs.sib, rs.nx, rs.ny))
    weight.start()
    for copy in late:
        copy.start()
    weight.ready()
    keep_w = pltpu.make_async_copy(w, w_out_ref, w_sem)
    keep_w.start()

    def product(block, at, out, n):
        left = h_ref[pl.ds(pl.multiple_of(block * rows + at.start, rows // 2), rows // 2), :]
        for c in range(0, w.shape[1], 512):
            out[n, at, c : c + 512] = nn(left, w[:, c : c + 512]).astype(BF16)

    def turn(step, carry):
        @pl.when(lax.rem(step, 4) < 2)
        def _():
            fetch(rs.block(step)).wait()

        rs.step(step, product)
        return carry

    lax.fori_loop(0, 16, turn, 0)
    for copy in late:
        copy.wait()
    rs.finish(diff_ref)
    error = jnp.zeros((rows, HEAD_SIZE), F32)
    for n in range(0, diff_ref.shape[1], HEAD_SIZE):
        at = slice(n, n + HEAD_SIZE)
        result = middle_ref[:, at] + diff_ref[:, at]
        o_ref[:, at] = result.astype(BF16)
        diff = (result - teacher_ref[:, at].astype(F32)) * valid_ref[...]
        diff_ref[:, at] = diff
        low_ref[:, at] = diff.astype(BF16)
        error += diff * diff
    error_ref[...] = jnp.sum(error, axis=0, keepdims=True)
    weight.finish()
    keep_w.wait()


def scatter_down(hidden, parts, middle, teacher, valid):
    rows, width = middle.shape
    ff = hidden.shape[1]
    low = jax.ShapeDtypeStruct((rows, width), BF16)
    return pl.pallas_call(
        down_kernel,
        out_shape=(
            low,
            low,
            jax.ShapeDtypeStruct((rows, width), F32),
            jax.ShapeDtypeStruct((1, HEAD_SIZE), F32),
            jax.ShapeDtypeStruct((ff, width), BF16),
        ),
        in_specs=[spec_any()] * 4 + [spec_vmem()],
        out_specs=(spec_vmem(),) * 4 + (spec_any(),),
        scratch_shapes=scatter_scratch(rows, width)
        + [
            pltpu.VMEM((ff, width), BF16),
            pltpu.SemaphoreType.DMA,
            pltpu.VMEM(hidden.shape, BF16),
            pltpu.SemaphoreType.DMA((8,)),
            pltpu.VMEM((rows, width), F32),
            pltpu.VMEM((rows, width), BF16),
            pltpu.SemaphoreType.DMA((2,)),
        ]
        + HALVES_SCRATCH,
        compiler_params=comm_params(6),
        cost_estimate=busy(62),
        name="scatter_down",
    )(hidden, parts, middle, teacher, valid)


def down_back_kernel(
    x_ref,
    w_ref,
    a_ref,
    b_ref,
    h_ref,
    d_ref,
    gw_ref,
    xs,
    local_sem,
    send_sems,
    recv_sems,
    stage,
    stage_sems,
    total,
    low,
    w,
    w_sem,
    factors,
    factor_sems,
    hidden,
    hidden_sems,
    s_local,
    s_sends,
    s_recvs,
):
    ring = Gather(x_ref, xs, local_sem, send_sems, recv_sems)
    rows, width = x_ref.shape
    ff = w_ref.shape[0]
    cols = ff // 2
    fetch_w = pltpu.make_async_copy(w_ref, w, w_sem)
    fetch_w.start()
    shares = Shares(gw_ref, s_local, s_sends, s_recvs)
    core = shares.core
    deep = width // 8

    def tile(z, c):
        return low.at[pl.ds(z * cols, cols), pl.ds(pl.multiple_of(c * deep, deep), deep)]

    def put(slot, block):
        return pltpu.make_async_copy(
            stage.at[slot], d_ref.at[pl.ds(block * rows, rows)], stage_sems.at[slot]
        )

    def factor(n, slot, block):
        ref = (a_ref, b_ref)[n]
        return pltpu.make_async_copy(
            ref.at[pl.ds(block * rows, rows)], factors.at[slot, n], factor_sems.at[slot, n]
        )

    def chip_hidden(slot, block):
        return pltpu.make_async_copy(
            h_ref.at[pl.ds(block // 2 * 2 * rows, 2 * rows)], hidden.at[slot], hidden_sems.at[slot]
        )

    def fetch(step):
        block = ring.block(step)
        for n in range(2):
            factor(n, lax.rem(step, 2), block).start()

        @pl.when(lax.rem(step, 2) == 0)
        def _():
            chip_hidden(lax.rem(step // 2, 2), block).start()

    fetch(jnp.int32(0))
    greet((ring.sib, ring.nx, ring.ny))
    ring.start()
    total[...] = jnp.zeros_like(total)
    fetch_w.wait()

    def turn(step, carry):
        ring.before(step)
        block = ring.block(step)
        slot = lax.rem(step, 2)
        pair_slot = lax.rem(step // 2, 2)

        @pl.when(step >= 2)
        def _():
            put(slot, block).wait()

        for n in range(2):
            factor(n, slot, block).wait()

        @pl.when(step < 7)
        def _():
            fetch(step + 1)

        for z in range(2):
            part = slice(z * cols, (z + 1) * cols)
            grad = nt(xs[block], w[part, :])
            for n in range(2):
                stage[slot, :, (2 * z + n) * cols : (2 * z + n + 1) * cols] = (
                    grad * factors[slot, n, :, part].astype(F32)
                ).astype(BF16)
        put(slot, block).start()

        @pl.when(slot == 1)
        def _():
            chip_hidden(pair_slot, block).wait()
            pair = block // 2
            for p in range(4):
                at = slice(p * 2 * deep, (p + 1) * 2 * deep)
                seen = xs[pl.ds(pair * 2, 2), :, at].reshape(2 * rows, 2 * deep)
                total[:, at] += tn(hidden[pair_slot], seen)

                @pl.when(step == 7)
                def _():
                    low[:, at] = total[:, at].astype(BF16)
                    for z in range(2):
                        shares.other(tile(z, 2 * p + 1 - core), z, p).start()
                        shares.own(tile(z, 2 * p + core), z, p).start()

        return carry

    lax.fori_loop(0, 8, turn, 0)
    ring.finish()
    for slot in range(2):
        put(slot, 0).wait()
    shares.arrive()
    for z in range(2):
        for p in range(4):
            shares.other(tile(z, 2 * p + 1 - core), z, p).wait_send()
            shares.own(tile(z, 2 * p + core), z, p).wait()


def gather_down_back(diff, w_down, a, b, hidden):
    rows, width = diff.shape
    ff = w_down.shape[0]
    dma = pltpu.SemaphoreType.DMA
    return pl.pallas_call(
        down_back_kernel,
        out_shape=(
            jax.ShapeDtypeStruct((8 * rows, 2 * ff), BF16),
            jax.ShapeDtypeStruct((4, 4, ff // 2, width // 8), BF16),
        ),
        in_specs=[spec_any()] * 5,
        out_specs=(spec_any(), spec_any()),
        scratch_shapes=gather_scratch(rows, width)
        + [
            pltpu.VMEM((2, rows, 2 * ff), BF16),
            dma((2,)),
            pltpu.VMEM((ff, width), F32),
            pltpu.VMEM((ff, width), BF16),
            pltpu.VMEM((ff, width), BF16),
            dma,
            pltpu.VMEM((2, 2, rows, ff), BF16),
            dma((2, 2)),
            pltpu.VMEM((2, 2 * rows, ff), BF16),
            dma((2,)),
        ]
        + SHARES_SCRATCH,
        compiler_params=comm_params(3),
        cost_estimate=busy(66),
        name="gather_down_back",
    )(diff, w_down, a, b, hidden)


def mix_kernel(
    mixed_ref,
    tokens_ref,
    gain_ref,
    w0_ref,
    w1_ref,
    w2_ref,
    w3_ref,
    middle_ref,
    post_ref,
    rows_ref,
    w_ref,
    held,
    w,
    m_sems,
    m_sends,
    m_recvs,
    w_local,
    w_sends,
    w_recvs,
    keep_sems,
):
    me, sib, nx, ny, dg = plane_neighbours()
    shift = sib - me
    away = others(me)
    rows, width = held.shape
    deep = width // 8
    greet(away)

    def block(c):
        return pl.ds(pl.multiple_of(c * rows, rows), rows)

    def lanes(c):
        return pl.ds(pl.multiple_of(c * deep, deep), deep)

    def give(n, c):
        return send(mixed_ref.at[block(c)], held.at[:, lanes(me)], m_sends.at[n], m_recvs.at[me], on_ctx(c))

    def take(c):
        return send(mixed_ref.at[block(c)], held.at[:, lanes(c)], m_sends.at[0], m_recvs.at[c], on_ctx(c))

    for n, c in enumerate(away):
        give(n, c).start()
    own = pltpu.make_async_copy(mixed_ref.at[block(me)], held.at[:, lanes(me)], m_sems)
    own.start()
    parts = ((w0_ref, me), (w1_ref, nx), (w2_ref, ny), (w3_ref, dg))

    def swap(n):
        part, c = parts[n]
        return send(part, w.at[:, lanes(c)], w_sends.at[n], w_recvs.at[n], on_ctx(sib))

    def place(n):
        part, c = parts[n]
        return pltpu.make_async_copy(part, w.at[:, lanes(c)], w_local.at[n])

    for n in range(4):
        swap(n).start()
        place(n).start()
    for n in range(4):
        place(n).wait()
        there = w.at[:, lanes(parts[n][1] + shift)]
        send(there, there, w_sends.at[n], w_recvs.at[n], on_ctx(sib)).wait_recv()
    own.wait()
    for c in away:
        take(c).wait_recv()
    keep_rows = pltpu.make_async_copy(held, rows_ref, keep_sems.at[0])
    keep_rows.start()
    keep_w = pltpu.make_async_copy(w, w_ref, keep_sems.at[1])
    keep_w.start()
    total = jnp.zeros((rows, 1), F32)
    for n in range(0, width, 512):
        at = slice(n, n + 512)
        middle = tokens_ref[:, at].astype(F32) + nn(held[...], w[:, at])
        middle_ref[:, at] = middle
        total += jnp.sum(middle * middle, axis=-1, keepdims=True)
    scale = lax.rsqrt(total / width + EPS)
    for n in range(0, width, 512):
        at = slice(n, n + 512)
        post_ref[:, at] = (middle_ref[:, at] * scale * gain_ref[:, at]).astype(BF16)
    for n, c in enumerate(away):
        give(n, c).wait_send()
    for n in range(4):
        swap(n).wait_send()
    keep_rows.wait()
    keep_w.wait()


def mix(mixed, tokens, post_gain, parts):
    rows, width = tokens.shape
    dma = pltpu.SemaphoreType.DMA
    return pl.pallas_call(
        mix_kernel,
        out_shape=(
            jax.ShapeDtypeStruct((rows, width), F32),
            jax.ShapeDtypeStruct((rows, width), BF16),
            jax.ShapeDtypeStruct((rows, width), BF16),
            jax.ShapeDtypeStruct((width, width), BF16),
        ),
        in_specs=[spec_any(), spec_vmem(), spec_vmem()] + [spec_any()] * 4,
        out_specs=(spec_vmem(), spec_vmem(), spec_any(), spec_any()),
        scratch_shapes=[
            pltpu.VMEM((rows, width), BF16),
            pltpu.VMEM((width, width), BF16),
            dma,
            dma((7,)),
            dma((8,)),
            dma((4,)),
            dma((4,)),
            dma((4,)),
            dma((2,)),
        ],
        compiler_params=comm_params(5),
        cost_estimate=busy(28),
        name="mix",
    )(mixed, tokens, post_gain.reshape(1, -1), *parts)


def mix_back_kernel(
    post_ref,
    middle_ref,
    diff_ref,
    gain_ref,
    w_any,
    rows_any,
    swap_ref,
    dm_ref,
    d_middle_ref,
    gp_ref,
    g0_ref,
    g1_ref,
    g2_ref,
    g3_ref,
    swapped_ref,
    w_ref,
    rows_ref,
    fetch_sems,
    d_ref,
    stage,
    to_sib,
    from_sib,
    own,
    out_sem,
    out_sends,
    out_recvs,
    s_sends,
    s_recvs,
    g_sems,
    *c_sems,
):
    me, sib, nx, ny, dg = plane_neighbours()
    shift = sib - me
    away = others(me)
    rows, width = d_ref.shape
    deep = width // 8
    fetch_w = pltpu.make_async_copy(w_any, w_ref, fetch_sems.at[0])
    fetch_w.start()
    fetch_rows = pltpu.make_async_copy(rows_any, rows_ref, fetch_sems.at[1])
    fetch_rows.start()
    greet(away)
    weight_swap = ChipSwap(swap_ref, swapped_ref, *c_sems)
    weight_swap.start()
    squares = jnp.zeros((rows, HEAD_SIZE), F32)
    dots = jnp.zeros((rows, HEAD_SIZE), F32)
    cuts = [slice(n, n + HEAD_SIZE) for n in range(0, width, HEAD_SIZE)]
    for at in cuts:
        middle = middle_ref[:, at]
        squares += middle * middle
        dots += post_ref[:, at] * gain_ref[:, at] * middle
    scale = lax.rsqrt(jnp.sum(squares, axis=-1, keepdims=True) / width + EPS)
    pull = scale * scale * scale * (jnp.sum(dots, axis=-1, keepdims=True) / width)
    for at in cuts:
        middle, post = middle_ref[:, at], post_ref[:, at]
        gp_ref[:, at] = jnp.sum(post * (middle * scale), axis=0, keepdims=True)
        d_middle = diff_ref[:, at] + scale * (post * gain_ref[:, at]) - middle * pull
        d_middle_ref[:, at] = d_middle
        d_ref[:, at] = d_middle.astype(BF16)
    outs = (g0_ref, g1_ref, g2_ref, g3_ref)
    chips = (me, nx, ny, dg)
    fetch_w.wait()
    fetch_rows.wait()

    def block(c):
        return pl.ds(pl.multiple_of(c * rows, rows), rows)

    def give(n, c):
        return send(stage.at[c], dm_ref.at[block(me)], out_sends.at[n], out_recvs.at[me], on_ctx(c))

    def take(c):
        return send(stage.at[c], dm_ref.at[block(c)], out_sends.at[0], out_recvs.at[c], on_ctx(c))

    def heads(n, carry):
        c = pick(n, away + (me,))
        at = pl.ds(pl.multiple_of(c * deep, deep), deep)
        stage[c] = nt(d_ref[...], w_ref[at, :]).astype(BF16)

        @pl.when(n < 7)
        def _():
            give(n, c).start()

        return carry

    lax.fori_loop(0, 8, heads, 0)
    keep = pltpu.make_async_copy(stage.at[me], dm_ref.at[block(me)], out_sem)
    keep.start()

    def swap(n):
        return send(to_sib.at[n], from_sib.at[n], s_sends.at[n], s_recvs.at[n], on_ctx(sib))

    def grad(n, out, c):
        at = pl.ds(pl.multiple_of(c * deep, deep), deep)
        out[n] = tn(rows_ref[...], d_ref[:, at]).astype(BF16)

    def theirs(n, carry):
        grad(n, to_sib, pick(n, chips) + shift)
        swap(n).start()
        return carry

    def ours(n, carry):
        grad(n, own, pick(n, chips))
        return carry

    lax.fori_loop(0, 4, theirs, 0)
    lax.fori_loop(0, 4, ours, 0)
    for n in range(4):
        swap(n).wait_recv()
        own[n] = (own[n].astype(F32) + from_sib[n].astype(F32)).astype(BF16)
        pltpu.make_async_copy(own.at[n], outs[n], g_sems.at[n]).start()
    for c in away:
        take(c).wait_recv()
    keep.wait()
    for n, c in enumerate(away):
        give(n, c).wait_send()
    for n in range(4):
        swap(n).wait_send()
        pltpu.make_async_copy(own.at[n], outs[n], g_sems.at[n]).wait()
    weight_swap.finish()


def mix_back(d_post, middle, diff, post_gain, w, mixed_rows, swap):
    rows, width = middle.shape
    deep = width // 8
    dma = pltpu.SemaphoreType.DMA
    four = pltpu.VMEM((4, width, deep), BF16)
    return pl.pallas_call(
        mix_back_kernel,
        out_shape=(
            jax.ShapeDtypeStruct((8 * rows, deep), BF16),
            jax.ShapeDtypeStruct((rows, width), F32),
            jax.ShapeDtypeStruct((1, width), F32),
        )
        + (jax.ShapeDtypeStruct((width, deep), BF16),) * 4
        + (jax.ShapeDtypeStruct(swap.shape, BF16),),
        in_specs=[spec_vmem()] * 4 + [spec_any()] * 3,
        out_specs=(spec_any(), spec_vmem(), spec_vmem()) + (spec_any(),) * 5,
        scratch_shapes=[
            pltpu.VMEM((width, width), BF16),
            pltpu.VMEM((rows, width), BF16),
            dma((2,)),
            pltpu.VMEM((rows, width), BF16),
            pltpu.VMEM((8, rows, deep), BF16),
            four,
            four,
            four,
            dma,
            dma((7,)),
            dma((8,)),
            dma((4,)),
            dma((4,)),
            dma((4,)),
        ]
        + SWAP_SCRATCH,
        compiler_params=comm_params(4),
        cost_estimate=busy(26),
        name="mix_back",
    )(d_post, middle, diff, post_gain.reshape(1, -1), w, mixed_rows, swap)


def columns(all_ref, slices, sems, c, slot):
    deep = slices.shape[-1]
    return pltpu.make_async_copy(
        all_ref.at[:, :, pl.ds(pl.multiple_of(c * deep, deep), deep)], slices.at[slot], sems.at[slot]
    )


EARLY = 1


def post_back_kernel(d_any, w_any, all_ref, o_ref, gw_ref, *scratch):
    rs = Scatter(*scratch[:N_SCATTER])
    slices, slice_sems, tile, d_ref, d_sems, w_ref, w_sems, s_local, s_sends, s_recvs = scratch[N_SCATTER:]
    shares = Shares(gw_ref, s_local, s_sends, s_recvs)
    rows = o_ref.shape[0]
    _, width, wide = w_ref.shape
    plane_rows = d_ref.shape[0]
    deep = width // 8
    fetch_w = [pltpu.make_async_copy(w_any.at[z], w_ref.at[z], w_sems.at[z]) for z in range(2)]

    def fetch(block):
        here = pl.ds(pl.multiple_of(block * rows, rows), rows)
        return pltpu.make_async_copy(d_any.at[here], d_ref.at[here], d_sems.at[block])

    order = rs.blocks()
    fetch(order[0]).start()
    for copy in fetch_w:
        copy.start()
    for block in order[1:]:
        fetch(block).start()
    columns(all_ref, slices, slice_sems, 0, 0).start()
    greet((rs.sib, rs.nx, rs.ny))
    for copy in fetch_w:
        copy.wait()

    def product(block, at, out, n):
        here = pl.ds(pl.multiple_of(block * rows + at.start, rows // 2), rows // 2)
        for c in range(0, width, 512):
            total = nt(d_ref[here, :wide], w_ref[0, c : c + 512, :])
            total += nt(d_ref[here, wide:], w_ref[1, c : c + 512, :])
            out[n, at, c : c + 512] = total.astype(BF16)

    def put(slot, p, act):
        @pl.when(slot == shares.core)
        def _():
            for z in range(2):
                copy = shares.own(tile.at[slot, z], z, p)
                copy.start() if act == "start" else copy.wait()

        @pl.when(slot != shares.core)
        def _():
            for z in range(2):
                copy = shares.other(tile.at[slot, z], z, p)
                copy.start() if act == "start" else copy.wait_send()

    def grad(c):
        slot = lax.rem(c, 2)
        columns(all_ref, slices, slice_sems, c, slot).wait()

        @pl.when(c < 7)
        def _():
            columns(all_ref, slices, slice_sems, c + 1, 1 - slot).start()

        @pl.when(c >= 2)
        def _():
            put(slot, c // 2 - 1, "wait")

        seen = slices[slot].reshape(plane_rows, deep)
        for z in range(2):
            tile[slot, z] = tn(seen, d_ref[:, z * wide : (z + 1) * wide]).astype(BF16)
        put(slot, c // 2, "start")

    def turn(t, carry):
        is_grad = ((t >= 10) & (t < 10 + EARLY)) | (t >= 16 + EARLY)

        for n in range(2):

            @pl.when(t == n)
            def _():
                fetch(order[n]).wait()

        @pl.when(t == 4)
        def _():
            for block in order[2:]:
                fetch(block).wait()

        @pl.when(is_grad)
        def _():
            grad(jnp.where(t < 10 + EARLY, t - 10, t - 16))

        @pl.when(jnp.logical_not(is_grad))
        def _():
            rs.step(jnp.where(t < 10, t, t - EARLY), product)

        return carry

    lax.fori_loop(0, 24, turn, 0)
    rs.finish(o_ref)
    for slot in range(2):
        put(slot, 3, "wait")
    shares.arrive()


def scatter_post(d_gu, w_gu, post_all):
    _, rows, width = post_all.shape
    wide = w_gu.shape[-1]
    deep = width // 8
    return pl.pallas_call(
        post_back_kernel,
        out_shape=(
            jax.ShapeDtypeStruct((rows, width), F32),
            jax.ShapeDtypeStruct((4, 4, deep, wide), BF16),
        ),
        in_specs=[spec_any()] * 3,
        out_specs=(spec_vmem(), spec_any()),
        scratch_shapes=scatter_scratch(rows, width)
        + [
            pltpu.VMEM((2, 8, rows, deep), BF16),
            pltpu.SemaphoreType.DMA((2,)),
            pltpu.VMEM((2, 2, deep, wide), BF16),
            pltpu.VMEM(d_gu.shape, BF16),
            pltpu.SemaphoreType.DMA((8,)),
            pltpu.VMEM(w_gu.shape, BF16),
            pltpu.SemaphoreType.DMA((2,)),
        ]
        + SHARES_SCRATCH,
        compiler_params=comm_params(7),
        cost_estimate=busy(66),
        name="scatter_post",
    )(d_gu, w_gu, post_all)


def normed_back_kernel(
    dq_ref,
    dkv_ref,
    to_lo_ref,
    to_hi_ref,
    lin_ref,
    w_ref,
    all_ref,
    swap_ref,
    wo_ref,
    tokens_ref,
    gp_ref,
    error_ref,
    qg_ref,
    kg_ref,
    ca_ref,
    sa_ref,
    cb_ref,
    sb_ref,
    o_ref,
    gw_ref,
    totals_ref,
    swapped_ref,
    wo_sum_ref,
    *scratch,
):
    rs = Scatter(*scratch[:N_SCATTER])
    (
        from_lo,
        from_hi,
        d_lin,
        slices,
        slice_sems,
        tiles,
        tiles_in,
        up_in,
        down_in,
        wo_up,
        wo_down,
        z_sends,
        z_recvs,
        t_sends,
        t_recvs,
        p_sends,
        p_recvs,
        o_sends,
        o_recvs,
        gains_ref,
        held,
        held_planes,
        v_sends,
        v_recvs,
        *c_sems,
    ) = scratch[N_SCATTER:]
    me = rs.me
    plane, planes = lax.axis_index("tp"), lax.axis_size("tp")
    rows, width = o_ref.shape
    deep = width // 8
    plane_rows = dq_ref.shape[0]
    units = rows // UNIT
    wide = 2 * HEAD_SIZE
    away = others(me)
    order = rs.blocks()

    from_lo[...] = jnp.zeros_like(from_lo)
    from_hi[...] = jnp.zeros_like(from_hi)
    line = Line(to_hi_ref, to_lo_ref, from_lo, from_hi, z_sends, z_recvs, rows, True)
    barrier = pltpu.get_barrier_semaphore()
    far = [lax.rem(plane + step, planes) for step in range(1, planes)]
    for where in [on_ctx(c) for c in away] + [on_plane(p) for p in far]:
        pl.semaphore_signal(barrier, inc=1, device_id=where, device_id_type=MESH)
    pl.semaphore_wait(barrier, len(away) + len(far))
    for block in order:
        line.start(block)
    columns(all_ref, slices, slice_sems, order[0], 0).start()
    gains_ref[...] = jnp.zeros_like(gains_ref)

    def head_back(grad, lin, gain_ref, rotation):
        back = rotation.back(grad)
        scale = lax.rsqrt(jnp.mean(lin * lin, axis=-1, keepdims=True) + EPS)
        normal = lin * scale
        gained = back * gain_ref[...]
        d = scale * (gained - normal * jnp.mean(gained * normal, axis=-1, keepdims=True))
        return d.astype(BF16), jnp.sum(back * normal, axis=0, keepdims=True)

    def rotation_of(unit):
        return Turn(ca_ref, sa_ref, cb_ref, sb_ref, unit)

    def prepare_queries(unit, carry):
        rotation = rotation_of(unit)
        here = pl.ds(pl.multiple_of(unit * UNIT, UNIT), UNIT)
        for h in range(2):
            lanes = slice(h * HEAD_SIZE, (h + 1) * HEAD_SIZE)
            d, gain = head_back(dq_ref[here, lanes].astype(F32) * HEAD_SIZE**-0.5, lin_ref[here, lanes], qg_ref, rotation)
            d_lin[here, lanes] = d
            gains_ref[0:1, :] += gain
        return carry

    def prepare_keys(block):
        line.arrived(block)
        for i in range(units):
            unit = block * units + i
            here = pl.ds(pl.multiple_of(unit * UNIT, UNIT), UNIT)
            d_kv = dkv_ref[here, :].astype(F32) + from_lo[here, :].astype(F32) + from_hi[here, :].astype(F32)
            lanes = slice(2 * HEAD_SIZE, 3 * HEAD_SIZE)
            d, gain = head_back(d_kv[:, :HEAD_SIZE], lin_ref[here, lanes], kg_ref, rotation_of(unit))
            d_lin[here, lanes] = d
            gains_ref[1:2, :] += gain
            d_lin[here, 3 * HEAD_SIZE :] = d_kv[:, HEAD_SIZE:].astype(BF16)

    def tile_to(part, n, device):
        return send(
            tiles.at[part, device],
            tiles_in.at[part, me],
            t_sends.at[part, n],
            t_recvs.at[part, me],
            on_ctx(device),
        )

    def tile_from(part, device):
        return send(
            tiles.at[part, device],
            tiles_in.at[part, device],
            t_sends.at[part, 0],
            t_recvs.at[part, device],
            on_ctx(device),
        )

    def grads(part):
        def grad(n, carry):
            c = pick(n, order)
            slot = lax.rem(n, 2)
            columns(all_ref, slices, slice_sems, c, slot).wait()

            @pl.when((n < 7) | (part == 0))
            def _():
                columns(all_ref, slices, slice_sems, pick(lax.rem(n + 1, 8), order), 1 - slot).start()

            lanes = slice(part * wide, (part + 1) * wide)
            value = tn(slices[slot].reshape(plane_rows, deep), d_lin[:, lanes]).astype(BF16)

            @pl.when(n < 7)
            def _():
                tiles[part, c] = value
                tile_to(part, n, c).start()

            @pl.when(n == 7)
            def _():
                tiles_in[part, me] = value

            return carry

        lax.fori_loop(0, 8, grad, 0)

    sums = [
        LineSum(
            lambda p, part=part: tiles_in.at[part, pl.ds(2 * p, 2)],
            up_in.at[part],
            down_in.at[part],
            p_sends.at[part],
            p_recvs.at[part],
        )
        for part in range(2)
    ]
    out_sum = LineSum(lambda p: wo_ref.at[p], wo_up, wo_down, o_sends, o_recvs)

    def tiles_there(part):
        for device in away:
            tile_from(part, device).wait_recv()

    def product(block, at, out, n):
        left = d_lin[pl.ds(pl.multiple_of(block * rows + at.start, rows // 2), rows // 2), :]
        for c in range(0, width, 512):
            out[n, at, c : c + 512] = nt(left, w_ref[c : c + 512, :]).astype(BF16)

    def turn(step, carry):
        @pl.when(lax.rem(step, 4) < 2)
        def _():
            prepare_keys(rs.block(step))

        rs.step(step, product, late=True)

        @pl.when(step == 4)
        def _():
            out_sum.stage(1)

        @pl.when(step == 7)
        def _():
            tiles_there(0)
            sums[0].stage(0)

        @pl.when(step == 9)
        def _():
            out_sum.stage(2)

        @pl.when(step == 12)
        def _():
            sums[0].stage(1)

        return carry

    swap = ChipSwap(swap_ref, swapped_ref, *c_sems)
    swap.start()
    out_sum.stage(0)
    lax.fori_loop(0, plane_rows // UNIT, prepare_queries, 0)
    grads(0)
    lax.fori_loop(0, 16, turn, 0)
    grads(1)
    for c in range(8):
        pltpu.make_async_copy(
            tokens_ref.at[:, pl.ds(c * deep, deep)], slices.at[0, c], slice_sems.at[0]
        ).start()
    rs.second_wave()
    sums[0].stage(2)
    tiles_there(1)
    for k in range(3):
        sums[1].stage(k)
    rs.finish(o_ref)
    total = Total(held, held_planes, v_sends, v_recvs)
    vector = held.at[me]
    pltpu.make_async_copy(slices.at[0], slices.at[0], slice_sems.at[0]).wait()
    squares = jnp.zeros((rows, deep), F32)
    for c in range(8):
        stream = slices[0, c].astype(F32)
        squares += stream * stream
    scale = lax.rsqrt(jnp.sum(squares, axis=-1, keepdims=True) / width + EPS)
    lanes_of = width // HEAD_SIZE
    for c in range(8):
        at = slice(c * deep, (c + 1) * deep)
        unit_in = slices[0, c].astype(F32) * scale
        gain = jnp.sum(o_ref[:, at].astype(F32) * unit_in, axis=0, keepdims=True)
        for i in range(2):
            n, lanes = 2 * c + i, slice(i * HEAD_SIZE, (i + 1) * HEAD_SIZE)
            vector[n : n + 1, :] = gain[:, lanes]
            vector[lanes_of + n : lanes_of + n + 1, :] = gp_ref[:, n * HEAD_SIZE : (n + 1) * HEAD_SIZE]
    vector[2 * lanes_of : 2 * lanes_of + 2, :] = gains_ref[0:2, :]
    vector[2 * lanes_of + 2 : 2 * lanes_of + 8, :] = jnp.broadcast_to(error_ref[...], (6, HEAD_SIZE))
    total.start()
    out_sum.collect(wo_sum_ref)
    for part in range(2):
        sums[part].collect(gw_ref.at[part])
    total.middle()
    swap.finish()
    total.finish(totals_ref)
    for line_sum in (out_sum, *sums):
        line_sum.finish()
    for part in range(2):
        for n, device in enumerate(order[:7]):
            tile_to(part, n, device).wait_send()

    def settle(block, carry):
        line.sent(block)
        return carry

    lax.fori_loop(0, 8, settle, 0)


def scatter_normed(d_queries, d_kv, to_lo, to_hi, lin, w_qkv, normed_all, swap, wo, tokens, gp, error, q_gain, k_gain, tables):
    _, rows, width = normed_all.shape
    deep = width // 8
    cols = w_qkv.shape[1]
    half = pltpu.VMEM(to_lo.shape, BF16)
    tiles = pltpu.VMEM((2, 8, deep, cols // 2), BF16)
    dma = pltpu.SemaphoreType.DMA
    return pl.pallas_call(
        normed_back_kernel,
        out_shape=(
            jax.ShapeDtypeStruct((rows, width), BF16),
            jax.ShapeDtypeStruct((2, 2, deep, cols // 2), F32),
            jax.ShapeDtypeStruct((2 * width // HEAD_SIZE + 8, HEAD_SIZE), F32),
            jax.ShapeDtypeStruct(swap.shape, BF16),
            jax.ShapeDtypeStruct(wo.shape[1:], F32),
        ),
        in_specs=[spec_vmem()] * 2
        + [spec_any()] * 2
        + [spec_vmem()] * 2
        + [spec_any()] * 2
        + [spec_vmem(), spec_any()]
        + [spec_vmem()] * 8,
        out_specs=(spec_vmem(),) * 3 + (spec_any(), spec_vmem()),
        scratch_shapes=scatter_scratch(rows, width)
        + [
            half,
            half,
            pltpu.VMEM((8 * rows, cols), BF16),
            pltpu.VMEM((2, 8, rows, deep), BF16),
            dma((2,)),
            tiles,
            tiles,
            pltpu.VMEM((2, 4, 2, deep, cols // 2), BF16),
            pltpu.VMEM((2, 4, 2, deep, cols // 2), BF16),
            pltpu.VMEM(wo.shape, BF16),
            pltpu.VMEM(wo.shape, BF16),
            dma((2, 8 * rows // UNIT)),
            dma((2, 8 * rows // UNIT)),
            dma((2, 7)),
            dma((2, 8)),
            dma((2, 2, 4)),
            dma((2, 2, 4)),
            dma((2, 4)),
            dma((2, 4)),
            pltpu.VMEM((8, HEAD_SIZE), F32),
            pltpu.VMEM((8, 2 * width // HEAD_SIZE + 8, HEAD_SIZE), F32),
            pltpu.VMEM((4, 2 * width // HEAD_SIZE + 8, HEAD_SIZE), F32),
            dma((10,)),
            dma((12,)),
        ]
        + SWAP_SCRATCH,
        compiler_params=comm_params(8),
        cost_estimate=busy(110),
        name="scatter_normed",
    )(
        d_queries,
        d_kv,
        to_lo,
        to_hi,
        lin,
        w_qkv,
        normed_all,
        swap,
        wo,
        tokens,
        gp,
        error,
        q_gain.reshape(1, -1),
        k_gain.reshape(1, -1),
        *tables,
    )


def finish_kernel(
    d_ref, tokens_ref, middle_ref, gain_ref, gu_ref, down_ref, qkv_ref, out_ref,
    dt_ref, gate_ref, up_ref, dw_ref, wq_ref, wk_ref, wv_ref, wo_ref,
):
    stream = tokens_ref[...].astype(F32)
    scale = lax.rsqrt(jnp.mean(stream * stream, axis=-1, keepdims=True) + EPS)
    gained = d_ref[...].astype(F32) * gain_ref[...]
    pull = scale * scale * scale * jnp.mean(gained * stream, axis=-1, keepdims=True)
    dt_ref[...] = (middle_ref[...] + (scale * gained - stream * pull)).astype(BF16)
    cols = gu_ref.shape[2] // 2
    for p in range(4):
        here = slice(p * cols, (p + 1) * cols)
        gate_ref[:, here] = gu_ref[p, :, :cols].astype(F32)
        up_ref[:, here] = gu_ref[p, :, cols:].astype(F32)
    dw_ref[...] = down_ref[...].astype(F32)
    wide = 2 * HEAD_SIZE
    for k in range(2):
        wq_ref[:, k * wide : (k + 1) * wide] = qkv_ref[0, k]
        wk_ref[:, k * HEAD_SIZE : (k + 1) * HEAD_SIZE] = qkv_ref[1, k, :, :HEAD_SIZE]
        wv_ref[:, k * HEAD_SIZE : (k + 1) * HEAD_SIZE] = qkv_ref[1, k, :, HEAD_SIZE:]
    wo_ref[...] = out_ref[...]


def finish(d_normed, tokens, d_middle, in_gain, gu, down, qkv, out):
    steps = 4

    def piece(shape, axis):
        block = list(shape)
        block[axis] //= steps
        return pl.BlockSpec(
            tuple(block), lambda i, axis=axis, n=len(shape): tuple(i if d == axis else 0 for d in range(n))
        )

    rows, width = tokens.shape
    deep, ff = gu.shape[1], 2 * gu.shape[2]
    one = (1, width)
    whole = pl.BlockSpec(one, lambda i: (0, 0))
    flat, square = (rows, width), (deep, 2 * HEAD_SIZE)
    ins = [(flat, 0), (flat, 0), (flat, 0), None, (gu.shape, 1), (down.shape, 1), (qkv.shape, 2), (out.shape, 0)]
    outs = [
        (flat, 0, BF16),
        ((deep, ff), 0, F32),
        ((deep, ff), 0, F32),
        (down.shape, 1, F32),
        ((deep, 4 * HEAD_SIZE), 0, F32),
        (square, 0, F32),
        (square, 0, F32),
        (out.shape, 0, F32),
    ]
    return pl.pallas_call(
        finish_kernel,
        grid=(steps,),
        out_shape=tuple(jax.ShapeDtypeStruct(o[0], o[2]) for o in outs),
        in_specs=[piece(*i) if i else whole for i in ins],
        out_specs=tuple(piece(o[0], o[1]) for o in outs),
        compiler_params=pltpu.CompilerParams(vmem_limit_bytes=VMEM_LIMIT),
        cost_estimate=busy(8),
        name="finish",
    )(d_normed, tokens, d_middle, in_gain.reshape(1, -1), gu, down, qkv, out)


class Places:
    def __init__(self, order_ref, lens_ref):
        self.order, self.lens = order_ref, lens_ref
        self.plane = lax.axis_index("tp")
        self.seq0 = (3 * self.plane) // 4
        self.seq1 = (3 * self.plane + 2) // 4

    def position(self, seq, quarter, c):
        return 2 * self.order[seq, 2 * c + quarter // 2] + lax.rem(quarter, 2)

    def unit(self, u):
        c = u // 3
        g = 3 * self.plane + lax.rem(u, 3)
        seq = g // 4
        return seq, seq - self.seq0, self.position(seq, lax.rem(g, 4), c)

    def each(self, visit):
        for slot, seq in ((0, self.seq0), (1, self.seq1)):

            @pl.when((slot == 0) | (self.seq1 != self.seq0))
            def _():
                def one(i, carry):
                    quarter, c = i // 8, lax.rem(i, 8)
                    g = 4 * seq + quarter
                    away = g // 3 - self.plane
                    row = pl.multiple_of((c * 3 + lax.rem(g, 3)) * UNIT, UNIT)
                    visit(slot, self.position(seq, quarter, c), away, row)
                    return carry

                lax.fori_loop(0, 32, one, 0)

    def fetch(self, sources, keys, values, key_sem, value_sem):
        def visit(slot, position, away, row):
            at = pl.ds(pl.multiple_of(position * UNIT, UNIT), UNIT)
            for n, source in enumerate(sources):

                @pl.when(away == n - 1)
                def _():
                    pltpu.make_async_copy(
                        source.at[pl.ds(row, UNIT), pl.ds(0, HEAD_SIZE)], keys.at[slot, at], key_sem.at[slot]
                    ).start()
                    pltpu.make_async_copy(
                        source.at[pl.ds(row, UNIT), pl.ds(HEAD_SIZE, HEAD_SIZE)],
                        values.at[slot, at, pl.ds(0, HEAD_SIZE)],
                        value_sem.at[slot],
                    ).start()

        self.each(visit)
        for slot in range(2):

            @pl.when((slot == 0) | (self.seq1 != self.seq0))
            def _():
                pltpu.make_async_copy(keys.at[slot], keys.at[slot], key_sem.at[slot]).wait()
                pltpu.make_async_copy(keys.at[slot], keys.at[slot], value_sem.at[slot]).wait()


def sweep(clear, part):
    def four(i, carry):
        part(i * 4 * KEYS, 4 * KEYS, False)
        return carry

    lax.fori_loop(0, clear // 4, four, 0)

    @pl.when(lax.rem(clear, 4) >= 2)
    def _():
        part(clear // 4 * 4 * KEYS, 2 * KEYS, False)


    odd = lax.rem(clear, 2)

    @pl.when(odd == 1)
    def _():
        part((clear - 1) * KEYS, 2 * KEYS, True)

    @pl.when(odd == 0)
    def _():
        part(clear * KEYS, KEYS, True)


def attend_kernel(
    order_ref, lens_ref, q_ref, lo_ref, own_ref, hi_ref, o_ref, lse_ref, keys, values, acc, key_sem, value_sem
):
    places = Places(order_ref, lens_ref)
    values[:, :, HEAD_SIZE:] = jnp.ones((2, values.shape[1], HEAD_SIZE), BF16)
    places.fetch((lo_ref, own_ref, hi_ref), keys, values, key_sem, value_sem)

    def one_unit(u, carry):
        seq, slot, position = places.unit(u)
        length = lens_ref[seq]
        rows = pl.ds(pl.multiple_of(u * UNIT, UNIT), UNIT)
        both = q_ref[rows, :]
        queries = jnp.concatenate([both[:, :HEAD_SIZE], both[:, HEAD_SIZE:]], axis=0)
        clear = jnp.minimum(position * UNIT, length) // KEYS
        acc[...] = jnp.zeros_like(acc)
        row = lax.rem(lax.broadcasted_iota(jnp.int32, (2 * UNIT, 1), 0), UNIT)

        def part(start, size, masked):
            at = pl.ds(pl.multiple_of(start, KEYS), size)
            weights = jnp.exp2(nt(queries, keys[slot, at, :]))
            if masked:
                last = jnp.minimum(row + (position * UNIT - start), length - 1 - start)
                weights = jnp.where(lax.broadcasted_iota(jnp.int32, weights.shape, 1) <= last, weights, 0.0)
            acc[:, :HEAD_SIZE] += nn(weights.astype(BF16), values[slot, at, :HEAD_SIZE])
            part_sum = weights[:, :HEAD_SIZE]
            for n in range(HEAD_SIZE, size, HEAD_SIZE):
                part_sum += weights[:, n : n + HEAD_SIZE]
            acc[:, HEAD_SIZE:] += part_sum

        sweep(clear, part)
        total = jnp.sum(acc[:, HEAD_SIZE:], axis=-1, keepdims=True)
        mixed = (acc[:, :HEAD_SIZE] / total).astype(BF16)
        o_ref[rows, :] = jnp.concatenate([mixed[:UNIT], mixed[UNIT:]], axis=1)
        lse_ref[u] = jnp.transpose(jnp.broadcast_to(jnp.log2(total), (2 * UNIT, HEAD_SIZE)))[:8, :]
        return carry

    lax.fori_loop(0, q_ref.shape[0] // UNIT, one_unit, 0)


def attend(order, lens, q, lo, own, hi, seq_len):
    rows = q.shape[0]
    return pl.pallas_call(
        attend_kernel,
        out_shape=(
            jax.ShapeDtypeStruct(q.shape, BF16),
            jax.ShapeDtypeStruct((rows // UNIT, 8, 2 * UNIT), F32),
        ),
        in_specs=[spec_smem(), spec_smem(), spec_vmem(), spec_any(), spec_any(), spec_any()],
        out_specs=(spec_vmem(), spec_vmem()),
        scratch_shapes=[
            pltpu.VMEM((2, seq_len, HEAD_SIZE), BF16),
            pltpu.VMEM((2, seq_len, 2 * HEAD_SIZE), BF16),
            pltpu.VMEM((2 * UNIT, 2 * HEAD_SIZE), F32),
            pltpu.SemaphoreType.DMA((2,)),
            pltpu.SemaphoreType.DMA((2,)),
        ],
        compiler_params=pltpu.CompilerParams(vmem_limit_bytes=VMEM_LIMIT),
        cost_estimate=busy(50),
        name="attend",
    )(order, lens, q, lo, own, hi)


def attend_back_kernel(
    order_ref,
    lens_ref,
    q_ref,
    do_ref,
    o_ref,
    lse_ref,
    lo_ref,
    own_ref,
    hi_ref,
    dq_ref,
    dlo_ref,
    down_ref,
    dhi_ref,
    keys,
    values,
    dkeys,
    dvalues,
    dq_acc,
    key_sem,
    value_sem,
):
    places = Places(order_ref, lens_ref)
    dkeys[...] = jnp.zeros_like(dkeys)
    dvalues[...] = jnp.zeros_like(dvalues)
    places.fetch((lo_ref, own_ref, hi_ref), keys, values, key_sem, value_sem)

    def stacked(ref, rows):
        both = ref[rows, :]
        return jnp.concatenate([both[:, :HEAD_SIZE], both[:, HEAD_SIZE:]], axis=0)

    def one_unit(u, carry):
        seq, slot, position = places.unit(u)
        length = lens_ref[seq]
        rows = pl.ds(pl.multiple_of(u * UNIT, UNIT), UNIT)
        queries = stacked(q_ref, rows)
        grads = stacked(do_ref, rows)
        product = grads.astype(F32) * stacked(o_ref, rows).astype(F32)
        delta = jnp.sum(jnp.transpose(product), axis=0, keepdims=True)
        lse = lse_ref[u][:1, :]
        clear = jnp.minimum(position * UNIT, length) // KEYS
        dq_acc[...] = jnp.zeros_like(dq_acc)
        row = lax.rem(lax.broadcasted_iota(jnp.int32, (1, 2 * UNIT), 1), UNIT)

        def part(start, size, masked):
            at = pl.ds(pl.multiple_of(start, KEYS), size)
            key = keys[slot, at, :]
            probs = jnp.exp2(nt(key, queries) - lse)
            if masked:
                last = jnp.minimum(row + (position * UNIT - start), length - 1 - start)
                probs = jnp.where(lax.broadcasted_iota(jnp.int32, probs.shape, 0) <= last, probs, 0.0)
            d_scores = (probs * (nt(values[slot, at, :], grads) - delta)).astype(BF16)
            dvalues[slot, at, :] += nn(probs.astype(BF16), grads)
            dkeys[slot, at, :] += nn(d_scores, queries)
            dq_acc[...] += tn(d_scores, key)

        sweep(clear, part)
        dq_ref[rows, :] = jnp.concatenate([dq_acc[:UNIT, :], dq_acc[UNIT:, :]], axis=1).astype(BF16)
        return carry

    lax.fori_loop(0, q_ref.shape[0] // UNIT, one_unit, 0)
    dlo_ref[...] = jnp.zeros_like(dlo_ref)
    dhi_ref[...] = jnp.zeros_like(dhi_ref)

    def spread(slot, position, away, row):
        at = pl.ds(pl.multiple_of(position * UNIT, UNIT), UNIT)
        for n, out in enumerate((dlo_ref, down_ref, dhi_ref)):

            @pl.when(away == n - 1)
            def _():
                out[pl.ds(row, UNIT), :HEAD_SIZE] = (dkeys[slot, at, :] * (1.0 / LOG2E)).astype(out.dtype)
                out[pl.ds(row, UNIT), HEAD_SIZE:] = dvalues[slot, at, :].astype(out.dtype)

    places.each(spread)


def attend_back(order, lens, q, d_mixed, mixed, lse, lo, own, hi, seq_len):
    flat = jax.ShapeDtypeStruct(q.shape, BF16)
    held = pltpu.VMEM((2, seq_len, HEAD_SIZE), BF16)
    summed = pltpu.VMEM((2, seq_len, HEAD_SIZE), F32)
    return pl.pallas_call(
        attend_back_kernel,
        out_shape=(flat,) * 4,
        in_specs=[spec_smem(), spec_smem()] + [spec_vmem()] * 4 + [spec_any()] * 3,
        out_specs=(spec_vmem(),) * 4,
        scratch_shapes=[
            held,
            held,
            summed,
            summed,
            pltpu.VMEM((2 * UNIT, HEAD_SIZE), F32),
            pltpu.SemaphoreType.DMA((2,)),
            pltpu.SemaphoreType.DMA((2,)),
        ],
        compiler_params=pltpu.CompilerParams(vmem_limit_bytes=VMEM_LIMIT),
        cost_estimate=busy(75),
        name="attend_back",
    )(order, lens, q, d_mixed, mixed, lse, lo, own, hi)


def angles(block_order, tok_rows):
    inverse = THETA ** (-jnp.arange(0, HEAD_SIZE, 2, dtype=F32) / HEAD_SIZE)
    inverse = jnp.concatenate([inverse, inverse])
    units = tok_rows // UNIT
    g = lax.axis_index("tp") * units + jnp.arange(units, dtype=jnp.int32)
    seq, quarter = g // 4, g % 4
    c = jnp.arange(lax.axis_size("ctx"), dtype=jnp.int32)
    where = 2 * block_order[seq[None, :], 2 * c[:, None] + (quarter // 2)[None, :]] + (quarter % 2)[None, :]
    starts = (where.reshape(-1) * UNIT).astype(F32)
    coarse = starts[:, None] * inverse[None, :]
    fine = jnp.arange(UNIT, dtype=F32)[:, None] * inverse[None, :]
    return jnp.cos(coarse), jnp.sin(coarse), jnp.cos(fine), jnp.sin(fine)


def after(value, *earlier):
    return lax.optimization_barrier((value,) + earlier)[0]


def local_plane(
    tokens,
    teacher,
    seq_lens,
    block_order,
    in_gain,
    w_query,
    key_weight_matrix,
    value_weight_matrix,
    q_gain,
    k_gain,
    w_out,
    post_gain,
    w_gate,
    w_up,
    w_down,
):
    me = lax.axis_index("ctx")
    core = me % 2
    plane = lax.axis_index("tp")
    tok_rows, width = tokens.shape
    plane_rows = 8 * tok_rows
    seq_len = 2 * 8 * BLK
    deep = width // 8
    cols = w_gate.shape[1] // 4
    stream = tokens.astype(F32)
    normed_rows = (stream * rms_scale(stream) * in_gain).astype(BF16)
    unit = plane * (tok_rows // UNIT) + jnp.arange(tok_rows // UNIT, dtype=jnp.int32)
    seq, quarter = unit // 4, unit % 4
    start = block_order[seq, 2 * me + quarter // 2] * BLK + (quarter % 2) * UNIT
    position = start[:, None] + jnp.arange(UNIT, dtype=jnp.int32)
    valid = (position < seq_lens[seq][:, None]).astype(F32).reshape(tok_rows, 1)

    qkv_home = jnp.concatenate(
        [
            w_query.reshape(deep, 2, 2 * HEAD_SIZE),
            key_weight_matrix.reshape(deep, 2, HEAD_SIZE),
            value_weight_matrix.reshape(deep, 2, HEAD_SIZE),
        ],
        axis=2,
    )
    tables = angles(block_order, tok_rows)
    normed_all, w_qkv, queries, kv, kv_lo, kv_hi, lin, gate_parts, *parts = gather_qkv(
        normed_rows,
        jnp.transpose(qkv_home, (1, 0, 2)),
        q_gain,
        k_gain,
        tables,
        w_gate,
        w_up,
        w_down.reshape(4, cols, deep),
        w_out.reshape(2, 2 * HEAD_SIZE, deep),
    )
    up_part, down_part, out_part = parts
    out_part = out_part.reshape(width, deep)
    out_parts = [out_part] + [lax.ppermute(out_part, "ctx", [(i, i ^ n) for i in range(8)]) for n in (2, 4, 6)]
    up_parts = lax.all_gather(up_part, "tp", axis=0)
    mixed, lse = attend(block_order, seq_lens, queries, kv_lo, kv, kv_hi, seq_len)
    down_parts = lax.all_gather(down_part, "tp", axis=0)
    middle, post_rows, mixed_rows, w_o = mix(mixed, tokens, post_gain, out_parts)
    post_all, w_gu, slope, active, hidden = gather_up(post_rows, gate_parts, up_parts)
    output, diff_low, diff, error, w_d = scatter_down(hidden, down_parts, middle, teacher, valid)
    d_gu, grad_wd = gather_down_back(diff_low, w_d, slope, active, hidden)
    d_post, grad_gu = scatter_post(d_gu, w_gu, post_all)

    def home_sum(parts):
        return lax.psum_scatter(parts, "tp", scatter_dimension=0, tiled=True)[0]

    grad_down = home_sum(grad_wd)
    grad_gu = home_sum(grad_gu)
    d_mixed, d_middle, grad_post, *grad_wo, grad_down = mix_back(
        d_post, middle, diff, post_gain, w_o, mixed_rows, grad_down
    )
    grad_wo = [grad_wo[0]] + [
        lax.ppermute(grad_wo[m], "ctx", [(i, i ^ n) for i in range(8)]) for m, n in ((1, 2), (2, 4), (3, 6))
    ]

    d_queries, to_lo, d_kv, to_hi = attend_back(
        block_order,
        seq_lens,
        queries,
        d_mixed,
        mixed,
        lse,
        kv_lo,
        kv,
        kv_hi,
        seq_len,
    )
    out_sum = sum(after(g, d_queries[:8]).astype(F32) for g in grad_wo).astype(BF16)
    d_normed, grad_qkv, totals, gu_sum, grad_out = scatter_normed(
        d_queries,
        d_kv,
        to_lo,
        to_hi,
        lin,
        w_qkv,
        normed_all,
        grad_gu,
        out_sum.reshape(4, 4 * HEAD_SIZE, deep),
        tokens,
        grad_post,
        error,
        q_gain,
        k_gain,
        tables,
    )
    d_tokens, grad_gate, grad_up, grad_down, grad_query, grad_key, grad_value, grad_out = finish(
        d_normed, tokens, d_middle, in_gain, gu_sum, grad_down, grad_qkv, grad_out
    )
    lanes = width // HEAD_SIZE
    count_valid = jnp.sum(seq_lens).astype(F32)
    loss = 0.5 * jnp.sum(totals[2 * lanes + 2]) / (count_valid * MODEL_WIDTH)
    return (
        output,
        loss,
        d_tokens,
        totals[:lanes].reshape(width),
        grad_query,
        grad_key,
        grad_value,
        totals[2 * lanes],
        totals[2 * lanes + 1],
        grad_out,
        totals[lanes : 2 * lanes].reshape(width),
        grad_gate,
        grad_up,
        grad_down.reshape(4 * cols, deep),
    )


def solution(mesh):
    in_specs = (
        P(("ctx", "tp"), None),
        P(("ctx", "tp"), None),
        P(),
        P(),
        P(),
        P("ctx", "tp"),
        P("ctx", "tp"),
        P("ctx", "tp"),
        P(),
        P(),
        P("tp", "ctx"),
        P(),
        P("ctx", "tp"),
        P("ctx", "tp"),
        P("tp", "ctx"),
    )
    out_specs = (
        P(("ctx", "tp"), None),
        P(),
        P(("ctx", "tp"), None),
        P(),
        P("ctx", "tp"),
        P("ctx", "tp"),
        P("ctx", "tp"),
        P(),
        P(),
        P("tp", "ctx"),
        P(),
        P("ctx", "tp"),
        P("ctx", "tp"),
        P("tp", "ctx"),
    )
    body = local_plane if (mesh.shape["ctx"], mesh.shape["tp"]) == (8, 4) else local
    return jax.shard_map(body, mesh=mesh, in_specs=in_specs, out_specs=out_specs, check_vma=False)
```
